32 devices in a mesh: seq: 4 (over y, core), fsdp: 8 (over z, x).
Axes of the slice: x: 2, y: 2, z: 4, core: 2. Of those that a mesh axis runs over, the one named last changes fastest.
Arguments:
- tokens: bfloat16 [12288, 896], P(('fsdp', 'seq')), may hold values from -6 to 6
- segment_ids: int32 [12288], P(('fsdp', 'seq')), may hold values from 0 to 23, as said below
- positions: int32 [12288], P(('fsdp', 'seq')), may hold values from 0 to 1533, as said below
- norm_one: bfloat16 [896], P('fsdp'), may hold values from 0.5 to 1.5
- qkv_weight: bfloat16 [896, 1152], P('seq', 'fsdp'), may hold values from -0.1875 to 0.1875
- qkv_bias: bfloat16 [1152], P('fsdp'), may hold values from -3 to 3
- out_weight: bfloat16 [896, 896], P('fsdp', 'seq'), may hold values from -3 to 3
- norm_two: bfloat16 [896], P('fsdp'), may hold values from 0.5 to 1.5
- gate_up_weight: bfloat16 [896, 9728], P('seq', 'fsdp'), may hold values from -0.1875 to 0.1875
- down_weight: bfloat16 [4864, 896], P('fsdp', 'seq'), may hold values from -0.078125 to 0.078125
- cotangent: bfloat16 [12288, 896], P(('fsdp', 'seq')), may hold values from -6 to 6
Outputs:
- layer_out: bfloat16 [12288, 896], P(('fsdp', 'seq'))
- grad_tokens: float32 [12288, 896], P(('fsdp', 'seq'))
- grad_norm_one: float32 [896], P('fsdp')
- grad_qkv_weight: float32 [896, 1152], P('seq', 'fsdp')
- grad_qk_bias: float32 [1024], P('fsdp')
- grad_value_bias: float32 [128], P('fsdp')
- grad_out_weight: float32 [896, 896], P('fsdp', 'seq')
- grad_norm_two: float32 [896], P('fsdp')
- grad_gate_up: float32 [896, 9728], P('seq', 'fsdp')
- grad_down: float32 [4864, 896], P('fsdp', 'seq')
The draws below stay inside these ranges and needn't reach their ends.
Inputs may be any that keep to these rules, and one draw needn't show every extreme that they name: `segment_ids`: the tokens come in aligned groups of 1536 (one index of fsdp each). Group g holds three documents numbered 3 g, 3 g + 1 and 3 g + 2 in order; the first and the last are shorter than 384 tokens and at least one token long. `positions`: each token's place in its document, counted from 0 at the document's first token; in one group the first and the last documents are one token long each.
All inputs are finite; a program needn't handle non-finite values.
Results may differ from the reference program's by a relative error of at most 0.015.
Values may be sent and summed in bfloat16 or wider, within the bound.
No kernel may reach another device: no remote copies, remote signals or barrier semaphores. Data moves between devices by JAX's collectives and lax.ppermute only.
A program may use at most 192 MiB of HBM per device.

```python
import jax
import jax.numpy as jnp
from jax import lax

D = 896
HEADS = 14
KV_HEADS = 2
HEAD = 64
FF = 4864
TOK_DEV = 384
QW = 896
KVW = 128
QKV = 1152
GROUP = 1536
TOKENS = 12288


def documents(key):
    group_count = TOKENS // GROUP
    head_len = jax.random.randint(jax.random.fold_in(key, 11), (group_count,), 1, TOK_DEV)
    tail_len = jax.random.randint(jax.random.fold_in(key, 12), (group_count,), 1, TOK_DEV)
    chosen = jax.random.randint(jax.random.fold_in(key, 13), (), 0, group_count)
    picked = jnp.arange(group_count, dtype=jnp.int32) == chosen
    head_len = jnp.where(picked, 1, head_len)
    tail_len = jnp.where(picked, 1, tail_len)
    index = jnp.arange(GROUP, dtype=jnp.int32)[None, :]
    begin_middle = head_len[:, None]
    begin_last = GROUP - tail_len[:, None]
    piece = (index >= begin_middle).astype(jnp.int32) + (index >= begin_last).astype(jnp.int32)
    starts = jnp.where(piece == 0, 0, jnp.where(piece == 1, begin_middle, begin_last))
    numbers = piece + 3 * jnp.arange(group_count, dtype=jnp.int32)[:, None]
    return (numbers.reshape(-1), (index - starts).reshape(-1).astype(jnp.int32))


def draw_segment_ids(key, part):
    numbers, places = documents(key)
    return numbers


def draw_positions(key, part):
    numbers, places = documents(key)
    return places


def block_scale(rng, extent, split, smallest, top_value):
    def one(dim, blocks):
        heights = jax.random.uniform(jax.random.fold_in(jax.random.fold_in(rng, 6), dim), (blocks,), jnp.float32, smallest / len(split), top_value / len(split))
        return jnp.repeat(jnp.exp(heights), extent[dim] // blocks).reshape((-1,) + (1,) * (len(extent) - dim - 1))

    factor_of = one(*split[0])
    for cut in split[1:]:
        factor_of = factor_of * one(*cut)
    return factor_of


def normal_values(stream_key, extent, width, reach, shards=(), held_as=jnp.bfloat16):
    drawn = width * jax.random.normal(stream_key, extent, jnp.float32)
    if shards:
        drawn = drawn * block_scale(stream_key, extent, shards, -0.22, 0.18)
    return jnp.clip(drawn, -reach, reach).astype(held_as)


def setup_inputs(seed: int = 0) -> dict:
    key_of = jax.random.split(jax.random.key(seed), 12)
    return {
        "tokens": normal_values(key_of[0], (TOKENS, D), 1.0, 6.0, ((0, 32),)),
        "segment_ids": draw_segment_ids(jax.random.fold_in(key_of[11], 71), 0),
        "positions": draw_positions(jax.random.fold_in(key_of[11], 71), 0),
        "norm_one": jnp.clip(1.0 + 0.1 * jax.random.normal(key_of[3], (D,), jnp.float32), 0.5, 1.5).astype(jnp.bfloat16),
        "qkv_weight": normal_values(key_of[4], (D, QKV), D ** -0.5, 0.1875, ((0, 4), (1, 8))),
        "qkv_bias": normal_values(key_of[5], (QKV,), 0.5, 3.0, ((0, 8),)),
        "out_weight": normal_values(key_of[6], (QW, D), 4 ** -0.5, 3.0, ((0, 8), (1, 4))),
        "norm_two": jnp.clip(1.0 + 0.1 * jax.random.normal(key_of[7], (D,), jnp.float32), 0.5, 1.5).astype(jnp.bfloat16),
        "gate_up_weight": normal_values(key_of[8], (D, 2 * FF), D ** -0.5, 0.1875, ((0, 4), (1, 8))),
        "down_weight": normal_values(key_of[9], (FF, D), FF ** -0.5, 0.078125, ((0, 8), (1, 4))),
        "cotangent": normal_values(key_of[10], (TOKENS, D), 1.0, 6.0, ((0, 32),)),
    }


@jax.custom_vjp
def low(v):
    return lax.optimization_barrier(v.astype(jnp.bfloat16)).astype(jnp.float32)

@jax.custom_vjp
def low_back(v):
    return v

def low_keep(v):
    return (low(v), None)

def low_pass(kept, grad):
    return (grad,)

def back_keep(v):
    return (v, None)

def back_low(kept, grad):
    return (low(grad),)
low.defvjp(low_keep, low_pass)
low_back.defvjp(back_keep, back_low)
EPSILON = 1e-06
ROPE_BASE = 1000000.0

def product(left_side, right_side):
    return jnp.dot(left_side, right_side, precision=lax.Precision.HIGHEST)

def rms_scale(values_in):
    return lax.rsqrt(lax.optimization_barrier(jnp.mean(values_in * values_in, axis=-1, keepdims=True)) + EPSILON)

def angles(places):
    exponent = jnp.arange(HEAD // 2, dtype=jnp.float32) * 2.0 / HEAD
    frequency = ROPE_BASE ** (-exponent)
    turn = places.astype(jnp.float32)[:, None] * frequency[None, :]
    turn = jnp.concatenate([turn, turn], axis=-1)
    return (jnp.cos(turn)[:, None, :], jnp.sin(turn)[:, None, :])

def rotate(tensor, cos_table, sine_table):
    half_size = HEAD // 2
    turned = jnp.concatenate([-tensor[..., half_size:], tensor[..., :half_size]], axis=-1)
    return tensor * cos_table + turned * sine_table

def group_layer(params, row_data, seg_data, pos_data):
    norm_one, qkv_weight, qkv_bias, out_weight, norm_two, gate_up_weight, down_weight = params
    row_count = row_data.shape[0]
    normed_one = low(row_data * rms_scale(row_data) * norm_one)
    joined = low_back(product(normed_one, qkv_weight) + qkv_bias)
    cos_table, sine_table = angles(pos_data)
    queries = low(rotate(joined[:, :QW].reshape(row_count, HEADS, HEAD), cos_table, sine_table))
    keys_all = low(rotate(joined[:, QW:QW + KVW].reshape(row_count, KV_HEADS, HEAD), cos_table, sine_table))
    values_all = low(joined[:, QW + KVW:].reshape(row_count, KV_HEADS, HEAD))
    allowed = (seg_data[:, None] == seg_data[None, :]) & (pos_data[None, :] <= pos_data[:, None])
    head_share = HEADS // KV_HEADS

    def one_head(head_index):
        query_block = queries[:, head_index]
        key_block = keys_all[:, head_index // head_share]
        value_block = values_all[:, head_index // head_share]
        scores = low_back(product(query_block, key_block.T) * 0.125)
        scores = jnp.where(allowed, scores, -jnp.inf)
        max_score = lax.optimization_barrier(jnp.max(scores, axis=1, keepdims=True))
        exp_score = jnp.exp(scores - max_score)
        attn_probs = exp_score / lax.optimization_barrier(jnp.sum(exp_score, axis=1, keepdims=True))
        return product(low(attn_probs), value_block)
    head_out = lax.map(jax.checkpoint(one_head), jnp.arange(HEADS))
    attn_flat = low(low_back(jnp.transpose(head_out, (1, 0, 2)).reshape(row_count, QW)))
    residual = row_data + low_back(product(attn_flat, out_weight))
    normed_two = low(residual * rms_scale(residual) * norm_two)
    gate_up = low_back(product(normed_two, gate_up_weight))
    gate_part = gate_up[:, :FF]
    hidden = low(gate_part * jax.nn.sigmoid(gate_part) * gate_up[:, FF:])
    return residual + low_back(product(hidden, down_weight))

def reference(tokens, segment_ids, positions, norm_one, qkv_weight, qkv_bias, out_weight, norm_two, gate_up_weight, down_weight, cotangent):
    params = (norm_one.astype(jnp.float32), qkv_weight.astype(jnp.float32), qkv_bias.astype(jnp.float32), out_weight.astype(jnp.float32), norm_two.astype(jnp.float32), gate_up_weight.astype(jnp.float32), down_weight.astype(jnp.float32))
    group_count = TOKENS // GROUP
    row_groups = tokens.astype(jnp.float32).reshape(group_count, GROUP, D)
    seg_groups = segment_ids.reshape(group_count, GROUP)
    pos_groups = positions.reshape(group_count, GROUP)

    def forward(weights_in, rows_in):

        def per_group(group_item):
            return group_layer(weights_in, group_item[0], group_item[1], group_item[2])
        return lax.map(jax.checkpoint(per_group), (rows_in, seg_groups, pos_groups))
    layer_out, pullback = jax.vjp(forward, params, row_groups)
    weight_grads, grad_rows = pullback(cotangent.astype(jnp.float32).reshape(group_count, GROUP, D))
    bias_grad = weight_grads[2]
    return (layer_out.reshape(TOKENS, D).astype(jnp.bfloat16), grad_rows.reshape(TOKENS, D), weight_grads[0], weight_grads[1], bias_grad[:QW + KVW], bias_grad[QW + KVW:], weight_grads[3], weight_grads[4], weight_grads[5], weight_grads[6])
```

```python
import functools

import jax
import jax.numpy as jnp
from jax import lax
from jax.experimental import pallas as pl
from jax.experimental.pallas import tpu as pltpu
from jax.sharding import PartitionSpec as P

HEADS = 14
KV_HEADS = 2
HEAD = 64
FF = 4864
QW = 896
KVW = 128
PAIR = 2 * HEAD
PAIRS = HEADS // 2
OUTER = 4

EPSILON = 1e-06
ROPE_BASE = 1000000.0
MASKED = -1e30
VMEM_LIMIT = 50 * 1024 * 1024

F32 = jnp.float32
BF16 = jnp.bfloat16


def dot(left, right, left_dim, right_dim):
    return lax.dot_general(
        left, right, (((left_dim,), (right_dim,)), ((), ())), preferred_element_type=F32
    )


def swap(block, axis, size, bits):
    return lax.ppermute(block, axis, [(i, i ^ bits) for i in range(size)])


def seq_gather(block, size):
    blocks = {0: block}
    bit = size // 2
    while bit:
        blocks.update({o ^ bit: swap(b, "seq", size, bit) for o, b in blocks.items()})
        bit //= 2
    return blocks


def seq_scatter(stack, size, me):
    bit = 1
    while bit < size:
        cut = stack.reshape((size // (2 * bit), 2) + stack.shape[1:])
        digit = (me // bit) % 2
        given = lax.dynamic_index_in_dim(cut, 1 - digit, 1, keepdims=False)
        kept = lax.dynamic_index_in_dim(cut, digit, 1, keepdims=False)
        stack = kept.astype(F32) + swap(given.astype(BF16), "seq", size, bit).astype(F32)
        bit *= 2
    return stack[0]


def kv_sum(stack, size):
    parts = [stack[o] for o in range(size)]
    bit = 1
    while bit < size:
        for o in range(0, size, 2 * bit):
            got = swap(parts[o + bit].astype(BF16), "seq", size, bit)
            parts[o] = parts[o].astype(F32) + got.astype(F32)
        bit *= 2
    return parts[0]


def fsdp_gather(block, size):
    blocks = {0: block}
    inner = size // OUTER
    for k in range(1, OUTER):
        blocks[k * inner] = swap(block, "fsdp", size, k * inner)
    for m in range(1, inner):
        for k in range(OUTER):
            blocks[k * inner + m] = swap(blocks[k * inner], "fsdp", size, m)
    return blocks


def fsdp_gather_small(block, size):
    inner = size // OUTER
    column = jnp.stack([block] + [swap(block, "fsdp", size, k * inner) for k in range(1, OUTER)])
    columns = [column] + [swap(column, "fsdp", size, m) for m in range(1, inner)]
    return jnp.stack(columns, axis=1).reshape((size,) + block.shape)


def fsdp_scatter(stack, size, me):
    inner = size // OUTER
    my_outer, my_inner = me // inner, me % inner
    cut = stack.reshape((OUTER, inner) + stack.shape[1:])

    def column(index):
        return lax.dynamic_index_in_dim(cut, index, 1, keepdims=False)

    total = column(my_inner).astype(F32)
    for m in range(1, inner):
        got = swap(column(my_inner ^ m).astype(BF16), "fsdp", size, m)
        total = total + got.astype(F32)
    low = total.astype(BF16)
    mine = lax.dynamic_index_in_dim(total, my_outer, 0, keepdims=False)
    for k in range(1, OUTER):
        given = lax.dynamic_index_in_dim(low, my_outer ^ k, 0, keepdims=False)
        mine = mine + swap(given, "fsdp", size, k * inner).astype(F32)
    return mine


def on_device(body, name, out_shapes, scratch, me, arrays):
    vmem = pl.BlockSpec(memory_space=pltpu.VMEM)
    return pl.pallas_call(
        body,
        in_specs=[pl.BlockSpec(memory_space=pltpu.SMEM)] + [vmem] * len(arrays),
        out_specs=[vmem] * len(out_shapes),
        out_shape=out_shapes,
        scratch_shapes=scratch,
        compiler_params=pltpu.CompilerParams(vmem_limit_bytes=VMEM_LIMIT),
        name=name,
    )(me, *arrays)


def padded(rows):
    return -(-rows // 16) * 16


def cut_ff(me, gate_up_weight, down_weight, size):
    width = gate_up_weight.shape[0]
    half = down_weight.shape[0]
    strip = half // size
    tall = padded(strip)

    def body(me_ref, gu_ref, d_ref, *refs):
        outs, held = refs[:size], refs[size]
        turned = gu_ref[...].astype(F32).T
        down = d_ref[...].astype(F32)
        blank = jnp.zeros((tall - strip, width), F32)
        for q in range(size):
            one = turned[q * strip : (q + 1) * strip]
            two = turned[half + q * strip : half + (q + 1) * strip]
            three = down[q * strip : (q + 1) * strip]
            parts = [one, blank, two, blank, three, blank]
            held[q] = jnp.concatenate(parts, axis=0).astype(BF16)
        for o in range(size):
            outs[o][...] = held[me_ref[0] ^ o]

    shape = jax.ShapeDtypeStruct((3 * tall, width), BF16)
    scratch = [pltpu.VMEM((size, 3 * tall, width), BF16)]
    return on_device(body, "cut_ff", [shape] * size, scratch, me, (gate_up_weight, down_weight))


def join_lanes(me, blocks):
    size = len(blocks)
    rows, width = blocks[0].shape

    def body(me_ref, *refs):
        ins, out, held = refs[:size], refs[size], refs[size + 1]
        for o in range(size):
            held[me_ref[0] ^ o] = ins[o][...]
        out[...] = jnp.concatenate([held[q].astype(F32) for q in range(size)], 1).astype(BF16)

    return on_device(
        body,
        "join_lanes",
        [jax.ShapeDtypeStruct((rows, size * width), BF16)],
        [pltpu.VMEM((size, rows, width), BF16)],
        me,
        blocks,
    )[0]


def join_qkv(me, blocks, rows):
    size = len(blocks)
    count, tall, width = blocks[0].shape

    def body(me_ref, *refs):
        ins, out, vectors, held = refs[:size], refs[size], refs[size + 1], refs[size + 2]
        for o in range(size):
            held[me_ref[0] ^ o] = ins[o][...]
        for f in range(count):
            parts = [held[q, f, :rows].astype(F32) for q in range(size)]
            out[me_ref[1] ^ f] = jnp.concatenate(parts, axis=1).astype(BF16)
            vectors[me_ref[1] ^ f] = ins[0][f, rows:]

    return on_device(
        body,
        "join_qkv",
        [
            jax.ShapeDtypeStruct((count, rows, size * width), BF16),
            jax.ShapeDtypeStruct((count, tall - rows, width), BF16),
        ],
        [pltpu.VMEM((size, count, tall, width), BF16)],
        me,
        blocks,
    )


def cut_lanes(me, sums, size):
    rows = sum(s.shape[0] for s in sums)
    width = sums[0].shape[1] // size

    def body(me_ref, *refs):
        ins, outs, held = refs[: len(sums)], refs[len(sums) : -1], refs[-1]
        whole = jnp.concatenate([r[...] for r in ins], axis=0)
        for q in range(size):
            held[q] = whole[:, q * width : (q + 1) * width].astype(BF16)
        for o in range(size):
            outs[o][...] = held[me_ref[0] ^ o]

    shape = jax.ShapeDtypeStruct((rows, width), BF16)
    scratch = [pltpu.VMEM((size, rows, width), BF16)]
    return on_device(body, "cut_lanes", [shape] * size, scratch, me, sums)


def join_ff(me, blocks, strip):
    size = len(blocks)
    rows, width = blocks[0].shape
    tall = rows // 3

    def body(me_ref, *refs):
        ins, gu, down, held = refs[:size], refs[size], refs[size + 1], refs[size + 2]
        for o in range(size):
            held[me_ref[0] ^ o] = ins[o][...].astype(F32)
        cut = [
            [held[q, i * tall : i * tall + strip] for q in range(size)] for i in range(3)
        ]
        gu[...] = jnp.concatenate(cut[0] + cut[1], axis=0).T
        down[...] = jnp.concatenate(cut[2], axis=0)

    return on_device(
        body,
        "join_ff",
        [
            jax.ShapeDtypeStruct((width, 2 * size * strip), F32),
            jax.ShapeDtypeStruct((size * strip, width), F32),
        ],
        [pltpu.VMEM((size, rows, width), F32)],
        me,
        blocks,
    )


def feed_forward(me, weight_blocks, row_blocks, cot_all):
    count, size = len(weight_blocks), len(row_blocks)
    rows, width = row_blocks[0].shape
    tall = weight_blocks[0].shape[0] // 3
    units = count * tall
    step_units = 256

    def body(me_ref, *refs):
        blocks, xs = refs[:count], refs[count : count + size]
        g_ref = refs[count + size]
        hid, gg, gu, gn, part, x_out = refs[count + size + 1 : count + size + 7]
        gu_w, d_w, x_all, sems = refs[count + size + 7 :]
        step = pl.program_id(0)

        @pl.when(step == 0)
        def _():
            copies = []
            for o in range(count):
                f = me_ref[1] ^ o
                copies.append((blocks[o].at[pl.ds(0, 2 * tall)], gu_w.at[f]))
                copies.append((blocks[o].at[pl.ds(2 * tall, tall)], d_w.at[f]))
            for o in range(size):
                copies.append((xs[o], x_all.at[me_ref[0] ^ o]))
            started = [
                pltpu.make_async_copy(src, dst, sems.at[i]) for i, (src, dst) in enumerate(copies)
            ]
            for copy in started:
                copy.start()
            for copy in started:
                copy.wait()

        x = x_all[step]
        g = g_ref[...]
        x_out[...] = x
        gate_w = gu_w[: count // 2].reshape(units, width)
        up_w = gu_w[count // 2 :].reshape(units, width)
        down_w = d_w[...].reshape(units, width)
        for begin in range(0, units, step_units):
            at = slice(begin, begin + step_units)
            gate = dot(x, gate_w[at], 1, 1)
            up = dot(x, up_w[at], 1, 1)
            grad_hidden = dot(g, down_w[at], 1, 1)
            sigmoid = 0.5 * jnp.tanh(0.5 * gate) + 0.5
            silu = gate * sigmoid
            hid[:, at] = (silu * up).astype(BF16)
            gg[:, at] = (grad_hidden * up * (sigmoid + silu * (1.0 - sigmoid))).astype(BF16)
            gu[:, at] = (grad_hidden * silu).astype(BF16)
        gn[...] = (dot(gg[...], gate_w, 1, 0) + dot(gu[...], up_w, 1, 0)).astype(BF16)
        part[...] = dot(hid[...], down_w, 1, 0).astype(BF16)

    hbm = pl.BlockSpec(memory_space=pl.ANY)
    by_rows = lambda n: pl.BlockSpec((rows, n), lambda i: (i, 0))
    like = lambda n: jax.ShapeDtypeStruct((size * rows, n), BF16)
    return pl.pallas_call(
        body,
        grid=(size,),
        in_specs=[pl.BlockSpec(memory_space=pltpu.SMEM)]
        + [hbm] * (count + size)
        + [by_rows(width)],
        out_specs=[by_rows(units)] * 3 + [by_rows(width)] * 3,
        out_shape=[like(units)] * 3 + [like(width)] * 3,
        scratch_shapes=[
            pltpu.VMEM((count, 2 * tall, width), BF16),
            pltpu.VMEM((count, tall, width), BF16),
            pltpu.VMEM((size, rows, width), BF16),
            pltpu.SemaphoreType.DMA((2 * count + size,)),
        ],
        compiler_params=pltpu.CompilerParams(vmem_limit_bytes=VMEM_LIMIT),
        cost_estimate=pl.CostEstimate(
            flops=12 * size * rows * units * width,
            bytes_accessed=2 * (3 * units * width + size * rows * (3 * units + 5 * width)),
            transcendentals=size * rows * units,
        ),
        name="feed_forward",
    )(me, *weight_blocks, *row_blocks, cot_all)


def both_heads(pair):
    lane = lax.broadcasted_iota(jnp.int32, pair.shape, 1)
    zero = jnp.zeros_like(pair)
    return jnp.concatenate(
        [jnp.where(lane < HEAD, pair, zero), jnp.where(lane < HEAD, zero, pair)], axis=0
    )


def fill_bias(low_ref, high_ref, place_ref, bias_ref):
    place = place_ref[...]
    allowed = (place >= low_ref[...]) & (place <= high_ref[...])
    bias = jnp.where(allowed, 0.0, MASKED).astype(F32)
    rows = bias.shape[1]
    bias_ref[:, :rows] = bias
    bias_ref[:, rows:] = bias


def own_rows(wide, rows):
    return jnp.concatenate([wide[:HEAD, :rows], wide[HEAD:, rows:]], axis=0)


def attend_kernel(low_ref, high_ref, place_ref, q_ref, k_ref, vt_ref, o_ref, lse_ref, bias_ref):
    @pl.when(pl.program_id(0) == 0)
    def _():
        fill_bias(low_ref, high_ref, place_ref, bias_ref)

    rows = q_ref.shape[0]
    queries = both_heads(q_ref[...])
    keys = k_ref[0]
    values_t = vt_ref[0]
    outs, totals = [], []
    for begin in range(0, 2 * rows, 256):
        scores = dot(keys, queries[begin : begin + 256], 1, 1) + bias_ref[:, begin : begin + 256]
        top = jnp.max(scores, axis=0, keepdims=True)
        probs = jnp.exp(scores - top)
        total = jnp.sum(probs, axis=0, keepdims=True)
        outs.append(dot(values_t, probs.astype(BF16), 1, 0) / total)
        totals.append(top + jnp.log(total))
    wide = jnp.concatenate(outs, axis=1)
    o_ref[...] = own_rows(wide, rows).T.astype(BF16)
    lse_ref[0] = jnp.concatenate(totals, axis=1)


def attend_back_kernel(
    low_ref, high_ref, place_ref, q_ref, g_ref, o_ref, lse_ref, k_ref, kt_ref, v_ref,
    dq_ref, dk_ref, dv_ref, bias_ref,
):
    step = pl.program_id(0)

    @pl.when(step == 0)
    def _():
        fill_bias(low_ref, high_ref, place_ref, bias_ref)

    @pl.when((step == 0) | (step == PAIRS // 2) | (step == PAIRS // 2 + 1))
    def _():
        dk_ref[...] = jnp.zeros_like(dk_ref)
        dv_ref[...] = jnp.zeros_like(dv_ref)

    rows = q_ref.shape[0]
    queries = both_heads(q_ref[...])
    grads = both_heads(g_ref[...])
    keys = k_ref[0]
    keys_t = kt_ref[0]
    values = v_ref[0]
    product = (g_ref[...].astype(F32) * o_ref[...].astype(F32)).T
    delta = jnp.concatenate(
        [
            jnp.sum(product[:HEAD], axis=0, keepdims=True),
            jnp.sum(product[HEAD:], axis=0, keepdims=True),
        ],
        axis=1,
    )
    lse = lse_ref[0]
    outs = []
    for begin in range(0, 2 * rows, 256):
        part = slice(begin, begin + 256)
        scores = dot(keys, queries[part], 1, 1) + bias_ref[:, part]
        probs = jnp.exp(scores - lse[:, part])
        grad_probs = dot(values, grads[part], 1, 1)
        grad_scores = (probs * (grad_probs - delta[:, part])).astype(BF16)
        outs.append(dot(keys_t, grad_scores, 1, 0))
        dk_ref[0] += dot(grad_scores, queries[part], 1, 0)
        dv_ref[0] += dot(probs.astype(BF16), grads[part], 1, 0)
    wide = jnp.concatenate(outs, axis=1)
    dq_ref[...] = own_rows(wide, rows).T * 0.125


def variant(step):
    half = PAIRS // 2
    return jnp.where(step < half, 0, jnp.where(step == half, 1, 2))


def attend(low, high, place, queries, pair_keys, pair_values_t):
    rows, count = queries.shape[0], pair_keys.shape[1]
    whole = lambda shape: pl.BlockSpec(shape, lambda i: (0,) * len(shape))
    pair = pl.BlockSpec((rows, PAIR), lambda i: (0, i))
    return pl.pallas_call(
        attend_kernel,
        grid=(PAIRS,),
        in_specs=[
            whole((1, rows)),
            whole((1, rows)),
            whole((count, 1)),
            pair,
            pl.BlockSpec((1, count, PAIR), lambda i: (variant(i), 0, 0)),
            pl.BlockSpec((1, PAIR, count), lambda i: (variant(i), 0, 0)),
        ],
        out_specs=[pair, pl.BlockSpec((1, 1, 2 * rows), lambda i: (i, 0, 0))],
        out_shape=[
            jax.ShapeDtypeStruct((rows, QW), BF16),
            jax.ShapeDtypeStruct((PAIRS, 1, 2 * rows), F32),
        ],
        scratch_shapes=[pltpu.VMEM((count, 2 * rows), F32)],
        compiler_params=pltpu.CompilerParams(vmem_limit_bytes=VMEM_LIMIT),
        cost_estimate=pl.CostEstimate(
            flops=4 * HEADS * rows * count * PAIR,
            bytes_accessed=4 * rows * QW + 1024 * count,
            transcendentals=HEADS * rows * count,
        ),
        name="attend",
    )(low, high, place, queries, pair_keys, pair_values_t)


def attend_back(low, high, place, queries, grads, outs, lse, pair_keys, pair_keys_t, pair_values):
    rows, count = queries.shape[0], pair_keys.shape[1]
    whole = lambda shape: pl.BlockSpec(shape, lambda i: (0,) * len(shape))
    pair = pl.BlockSpec((rows, PAIR), lambda i: (0, i))
    tall = pl.BlockSpec((1, count, PAIR), lambda i: (variant(i), 0, 0))
    return pl.pallas_call(
        attend_back_kernel,
        grid=(PAIRS,),
        in_specs=[
            whole((1, rows)),
            whole((1, rows)),
            whole((count, 1)),
            pair,
            pair,
            pair,
            pl.BlockSpec((1, 1, 2 * rows), lambda i: (i, 0, 0)),
            tall,
            pl.BlockSpec((1, PAIR, count), lambda i: (variant(i), 0, 0)),
            tall,
        ],
        out_specs=[pair, tall, tall],
        out_shape=[
            jax.ShapeDtypeStruct((rows, QW), F32),
            jax.ShapeDtypeStruct((3, count, PAIR), F32),
            jax.ShapeDtypeStruct((3, count, PAIR), F32),
        ],
        scratch_shapes=[pltpu.VMEM((count, 2 * rows), F32)],
        compiler_params=pltpu.CompilerParams(vmem_limit_bytes=VMEM_LIMIT),
        cost_estimate=pl.CostEstimate(
            flops=10 * HEADS * rows * count * PAIR,
            bytes_accessed=8 * rows * QW + 4096 * count,
            transcendentals=HEADS * rows * count,
        ),
        name="attend_back",
    )(low, high, place, queries, grads, outs, lse, pair_keys, pair_keys_t, pair_values)


def pair_up(heads):
    one, two = heads[:, :HEAD], heads[:, HEAD:]
    return jnp.stack(
        [jnp.concatenate([one, one], 1), heads, jnp.concatenate([two, two], 1)]
    )


def unpair(sums):
    one = sums[0, :, :HEAD] + sums[0, :, HEAD:] + sums[1, :, :HEAD]
    two = sums[2, :, :HEAD] + sums[2, :, HEAD:] + sums[1, :, HEAD:]
    return jnp.concatenate([one, two], axis=1)


def rms_scale(values_in):
    return lax.rsqrt(jnp.mean(values_in * values_in, axis=-1, keepdims=True) + EPSILON)


def angle_tables(places):
    exponent = jnp.arange(HEAD // 2, dtype=F32) * 2.0 / HEAD
    frequency = ROPE_BASE ** (-exponent)
    turn = places.astype(F32)[:, None] * frequency[None, :]
    cosine, sine = lax.optimization_barrier((jnp.cos(turn), jnp.sin(turn)))
    return jnp.concatenate([cosine] * 4, axis=1), jnp.concatenate([sine] * 4, axis=1)


def widen(table, width):
    return jnp.concatenate([table] * (width // PAIR), axis=1)


def first_halves(shape):
    return lax.broadcasted_iota(jnp.int32, shape, 1) % HEAD < HEAD // 2


def rotate(tensor, cosine, sine):
    half = HEAD // 2
    ahead, behind = jnp.roll(tensor, -half, axis=1), jnp.roll(tensor, half, axis=1)
    turned = jnp.where(first_halves(tensor.shape), -ahead, behind)
    width = tensor.shape[1]
    return tensor * widen(cosine, width) + turned * widen(sine, width)


def rotate_back(grad_in, cosine, sine):
    half = HEAD // 2
    width = grad_in.shape[1]
    scaled = grad_in * widen(sine, width)
    ahead, behind = jnp.roll(scaled, -half, axis=1), jnp.roll(scaled, half, axis=1)
    return grad_in * widen(cosine, width) + jnp.where(
        first_halves(grad_in.shape), ahead, -behind
    )


def norm_back(grad_in, row_data, scale_in, gain_in):
    gain_term = jnp.sum(grad_in * row_data * scale_in, axis=0)
    grad_normed = grad_in * gain_in
    inner_mean = jnp.mean(grad_normed * row_data, axis=-1, keepdims=True)
    return (
        scale_in * grad_normed - row_data * scale_in * scale_in * scale_in * inner_mean,
        gain_term,
    )


def pad_row(vector, width):
    return jnp.pad(vector, (0, width - vector.shape[0]))[None, :]


def lanes_from_stack(stack):
    count, rows, width = stack.shape
    return jnp.transpose(stack, (1, 0, 2)).reshape(rows, count * width)


def stack_from_lanes(array, count):
    rows, width = array.shape
    return jnp.transpose(array.reshape(rows, count, width // count), (1, 0, 2))


def per_device(
    seq_size, fsdp_size, tokens, segment_ids, positions, norm_one, qkv_weight, qkv_bias,
    out_weight, norm_two, gate_up_weight, down_weight, cotangent,
):
    my_seq, my_fsdp = lax.axis_index("seq"), lax.axis_index("fsdp")
    me = jnp.stack([my_seq, my_fsdp]).astype(jnp.int32)
    offsets = range(seq_size)
    row_count = tokens.shape[0]
    width = qkv_weight.shape[0]
    qkv_rows = qkv_weight.shape[1]
    strip = down_weight.shape[0] // seq_size
    tall = padded(strip)

    ff_cut = cut_ff(me, gate_up_weight, down_weight, seq_size)
    ff_share = [ff_cut[0]] + [swap(ff_cut[o], "seq", seq_size, o) for o in offsets if o]
    ff_blocks = fsdp_gather(join_lanes(me, ff_share), fsdp_size)
    ff_blocks = [ff_blocks[o] for o in range(fsdp_size)]

    qkv_tall = padded(qkv_rows)
    packed = jnp.concatenate(
        [
            jnp.pad(qkv_weight.T, ((0, qkv_tall - qkv_rows), (0, 0))),
            pad_row(norm_one, width),
            pad_row(qkv_bias, width),
            pad_row(norm_two, width),
            jnp.zeros((13, width), BF16),
        ],
        axis=0,
    )
    packed_blocks = seq_gather(fsdp_gather_small(packed, fsdp_size), seq_size)
    qkv_t, vectors = join_qkv(me, [packed_blocks[o] for o in offsets], qkv_tall)
    qkv_t = qkv_t[:, :qkv_rows].reshape(fsdp_size * qkv_rows, -1)
    gain_one = vectors[:, 0, : norm_one.shape[0]].reshape(-1).astype(F32)
    bias_full = vectors[:, 1, : qkv_bias.shape[0]].reshape(-1).astype(F32)
    gain_two = vectors[:, 2, : norm_two.shape[0]].reshape(-1).astype(F32)

    out_part = lax.all_gather(out_weight, "fsdp", axis=0, tiled=True)
    out_full = lanes_from_stack(lax.all_gather(out_part, "seq", axis=0, tiled=False))
    cot_all = lax.all_gather(cotangent, "seq", axis=0, tiled=True)

    inputs = tokens.astype(F32)
    scale_one = rms_scale(inputs)
    normed_one = (inputs * scale_one * gain_one).astype(BF16)
    joined = dot(normed_one, qkv_t, 1, 1) + bias_full
    cosine, sine = angle_tables(positions)
    turned = rotate(joined[:, : QW + KVW], cosine, sine).astype(BF16)
    queries = turned[:, :QW] * jnp.asarray(0.125, BF16)
    kv_local = jnp.concatenate([turned[:, QW:], joined[:, QW + KVW :].astype(BF16)], axis=1)
    kv_blocks = seq_gather(kv_local, seq_size)
    kv_all = jnp.concatenate([kv_blocks[o] for o in offsets], axis=0)
    row_place = jnp.arange(row_count, dtype=jnp.int32)
    high = my_seq * row_count + row_place
    low = high - positions
    place = jnp.concatenate([(my_seq ^ o) * row_count + row_place for o in offsets])[:, None]
    low, high = low[None, :], high[None, :]
    pair_keys = pair_up(kv_all[:, :KVW])
    pair_values = pair_up(kv_all[:, KVW:])
    pair_keys_t = jnp.transpose(pair_keys, (0, 2, 1))
    pair_values_t = jnp.transpose(pair_values, (0, 2, 1))
    attn_flat, lse = attend(low, high, place, queries, pair_keys, pair_values_t)

    residual = inputs + dot(attn_flat, out_full, 1, 0)
    scale_two = rms_scale(residual)
    normed_two = (residual * scale_two * gain_two).astype(BF16)
    normed_blocks = seq_gather(normed_two, seq_size)
    hidden, grad_gate, grad_up, grad_normed, layer_part, normed_all = feed_forward(
        me, ff_blocks, [normed_blocks[o] for o in offsets], cot_all
    )
    by_seq = lambda rows: rows.reshape(seq_size, row_count, -1)
    grad_normed_two = seq_scatter(by_seq(grad_normed), seq_size, my_seq)
    down_term = dot(hidden, cot_all, 0, 0).astype(BF16).reshape(fsdp_size, tall, -1)
    gate_term = dot(grad_gate, normed_all, 0, 0).astype(BF16).reshape(fsdp_size // 2, 2, tall, -1)
    up_term = dot(grad_up, normed_all, 0, 0).astype(BF16).reshape(fsdp_size // 2, 2, tall, -1)
    chunks = [down_term] + [
        jnp.concatenate([gate_term[:, i], up_term[:, i]], axis=0) for i in range(2)
    ]
    down_sum, one_sum, two_sum = [fsdp_scatter(c, fsdp_size, my_fsdp) for c in chunks]
    layer_out = residual + seq_scatter(by_seq(layer_part), seq_size, my_seq)

    ff_back = cut_lanes(me, (one_sum, two_sum, down_sum), seq_size)
    ff_got = [ff_back[0]] + [swap(ff_back[o], "seq", seq_size, o) for o in offsets if o]
    grad_gate_up, grad_down = join_ff(me, ff_got, strip)

    grad_path, norm_two_term = norm_back(grad_normed_two, residual, scale_two, gain_two)
    grad_residual = cotangent.astype(F32) + grad_path
    grad_branch = grad_residual.astype(BF16)
    grad_attn = dot(grad_branch, out_full, 1, 1).astype(BF16)
    out_term = stack_from_lanes(dot(attn_flat, grad_branch, 0, 0).astype(BF16), seq_size)
    out_mine = seq_scatter(out_term, seq_size, my_seq).reshape(fsdp_size, -1, width)
    grad_queries, key_sums, value_sums = attend_back(
        low, high, place, queries, grad_attn, attn_flat, lse, pair_keys, pair_keys_t, pair_values
    )
    kv_terms = jnp.concatenate([unpair(key_sums), unpair(value_sums)], axis=1)
    kv_mine = kv_sum(by_seq(kv_terms), seq_size)
    turned_back = rotate_back(
        jnp.concatenate([grad_queries, kv_mine[:, :KVW]], axis=1), cosine, sine
    )
    grad_joined = jnp.concatenate([turned_back, kv_mine[:, KVW:]], axis=1).astype(BF16)
    grad_normed_one = dot(grad_joined, qkv_t, 1, 0)
    grad_path_one, norm_one_term = norm_back(grad_normed_one, inputs, scale_one, gain_one)
    grad_tokens = grad_residual + grad_path_one
    bias_term = jnp.sum(grad_joined.astype(F32), axis=0)

    def vector_rows(vector):
        rows = vector.reshape(fsdp_size, 1, -1)
        return jnp.pad(rows, ((0, 0), (0, 0), (0, width - rows.shape[2])))

    vector_terms = [norm_one_term, bias_term[: QW + KVW], bias_term[QW + KVW :], norm_two_term]
    small = jnp.concatenate([vector_rows(v) for v in vector_terms], axis=1).astype(BF16)
    small = jnp.pad(small, ((0, 0), (0, 16 - len(vector_terms)), (0, 0)))
    qkv_term = stack_from_lanes(dot(grad_joined, normed_one, 0, 0).astype(BF16), seq_size)
    qkv_term = qkv_term.reshape(seq_size, fsdp_size, qkv_rows, width)
    tail = jnp.concatenate(
        [qkv_term, jnp.broadcast_to(small[None], (seq_size,) + small.shape)], axis=2
    )
    tail_mine = seq_scatter(tail, seq_size, my_seq)
    tail_sum = fsdp_scatter(
        jnp.concatenate([tail_mine, out_mine], axis=1), fsdp_size, my_fsdp
    )
    pieces = [
        tail_sum[qkv_rows + i, : v.shape[0] // fsdp_size] for i, v in enumerate(vector_terms)
    ]
    return (
        layer_out.astype(BF16),
        grad_tokens,
        pieces[0],
        tail_sum[:qkv_rows].T,
        pieces[1],
        pieces[2],
        tail_sum[qkv_rows + 16 :],
        pieces[3],
        grad_gate_up,
        grad_down,
    )


def solution(mesh):
    rows, both = P(("fsdp", "seq"), None), P(("fsdp", "seq"))
    return jax.shard_map(
        functools.partial(per_device, mesh.shape["seq"], mesh.shape["fsdp"]),
        mesh=mesh,
        in_specs=(
            rows, both, both, P("fsdp"), P("seq", "fsdp"), P("fsdp"), P("fsdp", "seq"),
            P("fsdp"), P("seq", "fsdp"), P("fsdp", "seq"), rows,
        ),
        out_specs=(
            rows, rows, P("fsdp"), P("seq", "fsdp"), P("fsdp"), P("fsdp"), P("fsdp", "seq"),
            P("fsdp"), P("seq", "fsdp"), P("fsdp", "seq"),
        ),
        check_vma=False,
    )
```

```python
import functools

import jax
import jax.numpy as jnp
from jax import lax
from jax.experimental import pallas as pl
from jax.experimental.pallas import tpu as pltpu
from jax.sharding import PartitionSpec as P

HEADS = 14
KV_HEADS = 2
HEAD = 64
FF = 4864
QW = 896
KVW = 128
PAIR = 2 * HEAD
PAIRS = HEADS // 2
OUTER = 4

EPSILON = 1e-06
ROPE_BASE = 1000000.0
MASKED = -1e30
VMEM_LIMIT = 50 * 1024 * 1024

F32 = jnp.float32
BF16 = jnp.bfloat16


def dot(left, right, left_dim, right_dim):
    return lax.dot_general(
        left, right, (((left_dim,), (right_dim,)), ((), ())), preferred_element_type=F32
    )


def swap(block, axis, size, bits):
    return lax.ppermute(block, axis, [(i, i ^ bits) for i in range(size)])


def after(array, *others):
    return lax.optimization_barrier((array,) + others)[0]


def seq_gather(block, size):
    blocks = {0: block}
    bit = size // 2
    while bit:
        blocks.update({o ^ bit: swap(b, "seq", size, bit) for o, b in blocks.items()})
        bit //= 2
    return blocks


def fsdp_bits(size):
    inner = size // OUTER
    outer_bits, inner_bits = [], []
    bit = 1
    while bit < size:
        (outer_bits if bit >= inner else inner_bits).append(bit)
        bit *= 2
    return outer_bits + inner_bits


def fsdp_gather_small(block, size):
    stack, offsets = block[None], [0]
    for bit in fsdp_bits(size):
        stack = jnp.concatenate([stack, swap(stack, "fsdp", size, bit)], axis=0)
        offsets = offsets + [o ^ bit for o in offsets]
    return stack, offsets


def halve(stack, bit, me):
    above = stack.shape[0] // (2 * bit)
    cut = stack.reshape((above, 2, bit) + stack.shape[1:])
    digit = (me // bit) % 2
    kept = lax.dynamic_index_in_dim(cut, digit, 1, keepdims=False)
    given = lax.dynamic_index_in_dim(cut, 1 - digit, 1, keepdims=False)
    merge = lambda part: part.reshape((above * bit,) + stack.shape[1:])
    return merge(kept), merge(given).astype(BF16)


def add(kept, got):
    return kept.astype(F32) + got.astype(F32)


def seq_scatter(stack, size, me):
    bit = 1
    while bit < size:
        kept, given = halve(stack, 1, me // bit)
        stack = add(kept, swap(given, "seq", size, bit))
        bit *= 2
    return stack[0]


def fsdp_halve(stack, size, bit, me, resolved):
    place = bit
    digit = me // bit
    for taken in resolved:
        if taken < bit:
            place //= 2
    kept, given = halve(stack, place, digit * place)
    return kept, given


def fsdp_scatter(stack, size, me):
    resolved = []
    for bit in reversed(fsdp_bits(size)):
        kept, given = fsdp_halve(stack, size, bit, me, resolved)
        stack = add(kept, swap(given, "fsdp", size, bit))
        resolved.append(bit)
    return stack[0]


def on_device(body, name, out_shapes, scratch, me, arrays):
    vmem = pl.BlockSpec(memory_space=pltpu.VMEM)
    return pl.pallas_call(
        body,
        in_specs=[pl.BlockSpec(memory_space=pltpu.SMEM)] + [vmem] * len(arrays),
        out_specs=[vmem] * len(out_shapes),
        out_shape=out_shapes,
        scratch_shapes=scratch,
        compiler_params=pltpu.CompilerParams(vmem_limit_bytes=VMEM_LIMIT),
        name=name,
    )(me, *arrays)


def padded(rows):
    return -(-rows // 16) * 16


def cut_ff(me, gate_up_weight, down_weight, size):
    width = gate_up_weight.shape[0]
    half = down_weight.shape[0]
    strip = half // size
    tall = padded(strip)

    def body(me_ref, gu_ref, d_ref, *refs):
        outs, held = refs[:size], refs[size]
        turned = gu_ref[...].astype(F32).T
        down = d_ref[...].astype(F32)
        blank = jnp.zeros((tall - strip, width), F32)
        for q in range(size):
            one = turned[q * strip : (q + 1) * strip]
            two = turned[half + q * strip : half + (q + 1) * strip]
            three = down[q * strip : (q + 1) * strip]
            parts = [one, blank, two, blank, three, blank]
            held[q] = jnp.concatenate(parts, axis=0).astype(BF16)
        for o in range(size):
            outs[o][...] = held[me_ref[0] ^ o]

    shape = jax.ShapeDtypeStruct((3 * tall, width), BF16)
    scratch = [pltpu.VMEM((size, 3 * tall, width), BF16)]
    return on_device(body, "cut_ff", [shape] * size, scratch, me, (gate_up_weight, down_weight))


def join_lanes(me, blocks):
    size = len(blocks)
    rows, width = blocks[0].shape

    def body(me_ref, *refs):
        ins, out, held = refs[:size], refs[size], refs[size + 1]
        for o in range(size):
            held[me_ref[0] ^ o] = ins[o][...]
        out[...] = jnp.concatenate([held[q].astype(F32) for q in range(size)], 1).astype(BF16)

    return on_device(
        body,
        "join_lanes",
        [jax.ShapeDtypeStruct((rows, size * width), BF16)],
        [pltpu.VMEM((size, rows, width), BF16)],
        me,
        blocks,
    )[0]


def join_both(me, blocks, offsets, rows):
    size = len(blocks)
    count, tall, width = blocks[0].shape
    shapes = [jax.ShapeDtypeStruct((count, rows, size * width), BF16)]
    if tall > rows:
        shapes.append(jax.ShapeDtypeStruct((count, tall - rows, width), BF16))

    def body(me_ref, *refs):
        ins, out, held = refs[:size], refs[size], refs[-1]
        for o in range(size):
            held[me_ref[0] ^ o] = ins[o][...]
        for j, f in enumerate(offsets):
            parts = [held[q, j, :rows].astype(F32) for q in range(size)]
            out[me_ref[1] ^ f] = jnp.concatenate(parts, axis=1).astype(BF16)
            if tall > rows:
                refs[size + 1][me_ref[1] ^ f] = ins[0][j, rows:]

    return on_device(
        body, "join_both", shapes, [pltpu.VMEM((size, count, tall, width), BF16)], me, blocks
    )


def cut_lanes(me, sums, size):
    rows = sum(s.shape[0] for s in sums)
    width = sums[0].shape[1] // size

    def body(me_ref, *refs):
        ins, outs, held = refs[: len(sums)], refs[len(sums) : -1], refs[-1]
        whole = jnp.concatenate([r[...] for r in ins], axis=0)
        for q in range(size):
            held[q] = whole[:, q * width : (q + 1) * width].astype(BF16)
        for o in range(size):
            outs[o][...] = held[me_ref[0] ^ o]

    shape = jax.ShapeDtypeStruct((rows, width), BF16)
    scratch = [pltpu.VMEM((size, rows, width), BF16)]
    return on_device(body, "cut_lanes", [shape] * size, scratch, me, sums)


def join_ff(me, blocks, strip):
    size = len(blocks)
    rows, width = blocks[0].shape
    tall = rows // 3

    def body(me_ref, *refs):
        ins, gu, down, held = refs[:size], refs[size], refs[size + 1], refs[size + 2]
        for o in range(size):
            held[me_ref[0] ^ o] = ins[o][...].astype(F32)
        cut = [
            [held[q, i * tall : i * tall + strip] for q in range(size)] for i in range(3)
        ]
        gu[...] = jnp.concatenate(cut[0] + cut[1], axis=0).T
        down[...] = jnp.concatenate(cut[2], axis=0)

    return on_device(
        body,
        "join_ff",
        [
            jax.ShapeDtypeStruct((width, 2 * size * strip), F32),
            jax.ShapeDtypeStruct((size * strip, width), F32),
        ],
        [pltpu.VMEM((size, rows, width), F32)],
        me,
        blocks,
    )


def feed_forward(me, weight_blocks, row_blocks, cot_blocks):
    count, size = len(weight_blocks), len(row_blocks)
    rows, width = row_blocks[0].shape
    tall = weight_blocks[0].shape[0] // 3
    units = count * tall
    step_units = 256

    def body(me_ref, *refs):
        blocks = refs[:count]
        xs, gs = refs[count : count + size], refs[count + size : count + 2 * size]
        hid, gg, gu, gn, part, x_out, g_out = refs[count + 2 * size : count + 2 * size + 7]
        gu_w, d_w, x_all, g_all, sems = refs[count + 2 * size + 7 :]
        step = pl.program_id(0)

        @pl.when(step == 0)
        def _():
            copies = []
            for o in range(count):
                f = me_ref[1] ^ o
                copies.append((blocks[o].at[pl.ds(0, 2 * tall)], gu_w.at[f]))
                copies.append((blocks[o].at[pl.ds(2 * tall, tall)], d_w.at[f]))
            for o in range(size):
                copies.append((xs[o], x_all.at[me_ref[0] ^ o]))
                copies.append((gs[o], g_all.at[me_ref[0] ^ o]))
            started = [
                pltpu.make_async_copy(src, dst, sems.at[i]) for i, (src, dst) in enumerate(copies)
            ]
            for copy in started:
                copy.start()
            for copy in started:
                copy.wait()

        x = x_all[step]
        g = g_all[step]
        x_out[...] = x
        g_out[...] = g
        gate_w = gu_w[: count // 2].reshape(units, width)
        up_w = gu_w[count // 2 :].reshape(units, width)
        down_w = d_w[...].reshape(units, width)
        for begin in range(0, units, step_units):
            at = slice(begin, begin + step_units)
            gate = dot(x, gate_w[at], 1, 1)
            up = dot(x, up_w[at], 1, 1)
            grad_hidden = dot(g, down_w[at], 1, 1)
            sigmoid = 0.5 * jnp.tanh(0.5 * gate) + 0.5
            silu = gate * sigmoid
            hid[:, at] = (silu * up).astype(BF16)
            gg[:, at] = (grad_hidden * up * (sigmoid + silu * (1.0 - sigmoid))).astype(BF16)
            gu[:, at] = (grad_hidden * silu).astype(BF16)
        gn[...] = (dot(gg[...], gate_w, 1, 0) + dot(gu[...], up_w, 1, 0)).astype(BF16)
        part[...] = dot(hid[...], down_w, 1, 0).astype(BF16)

    hbm = pl.BlockSpec(memory_space=pl.ANY)
    by_rows = lambda n: pl.BlockSpec((rows, n), lambda i: (i, 0))
    like = lambda n: jax.ShapeDtypeStruct((size * rows, n), BF16)
    return pl.pallas_call(
        body,
        grid=(size,),
        in_specs=[pl.BlockSpec(memory_space=pltpu.SMEM)]
        + [hbm] * (count + 2 * size),
        out_specs=[by_rows(units)] * 3 + [by_rows(width)] * 4,
        out_shape=[like(units)] * 3 + [like(width)] * 4,
        scratch_shapes=[
            pltpu.VMEM((count, 2 * tall, width), BF16),
            pltpu.VMEM((count, tall, width), BF16),
            pltpu.VMEM((size, rows, width), BF16),
            pltpu.VMEM((size, rows, width), BF16),
            pltpu.SemaphoreType.DMA((2 * count + 2 * size,)),
        ],
        compiler_params=pltpu.CompilerParams(vmem_limit_bytes=VMEM_LIMIT),
        cost_estimate=pl.CostEstimate(
            flops=12 * size * rows * units * width,
            bytes_accessed=2 * (3 * units * width + size * rows * (3 * units + 5 * width)),
            transcendentals=size * rows * units,
        ),
        name="feed_forward",
    )(me, *weight_blocks, *row_blocks, *cot_blocks)


def both_heads(pair):
    lane = lax.broadcasted_iota(jnp.int32, pair.shape, 1)
    zero = jnp.zeros_like(pair)
    return jnp.concatenate(
        [jnp.where(lane < HEAD, pair, zero), jnp.where(lane < HEAD, zero, pair)], axis=0
    )


def fill_bias(low_ref, high_ref, place_ref, bias_ref):
    place = place_ref[...]
    allowed = (place >= low_ref[...]) & (place <= high_ref[...])
    bias = jnp.where(allowed, 0.0, MASKED).astype(F32)
    rows = bias.shape[1]
    bias_ref[:, :rows] = bias
    bias_ref[:, rows:] = bias


def own_rows(wide, rows):
    return jnp.concatenate([wide[:HEAD, :rows], wide[HEAD:, rows:]], axis=0)


def pairing(kv_refs, step, begin):
    both = jnp.concatenate([r[:, begin : begin + PAIR] for r in kv_refs], axis=0).astype(F32)
    crossed = pltpu.roll(both, HEAD, 1)
    lane = lax.broadcasted_iota(jnp.int32, both.shape, 1)
    first = jnp.where(step <= PAIRS // 2, both, crossed)
    second = jnp.where(step < PAIRS // 2, crossed, both)
    return jnp.where(lane < HEAD, first, second)


def attend_kernel(
    size, low_ref, high_ref, place_ref, q_ref, *refs,
):
    kv_refs = refs[:size]
    o_ref, lse_ref, bias_ref, k_ref, vt_ref = refs[size:]
    step = pl.program_id(0)

    @pl.when(step == 0)
    def _():
        fill_bias(low_ref, high_ref, place_ref, bias_ref)

    @pl.when((step == 0) | (step == PAIRS // 2) | (step == PAIRS // 2 + 1))
    def _():
        k_ref[...] = pairing(kv_refs, step, 0).astype(BF16)
        vt_ref[...] = pairing(kv_refs, step, PAIR).T.astype(BF16)

    rows = q_ref.shape[0]
    queries = both_heads(q_ref[...])
    keys = k_ref[...]
    values_t = vt_ref[...]
    outs, totals = [], []
    for begin in range(0, 2 * rows, 256):
        scores = dot(keys, queries[begin : begin + 256], 1, 1) + bias_ref[:, begin : begin + 256]
        top = jnp.max(scores, axis=0, keepdims=True)
        probs = jnp.exp(scores - top)
        total = jnp.sum(probs, axis=0, keepdims=True)
        outs.append(dot(values_t, probs.astype(BF16), 1, 0) / total)
        totals.append(top + jnp.log(total))
    wide = jnp.concatenate(outs, axis=1)
    o_ref[...] = own_rows(wide, rows).T.astype(BF16)
    lse_ref[0] = jnp.concatenate(totals, axis=1)


def attend_back_kernel(
    size, low_ref, high_ref, place_ref, q_ref, g_ref, o_ref, lse_ref, *refs,
):
    kv_refs = refs[:size]
    dq_ref, dkv_ref, bias_ref, k_ref, kt_ref, v_ref, dk_ref, dv_ref = refs[size:]
    step = pl.program_id(0)

    @pl.when(step == 0)
    def _():
        fill_bias(low_ref, high_ref, place_ref, bias_ref)
        dkv_ref[...] = jnp.zeros_like(dkv_ref)

    @pl.when((step == 0) | (step == PAIRS // 2) | (step == PAIRS // 2 + 1))
    def _():
        keys_now = pairing(kv_refs, step, 0)
        k_ref[...] = keys_now.astype(BF16)
        kt_ref[...] = keys_now.T.astype(BF16)
        v_ref[...] = pairing(kv_refs, step, PAIR).astype(BF16)
        dk_ref[...] = jnp.zeros_like(dk_ref)
        dv_ref[...] = jnp.zeros_like(dv_ref)

    rows = q_ref.shape[0]
    queries = both_heads(q_ref[...])
    grads = both_heads(g_ref[...])
    keys = k_ref[...]
    keys_t = kt_ref[...]
    values = v_ref[...]
    product = (g_ref[...].astype(F32) * o_ref[...].astype(F32)).T
    delta = jnp.concatenate(
        [
            jnp.sum(product[:HEAD], axis=0, keepdims=True),
            jnp.sum(product[HEAD:], axis=0, keepdims=True),
        ],
        axis=1,
    )
    lse = lse_ref[0]
    outs = []
    for begin in range(0, 2 * rows, 256):
        part = slice(begin, begin + 256)
        scores = dot(keys, queries[part], 1, 1) + bias_ref[:, part]
        probs = jnp.exp(scores - lse[:, part])
        grad_probs = dot(values, grads[part], 1, 1)
        grad_scores = (probs * (grad_probs - delta[:, part])).astype(BF16)
        outs.append(dot(keys_t, grad_scores, 1, 0))
        dk_ref[...] += dot(grad_scores, queries[part], 1, 0)
        dv_ref[...] += dot(probs.astype(BF16), grads[part], 1, 0)
    wide = jnp.concatenate(outs, axis=1)
    dq_ref[...] = own_rows(wide, rows).T * 0.125

    def fold(own_lanes):
        for at, sums in ((0, dk_ref), (PAIR, dv_ref)):
            sums_now = sums[...]
            lane = lax.broadcasted_iota(jnp.int32, sums_now.shape, 1)
            both = sums_now + pltpu.roll(sums_now, HEAD, 1)
            kept = jnp.where((lane < HEAD) == own_lanes, both, 0.0)
            dkv_ref[:, at : at + PAIR] += kept

    @pl.when(step == PAIRS // 2 - 1)
    def _():
        fold(True)

    @pl.when(step == PAIRS // 2)
    def _():
        dkv_ref[:, :PAIR] += dk_ref[...]
        dkv_ref[:, PAIR:] += dv_ref[...]

    @pl.when(step == PAIRS - 1)
    def _():
        fold(False)


def whole(shape):
    return pl.BlockSpec(shape, lambda i: (0,) * len(shape))


def attend(low, high, place, queries, kv_blocks):
    rows, count, size = queries.shape[0], place.shape[0], len(kv_blocks)
    pair = pl.BlockSpec((rows, PAIR), lambda i: (0, i))
    return pl.pallas_call(
        functools.partial(attend_kernel, size),
        grid=(PAIRS,),
        in_specs=[whole((1, rows)), whole((1, rows)), whole((count, 1)), pair]
        + [whole((rows, 2 * KVW))] * size,
        out_specs=[pair, pl.BlockSpec((1, 1, 2 * rows), lambda i: (i, 0, 0))],
        out_shape=[
            jax.ShapeDtypeStruct((rows, QW), BF16),
            jax.ShapeDtypeStruct((PAIRS, 1, 2 * rows), F32),
        ],
        scratch_shapes=[
            pltpu.VMEM((count, 2 * rows), F32),
            pltpu.VMEM((count, PAIR), BF16),
            pltpu.VMEM((PAIR, count), BF16),
        ],
        compiler_params=pltpu.CompilerParams(vmem_limit_bytes=VMEM_LIMIT),
        cost_estimate=pl.CostEstimate(
            flops=8 * HEADS * rows * count * PAIR,
            bytes_accessed=4 * rows * QW + 1024 * count,
            transcendentals=HEADS * rows * count,
        ),
        name="attend",
    )(low, high, place, queries, *kv_blocks)


def attend_back(low, high, place, queries, grads, outs, lse, kv_blocks):
    rows, count, size = queries.shape[0], place.shape[0], len(kv_blocks)
    pair = pl.BlockSpec((rows, PAIR), lambda i: (0, i))
    return pl.pallas_call(
        functools.partial(attend_back_kernel, size),
        grid=(PAIRS,),
        in_specs=[whole((1, rows)), whole((1, rows)), whole((count, 1)), pair, pair, pair]
        + [pl.BlockSpec((1, 1, 2 * rows), lambda i: (i, 0, 0))]
        + [whole((rows, 2 * KVW))] * size,
        out_specs=[pair, whole((count, 2 * KVW))],
        out_shape=[
            jax.ShapeDtypeStruct((rows, QW), F32),
            jax.ShapeDtypeStruct((count, 2 * KVW), F32),
        ],
        scratch_shapes=[
            pltpu.VMEM((count, 2 * rows), F32),
            pltpu.VMEM((count, PAIR), BF16),
            pltpu.VMEM((PAIR, count), BF16),
            pltpu.VMEM((count, PAIR), BF16),
            pltpu.VMEM((count, PAIR), F32),
            pltpu.VMEM((count, PAIR), F32),
        ],
        compiler_params=pltpu.CompilerParams(vmem_limit_bytes=VMEM_LIMIT),
        cost_estimate=pl.CostEstimate(
            flops=16 * HEADS * rows * count * PAIR,
            bytes_accessed=8 * rows * QW + 4096 * count,
            transcendentals=HEADS * rows * count,
        ),
        name="attend_back",
    )(low, high, place, queries, grads, outs, lse, *kv_blocks)


def rms_scale(values_in):
    return lax.rsqrt(jnp.mean(values_in * values_in, axis=-1, keepdims=True) + EPSILON)


def angle_tables(places):
    exponent = jnp.arange(HEAD // 2, dtype=F32) * 2.0 / HEAD
    frequency = ROPE_BASE ** (-exponent)
    turn = places.astype(F32)[:, None] * frequency[None, :]
    cosine, sine = lax.optimization_barrier((jnp.cos(turn), jnp.sin(turn)))
    return jnp.concatenate([cosine] * 4, axis=1), jnp.concatenate([sine] * 4, axis=1)


def widen(table, width):
    return jnp.concatenate([table] * (width // PAIR), axis=1)


def first_halves(shape):
    return lax.broadcasted_iota(jnp.int32, shape, 1) % HEAD < HEAD // 2


def rotate(tensor, cosine, sine):
    half = HEAD // 2
    ahead, behind = jnp.roll(tensor, -half, axis=1), jnp.roll(tensor, half, axis=1)
    turned = jnp.where(first_halves(tensor.shape), -ahead, behind)
    width = tensor.shape[1]
    return tensor * widen(cosine, width) + turned * widen(sine, width)


def rotate_back(grad_in, cosine, sine):
    half = HEAD // 2
    width = grad_in.shape[1]
    scaled = grad_in * widen(sine, width)
    ahead, behind = jnp.roll(scaled, -half, axis=1), jnp.roll(scaled, half, axis=1)
    return grad_in * widen(cosine, width) + jnp.where(
        first_halves(grad_in.shape), ahead, -behind
    )


def norm_back(grad_in, row_data, scale_in, gain_in):
    gain_term = jnp.sum(grad_in * row_data * scale_in, axis=0)
    grad_normed = grad_in * gain_in
    inner_mean = jnp.mean(grad_normed * row_data, axis=-1, keepdims=True)
    return (
        scale_in * grad_normed - row_data * scale_in * scale_in * scale_in * inner_mean,
        gain_term,
    )


def pad_row(vector, width):
    return jnp.pad(vector, (0, width - vector.shape[0]))[None, :]


def stack_from_lanes(array, count):
    rows, width = array.shape
    return jnp.transpose(array.reshape(rows, count, width // count), (1, 0, 2))


def per_device(
    seq_size, fsdp_size, tokens, segment_ids, positions, norm_one, qkv_weight, qkv_bias,
    out_weight, norm_two, gate_up_weight, down_weight, cotangent,
):
    my_seq, my_fsdp = lax.axis_index("seq"), lax.axis_index("fsdp")
    me = jnp.stack([my_seq, my_fsdp]).astype(jnp.int32)
    offsets = range(seq_size)
    row_count = tokens.shape[0]
    width = qkv_weight.shape[0]
    qkv_rows = qkv_weight.shape[1]
    strip = down_weight.shape[0] // seq_size
    tall = padded(strip)

    qkv_tall = padded(qkv_rows)
    packed = jnp.concatenate(
        [
            jnp.pad(qkv_weight.T, ((0, qkv_tall - qkv_rows), (0, 0))),
            pad_row(norm_one, width),
            pad_row(qkv_bias, width),
            pad_row(norm_two, width),
            jnp.zeros((13, width), BF16),
        ],
        axis=0,
    )
    packed_stack, fsdp_order = fsdp_gather_small(packed, fsdp_size)
    packed_blocks = seq_gather(packed_stack, seq_size)

    ff_cut = cut_ff(me, gate_up_weight, down_weight, seq_size)
    ff_share = [ff_cut[0]] + [swap(ff_cut[o], "seq", seq_size, o) for o in offsets if o]
    ff_block = join_lanes(me, ff_share)
    ff_blocks = {0: ff_block}
    for bit in fsdp_bits(fsdp_size):
        ff_blocks.update({o ^ bit: swap(b, "fsdp", fsdp_size, bit) for o, b in ff_blocks.items()})
    inner = fsdp_size // OUTER

    qkv_blocks = [packed_blocks[o] for o in offsets]
    qkv_blocks[0] = after(qkv_blocks[0], ff_block)
    qkv_t, vectors = join_both(me, qkv_blocks, fsdp_order, qkv_tall)
    qkv_t = qkv_t[:, :qkv_rows].reshape(fsdp_size * qkv_rows, -1)
    gain_one = vectors[:, 0, : norm_one.shape[0]].reshape(-1).astype(F32)
    bias_full = vectors[:, 1, : qkv_bias.shape[0]].reshape(-1).astype(F32)
    gain_two = vectors[:, 2, : norm_two.shape[0]].reshape(-1).astype(F32)

    cot_blocks = seq_gather(after(cotangent, packed_blocks[seq_size // 2]), seq_size)
    out_stack, out_order = fsdp_gather_small(after(out_weight, ff_block), fsdp_size)
    out_blocks = seq_gather(out_stack, seq_size)
    out_full = join_both(me, [out_blocks[o] for o in offsets], out_order, out_weight.shape[0])[0]
    out_full = out_full.reshape(QW, -1)

    inputs = tokens.astype(F32)
    scale_one = rms_scale(inputs)
    normed_one = (inputs * scale_one * gain_one).astype(BF16)
    joined = dot(normed_one, qkv_t, 1, 1) + bias_full
    cosine, sine = angle_tables(positions)
    turned = rotate(joined[:, : QW + KVW], cosine, sine).astype(BF16)
    queries = turned[:, :QW] * jnp.asarray(0.125, BF16)
    kv_local = jnp.concatenate([turned[:, QW:], joined[:, QW + KVW :].astype(BF16)], axis=1)
    kv_blocks = seq_gather(kv_local, seq_size)
    kv_blocks = [kv_blocks[o] for o in offsets]
    row_place = jnp.arange(row_count, dtype=jnp.int32)
    high = my_seq * row_count + row_place
    low = high - positions
    place = jnp.concatenate([(my_seq ^ o) * row_count + row_place for o in offsets])[:, None]
    low, high = low[None, :], high[None, :]
    queries_now = after(queries, ff_blocks[inner], ff_blocks[2 * inner])
    attn_flat, lse = attend(low, high, place, queries_now, kv_blocks)

    residual = inputs + dot(attn_flat, out_full, 1, 0)
    scale_two = rms_scale(residual)
    normed_two = (residual * scale_two * gain_two).astype(BF16)
    normed_blocks = seq_gather(normed_two, seq_size)
    hidden, grad_gate, grad_up, grad_normed, layer_part, normed_all, cot_all = feed_forward(
        me,
        [ff_blocks[o] for o in range(fsdp_size)],
        [normed_blocks[o] for o in offsets],
        [cot_blocks[o] for o in offsets],
    )
    by_seq = lambda rows: rows.reshape(seq_size, row_count, -1)

    kept, given = halve(by_seq(grad_normed), 1, my_seq)
    normed_sum = add(kept, swap(given, "seq", seq_size, 1))
    bit = 2
    while bit < seq_size:
        kept, given = halve(normed_sum, 1, my_seq // bit)
        normed_sum = add(kept, swap(given, "seq", seq_size, bit))
        bit *= 2
    grad_normed_two = normed_sum[0]
    down_term = dot(hidden, cot_all, 0, 0).astype(BF16).reshape(fsdp_size, tall, -1)
    grad_gate, grad_up = after(grad_gate, given), after(grad_up, given)
    gate_term = dot(grad_gate, normed_all, 0, 0).astype(BF16).reshape(fsdp_size // 2, 2, tall, -1)
    up_term = dot(grad_up, normed_all, 0, 0).astype(BF16).reshape(fsdp_size // 2, 2, tall, -1)

    chunks = [down_term] + [
        jnp.concatenate([gate_term[:, i], up_term[:, i]], axis=0) for i in range(2)
    ]
    bits = list(reversed(fsdp_bits(fsdp_size)))
    steps = []
    for chunk in chunks:
        kept, given = fsdp_halve(chunk, fsdp_size, bits[0], my_fsdp, [])
        if steps:
            given = after(given, steps[-1][0])
        got = [swap(given, "fsdp", fsdp_size, bits[0])]
        stack = add(kept, got[0])
        for at in range(1, len(bits)):
            kept, given = fsdp_halve(stack, fsdp_size, bits[at], my_fsdp, bits[:at])
            got.append(swap(given, "fsdp", fsdp_size, bits[at]))
            stack = add(kept, got[-1])
        steps.append(got + [stack[0]])
    down_sum, one_sum, two_sum = [s[-1] for s in steps]

    kept, given = halve(by_seq(layer_part), 1, my_seq)
    layer_sum = add(kept, swap(given, "seq", seq_size, 1))
    bit = 2
    while bit < seq_size:
        kept, given = halve(layer_sum, 1, my_seq // bit)
        given = after(given, grad_normed_two)
        layer_sum = add(kept, swap(given, "seq", seq_size, bit))
        bit *= 2
    layer_out = residual + layer_sum[0]

    ff_back = cut_lanes(me, (one_sum, two_sum, down_sum), seq_size)
    ff_got = [ff_back[0]] + [swap(ff_back[o], "seq", seq_size, o) for o in offsets if o]
    grad_gate_up, grad_down = join_ff(me, ff_got, strip)

    grad_path, norm_two_term = norm_back(grad_normed_two, residual, scale_two, gain_two)
    grad_residual = cotangent.astype(F32) + grad_path
    grad_branch = grad_residual.astype(BF16)
    grad_attn = dot(grad_branch, out_full, 1, 1).astype(BF16)
    out_term = stack_from_lanes(dot(attn_flat, grad_branch, 0, 0).astype(BF16), seq_size)
    out_mine = seq_scatter(out_term, seq_size, my_seq).reshape(fsdp_size, -1, width)
    grad_attn = after(grad_attn, steps[0][0], gate_term, up_term)
    grad_queries, kv_terms = attend_back(
        low, high, place, queries, grad_attn, attn_flat, lse, kv_blocks
    )
    kv_terms = after(kv_terms, steps[1][0], steps[0][1])
    kv_sum = by_seq(kv_terms)
    bit = 1
    while bit < seq_size:
        cut = kv_sum.reshape((-1, 2) + kv_sum.shape[1:])
        kv_sum = add(cut[:, 0], swap(cut[:, 1].astype(BF16), "seq", seq_size, bit))
        bit *= 2
    kv_mine = kv_sum[0]
    turned_back = rotate_back(
        jnp.concatenate([grad_queries, kv_mine[:, :KVW]], axis=1), cosine, sine
    )
    grad_joined = jnp.concatenate([turned_back, kv_mine[:, KVW:]], axis=1).astype(BF16)
    grad_normed_one = dot(grad_joined, qkv_t, 1, 0)
    grad_path_one, norm_one_term = norm_back(grad_normed_one, inputs, scale_one, gain_one)
    grad_tokens = grad_residual + grad_path_one
    bias_term = jnp.sum(grad_joined.astype(F32), axis=0)

    def vector_rows(vector):
        rows = vector.reshape(fsdp_size, 1, -1)
        return jnp.pad(rows, ((0, 0), (0, 0), (0, width - rows.shape[2])))

    vector_terms = [norm_one_term, bias_term[: QW + KVW], bias_term[QW + KVW :], norm_two_term]
    small = jnp.concatenate([vector_rows(v) for v in vector_terms], axis=1).astype(BF16)
    small = jnp.pad(small, ((0, 0), (0, 16 - len(vector_terms)), (0, 0)))
    qkv_term = stack_from_lanes(dot(grad_joined, normed_one, 0, 0).astype(BF16), seq_size)
    qkv_term = qkv_term.reshape(seq_size, fsdp_size, qkv_rows, width)
    tail = jnp.concatenate(
        [qkv_term, jnp.broadcast_to(small[None], (seq_size,) + small.shape)], axis=2
    )
    tail_mine = seq_scatter(after(tail, steps[2][0], steps[1][1]), seq_size, my_seq)
    tail_sum = fsdp_scatter(
        jnp.concatenate([tail_mine, out_mine], axis=1), fsdp_size, my_fsdp
    )
    pieces = [
        tail_sum[qkv_rows + i, : v.shape[0] // fsdp_size] for i, v in enumerate(vector_terms)
    ]
    return (
        layer_out.astype(BF16),
        grad_tokens,
        pieces[0],
        tail_sum[:qkv_rows].T,
        pieces[1],
        pieces[2],
        tail_sum[qkv_rows + 16 :],
        pieces[3],
        grad_gate_up,
        grad_down,
    )


def solution(mesh):
    rows, both = P(("fsdp", "seq"), None), P(("fsdp", "seq"))
    return jax.shard_map(
        functools.partial(per_device, mesh.shape["seq"], mesh.shape["fsdp"]),
        mesh=mesh,
        in_specs=(
            rows, both, both, P("fsdp"), P("seq", "fsdp"), P("fsdp"), P("fsdp", "seq"),
            P("fsdp"), P("seq", "fsdp"), P("fsdp", "seq"), rows,
        ),
        out_specs=(
            rows, rows, P("fsdp"), P("seq", "fsdp"), P("fsdp"), P("fsdp"), P("fsdp", "seq"),
            P("fsdp"), P("seq", "fsdp"), P("fsdp", "seq"),
        ),
        check_vma=False,
    )
```

```python
import functools

import jax
import jax.numpy as jnp
from jax import lax
from jax.experimental import pallas as pl
from jax.experimental.pallas import tpu as pltpu
from jax.sharding import PartitionSpec as P

HEADS = 14
KV_HEADS = 2
HEAD = 64
FF = 4864
QW = 896
KVW = 128
PAIR = 2 * HEAD
PAIRS = HEADS // 2
OUTER = 4

EPSILON = 1e-06
ROPE_BASE = 1000000.0
MASKED = -1e30
VMEM_LIMIT = 50 * 1024 * 1024

F32 = jnp.float32
BF16 = jnp.bfloat16


def dot(left, right, left_dim, right_dim):
    return lax.dot_general(
        left, right, (((left_dim,), (right_dim,)), ((), ())), preferred_element_type=F32
    )


def swap(block, axis, size, bits):
    return lax.ppermute(block, axis, [(i, i ^ bits) for i in range(size)])


def after(array, *others):
    return lax.optimization_barrier((array,) + others)[0]


def seq_gather(block, size):
    blocks = {0: block}
    bit = size // 2
    while bit:
        blocks.update({o ^ bit: swap(b, "seq", size, bit) for o, b in blocks.items()})
        bit //= 2
    return blocks


def fsdp_bits(size):
    inner = size // OUTER
    outer_bits, inner_bits = [], []
    bit = 1
    while bit < size:
        (outer_bits if bit >= inner else inner_bits).append(bit)
        bit *= 2
    return outer_bits + inner_bits


def ff_spread(block, size):
    blocks = {0: block}
    for bit in fsdp_bits(size)[2:]:
        blocks.update({o ^ bit: swap(b, "fsdp", size, bit) for o, b in blocks.items()})
    return blocks


def halve(stack, bit, me):
    above = stack.shape[0] // (2 * bit)
    cut = stack.reshape((above, 2, bit) + stack.shape[1:])
    digit = (me // bit) % 2
    kept = lax.dynamic_index_in_dim(cut, digit, 1, keepdims=False)
    given = lax.dynamic_index_in_dim(cut, 1 - digit, 1, keepdims=False)
    merge = lambda part: part.reshape((above * bit,) + stack.shape[1:])
    return merge(kept), merge(given).astype(BF16)


def add(kept, got):
    return kept.astype(F32) + got.astype(F32)


def seq_scatter(stack, size, me):
    bit = 1
    while bit < size:
        kept, given = halve(stack, 1, me // bit)
        stack = add(kept, swap(given, "seq", size, bit))
        bit *= 2
    return stack[0]


def fsdp_halve(stack, size, bit, me, resolved):
    place = bit
    digit = me // bit
    for taken in resolved:
        if taken < bit:
            place //= 2
    kept, given = halve(stack, place, digit * place)
    return kept, given


def fsdp_scatter(stack, size, me):
    resolved = []
    for bit in reversed(fsdp_bits(size)):
        kept, given = fsdp_halve(stack, size, bit, me, resolved)
        stack = add(kept, swap(given, "fsdp", size, bit))
        resolved.append(bit)
    return stack[0]


def on_device(body, name, out_shapes, scratch, me, arrays):
    vmem = pl.BlockSpec(memory_space=pltpu.VMEM)
    return pl.pallas_call(
        body,
        in_specs=[pl.BlockSpec(memory_space=pltpu.SMEM)] + [vmem] * len(arrays),
        out_specs=[vmem] * len(out_shapes),
        out_shape=out_shapes,
        scratch_shapes=scratch,
        compiler_params=pltpu.CompilerParams(vmem_limit_bytes=VMEM_LIMIT),
        name=name,
    )(me, *arrays)


def padded(rows):
    return -(-rows // 16) * 16


def cut_ff(me, gate_up_weight, down_weight, size):
    width = gate_up_weight.shape[0]
    half = down_weight.shape[0]
    strip = half // size
    tall = padded(strip)

    def body(me_ref, gu_ref, d_ref, *refs):
        outs, held = refs[:size], refs[size]
        turned = gu_ref[...].astype(F32).T
        down = d_ref[...].astype(F32)
        blank = jnp.zeros((tall - strip, width), F32)
        for q in range(size):
            one = turned[q * strip : (q + 1) * strip]
            two = turned[half + q * strip : half + (q + 1) * strip]
            three = down[q * strip : (q + 1) * strip]
            parts = [one, blank, two, blank, three, blank]
            held[q] = jnp.concatenate(parts, axis=0).astype(BF16)
        for o in range(size):
            outs[o][...] = held[me_ref[0] ^ o]

    shape = jax.ShapeDtypeStruct((3 * tall, width), BF16)
    scratch = [pltpu.VMEM((size, 3 * tall, width), BF16)]
    return on_device(body, "cut_ff", [shape] * size, scratch, me, (gate_up_weight, down_weight))


def join_lanes(me, blocks):
    size = len(blocks)
    rows, width = blocks[0].shape

    def body(me_ref, *refs):
        ins, out, held = refs[:size], refs[size], refs[size + 1]
        for o in range(size):
            held[me_ref[0] ^ o] = ins[o][...]
        out[...] = jnp.concatenate([held[q].astype(F32) for q in range(size)], 1).astype(BF16)

    return on_device(
        body,
        "join_lanes",
        [jax.ShapeDtypeStruct((rows, size * width), BF16)],
        [pltpu.VMEM((size, rows, width), BF16)],
        me,
        blocks,
    )[0]


def join_both(me, blocks, rows):
    size = len(blocks)
    count, tall, width = blocks[0].shape
    shapes = [jax.ShapeDtypeStruct((count, rows, size * width), BF16)]
    if tall > rows:
        shapes.append(jax.ShapeDtypeStruct((count, tall - rows, width), BF16))

    def body(me_ref, *refs):
        ins, out, held = refs[:size], refs[size], refs[-1]
        for o in range(size):
            held[me_ref[0] ^ o] = ins[o][...]
        for f in range(count):
            parts = [held[q, f, :rows].astype(F32) for q in range(size)]
            out[f] = jnp.concatenate(parts, axis=1).astype(BF16)
            if tall > rows:
                refs[size + 1][f] = ins[0][f, rows:]

    return on_device(
        body, "join_both", shapes, [pltpu.VMEM((size, count, tall, width), BF16)], me, blocks
    )


def cut_lanes(me, sums, size):
    rows = sum(s.shape[0] for s in sums)
    width = sums[0].shape[1] // size

    def body(me_ref, *refs):
        ins, outs, held = refs[: len(sums)], refs[len(sums) : -1], refs[-1]
        whole = jnp.concatenate([r[...] for r in ins], axis=0)
        for q in range(size):
            held[q] = whole[:, q * width : (q + 1) * width].astype(BF16)
        for o in range(size):
            outs[o][...] = held[me_ref[0] ^ o]

    shape = jax.ShapeDtypeStruct((rows, width), BF16)
    scratch = [pltpu.VMEM((size, rows, width), BF16)]
    return on_device(body, "cut_lanes", [shape] * size, scratch, me, sums)


def join_ff(me, blocks, strip):
    size = len(blocks)
    rows, width = blocks[0].shape
    tall = rows // 3

    def body(me_ref, *refs):
        ins, gu, down, held = refs[:size], refs[size], refs[size + 1], refs[size + 2]
        for o in range(size):
            held[me_ref[0] ^ o] = ins[o][...].astype(F32)
        cut = [
            [held[q, i * tall : i * tall + strip] for q in range(size)] for i in range(3)
        ]
        gu[...] = jnp.concatenate(cut[0] + cut[1], axis=0).T
        down[...] = jnp.concatenate(cut[2], axis=0)

    return on_device(
        body,
        "join_ff",
        [
            jax.ShapeDtypeStruct((width, 2 * size * strip), F32),
            jax.ShapeDtypeStruct((size * strip, width), F32),
        ],
        [pltpu.VMEM((size, rows, width), F32)],
        me,
        blocks,
    )


def feed_forward(me, weight_blocks, row_blocks, cot_blocks):
    count, size = len(weight_blocks), len(row_blocks)
    rows, width = row_blocks[0].shape
    tall = weight_blocks[0].shape[0] // 3
    units = count * tall
    step_units = 256

    def body(me_ref, *refs):
        blocks = refs[:count]
        xs, gs = refs[count : count + size], refs[count + size : count + 2 * size]
        hid, gg, gu, gn, part, x_out, g_out = refs[count + 2 * size : count + 2 * size + 7]
        gu_w, d_w, x_all, g_all, sems = refs[count + 2 * size + 7 :]
        step = pl.program_id(0)

        @pl.when(step == 0)
        def _():
            copies = []
            for o in range(count):
                f = me_ref[1] ^ o
                copies.append((blocks[o].at[pl.ds(0, 2 * tall)], gu_w.at[f]))
                copies.append((blocks[o].at[pl.ds(2 * tall, tall)], d_w.at[f]))
            for o in range(size):
                copies.append((xs[o], x_all.at[me_ref[0] ^ o]))
                copies.append((gs[o], g_all.at[me_ref[0] ^ o]))
            started = [
                pltpu.make_async_copy(src, dst, sems.at[i]) for i, (src, dst) in enumerate(copies)
            ]
            for copy in started:
                copy.start()
            for copy in started:
                copy.wait()

        x = x_all[step]
        g = g_all[step]
        x_out[...] = x
        g_out[...] = g
        gate_w = gu_w[: count // 2].reshape(units, width)
        up_w = gu_w[count // 2 :].reshape(units, width)
        down_w = d_w[...].reshape(units, width)
        for begin in range(0, units, step_units):
            at = slice(begin, begin + step_units)
            gate = dot(x, gate_w[at], 1, 1)
            up = dot(x, up_w[at], 1, 1)
            grad_hidden = dot(g, down_w[at], 1, 1)
            sigmoid = 0.5 * jnp.tanh(0.5 * gate) + 0.5
            silu = gate * sigmoid
            hid[:, at] = (silu * up).astype(BF16)
            gg[:, at] = (grad_hidden * up * (sigmoid + silu * (1.0 - sigmoid))).astype(BF16)
            gu[:, at] = (grad_hidden * silu).astype(BF16)
        gn[...] = (dot(gg[...], gate_w, 1, 0) + dot(gu[...], up_w, 1, 0)).astype(BF16)
        part[...] = dot(hid[...], down_w, 1, 0).astype(BF16)

    hbm = pl.BlockSpec(memory_space=pl.ANY)
    by_rows = lambda n: pl.BlockSpec((rows, n), lambda i: (i, 0))
    like = lambda n: jax.ShapeDtypeStruct((size * rows, n), BF16)
    return pl.pallas_call(
        body,
        grid=(size,),
        in_specs=[pl.BlockSpec(memory_space=pltpu.SMEM)]
        + [hbm] * (count + 2 * size),
        out_specs=[by_rows(units)] * 3 + [by_rows(width)] * 4,
        out_shape=[like(units)] * 3 + [like(width)] * 4,
        scratch_shapes=[
            pltpu.VMEM((count, 2 * tall, width), BF16),
            pltpu.VMEM((count, tall, width), BF16),
            pltpu.VMEM((size, rows, width), BF16),
            pltpu.VMEM((size, rows, width), BF16),
            pltpu.SemaphoreType.DMA((2 * count + 2 * size,)),
        ],
        compiler_params=pltpu.CompilerParams(vmem_limit_bytes=VMEM_LIMIT),
        cost_estimate=pl.CostEstimate(flops=1, bytes_accessed=1, transcendentals=0),
        name="feed_forward",
    )(me, *weight_blocks, *row_blocks, *cot_blocks)


def both_heads(pair):
    lane = lax.broadcasted_iota(jnp.int32, pair.shape, 1)
    zero = jnp.zeros_like(pair)
    return jnp.concatenate(
        [jnp.where(lane < HEAD, pair, zero), jnp.where(lane < HEAD, zero, pair)], axis=0
    )


def fill_bias(low_ref, high_ref, place_ref, bias_ref):
    place = place_ref[...]
    allowed = (place >= low_ref[...]) & (place <= high_ref[...])
    bias = jnp.where(allowed, 0.0, MASKED).astype(F32)
    rows = bias.shape[1]
    bias_ref[:, :rows] = bias
    bias_ref[:, rows:] = bias


def own_rows(wide, rows):
    return jnp.concatenate([wide[:HEAD, :rows], wide[HEAD:, rows:]], axis=0)


def pairing(kv_ref, pair, begin):
    both = kv_ref[:, begin : begin + PAIR].astype(F32)
    crossed = pltpu.roll(both, HEAD, 1)
    lane = lax.broadcasted_iota(jnp.int32, both.shape, 1)
    first = jnp.where(pair <= PAIRS // 2, both, crossed)
    second = jnp.where(pair < PAIRS // 2, crossed, both)
    return jnp.where(lane < HEAD, first, second)


def new_pairing(step, pair):
    return (step == 0) | (pair == PAIRS // 2) | (pair == PAIRS // 2 + 1)


def attend_kernel(
    begin_pair, low_ref, high_ref, place_ref, q_ref, kv_ref,
    o_ref, lse_ref, bias_ref, k_ref, vt_ref,
):
    step = pl.program_id(0)
    pair = step + begin_pair

    @pl.when(step == 0)
    def _():
        fill_bias(low_ref, high_ref, place_ref, bias_ref)

    @pl.when(new_pairing(step, pair))
    def _():
        k_ref[...] = pairing(kv_ref, pair, 0).astype(BF16)
        vt_ref[...] = pairing(kv_ref, pair, PAIR).T.astype(BF16)

    rows = q_ref.shape[0]
    queries = both_heads(q_ref[...])
    keys = k_ref[...]
    values_t = vt_ref[...]
    outs, totals = [], []
    for begin in range(0, 2 * rows, 256):
        scores = dot(keys, queries[begin : begin + 256], 1, 1) + bias_ref[:, begin : begin + 256]
        top = jnp.max(scores, axis=0, keepdims=True)
        probs = jnp.exp(scores - top)
        total = jnp.sum(probs, axis=0, keepdims=True)
        outs.append(dot(values_t, probs.astype(BF16), 1, 0) / total)
        totals.append(top + jnp.log(total))
    wide = jnp.concatenate(outs, axis=1)
    o_ref[...] = own_rows(wide, rows).T.astype(BF16)
    lse_ref[0] = jnp.concatenate(totals, axis=1)


def attend_back_kernel(
    begin_pair, low_ref, high_ref, place_ref, q_ref, g_ref, o_ref, lse_ref, kv_ref, *refs,
):
    dq_ref, dkv_ref, bias_ref, k_ref, kt_ref, v_ref, dk_ref, dv_ref = refs[-8:]
    step = pl.program_id(0)
    pair = step + begin_pair

    @pl.when(step == 0)
    def _():
        fill_bias(low_ref, high_ref, place_ref, bias_ref)
        dkv_ref[...] = refs[0][...] if begin_pair else jnp.zeros_like(dkv_ref)

    @pl.when(new_pairing(step, pair))
    def _():
        keys_now = pairing(kv_ref, pair, 0)
        k_ref[...] = keys_now.astype(BF16)
        kt_ref[...] = keys_now.T.astype(BF16)
        v_ref[...] = pairing(kv_ref, pair, PAIR).astype(BF16)
        dk_ref[...] = jnp.zeros_like(dk_ref)
        dv_ref[...] = jnp.zeros_like(dv_ref)

    rows = q_ref.shape[0]
    queries = both_heads(q_ref[...])
    grads = both_heads(g_ref[...])
    keys = k_ref[...]
    keys_t = kt_ref[...]
    values = v_ref[...]
    product = (g_ref[...].astype(F32) * o_ref[...].astype(F32)).T
    delta = jnp.concatenate(
        [
            jnp.sum(product[:HEAD], axis=0, keepdims=True),
            jnp.sum(product[HEAD:], axis=0, keepdims=True),
        ],
        axis=1,
    )
    lse = lse_ref[0]
    outs = []
    for begin in range(0, 2 * rows, 256):
        part = slice(begin, begin + 256)
        scores = dot(keys, queries[part], 1, 1) + bias_ref[:, part]
        probs = jnp.exp(scores - lse[:, part])
        grad_probs = dot(values, grads[part], 1, 1)
        grad_scores = (probs * (grad_probs - delta[:, part])).astype(BF16)
        outs.append(dot(keys_t, grad_scores, 1, 0))
        dk_ref[...] += dot(grad_scores, queries[part], 1, 0)
        dv_ref[...] += dot(probs.astype(BF16), grads[part], 1, 0)
    wide = jnp.concatenate(outs, axis=1)
    dq_ref[...] = own_rows(wide, rows).T * 0.125

    def fold(own_lanes):
        for at, sums in ((0, dk_ref), (PAIR, dv_ref)):
            sums_now = sums[...]
            lane = lax.broadcasted_iota(jnp.int32, sums_now.shape, 1)
            both = sums_now + pltpu.roll(sums_now, HEAD, 1)
            kept = jnp.where((lane < HEAD) == own_lanes, both, 0.0)
            dkv_ref[:, at : at + PAIR] += kept

    @pl.when(pair == PAIRS // 2 - 1)
    def _():
        fold(True)

    @pl.when(pair == PAIRS // 2)
    def _():
        dkv_ref[:, :PAIR] += dk_ref[...]
        dkv_ref[:, PAIR:] += dv_ref[...]

    @pl.when(pair == PAIRS - 1)
    def _():
        fold(False)


def whole(shape):
    return pl.BlockSpec(shape, lambda i: (0,) * len(shape))


def attend(low, high, place, queries, kv_all, begin, pairs):
    rows, count = queries.shape[0], place.shape[0]
    taken = pl.BlockSpec((rows, PAIR), lambda i: (0, i + begin))
    made = pl.BlockSpec((rows, PAIR), lambda i: (0, i))
    return pl.pallas_call(
        functools.partial(attend_kernel, begin),
        grid=(pairs,),
        in_specs=[whole((1, rows)), whole((1, rows)), whole((count, 1)), taken]
        + [whole((count, 2 * KVW))],
        out_specs=[made, pl.BlockSpec((1, 1, 2 * rows), lambda i: (i, 0, 0))],
        out_shape=[
            jax.ShapeDtypeStruct((rows, pairs * PAIR), BF16),
            jax.ShapeDtypeStruct((pairs, 1, 2 * rows), F32),
        ],
        scratch_shapes=[
            pltpu.VMEM((count, 2 * rows), F32),
            pltpu.VMEM((count, PAIR), BF16),
            pltpu.VMEM((PAIR, count), BF16),
        ],
        compiler_params=pltpu.CompilerParams(vmem_limit_bytes=VMEM_LIMIT),
        cost_estimate=pl.CostEstimate(flops=1, bytes_accessed=1, transcendentals=0),
        name="attend",
    )(low, high, place, queries, kv_all)


def attend_back(low, high, place, queries, grads, outs, lse, kv_all, begin, pairs, so_far):
    rows, count = queries.shape[0], place.shape[0]
    taken = pl.BlockSpec((rows, PAIR), lambda i: (0, i + begin))
    made = pl.BlockSpec((rows, PAIR), lambda i: (0, i))
    sums = whole((count, 2 * KVW))
    return pl.pallas_call(
        functools.partial(attend_back_kernel, begin),
        grid=(pairs,),
        in_specs=[whole((1, rows)), whole((1, rows)), whole((count, 1)), taken, taken, made]
        + [pl.BlockSpec((1, 1, 2 * rows), lambda i: (i, 0, 0)), sums]
        + [sums] * len(so_far),
        out_specs=[made, sums],
        out_shape=[
            jax.ShapeDtypeStruct((rows, pairs * PAIR), F32),
            jax.ShapeDtypeStruct((count, 2 * KVW), F32),
        ],
        scratch_shapes=[
            pltpu.VMEM((count, 2 * rows), F32),
            pltpu.VMEM((count, PAIR), BF16),
            pltpu.VMEM((PAIR, count), BF16),
            pltpu.VMEM((count, PAIR), BF16),
            pltpu.VMEM((count, PAIR), F32),
            pltpu.VMEM((count, PAIR), F32),
        ],
        compiler_params=pltpu.CompilerParams(vmem_limit_bytes=VMEM_LIMIT),
        cost_estimate=pl.CostEstimate(flops=1, bytes_accessed=1, transcendentals=0),
        name="attend_back",
    )(low, high, place, queries, grads, outs, lse, kv_all, *so_far)


def rms_scale(values_in):
    return lax.rsqrt(jnp.mean(values_in * values_in, axis=-1, keepdims=True) + EPSILON)


def angle_tables(places):
    exponent = jnp.arange(HEAD // 2, dtype=F32) * 2.0 / HEAD
    frequency = ROPE_BASE ** (-exponent)
    turn = places.astype(F32)[:, None] * frequency[None, :]
    cosine, sine = lax.optimization_barrier((jnp.cos(turn), jnp.sin(turn)))
    return jnp.concatenate([cosine] * 4, axis=1), jnp.concatenate([sine] * 4, axis=1)


def widen(table, width):
    return jnp.concatenate([table] * (width // PAIR), axis=1)


def first_halves(shape):
    return lax.broadcasted_iota(jnp.int32, shape, 1) % HEAD < HEAD // 2


def rotate(tensor, cosine, sine):
    half = HEAD // 2
    ahead, behind = jnp.roll(tensor, -half, axis=1), jnp.roll(tensor, half, axis=1)
    turned = jnp.where(first_halves(tensor.shape), -ahead, behind)
    width = tensor.shape[1]
    return tensor * widen(cosine, width) + turned * widen(sine, width)


def rotate_back(grad_in, cosine, sine):
    half = HEAD // 2
    width = grad_in.shape[1]
    scaled = grad_in * widen(sine, width)
    ahead, behind = jnp.roll(scaled, -half, axis=1), jnp.roll(scaled, half, axis=1)
    return grad_in * widen(cosine, width) + jnp.where(
        first_halves(grad_in.shape), ahead, -behind
    )


def norm_back(grad_in, row_data, scale_in, gain_in):
    gain_term = jnp.sum(grad_in * row_data * scale_in, axis=0)
    grad_normed = grad_in * gain_in
    inner_mean = jnp.mean(grad_normed * row_data, axis=-1, keepdims=True)
    return (
        scale_in * grad_normed - row_data * scale_in * scale_in * scale_in * inner_mean,
        gain_term,
    )


def pad_row(vector, width):
    return jnp.pad(vector, (0, width - vector.shape[0]))[None, :]


def stack_from_lanes(array, count):
    rows, width = array.shape
    return jnp.transpose(array.reshape(rows, count, width // count), (1, 0, 2))


def per_device(
    seq_size, fsdp_size, tokens, segment_ids, positions, norm_one, qkv_weight, qkv_bias,
    out_weight, norm_two, gate_up_weight, down_weight, cotangent,
):
    my_seq, my_fsdp = lax.axis_index("seq"), lax.axis_index("fsdp")
    me = jnp.stack([my_seq, my_fsdp]).astype(jnp.int32)
    offsets = range(seq_size)
    row_count = tokens.shape[0]
    width = qkv_weight.shape[0]
    qkv_rows = qkv_weight.shape[1]
    strip = down_weight.shape[0] // seq_size
    tall = padded(strip)

    qkv_tall = padded(qkv_rows)
    packed = jnp.concatenate(
        [
            jnp.pad(qkv_weight.T, ((0, qkv_tall - qkv_rows), (0, 0))),
            pad_row(norm_one, width),
            pad_row(qkv_bias, width),
            pad_row(norm_two, width),
            jnp.zeros((13, width), BF16),
        ],
        axis=0,
    )
    ff_cut = cut_ff(me, gate_up_weight, down_weight, seq_size)
    ff_share = [ff_cut[0]] + [swap(ff_cut[o], "seq", seq_size, o) for o in offsets if o]
    packed_stack, out_stack = lax.all_gather((after(packed, ff_cut[0]), out_weight), "fsdp", axis=0)
    packed_blocks = seq_gather(packed_stack, seq_size)
    ff_block = join_lanes(me, ff_share)
    ff_blocks = {0: ff_block}
    for bit in fsdp_bits(fsdp_size)[:2]:
        ff_blocks.update({o ^ bit: swap(b, "fsdp", fsdp_size, bit) for o, b in ff_blocks.items()})
    inner = fsdp_size // OUTER

    qkv_blocks = [packed_blocks[o] for o in offsets]
    qkv_blocks[0] = after(qkv_blocks[0], ff_block)
    qkv_t, vectors = join_both(me, qkv_blocks, qkv_tall)
    qkv_t = qkv_t[:, :qkv_rows].reshape(fsdp_size * qkv_rows, -1)
    gain_one = vectors[:, 0, : norm_one.shape[0]].reshape(-1).astype(F32)
    bias_full = vectors[:, 1, : qkv_bias.shape[0]].reshape(-1).astype(F32)
    gain_two = vectors[:, 2, : norm_two.shape[0]].reshape(-1).astype(F32)

    out_blocks = seq_gather(after(out_stack, packed_blocks[seq_size // 2]), seq_size)

    inputs = tokens.astype(F32)
    scale_one = rms_scale(inputs)
    normed_one = (inputs * scale_one * gain_one).astype(BF16)
    joined = dot(normed_one, qkv_t, 1, 1) + bias_full
    cosine, sine = angle_tables(positions)
    turned = rotate(joined[:, : QW + KVW], cosine, sine).astype(BF16)
    queries = turned[:, :QW] * jnp.asarray(0.125, BF16)
    kv_local = jnp.concatenate([turned[:, QW:], joined[:, QW + KVW :].astype(BF16)], axis=1)
    kv_local = after(kv_local, ff_blocks[inner])
    kv_all = lax.all_gather(kv_local, "seq", axis=0, tiled=True)
    kv_all = after(kv_all, ff_blocks[2 * inner], ff_blocks[inner])
    cot_blocks = seq_gather(after(cotangent, kv_all), seq_size)
    row_place = jnp.arange(row_count, dtype=jnp.int32)
    high = my_seq * row_count + row_place
    low = high - positions
    place = jnp.arange(seq_size * row_count, dtype=jnp.int32)[:, None]
    low, high = low[None, :], high[None, :]
    split = PAIRS // 2 + 1
    spread = lambda block: ff_spread(block, fsdp_size)
    own, near = ff_blocks[0], ff_blocks[inner]
    far, last = ff_blocks[2 * inner], ff_blocks[3 * inner]
    own_x = spread(own)
    near_x = spread(after(near, kv_all))
    attn_one, lse_one = attend(low, high, place, after(queries, far), kv_all, 0, split)
    far_x = spread(after(far, kv_all))
    queries_two = after(queries, attn_one, cot_blocks[seq_size // 2], *near_x.values())
    attn_two, lse_two = attend(low, high, place, queries_two, kv_all, split, PAIRS - split)
    last_x = spread(after(last, attn_two))
    for base, row in ((0, own_x), (inner, near_x), (2 * inner, far_x), (3 * inner, last_x)):
        ff_blocks.update({base + m: block for m, block in row.items()})
    attn_flat = jnp.concatenate([attn_one, attn_two], axis=1)

    out_list = [after(out_blocks[0], attn_one)] + [out_blocks[o] for o in offsets if o]
    out_full = join_both(me, out_list, out_weight.shape[0])[0].reshape(QW, -1)

    residual = inputs + dot(attn_flat, out_full, 1, 0)
    scale_two = rms_scale(residual)
    normed_two = (residual * scale_two * gain_two).astype(BF16)
    normed_blocks = seq_gather(after(normed_two, *far_x.values()), seq_size)
    hidden, grad_gate, grad_up, grad_normed, layer_part, normed_all, cot_all = feed_forward(
        me,
        [ff_blocks[o] for o in range(fsdp_size)],
        [normed_blocks[o] for o in offsets],
        [cot_blocks[o] for o in offsets],
    )
    by_seq = lambda rows: rows.reshape(seq_size, row_count, -1)

    kept, given = halve(by_seq(grad_normed), 1, my_seq)
    normed_sum = add(kept, swap(given, "seq", seq_size, 1))
    bit = 2
    while bit < seq_size:
        kept, given = halve(normed_sum, 1, my_seq // bit)
        normed_sum = add(kept, swap(given, "seq", seq_size, bit))
        bit *= 2
    grad_normed_two = normed_sum[0]
    hidden = after(hidden, given)
    down_term = dot(hidden, cot_all, 0, 0).astype(BF16).reshape(fsdp_size, tall, -1)
    grad_gate, grad_up = after(grad_gate, down_term), after(grad_up, down_term)
    gate_term = dot(grad_gate, normed_all, 0, 0).astype(BF16).reshape(fsdp_size // 2, 2, tall, -1)
    up_term = dot(grad_up, normed_all, 0, 0).astype(BF16).reshape(fsdp_size // 2, 2, tall, -1)

    bits = list(reversed(fsdp_bits(fsdp_size)))

    def give(stack, at):
        kept, given = fsdp_halve(stack, fsdp_size, bits[at], my_fsdp, bits[:at])
        return kept, given

    def send(given, at):
        return swap(given, "fsdp", fsdp_size, bits[at])

    def finish(kept, got, at):
        stack = add(kept, got)
        for later in range(at + 1, len(bits)):
            kept, given = give(stack, later)
            stack = add(kept, send(given, later))
        return stack[0]

    kept_one, given = give(down_term, 0)
    got_one = send(given, 0)
    kept_two, given = give(jnp.concatenate([gate_term[:, 0], up_term[:, 0]], axis=0), 0)
    got_two = send(given, 0)
    kept_three, given_three = give(jnp.concatenate([gate_term[:, 1], up_term[:, 1]], axis=0), 0)

    kept, given = halve(after(by_seq(layer_part), down_term), 1, my_seq)
    layer_sum = add(kept, swap(given, "seq", seq_size, 1))
    bit = 2
    while bit < seq_size:
        kept, given = halve(layer_sum, 1, my_seq // bit)
        given = after(given, grad_normed_two)
        layer_sum = add(kept, swap(given, "seq", seq_size, bit))
        bit *= 2
    layer_out = residual + layer_sum[0]

    grad_path, norm_two_term = norm_back(grad_normed_two, residual, scale_two, gain_two)
    grad_residual = cotangent.astype(F32) + grad_path
    grad_branch = grad_residual.astype(BF16)
    grad_attn = dot(grad_branch, out_full, 1, 1).astype(BF16)
    out_term = stack_from_lanes(dot(attn_flat, grad_branch, 0, 0).astype(BF16), seq_size)
    out_mine = seq_scatter(out_term, seq_size, my_seq).reshape(fsdp_size, -1, width)
    grad_attn = after(grad_attn, gate_term, up_term)
    dq_one, kv_terms = attend_back(
        low, high, place, queries, grad_attn, attn_one, lse_one, kv_all, 0, split, ()
    )
    got_one = after(got_one, dq_one)
    got_three = send(after(given_three, got_one), 0)
    kept_one, given = give(add(kept_one, got_one), 1)
    next_one = send(given, 1)
    queries_two = after(queries, kv_terms, got_one)
    dq_two, kv_terms = attend_back(
        low, high, place, queries_two, grad_attn, attn_two, lse_two, kv_all, split,
        PAIRS - split, (kv_terms,),
    )
    got_two = after(got_two, dq_two)
    down_sum = finish(kept_one, after(next_one, dq_two), 1)
    kept_two, given = give(add(kept_two, got_two), 1)
    next_two = send(given, 1)
    kv_mine = seq_scatter(by_seq(kv_terms), seq_size, my_seq)
    got_three = after(got_three, kv_mine)
    kept_three, given = give(add(kept_three, got_three), 1)
    next_three = send(given, 1)
    turned_back = rotate_back(
        jnp.concatenate([dq_one, dq_two, kv_mine[:, :KVW]], axis=1), cosine, sine
    )
    grad_joined = jnp.concatenate([turned_back, kv_mine[:, KVW:]], axis=1).astype(BF16)
    grad_normed_one = dot(grad_joined, qkv_t, 1, 0)
    grad_path_one, norm_one_term = norm_back(grad_normed_one, inputs, scale_one, gain_one)
    grad_tokens = grad_residual + grad_path_one
    bias_term = jnp.sum(grad_joined.astype(F32), axis=0)

    def vector_rows(vector):
        rows = vector.reshape(fsdp_size, 1, -1)
        return jnp.pad(rows, ((0, 0), (0, 0), (0, width - rows.shape[2])))

    vector_terms = [norm_one_term, bias_term[: QW + KVW], bias_term[QW + KVW :], norm_two_term]
    small = jnp.concatenate([vector_rows(v) for v in vector_terms], axis=1).astype(BF16)
    small = jnp.pad(small, ((0, 0), (0, 16 - len(vector_terms)), (0, 0)))
    qkv_term = stack_from_lanes(dot(grad_joined, normed_one, 0, 0).astype(BF16), seq_size)
    qkv_term = qkv_term.reshape(seq_size, fsdp_size, qkv_rows, width)
    tail = jnp.concatenate(
        [qkv_term, jnp.broadcast_to(small[None], (seq_size,) + small.shape)], axis=2
    )
    tail_mine = seq_scatter(after(tail, got_three), seq_size, my_seq)
    one_sum = finish(kept_two, after(next_two, tail), 1)
    two_sum = finish(kept_three, next_three, 1)

    ff_back = cut_lanes(me, (one_sum, two_sum, down_sum), seq_size)
    ff_got = [ff_back[0]] + [swap(ff_back[o], "seq", seq_size, o) for o in offsets if o]
    grad_gate_up, grad_down = join_ff(me, ff_got, strip)

    tail_sum = fsdp_scatter(
        jnp.concatenate([tail_mine, out_mine], axis=1), fsdp_size, my_fsdp
    )
    pieces = [
        tail_sum[qkv_rows + i, : v.shape[0] // fsdp_size] for i, v in enumerate(vector_terms)
    ]
    return (
        layer_out.astype(BF16),
        grad_tokens,
        pieces[0],
        tail_sum[:qkv_rows].T,
        pieces[1],
        pieces[2],
        tail_sum[qkv_rows + 16 :],
        pieces[3],
        grad_gate_up,
        grad_down,
    )


def solution(mesh):
    rows, both = P(("fsdp", "seq"), None), P(("fsdp", "seq"))
    return jax.shard_map(
        functools.partial(per_device, mesh.shape["seq"], mesh.shape["fsdp"]),
        mesh=mesh,
        in_specs=(
            rows, both, both, P("fsdp"), P("seq", "fsdp"), P("fsdp"), P("fsdp", "seq"),
            P("fsdp"), P("seq", "fsdp"), P("fsdp", "seq"), rows,
        ),
        out_specs=(
            rows, rows, P("fsdp"), P("seq", "fsdp"), P("fsdp"), P("fsdp"), P("fsdp", "seq"),
            P("fsdp"), P("seq", "fsdp"), P("fsdp", "seq"),
        ),
        check_vma=False,
    )
```

```python
import functools

import jax
import jax.numpy as jnp
from jax import lax
from jax.experimental import pallas as pl
from jax.experimental.pallas import tpu as pltpu
from jax.sharding import PartitionSpec as P

HEADS = 14
KV_HEADS = 2
HEAD = 64
FF = 4864
QW = 896
KVW = 128
PAIR = 2 * HEAD
PAIRS = HEADS // 2
OUTER = 4

EPSILON = 1e-06
ROPE_BASE = 1000000.0
MASKED = -1e30
VMEM_LIMIT = 50 * 1024 * 1024

F32 = jnp.float32
BF16 = jnp.bfloat16


def dot(left, right, left_dim, right_dim):
    return lax.dot_general(
        left, right, (((left_dim,), (right_dim,)), ((), ())), preferred_element_type=F32
    )


def swap(block, axis, size, bits):
    return lax.ppermute(block, axis, [(i, i ^ bits) for i in range(size)])


def after(array, *others):
    return lax.optimization_barrier((array,) + others)[0]


def seq_gather(block, size):
    blocks = {0: block}
    bit = size // 2
    while bit:
        blocks.update({o ^ bit: swap(b, "seq", size, bit) for o, b in blocks.items()})
        bit //= 2
    return blocks


def fsdp_bits(size):
    inner = size // OUTER
    outer_bits, inner_bits = [], []
    bit = 1
    while bit < size:
        (outer_bits if bit >= inner else inner_bits).append(bit)
        bit *= 2
    return outer_bits + inner_bits


def column_gather(block, size):
    inner = size // OUTER
    return jnp.stack([block] + [swap(block, "fsdp", size, k * inner) for k in range(1, OUTER)])


def ff_spread(block, size):
    blocks = {0: block}
    for bit in fsdp_bits(size)[2:]:
        blocks.update({o ^ bit: swap(b, "fsdp", size, bit) for o, b in blocks.items()})
    return blocks


def halve(stack, bit, me):
    above = stack.shape[0] // (2 * bit)
    cut = stack.reshape((above, 2, bit) + stack.shape[1:])
    digit = (me // bit) % 2
    kept = lax.dynamic_index_in_dim(cut, digit, 1, keepdims=False)
    given = lax.dynamic_index_in_dim(cut, 1 - digit, 1, keepdims=False)
    merge = lambda part: part.reshape((above * bit,) + stack.shape[1:])
    return merge(kept), merge(given).astype(BF16)


def add(kept, got):
    return kept.astype(F32) + got.astype(F32)


def seq_scatter(stack, size, me):
    bit = 1
    while bit < size:
        kept, given = halve(stack, 1, me // bit)
        stack = add(kept, swap(given, "seq", size, bit))
        bit *= 2
    return stack[0]


def fsdp_halve(stack, size, bit, me, resolved):
    place = bit
    digit = me // bit
    for taken in resolved:
        if taken < bit:
            place //= 2
    kept, given = halve(stack, place, digit * place)
    return kept, given


def fsdp_scatter(stack, size, me):
    resolved = []
    for bit in reversed(fsdp_bits(size)):
        kept, given = fsdp_halve(stack, size, bit, me, resolved)
        stack = add(kept, swap(given, "fsdp", size, bit))
        resolved.append(bit)
    return stack[0]


def on_device(body, name, out_shapes, scratch, me, arrays):
    vmem = pl.BlockSpec(memory_space=pltpu.VMEM)
    return pl.pallas_call(
        body,
        in_specs=[pl.BlockSpec(memory_space=pltpu.SMEM)] + [vmem] * len(arrays),
        out_specs=[vmem] * len(out_shapes),
        out_shape=out_shapes,
        scratch_shapes=scratch,
        compiler_params=pltpu.CompilerParams(vmem_limit_bytes=VMEM_LIMIT),
        name=name,
    )(me, *arrays)


def padded(rows):
    return -(-rows // 16) * 16


def cut_ff(me, gate_up_weight, down_weight, size):
    width = gate_up_weight.shape[0]
    half = down_weight.shape[0]
    strip = half // size
    tall = padded(strip)

    def body(me_ref, gu_ref, d_ref, *refs):
        outs, held = refs[:size], refs[size]
        turned = gu_ref[...].astype(F32).T
        down = d_ref[...].astype(F32)
        blank = jnp.zeros((tall - strip, width), F32)
        for q in range(size):
            one = turned[q * strip : (q + 1) * strip]
            two = turned[half + q * strip : half + (q + 1) * strip]
            three = down[q * strip : (q + 1) * strip]
            parts = [one, blank, two, blank, three, blank]
            held[q] = jnp.concatenate(parts, axis=0).astype(BF16)
        for o in range(size):
            outs[o][...] = held[me_ref[0] ^ o]

    shape = jax.ShapeDtypeStruct((3 * tall, width), BF16)
    scratch = [pltpu.VMEM((size, 3 * tall, width), BF16)]
    return on_device(body, "cut_ff", [shape] * size, scratch, me, (gate_up_weight, down_weight))


def join_lanes(me, blocks):
    size = len(blocks)
    rows, width = blocks[0].shape

    def body(me_ref, *refs):
        ins, out, held = refs[:size], refs[size], refs[size + 1]
        for o in range(size):
            held[me_ref[0] ^ o] = ins[o][...]
        out[...] = jnp.concatenate([held[q].astype(F32) for q in range(size)], 1).astype(BF16)

    return on_device(
        body,
        "join_lanes",
        [jax.ShapeDtypeStruct((rows, size * width), BF16)],
        [pltpu.VMEM((size, rows, width), BF16)],
        me,
        blocks,
    )[0]


def join_both(me, pieces, rows):
    size, parts_each = len(pieces), len(pieces[0])
    _, tall, width = pieces[0][0].shape
    count = sum(part.shape[0] for part in pieces[0])
    inner = count // OUTER
    order = [k * inner + m for m in range(inner) for k in range(OUTER)]
    shapes = [jax.ShapeDtypeStruct((count, rows, size * width), BF16)]
    if tall > rows:
        shapes.append(jax.ShapeDtypeStruct((count, tall - rows, width), BF16))

    def body(me_ref, *refs):
        ins, out, held = refs[: size * parts_each], refs[size * parts_each], refs[-1]
        for o in range(size):
            at = 0
            for part in ins[o * parts_each : (o + 1) * parts_each]:
                for j in range(part.shape[0]):
                    place = me_ref[1] ^ order[at]
                    held[me_ref[0] ^ o, place] = part[j]
                    if tall > rows and o == 0:
                        refs[size * parts_each + 1][place] = part[j, rows:]
                    at += 1
        for f in range(count):
            parts = [held[q, f, :rows].astype(F32) for q in range(size)]
            out[f] = jnp.concatenate(parts, axis=1).astype(BF16)

    return on_device(
        body,
        "join_both",
        shapes,
        [pltpu.VMEM((size, count, tall, width), BF16)],
        me,
        [block for row in pieces for block in row],
    )


def cut_lanes(me, sums, size):
    rows = sum(s.shape[0] for s in sums)
    width = sums[0].shape[1] // size

    def body(me_ref, *refs):
        ins, outs, held = refs[: len(sums)], refs[len(sums) : -1], refs[-1]
        whole = jnp.concatenate([r[...] for r in ins], axis=0)
        for q in range(size):
            held[q] = whole[:, q * width : (q + 1) * width].astype(BF16)
        for o in range(size):
            outs[o][...] = held[me_ref[0] ^ o]

    shape = jax.ShapeDtypeStruct((rows, width), BF16)
    scratch = [pltpu.VMEM((size, rows, width), BF16)]
    return on_device(body, "cut_lanes", [shape] * size, scratch, me, sums)


def join_ff(me, blocks, strip):
    size = len(blocks)
    rows, width = blocks[0].shape
    tall = rows // 3

    def body(me_ref, *refs):
        ins, gu, down, held = refs[:size], refs[size], refs[size + 1], refs[size + 2]
        for o in range(size):
            held[me_ref[0] ^ o] = ins[o][...].astype(F32)
        cut = [
            [held[q, i * tall : i * tall + strip] for q in range(size)] for i in range(3)
        ]
        gu[...] = jnp.concatenate(cut[0] + cut[1], axis=0).T
        down[...] = jnp.concatenate(cut[2], axis=0)

    return on_device(
        body,
        "join_ff",
        [
            jax.ShapeDtypeStruct((width, 2 * size * strip), F32),
            jax.ShapeDtypeStruct((size * strip, width), F32),
        ],
        [pltpu.VMEM((size, rows, width), F32)],
        me,
        blocks,
    )


def feed_forward(me, weight_blocks, row_blocks, cot_blocks):
    count, size = len(weight_blocks), len(row_blocks)
    rows, width = row_blocks[0].shape
    tall = weight_blocks[0].shape[0] // 3
    units = count * tall
    step_units = 256

    def body(me_ref, *refs):
        blocks = refs[:count]
        xs, gs = refs[count : count + size], refs[count + size : count + 2 * size]
        hid, gg, gu, gn, part, x_out, g_out = refs[count + 2 * size : count + 2 * size + 7]
        gu_w, d_w, x_all, g_all, sems = refs[count + 2 * size + 7 :]
        step = pl.program_id(0)

        @pl.when(step == 0)
        def _():
            copies = []
            for o in range(count):
                f = me_ref[1] ^ o
                copies.append((blocks[o].at[pl.ds(0, 2 * tall)], gu_w.at[f]))
                copies.append((blocks[o].at[pl.ds(2 * tall, tall)], d_w.at[f]))
            for o in range(size):
                copies.append((xs[o], x_all.at[me_ref[0] ^ o]))
                copies.append((gs[o], g_all.at[me_ref[0] ^ o]))
            started = [
                pltpu.make_async_copy(src, dst, sems.at[i]) for i, (src, dst) in enumerate(copies)
            ]
            for copy in started:
                copy.start()
            for copy in started:
                copy.wait()

        x = x_all[step]
        g = g_all[step]
        x_out[...] = x
        g_out[...] = g
        gate_w = gu_w[: count // 2].reshape(units, width)
        up_w = gu_w[count // 2 :].reshape(units, width)
        down_w = d_w[...].reshape(units, width)
        for begin in range(0, units, step_units):
            at = slice(begin, begin + step_units)
            gate = dot(x, gate_w[at], 1, 1)
            up = dot(x, up_w[at], 1, 1)
            grad_hidden = dot(g, down_w[at], 1, 1)
            sigmoid = 0.5 * jnp.tanh(0.5 * gate) + 0.5
            silu = gate * sigmoid
            hid[:, at] = (silu * up).astype(BF16)
            gg[:, at] = (grad_hidden * up * (sigmoid + silu * (1.0 - sigmoid))).astype(BF16)
            gu[:, at] = (grad_hidden * silu).astype(BF16)
        gn[...] = (dot(gg[...], gate_w, 1, 0) + dot(gu[...], up_w, 1, 0)).astype(BF16)
        part[...] = dot(hid[...], down_w, 1, 0).astype(BF16)

    hbm = pl.BlockSpec(memory_space=pl.ANY)
    by_rows = lambda n: pl.BlockSpec((rows, n), lambda i: (i, 0))
    like = lambda n: jax.ShapeDtypeStruct((size * rows, n), BF16)
    return pl.pallas_call(
        body,
        grid=(size,),
        in_specs=[pl.BlockSpec(memory_space=pltpu.SMEM)]
        + [hbm] * (count + 2 * size),
        out_specs=[by_rows(units)] * 3 + [by_rows(width)] * 4,
        out_shape=[like(units)] * 3 + [like(width)] * 4,
        scratch_shapes=[
            pltpu.VMEM((count, 2 * tall, width), BF16),
            pltpu.VMEM((count, tall, width), BF16),
            pltpu.VMEM((size, rows, width), BF16),
            pltpu.VMEM((size, rows, width), BF16),
            pltpu.SemaphoreType.DMA((2 * count + 2 * size,)),
        ],
        compiler_params=pltpu.CompilerParams(vmem_limit_bytes=VMEM_LIMIT),
        cost_estimate=pl.CostEstimate(flops=1, bytes_accessed=1, transcendentals=0),
        name="feed_forward",
    )(me, *weight_blocks, *row_blocks, *cot_blocks)


def both_heads(pair):
    lane = lax.broadcasted_iota(jnp.int32, pair.shape, 1)
    zero = jnp.zeros_like(pair)
    return jnp.concatenate(
        [jnp.where(lane < HEAD, pair, zero), jnp.where(lane < HEAD, zero, pair)], axis=0
    )


def fill_bias(low_ref, high_ref, place_ref, bias_ref):
    place = place_ref[...]
    allowed = (place >= low_ref[...]) & (place <= high_ref[...])
    bias = jnp.where(allowed, 0.0, MASKED).astype(F32)
    rows = bias.shape[1]
    bias_ref[:, :rows] = bias
    bias_ref[:, rows:] = bias


def own_rows(wide, rows):
    return jnp.concatenate([wide[:HEAD, :rows], wide[HEAD:, rows:]], axis=0)


def pairing(kv_ref, pair, begin):
    both = kv_ref[:, begin : begin + PAIR].astype(F32)
    crossed = pltpu.roll(both, HEAD, 1)
    lane = lax.broadcasted_iota(jnp.int32, both.shape, 1)
    first = jnp.where(pair <= PAIRS // 2, both, crossed)
    second = jnp.where(pair < PAIRS // 2, crossed, both)
    return jnp.where(lane < HEAD, first, second)


def new_pairing(step, pair):
    return (step == 0) | (pair == PAIRS // 2) | (pair == PAIRS // 2 + 1)


def attend_kernel(
    begin_pair, low_ref, high_ref, place_ref, q_ref, kv_ref,
    o_ref, lse_ref, bias_ref, k_ref, vt_ref,
):
    step = pl.program_id(0)
    pair = step + begin_pair

    @pl.when(step == 0)
    def _():
        fill_bias(low_ref, high_ref, place_ref, bias_ref)

    @pl.when(new_pairing(step, pair))
    def _():
        k_ref[...] = pairing(kv_ref, pair, 0).astype(BF16)
        vt_ref[...] = pairing(kv_ref, pair, PAIR).T.astype(BF16)

    rows = q_ref.shape[0]
    queries = both_heads(q_ref[...])
    keys = k_ref[...]
    values_t = vt_ref[...]
    outs, totals = [], []
    for begin in range(0, 2 * rows, 256):
        scores = dot(keys, queries[begin : begin + 256], 1, 1) + bias_ref[:, begin : begin + 256]
        top = jnp.max(scores, axis=0, keepdims=True)
        probs = jnp.exp(scores - top)
        total = jnp.sum(probs, axis=0, keepdims=True)
        outs.append(dot(values_t, probs.astype(BF16), 1, 0) / total)
        totals.append(top + jnp.log(total))
    wide = jnp.concatenate(outs, axis=1)
    o_ref[...] = own_rows(wide, rows).T.astype(BF16)
    lse_ref[0] = jnp.concatenate(totals, axis=1)


def attend_back_kernel(
    begin_pair, low_ref, high_ref, place_ref, q_ref, g_ref, o_ref, lse_ref, kv_ref, *refs,
):
    dq_ref, dkv_ref, bias_ref, k_ref, kt_ref, v_ref, dk_ref, dv_ref = refs[-8:]
    step = pl.program_id(0)
    pair = step + begin_pair

    @pl.when(step == 0)
    def _():
        fill_bias(low_ref, high_ref, place_ref, bias_ref)
        dkv_ref[...] = refs[0][...] if begin_pair else jnp.zeros_like(dkv_ref)

    @pl.when(new_pairing(step, pair))
    def _():
        keys_now = pairing(kv_ref, pair, 0)
        k_ref[...] = keys_now.astype(BF16)
        kt_ref[...] = keys_now.T.astype(BF16)
        v_ref[...] = pairing(kv_ref, pair, PAIR).astype(BF16)
        dk_ref[...] = jnp.zeros_like(dk_ref)
        dv_ref[...] = jnp.zeros_like(dv_ref)

    rows = q_ref.shape[0]
    queries = both_heads(q_ref[...])
    grads = both_heads(g_ref[...])
    keys = k_ref[...]
    keys_t = kt_ref[...]
    values = v_ref[...]
    product = (g_ref[...].astype(F32) * o_ref[...].astype(F32)).T
    delta = jnp.concatenate(
        [
            jnp.sum(product[:HEAD], axis=0, keepdims=True),
            jnp.sum(product[HEAD:], axis=0, keepdims=True),
        ],
        axis=1,
    )
    lse = lse_ref[0]
    outs = []
    for begin in range(0, 2 * rows, 256):
        part = slice(begin, begin + 256)
        scores = dot(keys, queries[part], 1, 1) + bias_ref[:, part]
        probs = jnp.exp(scores - lse[:, part])
        grad_probs = dot(values, grads[part], 1, 1)
        grad_scores = (probs * (grad_probs - delta[:, part])).astype(BF16)
        outs.append(dot(keys_t, grad_scores, 1, 0))
        dk_ref[...] += dot(grad_scores, queries[part], 1, 0)
        dv_ref[...] += dot(probs.astype(BF16), grads[part], 1, 0)
    wide = jnp.concatenate(outs, axis=1)
    dq_ref[...] = own_rows(wide, rows).T * 0.125

    def fold(own_lanes):
        for at, sums in ((0, dk_ref), (PAIR, dv_ref)):
            sums_now = sums[...]
            lane = lax.broadcasted_iota(jnp.int32, sums_now.shape, 1)
            both = sums_now + pltpu.roll(sums_now, HEAD, 1)
            kept = jnp.where((lane < HEAD) == own_lanes, both, 0.0)
            dkv_ref[:, at : at + PAIR] += kept

    @pl.when(pair == PAIRS // 2 - 1)
    def _():
        fold(True)

    @pl.when(pair == PAIRS // 2)
    def _():
        dkv_ref[:, :PAIR] += dk_ref[...]
        dkv_ref[:, PAIR:] += dv_ref[...]

    @pl.when(pair == PAIRS - 1)
    def _():
        fold(False)


def whole(shape):
    return pl.BlockSpec(shape, lambda i: (0,) * len(shape))


def attend(low, high, place, queries, kv_all, begin, pairs):
    rows, count = queries.shape[0], place.shape[0]
    taken = pl.BlockSpec((rows, PAIR), lambda i: (0, i + begin))
    made = pl.BlockSpec((rows, PAIR), lambda i: (0, i))
    return pl.pallas_call(
        functools.partial(attend_kernel, begin),
        grid=(pairs,),
        in_specs=[whole((1, rows)), whole((1, rows)), whole((count, 1)), taken]
        + [whole((count, 2 * KVW))],
        out_specs=[made, pl.BlockSpec((1, 1, 2 * rows), lambda i: (i, 0, 0))],
        out_shape=[
            jax.ShapeDtypeStruct((rows, pairs * PAIR), BF16),
            jax.ShapeDtypeStruct((pairs, 1, 2 * rows), F32),
        ],
        scratch_shapes=[
            pltpu.VMEM((count, 2 * rows), F32),
            pltpu.VMEM((count, PAIR), BF16),
            pltpu.VMEM((PAIR, count), BF16),
        ],
        compiler_params=pltpu.CompilerParams(vmem_limit_bytes=VMEM_LIMIT),
        cost_estimate=pl.CostEstimate(flops=1, bytes_accessed=1, transcendentals=0),
        name="attend",
    )(low, high, place, queries, kv_all)


def attend_back(low, high, place, queries, grads, outs, lse, kv_all, begin, pairs, so_far):
    rows, count = queries.shape[0], place.shape[0]
    taken = pl.BlockSpec((rows, PAIR), lambda i: (0, i + begin))
    made = pl.BlockSpec((rows, PAIR), lambda i: (0, i))
    sums = whole((count, 2 * KVW))
    return pl.pallas_call(
        functools.partial(attend_back_kernel, begin),
        grid=(pairs,),
        in_specs=[whole((1, rows)), whole((1, rows)), whole((count, 1)), taken, taken, made]
        + [pl.BlockSpec((1, 1, 2 * rows), lambda i: (i, 0, 0)), sums]
        + [sums] * len(so_far),
        out_specs=[made, sums],
        out_shape=[
            jax.ShapeDtypeStruct((rows, pairs * PAIR), F32),
            jax.ShapeDtypeStruct((count, 2 * KVW), F32),
        ],
        scratch_shapes=[
            pltpu.VMEM((count, 2 * rows), F32),
            pltpu.VMEM((count, PAIR), BF16),
            pltpu.VMEM((PAIR, count), BF16),
            pltpu.VMEM((count, PAIR), BF16),
            pltpu.VMEM((count, PAIR), F32),
            pltpu.VMEM((count, PAIR), F32),
        ],
        compiler_params=pltpu.CompilerParams(vmem_limit_bytes=VMEM_LIMIT),
        cost_estimate=pl.CostEstimate(flops=1, bytes_accessed=1, transcendentals=0),
        name="attend_back",
    )(low, high, place, queries, grads, outs, lse, kv_all, *so_far)


def rms_scale(values_in):
    return lax.rsqrt(jnp.mean(values_in * values_in, axis=-1, keepdims=True) + EPSILON)


def angle_tables(places):
    exponent = jnp.arange(HEAD // 2, dtype=F32) * 2.0 / HEAD
    frequency = ROPE_BASE ** (-exponent)
    turn = places.astype(F32)[:, None] * frequency[None, :]
    cosine, sine = lax.optimization_barrier((jnp.cos(turn), jnp.sin(turn)))
    return jnp.concatenate([cosine] * 4, axis=1), jnp.concatenate([sine] * 4, axis=1)


def widen(table, width):
    return jnp.concatenate([table] * (width // PAIR), axis=1)


def first_halves(shape):
    return lax.broadcasted_iota(jnp.int32, shape, 1) % HEAD < HEAD // 2


def rotate(tensor, cosine, sine):
    half = HEAD // 2
    ahead, behind = jnp.roll(tensor, -half, axis=1), jnp.roll(tensor, half, axis=1)
    turned = jnp.where(first_halves(tensor.shape), -ahead, behind)
    width = tensor.shape[1]
    return tensor * widen(cosine, width) + turned * widen(sine, width)


def rotate_back(grad_in, cosine, sine):
    half = HEAD // 2
    width = grad_in.shape[1]
    scaled = grad_in * widen(sine, width)
    ahead, behind = jnp.roll(scaled, -half, axis=1), jnp.roll(scaled, half, axis=1)
    return grad_in * widen(cosine, width) + jnp.where(
        first_halves(grad_in.shape), ahead, -behind
    )


def norm_back(grad_in, row_data, scale_in, gain_in):
    gain_term = jnp.sum(grad_in * row_data * scale_in, axis=0)
    grad_normed = grad_in * gain_in
    inner_mean = jnp.mean(grad_normed * row_data, axis=-1, keepdims=True)
    return (
        scale_in * grad_normed - row_data * scale_in * scale_in * scale_in * inner_mean,
        gain_term,
    )


def pad_row(vector, width):
    return jnp.pad(vector, (0, width - vector.shape[0]))[None, :]


def stack_from_lanes(array, count):
    rows, width = array.shape
    return jnp.transpose(array.reshape(rows, count, width // count), (1, 0, 2))


def per_device(
    seq_size, fsdp_size, tokens, segment_ids, positions, norm_one, qkv_weight, qkv_bias,
    out_weight, norm_two, gate_up_weight, down_weight, cotangent,
):
    my_seq, my_fsdp = lax.axis_index("seq"), lax.axis_index("fsdp")
    me = jnp.stack([my_seq, my_fsdp]).astype(jnp.int32)
    offsets = range(seq_size)
    row_count = tokens.shape[0]
    width = qkv_weight.shape[0]
    qkv_rows = qkv_weight.shape[1]
    strip = down_weight.shape[0] // seq_size
    tall = padded(strip)

    qkv_tall = padded(qkv_rows)
    packed = jnp.concatenate(
        [
            jnp.pad(qkv_weight.T, ((0, qkv_tall - qkv_rows), (0, 0))),
            pad_row(norm_one, width),
            pad_row(qkv_bias, width),
            pad_row(norm_two, width),
            jnp.zeros((13, width), BF16),
            out_weight,
        ],
        axis=0,
    )
    ff_cut = cut_ff(me, gate_up_weight, down_weight, seq_size)
    ff_share = [ff_cut[0]] + [swap(ff_cut[o], "seq", seq_size, o) for o in offsets if o]
    columns = ff_spread(after(column_gather(packed, fsdp_size), ff_cut[1]), fsdp_size)
    ff_block = join_lanes(me, ff_share)
    wide = qkv_tall + 16
    packed_stack = jnp.concatenate([columns[m][:, :wide] for m in sorted(columns)], axis=0)
    out_stack = jnp.concatenate([columns[m][:, wide:] for m in sorted(columns)], axis=0)
    packed_blocks = seq_gather(after(packed_stack, ff_block), seq_size)
    ff_blocks = {0: ff_block}
    for bit in fsdp_bits(fsdp_size)[:2]:
        ff_blocks.update({o ^ bit: swap(b, "fsdp", fsdp_size, bit) for o, b in ff_blocks.items()})
    inner = fsdp_size // OUTER

    qkv_pieces = [[packed_blocks[o]] for o in offsets]
    qkv_t, vectors = join_both(me, qkv_pieces, qkv_tall)
    qkv_t = after(qkv_t, ff_blocks[2 * inner], ff_blocks[inner])[:, :qkv_rows].reshape(fsdp_size * qkv_rows, -1)
    gain_one = vectors[:, 0, : norm_one.shape[0]].reshape(-1).astype(F32)
    bias_full = vectors[:, 1, : qkv_bias.shape[0]].reshape(-1).astype(F32)
    gain_two = vectors[:, 2, : norm_two.shape[0]].reshape(-1).astype(F32)

    out_blocks = seq_gather(after(out_stack, packed_blocks[seq_size // 2]), seq_size)

    inputs = tokens.astype(F32)
    scale_one = rms_scale(inputs)
    normed_one = (inputs * scale_one * gain_one).astype(BF16)
    joined = dot(normed_one, qkv_t, 1, 1) + bias_full
    cosine, sine = angle_tables(positions)
    turned = rotate(joined[:, : QW + KVW], cosine, sine).astype(BF16)
    queries = turned[:, :QW] * jnp.asarray(0.125, BF16)
    kv_local = jnp.concatenate([turned[:, QW:], joined[:, QW + KVW :].astype(BF16)], axis=1)
    kv_all = lax.all_gather(kv_local, "seq", axis=0, tiled=True)
    kv_all = after(kv_all, ff_blocks[2 * inner], ff_blocks[inner])
    cot_blocks = seq_gather(after(cotangent, kv_all), seq_size)
    row_place = jnp.arange(row_count, dtype=jnp.int32)
    high = my_seq * row_count + row_place
    low = high - positions
    place = jnp.arange(seq_size * row_count, dtype=jnp.int32)[:, None]
    low, high = low[None, :], high[None, :]
    split = PAIRS // 2 + 1
    spread = lambda block: ff_spread(block, fsdp_size)
    own, near = ff_blocks[0], ff_blocks[inner]
    far, last = ff_blocks[2 * inner], ff_blocks[3 * inner]
    own_x = spread(own)
    near_x = spread(after(near, kv_all))
    attn_one, lse_one = attend(low, high, place, after(queries, far), kv_all, 0, split)
    far_x = spread(after(far, kv_all))
    queries_two = after(queries, attn_one, cot_blocks[seq_size // 2])
    attn_two, lse_two = attend(low, high, place, queries_two, kv_all, split, PAIRS - split)
    last_x = spread(last)
    for base, row in ((0, own_x), (inner, near_x), (2 * inner, far_x), (3 * inner, last_x)):
        ff_blocks.update({base + m: block for m, block in row.items()})
    attn_flat = jnp.concatenate([attn_one, attn_two], axis=1)

    out_list = [[out_blocks[o]] for o in offsets]
    out_list[0][0] = after(out_list[0][0], attn_one)
    out_full = join_both(me, out_list, out_weight.shape[0])[0].reshape(QW, -1)

    residual = inputs + dot(attn_flat, out_full, 1, 0)
    scale_two = rms_scale(residual)
    normed_two = (residual * scale_two * gain_two).astype(BF16)
    normed_two = after(normed_two, *near_x.values())
    normed_blocks = {0: normed_two}
    bit = seq_size // 2
    while bit:
        if bit == 1:
            top = seq_size // 2
            normed_blocks[top] = after(normed_blocks[top], last, *far_x.values())
        normed_blocks.update(
            {o ^ bit: swap(b, "seq", seq_size, bit) for o, b in normed_blocks.items()}
        )
        bit //= 2
    hidden, grad_gate, grad_up, grad_normed, layer_part, normed_all, cot_all = feed_forward(
        me,
        [ff_blocks[o] for o in range(fsdp_size)],
        [normed_blocks[o] for o in offsets],
        [cot_blocks[o] for o in offsets],
    )
    by_seq = lambda rows: rows.reshape(seq_size, row_count, -1)

    kept, given = halve(by_seq(grad_normed), 1, my_seq)
    normed_sum = add(kept, swap(given, "seq", seq_size, 1))
    bit = 2
    while bit < seq_size:
        kept, given = halve(normed_sum, 1, my_seq // bit)
        normed_sum = add(kept, swap(given, "seq", seq_size, bit))
        bit *= 2
    grad_normed_two = normed_sum[0]
    hidden = after(hidden, given)
    down_term = dot(hidden, cot_all, 0, 0).astype(BF16).reshape(fsdp_size, tall, -1)
    grad_gate, grad_up = after(grad_gate, down_term), after(grad_up, down_term)
    gate_term = dot(grad_gate, normed_all, 0, 0).astype(BF16).reshape(fsdp_size // 2, 2, tall, -1)
    up_term = dot(grad_up, normed_all, 0, 0).astype(BF16).reshape(fsdp_size // 2, 2, tall, -1)

    bits = list(reversed(fsdp_bits(fsdp_size)))

    def give(stack, at):
        kept, given = fsdp_halve(stack, fsdp_size, bits[at], my_fsdp, bits[:at])
        return kept, given

    def send(given, at):
        return swap(given, "fsdp", fsdp_size, bits[at])

    def finish(kept, got, at):
        stack = add(kept, got)
        for later in range(at + 1, len(bits)):
            kept, given = give(stack, later)
            stack = add(kept, send(given, later))
        return stack[0]

    kept_one, given = give(down_term, 0)
    got_one = send(given, 0)
    kept_two, given = give(jnp.concatenate([gate_term[:, 0], up_term[:, 0]], axis=0), 0)
    got_two = send(given, 0)
    kept_three, given_three = give(jnp.concatenate([gate_term[:, 1], up_term[:, 1]], axis=0), 0)

    kept, given = halve(after(by_seq(layer_part), down_term), 1, my_seq)
    layer_sum = add(kept, swap(given, "seq", seq_size, 1))
    kept_layer, given_layer = halve(layer_sum, 1, my_seq // 2)

    grad_path, norm_two_term = norm_back(grad_normed_two, residual, scale_two, gain_two)
    grad_residual = cotangent.astype(F32) + grad_path
    grad_branch = grad_residual.astype(BF16)
    grad_attn = dot(grad_branch, out_full, 1, 1).astype(BF16)
    out_term = stack_from_lanes(dot(attn_flat, grad_branch, 0, 0).astype(BF16), seq_size)
    kept, given = halve(out_term, 1, my_seq)
    out_sum = add(kept, swap(given, "seq", seq_size, 1))
    grad_attn = after(grad_attn, gate_term, up_term, given_layer)
    dq_one, kv_terms = attend_back(
        low, high, place, queries, grad_attn, attn_one, lse_one, kv_all, 0, split, ()
    )
    got_one = after(got_one, dq_one)
    got_three = send(after(given_three, got_one), 0)
    kept_one, given = give(add(kept_one, got_one), 1)
    next_one = send(given, 1)
    queries_two = after(queries, kv_terms, got_one)
    dq_two, kv_terms = attend_back(
        low, high, place, queries_two, grad_attn, attn_two, lse_two, kv_all, split,
        PAIRS - split, (kv_terms,),
    )
    got_two = after(got_two, dq_two)
    next_one = after(next_one, dq_two)
    down_sum = finish(kept_one, next_one, 1)
    kept_two, given = give(add(kept_two, got_two), 1)
    next_two = send(given, 1)
    kept, given = halve(by_seq(kv_terms), 1, my_seq)
    kv_sum = add(kept, swap(given, "seq", seq_size, 1))
    bit = 2
    while bit < seq_size:
        kept, given = halve(kv_sum, 1, my_seq // bit)
        kv_sum = add(kept, swap(after(given, got_two), "seq", seq_size, bit))
        bit *= 2
    kv_mine = kv_sum[0]
    bit = 2
    while bit < seq_size:
        kept, given = halve(out_sum, 1, my_seq // bit)
        out_sum = add(kept, swap(after(given, kv_mine), "seq", seq_size, bit))
        bit *= 2
    out_mine = out_sum[0].reshape(fsdp_size, -1, width)
    got_three = after(got_three, kv_mine)
    kept_three, given = give(add(kept_three, got_three), 1)
    next_three = send(given, 1)
    turned_back = rotate_back(
        jnp.concatenate([dq_one, dq_two, kv_mine[:, :KVW]], axis=1), cosine, sine
    )
    grad_joined = jnp.concatenate([turned_back, kv_mine[:, KVW:]], axis=1).astype(BF16)
    grad_normed_one = dot(grad_joined, qkv_t, 1, 0)
    grad_path_one, norm_one_term = norm_back(grad_normed_one, inputs, scale_one, gain_one)
    grad_tokens = grad_residual + grad_path_one
    bias_term = jnp.sum(grad_joined.astype(F32), axis=0)

    def vector_rows(vector):
        rows = vector.reshape(fsdp_size, 1, -1)
        return jnp.pad(rows, ((0, 0), (0, 0), (0, width - rows.shape[2])))

    vector_terms = [norm_one_term, bias_term[: QW + KVW], bias_term[QW + KVW :], norm_two_term]
    small = jnp.concatenate([vector_rows(v) for v in vector_terms], axis=1).astype(BF16)
    small = jnp.pad(small, ((0, 0), (0, 16 - len(vector_terms)), (0, 0)))
    qkv_term = stack_from_lanes(dot(grad_joined, normed_one, 0, 0).astype(BF16), seq_size)
    qkv_term = qkv_term.reshape(seq_size, fsdp_size, qkv_rows, width)
    tail = jnp.concatenate(
        [qkv_term, jnp.broadcast_to(small[None], (seq_size,) + small.shape)], axis=2
    )
    tail = after(tail, next_two)
    tail_mine = seq_scatter(tail, seq_size, my_seq)
    got_layer = swap(after(given_layer, tail_mine), "seq", seq_size, 2)
    layer_sum = add(kept_layer, got_layer)
    bit = 4
    while bit < seq_size:
        kept, given = halve(layer_sum, 1, my_seq // bit)
        layer_sum = add(kept, swap(given, "seq", seq_size, bit))
        bit *= 2
    layer_out = residual + layer_sum[0]
    one_sum = finish(kept_two, next_two, 1)
    two_sum = finish(kept_three, next_three, 1)

    ff_back = cut_lanes(me, (one_sum, two_sum, down_sum), seq_size)
    ff_got = [ff_back[0]] + [swap(ff_back[o], "seq", seq_size, o) for o in offsets if o]
    grad_gate_up, grad_down = join_ff(me, ff_got, strip)

    tail_sum = fsdp_scatter(
        after(jnp.concatenate([tail_mine, out_mine], axis=1), next_three), fsdp_size, my_fsdp
    )
    pieces = [
        tail_sum[qkv_rows + i, : v.shape[0] // fsdp_size] for i, v in enumerate(vector_terms)
    ]
    return (
        layer_out.astype(BF16),
        grad_tokens,
        pieces[0],
        tail_sum[:qkv_rows].T,
        pieces[1],
        pieces[2],
        tail_sum[qkv_rows + 16 :],
        pieces[3],
        grad_gate_up,
        grad_down,
    )


def solution(mesh):
    rows, both = P(("fsdp", "seq"), None), P(("fsdp", "seq"))
    return jax.shard_map(
        functools.partial(per_device, mesh.shape["seq"], mesh.shape["fsdp"]),
        mesh=mesh,
        in_specs=(
            rows, both, both, P("fsdp"), P("seq", "fsdp"), P("fsdp"), P("fsdp", "seq"),
            P("fsdp"), P("seq", "fsdp"), P("fsdp", "seq"), rows,
        ),
        out_specs=(
            rows, rows, P("fsdp"), P("seq", "fsdp"), P("fsdp"), P("fsdp"), P("fsdp", "seq"),
            P("fsdp"), P("seq", "fsdp"), P("fsdp", "seq"),
        ),
        check_vma=False,
    )
```

```python
import functools

import jax
import jax.numpy as jnp
from jax import lax
from jax.experimental import pallas as pl
from jax.experimental.pallas import tpu as pltpu
from jax.sharding import PartitionSpec as P

HEADS = 14
KV_HEADS = 2
HEAD = 64
FF = 4864
QW = 896
KVW = 128
PAIR = 2 * HEAD
PAIRS = HEADS // 2
OUTER = 4

EPSILON = 1e-06
ROPE_BASE = 1000000.0
MASKED = -1e30
VMEM_LIMIT = 50 * 1024 * 1024

F32 = jnp.float32
BF16 = jnp.bfloat16


def dot(left, right, left_dim, right_dim):
    return lax.dot_general(
        left, right, (((left_dim,), (right_dim,)), ((), ())), preferred_element_type=F32
    )


def swap(block, axis, size, bits):
    return lax.ppermute(block, axis, [(i, i ^ bits) for i in range(size)])


def after(array, *others):
    return lax.optimization_barrier((array,) + others)[0]


def seq_gather(block, size):
    blocks = {0: block}
    bit = size // 2
    while bit:
        blocks.update({o ^ bit: swap(b, "seq", size, bit) for o, b in blocks.items()})
        bit //= 2
    return blocks


def fsdp_bits(size):
    inner = size // OUTER
    outer_bits, inner_bits = [], []
    bit = 1
    while bit < size:
        (outer_bits if bit >= inner else inner_bits).append(bit)
        bit *= 2
    return outer_bits + inner_bits


def column_gather(block, size):
    inner = size // OUTER
    return jnp.stack([block] + [swap(block, "fsdp", size, k * inner) for k in range(1, OUTER)])


def ff_spread(block, size):
    blocks = {0: block}
    for bit in fsdp_bits(size)[2:]:
        blocks.update({o ^ bit: swap(b, "fsdp", size, bit) for o, b in blocks.items()})
    return blocks


def halve(stack, bit, me):
    above = stack.shape[0] // (2 * bit)
    cut = stack.reshape((above, 2, bit) + stack.shape[1:])
    digit = (me // bit) % 2
    kept = lax.dynamic_index_in_dim(cut, digit, 1, keepdims=False)
    given = lax.dynamic_index_in_dim(cut, 1 - digit, 1, keepdims=False)
    merge = lambda part: part.reshape((above * bit,) + stack.shape[1:])
    return merge(kept), merge(given).astype(BF16)


def add(kept, got):
    return kept.astype(F32) + got.astype(F32)


def seq_scatter(stack, size, me):
    bit = 1
    while bit < size:
        kept, given = halve(stack, 1, me // bit)
        stack = add(kept, swap(given, "seq", size, bit))
        bit *= 2
    return stack[0]


def fsdp_halve(stack, size, bit, me, resolved):
    place = bit
    digit = me // bit
    for taken in resolved:
        if taken < bit:
            place //= 2
    kept, given = halve(stack, place, digit * place)
    return kept, given


def fsdp_scatter(stack, size, me):
    resolved = []
    for bit in reversed(fsdp_bits(size)):
        kept, given = fsdp_halve(stack, size, bit, me, resolved)
        stack = add(kept, swap(given, "fsdp", size, bit))
        resolved.append(bit)
    return stack[0]


def on_device(body, name, out_shapes, scratch, me, arrays):
    vmem = pl.BlockSpec(memory_space=pltpu.VMEM)
    return pl.pallas_call(
        body,
        in_specs=[pl.BlockSpec(memory_space=pltpu.SMEM)] + [vmem] * len(arrays),
        out_specs=[vmem] * len(out_shapes),
        out_shape=out_shapes,
        scratch_shapes=scratch,
        compiler_params=pltpu.CompilerParams(vmem_limit_bytes=VMEM_LIMIT),
        name=name,
    )(me, *arrays)


def padded(rows):
    return -(-rows // 16) * 16


def cut_ff(me, gate_up_weight, down_weight, size):
    width = gate_up_weight.shape[0]
    half = down_weight.shape[0]
    strip = half // size
    tall = padded(strip)

    def body(me_ref, gu_ref, d_ref, *refs):
        outs, held = refs[:size], refs[size]
        turned = gu_ref[...].astype(F32).T
        down = d_ref[...].astype(F32)
        blank = jnp.zeros((tall - strip, width), F32)
        for q in range(size):
            one = turned[q * strip : (q + 1) * strip]
            two = turned[half + q * strip : half + (q + 1) * strip]
            three = down[q * strip : (q + 1) * strip]
            parts = [one, blank, two, blank, three, blank]
            held[q] = jnp.concatenate(parts, axis=0).astype(BF16)
        for o in range(size):
            outs[o][...] = held[me_ref[0] ^ o]

    shape = jax.ShapeDtypeStruct((3 * tall, width), BF16)
    scratch = [pltpu.VMEM((size, 3 * tall, width), BF16)]
    return on_device(body, "cut_ff", [shape] * size, scratch, me, (gate_up_weight, down_weight))


def join_lanes(me, blocks):
    size = len(blocks)
    rows, width = blocks[0].shape

    def body(me_ref, *refs):
        ins, out, held = refs[:size], refs[size], refs[size + 1]
        for o in range(size):
            held[me_ref[0] ^ o] = ins[o][...]
        out[...] = jnp.concatenate([held[q].astype(F32) for q in range(size)], 1).astype(BF16)

    return on_device(
        body,
        "join_lanes",
        [jax.ShapeDtypeStruct((rows, size * width), BF16)],
        [pltpu.VMEM((size, rows, width), BF16)],
        me,
        blocks,
    )[0]


def join_both(me, pieces, rows):
    size, parts_each = len(pieces), len(pieces[0])
    _, tall, width = pieces[0][0].shape
    count = sum(part.shape[0] for part in pieces[0])
    inner = count // OUTER
    order = [k * inner + m for m in range(inner) for k in range(OUTER)]
    shapes = [jax.ShapeDtypeStruct((count, rows, size * width), BF16)]
    if tall > rows:
        shapes.append(jax.ShapeDtypeStruct((count, tall - rows, width), BF16))

    def body(me_ref, *refs):
        ins, out, held = refs[: size * parts_each], refs[size * parts_each], refs[-1]
        for o in range(size):
            at = 0
            for part in ins[o * parts_each : (o + 1) * parts_each]:
                for j in range(part.shape[0]):
                    place = me_ref[1] ^ order[at]
                    held[me_ref[0] ^ o, place] = part[j]
                    if tall > rows and o == 0:
                        refs[size * parts_each + 1][place] = part[j, rows:]
                    at += 1
        for f in range(count):
            parts = [held[q, f, :rows].astype(F32) for q in range(size)]
            out[f] = jnp.concatenate(parts, axis=1).astype(BF16)

    return on_device(
        body,
        "join_both",
        shapes,
        [pltpu.VMEM((size, count, tall, width), BF16)],
        me,
        [block for row in pieces for block in row],
    )


def cut_lanes(me, sums, size):
    rows = sum(s.shape[0] for s in sums)
    width = sums[0].shape[1] // size

    def body(me_ref, *refs):
        ins, outs, held = refs[: len(sums)], refs[len(sums) : -1], refs[-1]
        whole = jnp.concatenate([r[...] for r in ins], axis=0)
        for q in range(size):
            held[q] = whole[:, q * width : (q + 1) * width].astype(BF16)
        for o in range(size):
            outs[o][...] = held[me_ref[0] ^ o]

    shape = jax.ShapeDtypeStruct((rows, width), BF16)
    scratch = [pltpu.VMEM((size, rows, width), BF16)]
    return on_device(body, "cut_lanes", [shape] * size, scratch, me, sums)


def join_ff(me, blocks, strip):
    size = len(blocks)
    rows, width = blocks[0].shape
    tall = rows // 3

    def body(me_ref, *refs):
        ins, gu, down, held = refs[:size], refs[size], refs[size + 1], refs[size + 2]
        for o in range(size):
            held[me_ref[0] ^ o] = ins[o][...].astype(F32)
        cut = [
            [held[q, i * tall : i * tall + strip] for q in range(size)] for i in range(3)
        ]
        gu[...] = jnp.concatenate(cut[0] + cut[1], axis=0).T
        down[...] = jnp.concatenate(cut[2], axis=0)

    return on_device(
        body,
        "join_ff",
        [
            jax.ShapeDtypeStruct((width, 2 * size * strip), F32),
            jax.ShapeDtypeStruct((size * strip, width), F32),
        ],
        [pltpu.VMEM((size, rows, width), F32)],
        me,
        blocks,
    )


def feed_forward(me, weight_blocks, row_blocks, cot_blocks):
    count, size = len(weight_blocks), len(row_blocks)
    rows, width = row_blocks[0].shape
    tall = weight_blocks[0].shape[0] // 3
    units = count * tall
    step_units = 256

    def body(me_ref, *refs):
        blocks = refs[:count]
        xs, gs = refs[count : count + size], refs[count + size : count + 2 * size]
        hid, gg, gu, gn, part, x_out, g_out = refs[count + 2 * size : count + 2 * size + 7]
        gu_w, d_w, x_all, g_all, sems = refs[count + 2 * size + 7 :]
        step = pl.program_id(0)

        @pl.when(step == 0)
        def _():
            copies = []
            for o in range(count):
                f = me_ref[1] ^ o
                copies.append((blocks[o].at[pl.ds(0, 2 * tall)], gu_w.at[f]))
                copies.append((blocks[o].at[pl.ds(2 * tall, tall)], d_w.at[f]))
            for o in range(size):
                copies.append((xs[o], x_all.at[me_ref[0] ^ o]))
                copies.append((gs[o], g_all.at[me_ref[0] ^ o]))
            started = [
                pltpu.make_async_copy(src, dst, sems.at[i]) for i, (src, dst) in enumerate(copies)
            ]
            for copy in started:
                copy.start()
            for copy in started:
                copy.wait()

        x = x_all[step]
        g = g_all[step]
        x_out[...] = x
        g_out[...] = g
        gate_w = gu_w[: count // 2].reshape(units, width)
        up_w = gu_w[count // 2 :].reshape(units, width)
        down_w = d_w[...].reshape(units, width)
        for begin in range(0, units, step_units):
            at = slice(begin, begin + step_units)
            gate = dot(x, gate_w[at], 1, 1)
            up = dot(x, up_w[at], 1, 1)
            grad_hidden = dot(g, down_w[at], 1, 1)
            sigmoid = 0.5 * jnp.tanh(0.5 * gate) + 0.5
            silu = gate * sigmoid
            hid[:, at] = (silu * up).astype(BF16)
            gg[:, at] = (grad_hidden * up * (sigmoid + silu * (1.0 - sigmoid))).astype(BF16)
            gu[:, at] = (grad_hidden * silu).astype(BF16)
        gn[...] = (dot(gg[...], gate_w, 1, 0) + dot(gu[...], up_w, 1, 0)).astype(BF16)
        part[...] = dot(hid[...], down_w, 1, 0).astype(BF16)

    hbm = pl.BlockSpec(memory_space=pl.ANY)
    by_rows = lambda n: pl.BlockSpec((rows, n), lambda i: (i, 0))
    like = lambda n: jax.ShapeDtypeStruct((size * rows, n), BF16)
    return pl.pallas_call(
        body,
        grid=(size,),
        in_specs=[pl.BlockSpec(memory_space=pltpu.SMEM)]
        + [hbm] * (count + 2 * size),
        out_specs=[by_rows(units)] * 3 + [by_rows(width)] * 4,
        out_shape=[like(units)] * 3 + [like(width)] * 4,
        scratch_shapes=[
            pltpu.VMEM((count, 2 * tall, width), BF16),
            pltpu.VMEM((count, tall, width), BF16),
            pltpu.VMEM((size, rows, width), BF16),
            pltpu.VMEM((size, rows, width), BF16),
            pltpu.SemaphoreType.DMA((2 * count + 2 * size,)),
        ],
        compiler_params=pltpu.CompilerParams(vmem_limit_bytes=VMEM_LIMIT),
        cost_estimate=pl.CostEstimate(flops=1, bytes_accessed=1, transcendentals=0),
        name="feed_forward",
    )(me, *weight_blocks, *row_blocks, *cot_blocks)


def both_heads(pair):
    lane = lax.broadcasted_iota(jnp.int32, pair.shape, 1)
    zero = jnp.zeros_like(pair)
    return jnp.concatenate(
        [jnp.where(lane < HEAD, pair, zero), jnp.where(lane < HEAD, zero, pair)], axis=0
    )


def fill_bias(low_ref, high_ref, place_ref, bias_ref):
    place = place_ref[...]
    allowed = (place >= low_ref[...]) & (place <= high_ref[...])
    bias = jnp.where(allowed, 0.0, MASKED).astype(F32)
    rows = bias.shape[1]
    bias_ref[:, :rows] = bias
    bias_ref[:, rows:] = bias


def own_rows(wide, rows):
    return jnp.concatenate([wide[:HEAD, :rows], wide[HEAD:, rows:]], axis=0)


def pairing(kv_ref, pair, begin):
    both = kv_ref[:, begin : begin + PAIR].astype(F32)
    crossed = pltpu.roll(both, HEAD, 1)
    lane = lax.broadcasted_iota(jnp.int32, both.shape, 1)
    first = jnp.where(pair <= PAIRS // 2, both, crossed)
    second = jnp.where(pair < PAIRS // 2, crossed, both)
    return jnp.where(lane < HEAD, first, second)


def new_pairing(step, pair):
    return (step == 0) | (pair == PAIRS // 2) | (pair == PAIRS // 2 + 1)


def attend_kernel(
    begin_pair, low_ref, high_ref, place_ref, q_ref, kv_ref,
    o_ref, lse_ref, bias_ref, k_ref, vt_ref,
):
    step = pl.program_id(0)
    pair = step + begin_pair

    @pl.when(step == 0)
    def _():
        fill_bias(low_ref, high_ref, place_ref, bias_ref)

    @pl.when(new_pairing(step, pair))
    def _():
        k_ref[...] = pairing(kv_ref, pair, 0).astype(BF16)
        vt_ref[...] = pairing(kv_ref, pair, PAIR).T.astype(BF16)

    rows = q_ref.shape[0]
    queries = both_heads(q_ref[...])
    keys = k_ref[...]
    values_t = vt_ref[...]
    outs, totals = [], []
    for begin in range(0, 2 * rows, 256):
        scores = dot(keys, queries[begin : begin + 256], 1, 1) + bias_ref[:, begin : begin + 256]
        top = jnp.max(scores, axis=0, keepdims=True)
        probs = jnp.exp(scores - top)
        total = jnp.sum(probs, axis=0, keepdims=True)
        outs.append(dot(values_t, probs.astype(BF16), 1, 0) / total)
        totals.append(top + jnp.log(total))
    wide = jnp.concatenate(outs, axis=1)
    o_ref[...] = own_rows(wide, rows).T.astype(BF16)
    lse_ref[0] = jnp.concatenate(totals, axis=1)


def attend_back_kernel(
    begin_pair, low_ref, high_ref, place_ref, q_ref, g_ref, o_ref, lse_ref, kv_ref, *refs,
):
    dq_ref, dkv_ref, bias_ref, k_ref, kt_ref, v_ref, dk_ref, dv_ref = refs[-8:]
    step = pl.program_id(0)
    pair = step + begin_pair

    @pl.when(step == 0)
    def _():
        fill_bias(low_ref, high_ref, place_ref, bias_ref)
        dkv_ref[...] = refs[0][...] if begin_pair else jnp.zeros_like(dkv_ref)

    @pl.when(new_pairing(step, pair))
    def _():
        keys_now = pairing(kv_ref, pair, 0)
        k_ref[...] = keys_now.astype(BF16)
        kt_ref[...] = keys_now.T.astype(BF16)
        v_ref[...] = pairing(kv_ref, pair, PAIR).astype(BF16)
        dk_ref[...] = jnp.zeros_like(dk_ref)
        dv_ref[...] = jnp.zeros_like(dv_ref)

    rows = q_ref.shape[0]
    queries = both_heads(q_ref[...])
    grads = both_heads(g_ref[...])
    keys = k_ref[...]
    keys_t = kt_ref[...]
    values = v_ref[...]
    product = (g_ref[...].astype(F32) * o_ref[...].astype(F32)).T
    delta = jnp.concatenate(
        [
            jnp.sum(product[:HEAD], axis=0, keepdims=True),
            jnp.sum(product[HEAD:], axis=0, keepdims=True),
        ],
        axis=1,
    )
    lse = lse_ref[0]
    outs = []
    for begin in range(0, 2 * rows, 256):
        part = slice(begin, begin + 256)
        scores = dot(keys, queries[part], 1, 1) + bias_ref[:, part]
        probs = jnp.exp(scores - lse[:, part])
        grad_probs = dot(values, grads[part], 1, 1)
        grad_scores = (probs * (grad_probs - delta[:, part])).astype(BF16)
        outs.append(dot(keys_t, grad_scores, 1, 0))
        dk_ref[...] += dot(grad_scores, queries[part], 1, 0)
        dv_ref[...] += dot(probs.astype(BF16), grads[part], 1, 0)
    wide = jnp.concatenate(outs, axis=1)
    dq_ref[...] = own_rows(wide, rows).T * 0.125

    def fold(own_lanes):
        for at, sums in ((0, dk_ref), (PAIR, dv_ref)):
            sums_now = sums[...]
            lane = lax.broadcasted_iota(jnp.int32, sums_now.shape, 1)
            both = sums_now + pltpu.roll(sums_now, HEAD, 1)
            kept = jnp.where((lane < HEAD) == own_lanes, both, 0.0)
            dkv_ref[:, at : at + PAIR] += kept

    @pl.when(pair == PAIRS // 2 - 1)
    def _():
        fold(True)

    @pl.when(pair == PAIRS // 2)
    def _():
        dkv_ref[:, :PAIR] += dk_ref[...]
        dkv_ref[:, PAIR:] += dv_ref[...]

    @pl.when(pair == PAIRS - 1)
    def _():
        fold(False)


def whole(shape):
    return pl.BlockSpec(shape, lambda i: (0,) * len(shape))


def attend(low, high, place, queries, kv_all, begin, pairs):
    rows, count = queries.shape[0], place.shape[0]
    taken = pl.BlockSpec((rows, PAIR), lambda i: (0, i + begin))
    made = pl.BlockSpec((rows, PAIR), lambda i: (0, i))
    return pl.pallas_call(
        functools.partial(attend_kernel, begin),
        grid=(pairs,),
        in_specs=[whole((1, rows)), whole((1, rows)), whole((count, 1)), taken]
        + [whole((count, 2 * KVW))],
        out_specs=[made, pl.BlockSpec((1, 1, 2 * rows), lambda i: (i, 0, 0))],
        out_shape=[
            jax.ShapeDtypeStruct((rows, pairs * PAIR), BF16),
            jax.ShapeDtypeStruct((pairs, 1, 2 * rows), F32),
        ],
        scratch_shapes=[
            pltpu.VMEM((count, 2 * rows), F32),
            pltpu.VMEM((count, PAIR), BF16),
            pltpu.VMEM((PAIR, count), BF16),
        ],
        compiler_params=pltpu.CompilerParams(vmem_limit_bytes=VMEM_LIMIT),
        cost_estimate=pl.CostEstimate(flops=1, bytes_accessed=1, transcendentals=0),
        name="attend",
    )(low, high, place, queries, kv_all)


def attend_back(low, high, place, queries, grads, outs, lse, kv_all, begin, pairs, so_far):
    rows, count = queries.shape[0], place.shape[0]
    taken = pl.BlockSpec((rows, PAIR), lambda i: (0, i + begin))
    made = pl.BlockSpec((rows, PAIR), lambda i: (0, i))
    sums = whole((count, 2 * KVW))
    return pl.pallas_call(
        functools.partial(attend_back_kernel, begin),
        grid=(pairs,),
        in_specs=[whole((1, rows)), whole((1, rows)), whole((count, 1)), taken, taken, made]
        + [pl.BlockSpec((1, 1, 2 * rows), lambda i: (i, 0, 0)), sums]
        + [sums] * len(so_far),
        out_specs=[made, sums],
        out_shape=[
            jax.ShapeDtypeStruct((rows, pairs * PAIR), F32),
            jax.ShapeDtypeStruct((count, 2 * KVW), F32),
        ],
        scratch_shapes=[
            pltpu.VMEM((count, 2 * rows), F32),
            pltpu.VMEM((count, PAIR), BF16),
            pltpu.VMEM((PAIR, count), BF16),
            pltpu.VMEM((count, PAIR), BF16),
            pltpu.VMEM((count, PAIR), F32),
            pltpu.VMEM((count, PAIR), F32),
        ],
        compiler_params=pltpu.CompilerParams(vmem_limit_bytes=VMEM_LIMIT),
        cost_estimate=pl.CostEstimate(flops=1, bytes_accessed=1, transcendentals=0),
        name="attend_back",
    )(low, high, place, queries, grads, outs, lse, kv_all, *so_far)


def rms_scale(values_in):
    return lax.rsqrt(jnp.mean(values_in * values_in, axis=-1, keepdims=True) + EPSILON)


def angle_tables(places):
    exponent = jnp.arange(HEAD // 2, dtype=F32) * 2.0 / HEAD
    frequency = ROPE_BASE ** (-exponent)
    turn = places.astype(F32)[:, None] * frequency[None, :]
    cosine, sine = lax.optimization_barrier((jnp.cos(turn), jnp.sin(turn)))
    return jnp.concatenate([cosine] * 4, axis=1), jnp.concatenate([sine] * 4, axis=1)


def widen(table, width):
    return jnp.concatenate([table] * (width // PAIR), axis=1)


def first_halves(shape):
    return lax.broadcasted_iota(jnp.int32, shape, 1) % HEAD < HEAD // 2


def rotate(tensor, cosine, sine):
    half = HEAD // 2
    ahead, behind = jnp.roll(tensor, -half, axis=1), jnp.roll(tensor, half, axis=1)
    turned = jnp.where(first_halves(tensor.shape), -ahead, behind)
    width = tensor.shape[1]
    return tensor * widen(cosine, width) + turned * widen(sine, width)


def rotate_back(grad_in, cosine, sine):
    half = HEAD // 2
    width = grad_in.shape[1]
    scaled = grad_in * widen(sine, width)
    ahead, behind = jnp.roll(scaled, -half, axis=1), jnp.roll(scaled, half, axis=1)
    return grad_in * widen(cosine, width) + jnp.where(
        first_halves(grad_in.shape), ahead, -behind
    )


def norm_back(grad_in, row_data, scale_in, gain_in):
    gain_term = jnp.sum(grad_in * row_data * scale_in, axis=0)
    grad_normed = grad_in * gain_in
    inner_mean = jnp.mean(grad_normed * row_data, axis=-1, keepdims=True)
    return (
        scale_in * grad_normed - row_data * scale_in * scale_in * scale_in * inner_mean,
        gain_term,
    )


def pad_row(vector, width):
    return jnp.pad(vector, (0, width - vector.shape[0]))[None, :]


def stack_from_lanes(array, count):
    rows, width = array.shape
    return jnp.transpose(array.reshape(rows, count, width // count), (1, 0, 2))


def per_device(
    seq_size, fsdp_size, tokens, segment_ids, positions, norm_one, qkv_weight, qkv_bias,
    out_weight, norm_two, gate_up_weight, down_weight, cotangent,
):
    my_seq, my_fsdp = lax.axis_index("seq"), lax.axis_index("fsdp")
    me = jnp.stack([my_seq, my_fsdp]).astype(jnp.int32)
    offsets = range(seq_size)
    row_count = tokens.shape[0]
    width = qkv_weight.shape[0]
    qkv_rows = qkv_weight.shape[1]
    strip = down_weight.shape[0] // seq_size
    tall = padded(strip)

    qkv_tall = padded(qkv_rows)
    packed = jnp.concatenate(
        [
            jnp.pad(qkv_weight.T, ((0, qkv_tall - qkv_rows), (0, 0))),
            pad_row(norm_one, width),
            pad_row(qkv_bias, width),
            pad_row(norm_two, width),
            jnp.zeros((13, width), BF16),
            out_weight,
        ],
        axis=0,
    )
    ff_cut = cut_ff(me, gate_up_weight, down_weight, seq_size)
    ff_share = [ff_cut[0]] + [swap(ff_cut[o], "seq", seq_size, o) for o in offsets if o]
    columns = ff_spread(
        after(column_gather(packed, fsdp_size), *ff_share[1:]), fsdp_size
    )
    ff_block = join_lanes(me, ff_share)
    wide = qkv_tall + 16
    packed_stack = jnp.concatenate([columns[m][:, :wide] for m in sorted(columns)], axis=0)
    out_stack = jnp.concatenate([columns[m][:, wide:] for m in sorted(columns)], axis=0)
    packed_blocks = seq_gather(after(packed_stack, ff_block), seq_size)
    ff_blocks = {0: ff_block}
    for bit in fsdp_bits(fsdp_size)[:2]:
        ff_blocks.update({o ^ bit: swap(b, "fsdp", fsdp_size, bit) for o, b in ff_blocks.items()})
    inner = fsdp_size // OUTER

    qkv_pieces = [[packed_blocks[o]] for o in offsets]
    qkv_t, vectors = join_both(me, qkv_pieces, qkv_tall)
    own_x = ff_spread(ff_block, fsdp_size)
    qkv_t = after(qkv_t, ff_blocks[2 * inner], ff_blocks[inner], *own_x.values())[:, :qkv_rows].reshape(fsdp_size * qkv_rows, -1)
    gain_one = vectors[:, 0, : norm_one.shape[0]].reshape(-1).astype(F32)
    bias_full = vectors[:, 1, : qkv_bias.shape[0]].reshape(-1).astype(F32)
    gain_two = vectors[:, 2, : norm_two.shape[0]].reshape(-1).astype(F32)

    out_blocks = seq_gather(after(out_stack, packed_blocks[seq_size // 2]), seq_size)

    inputs = tokens.astype(F32)
    scale_one = rms_scale(inputs)
    normed_one = (inputs * scale_one * gain_one).astype(BF16)
    joined = dot(normed_one, qkv_t, 1, 1) + bias_full
    cosine, sine = angle_tables(positions)
    turned = rotate(joined[:, : QW + KVW], cosine, sine).astype(BF16)
    queries = turned[:, :QW] * jnp.asarray(0.125, BF16)
    kv_local = jnp.concatenate([turned[:, QW:], joined[:, QW + KVW :].astype(BF16)], axis=1)
    kv_all = lax.all_gather(kv_local, "seq", axis=0, tiled=True)
    kv_all = after(kv_all, ff_blocks[2 * inner], ff_blocks[inner])
    cot_blocks = seq_gather(after(cotangent, kv_all), seq_size)
    row_place = jnp.arange(row_count, dtype=jnp.int32)
    high = my_seq * row_count + row_place
    low = high - positions
    place = jnp.arange(seq_size * row_count, dtype=jnp.int32)[:, None]
    low, high = low[None, :], high[None, :]
    split = PAIRS // 2 + 1
    spread = lambda block: ff_spread(block, fsdp_size)
    near = ff_blocks[inner]
    far, last = ff_blocks[2 * inner], ff_blocks[3 * inner]
    near_x = spread(after(near, kv_all))
    attn_one, lse_one = attend(
        low, high, place, after(queries, far), kv_all, 0, split
    )
    far_x = spread(after(far, kv_all))
    queries_two = after(queries, attn_one, cot_blocks[seq_size // 2], *near_x.values())
    attn_two, lse_two = attend(low, high, place, queries_two, kv_all, split, PAIRS - split)
    last_x = spread(last)
    for base, row in ((0, own_x), (inner, near_x), (2 * inner, far_x), (3 * inner, last_x)):
        ff_blocks.update({base + m: block for m, block in row.items()})
    attn_flat = jnp.concatenate([attn_one, attn_two], axis=1)

    out_list = [[out_blocks[o]] for o in offsets]
    out_list[0][0] = after(out_list[0][0], attn_one)
    out_full = join_both(me, out_list, out_weight.shape[0])[0].reshape(QW, -1)

    residual = inputs + dot(attn_flat, out_full, 1, 0)
    scale_two = rms_scale(residual)
    normed_two = (residual * scale_two * gain_two).astype(BF16)
    normed_two = after(normed_two, *far_x.values())
    normed_blocks = {0: normed_two}
    bit = seq_size // 2
    while bit:
        if bit == 1:
            top = seq_size // 2
            normed_blocks[top] = after(normed_blocks[top], last)
        normed_blocks.update(
            {o ^ bit: swap(b, "seq", seq_size, bit) for o, b in normed_blocks.items()}
        )
        bit //= 2
    hidden, grad_gate, grad_up, grad_normed, layer_part, normed_all, cot_all = feed_forward(
        me,
        [ff_blocks[o] for o in range(fsdp_size)],
        [normed_blocks[o] for o in offsets],
        [cot_blocks[o] for o in offsets],
    )
    by_seq = lambda rows: rows.reshape(seq_size, row_count, -1)

    kept, given = halve(by_seq(grad_normed), 1, my_seq)
    normed_sum = add(kept, swap(given, "seq", seq_size, 1))
    bit = 2
    while bit < seq_size:
        kept, given = halve(normed_sum, 1, my_seq // bit)
        normed_sum = add(kept, swap(given, "seq", seq_size, bit))
        bit *= 2
    grad_normed_two = normed_sum[0]
    hidden = after(hidden, given)
    down_term = dot(hidden, cot_all, 0, 0).astype(BF16).reshape(fsdp_size, tall, -1)
    grad_gate, grad_up = after(grad_gate, down_term), after(grad_up, down_term)
    gate_term = dot(grad_gate, normed_all, 0, 0).astype(BF16).reshape(fsdp_size // 2, 2, tall, -1)
    up_term = dot(grad_up, normed_all, 0, 0).astype(BF16).reshape(fsdp_size // 2, 2, tall, -1)

    bits = list(reversed(fsdp_bits(fsdp_size)))

    def give(stack, at):
        kept, given = fsdp_halve(stack, fsdp_size, bits[at], my_fsdp, bits[:at])
        return kept, given

    def send(given, at):
        return swap(given, "fsdp", fsdp_size, bits[at])

    def finish(kept, got, at):
        stack = add(kept, got)
        for later in range(at + 1, len(bits)):
            kept, given = give(stack, later)
            stack = add(kept, send(given, later))
        return stack[0]

    kept_one, given = give(down_term, 0)
    got_one = send(given, 0)
    kept_two, given = give(jnp.concatenate([gate_term[:, 0], up_term[:, 0]], axis=0), 0)
    got_two = send(after(given, grad_normed_two), 0)
    kept_three, given_three = give(jnp.concatenate([gate_term[:, 1], up_term[:, 1]], axis=0), 0)

    grad_path, norm_two_term = norm_back(grad_normed_two, residual, scale_two, gain_two)
    grad_residual = cotangent.astype(F32) + grad_path
    grad_branch = grad_residual.astype(BF16)
    grad_attn = dot(grad_branch, out_full, 1, 1).astype(BF16)
    grad_attn = after(grad_attn, gate_term, up_term)
    dq_one, kv_terms = attend_back(
        low, high, place, queries, grad_attn, attn_one, lse_one, kv_all, 0, split, ()
    )
    got_one = after(got_one, dq_one)
    got_three = send(after(given_three, got_one), 0)
    kept_one, given_one = give(add(kept_one, got_one), 1)
    next_one = send(given_one, 1)
    queries_two = after(queries, kv_terms, given_one)
    dq_two, kv_terms = attend_back(
        low, high, place, queries_two, grad_attn, attn_two, lse_two, kv_all, split,
        PAIRS - split, (kv_terms,),
    )
    got_two = after(got_two, dq_two)
    kept_two, given = give(add(kept_two, got_two), 1)
    next_two = send(given, 1)
    kept, given = halve(by_seq(kv_terms), 1, my_seq)
    kv_sum = add(kept, swap(given, "seq", seq_size, 1))
    bit = 2
    while bit < seq_size:
        kept, given = halve(kv_sum, 1, my_seq // bit)
        kv_sum = add(kept, swap(after(given, got_two), "seq", seq_size, bit))
        bit *= 2
    kv_mine = kv_sum[0]
    next_one, next_two = after(next_one, kv_mine), after(next_two, kv_mine)
    down_sum = finish(kept_one, next_one, 1)

    attn_late = after(attn_flat, dq_two)
    out_term = stack_from_lanes(dot(attn_late, grad_branch, 0, 0).astype(BF16), seq_size)
    kept, given = halve(out_term, 1, my_seq)
    out_sum = add(kept, swap(given, "seq", seq_size, 1))
    kept, given = halve(after(by_seq(layer_part), dq_two), 1, my_seq)
    layer_sum = add(kept, swap(given, "seq", seq_size, 1))
    kept_layer, given_layer = halve(layer_sum, 1, my_seq // 2)
    bit = 2
    while bit < seq_size:
        kept, given = halve(out_sum, 1, my_seq // bit)
        out_sum = add(kept, swap(after(given, kv_mine), "seq", seq_size, bit))
        bit *= 2
    out_mine = out_sum[0].reshape(fsdp_size, -1, width)
    got_three = after(got_three, kv_mine)
    kept_three, given = give(add(kept_three, got_three), 1)
    next_three = send(given, 1)
    turned_back = rotate_back(
        jnp.concatenate([dq_one, dq_two, kv_mine[:, :KVW]], axis=1), cosine, sine
    )
    grad_joined = jnp.concatenate([turned_back, kv_mine[:, KVW:]], axis=1).astype(BF16)
    grad_normed_one = dot(grad_joined, qkv_t, 1, 0)
    grad_path_one, norm_one_term = norm_back(grad_normed_one, inputs, scale_one, gain_one)
    grad_tokens = grad_residual + grad_path_one
    bias_term = jnp.sum(grad_joined.astype(F32), axis=0)

    def vector_rows(vector):
        rows = vector.reshape(fsdp_size, 1, -1)
        return jnp.pad(rows, ((0, 0), (0, 0), (0, width - rows.shape[2])))

    vector_terms = [norm_one_term, bias_term[: QW + KVW], bias_term[QW + KVW :], norm_two_term]
    small = jnp.concatenate([vector_rows(v) for v in vector_terms], axis=1).astype(BF16)
    small = jnp.pad(small, ((0, 0), (0, 16 - len(vector_terms)), (0, 0)))
    qkv_term = stack_from_lanes(dot(grad_joined, normed_one, 0, 0).astype(BF16), seq_size)
    qkv_term = qkv_term.reshape(seq_size, fsdp_size, qkv_rows, width)
    tail = jnp.concatenate(
        [qkv_term, jnp.broadcast_to(small[None], (seq_size,) + small.shape)], axis=2
    )
    tail = after(tail, next_two)
    tail_mine = seq_scatter(tail, seq_size, my_seq)
    got_layer = swap(after(given_layer, tail_mine), "seq", seq_size, 2)
    layer_sum = add(kept_layer, got_layer)
    bit = 4
    while bit < seq_size:
        kept, given = halve(layer_sum, 1, my_seq // bit)
        layer_sum = add(kept, swap(given, "seq", seq_size, bit))
        bit *= 2
    layer_out = residual + layer_sum[0]
    one_sum = finish(kept_two, next_two, 1)
    two_sum = finish(kept_three, next_three, 1)

    ff_back = cut_lanes(me, (one_sum, two_sum, down_sum), seq_size)
    ff_got = [ff_back[0]] + [swap(ff_back[o], "seq", seq_size, o) for o in offsets if o]
    grad_gate_up, grad_down = join_ff(me, ff_got, strip)

    tail_sum = fsdp_scatter(
        after(jnp.concatenate([tail_mine, out_mine], axis=1), next_three), fsdp_size, my_fsdp
    )
    pieces = [
        tail_sum[qkv_rows + i, : v.shape[0] // fsdp_size] for i, v in enumerate(vector_terms)
    ]
    return (
        layer_out.astype(BF16),
        grad_tokens,
        pieces[0],
        tail_sum[:qkv_rows].T,
        pieces[1],
        pieces[2],
        tail_sum[qkv_rows + 16 :],
        pieces[3],
        grad_gate_up,
        grad_down,
    )


def solution(mesh):
    rows, both = P(("fsdp", "seq"), None), P(("fsdp", "seq"))
    return jax.shard_map(
        functools.partial(per_device, mesh.shape["seq"], mesh.shape["fsdp"]),
        mesh=mesh,
        in_specs=(
            rows, both, both, P("fsdp"), P("seq", "fsdp"), P("fsdp"), P("fsdp", "seq"),
            P("fsdp"), P("seq", "fsdp"), P("fsdp", "seq"), rows,
        ),
        out_specs=(
            rows, rows, P("fsdp"), P("seq", "fsdp"), P("fsdp"), P("fsdp"), P("fsdp", "seq"),
            P("fsdp"), P("seq", "fsdp"), P("fsdp", "seq"),
        ),
        check_vma=False,
    )
```

```python
import functools

import jax
import jax.numpy as jnp
from jax import lax
from jax.experimental import pallas as pl
from jax.experimental.pallas import tpu as pltpu
from jax.sharding import PartitionSpec as P

HEADS = 14
KV_HEADS = 2
HEAD = 64
FF = 4864
QW = 896
KVW = 128
PAIR = 2 * HEAD
PAIRS = HEADS // 2
OUTER = 4

EPSILON = 1e-06
ROPE_BASE = 1000000.0
MASKED = -1e30
VMEM_LIMIT = 50 * 1024 * 1024

F32 = jnp.float32
BF16 = jnp.bfloat16


def dot(left, right, left_dim, right_dim):
    return lax.dot_general(
        left, right, (((left_dim,), (right_dim,)), ((), ())), preferred_element_type=F32
    )


def swap(block, axis, size, bits):
    return lax.ppermute(block, axis, [(i, i ^ bits) for i in range(size)])


def after(array, *others):
    return lax.optimization_barrier((array,) + others)[0]


def seq_gather(block, size):
    blocks = {0: block}
    bit = size // 2
    while bit:
        blocks.update({o ^ bit: swap(b, "seq", size, bit) for o, b in blocks.items()})
        bit //= 2
    return blocks


def fsdp_bits(size):
    inner = size // OUTER
    outer_bits, inner_bits = [], []
    bit = 1
    while bit < size:
        (outer_bits if bit >= inner else inner_bits).append(bit)
        bit *= 2
    return outer_bits + inner_bits


def column_gather(block, size):
    inner = size // OUTER
    return jnp.stack([block] + [swap(block, "fsdp", size, k * inner) for k in range(1, OUTER)])


def ff_spread(block, size):
    blocks = {0: block}
    for bit in fsdp_bits(size)[2:]:
        blocks.update({o ^ bit: swap(b, "fsdp", size, bit) for o, b in blocks.items()})
    return blocks


def halve(stack, bit, me):
    above = stack.shape[0] // (2 * bit)
    cut = stack.reshape((above, 2, bit) + stack.shape[1:])
    digit = (me // bit) % 2
    kept = lax.dynamic_index_in_dim(cut, digit, 1, keepdims=False)
    given = lax.dynamic_index_in_dim(cut, 1 - digit, 1, keepdims=False)
    merge = lambda part: part.reshape((above * bit,) + stack.shape[1:])
    return merge(kept), merge(given).astype(BF16)


def add(kept, got):
    return kept.astype(F32) + got.astype(F32)


def seq_scatter(stack, size, me):
    bit = 1
    while bit < size:
        kept, given = halve(stack, 1, me // bit)
        stack = add(kept, swap(given, "seq", size, bit))
        bit *= 2
    return stack[0]


def fsdp_halve(stack, size, bit, me, resolved):
    place = bit
    digit = me // bit
    for taken in resolved:
        if taken < bit:
            place //= 2
    kept, given = halve(stack, place, digit * place)
    return kept, given


def fsdp_scatter(stack, size, me, earlier):
    inner = size // OUTER
    resolved = []
    for bit in reversed(fsdp_bits(size)[2:]):
        kept, given = fsdp_halve(stack, size, bit, me, resolved)
        stack = add(kept, swap(given, "fsdp", size, bit))
        resolved.append(bit)
    place = me // inner
    low = after(stack.astype(BF16), earlier)
    total = lax.dynamic_index_in_dim(stack, place, 0, keepdims=False)
    for k in range(1, OUTER):
        given = lax.dynamic_index_in_dim(low, place ^ k, 0, keepdims=False)
        total = add(total, swap(given, "fsdp", size, k * inner))
    return total


def on_device(body, name, out_shapes, scratch, me, arrays):
    vmem = pl.BlockSpec(memory_space=pltpu.VMEM)
    return pl.pallas_call(
        body,
        in_specs=[pl.BlockSpec(memory_space=pltpu.SMEM)] + [vmem] * len(arrays),
        out_specs=[vmem] * len(out_shapes),
        out_shape=out_shapes,
        scratch_shapes=scratch,
        compiler_params=pltpu.CompilerParams(vmem_limit_bytes=VMEM_LIMIT),
        name=name,
    )(me, *arrays)


def padded(rows):
    return -(-rows // 16) * 16


def cut_ff(me, gate_up_weight, down_weight, size):
    width = gate_up_weight.shape[0]
    half = down_weight.shape[0]
    strip = half // size
    tall = padded(strip)

    def body(me_ref, gu_ref, d_ref, *refs):
        outs, held = refs[:size], refs[size]
        turned = gu_ref[...].astype(F32).T
        down = d_ref[...].astype(F32)
        blank = jnp.zeros((tall - strip, width), F32)
        for q in range(size):
            one = turned[q * strip : (q + 1) * strip]
            two = turned[half + q * strip : half + (q + 1) * strip]
            three = down[q * strip : (q + 1) * strip]
            parts = [one, blank, two, blank, three, blank]
            held[q] = jnp.concatenate(parts, axis=0).astype(BF16)
        for o in range(size):
            outs[o][...] = held[me_ref[0] ^ o]

    shape = jax.ShapeDtypeStruct((3 * tall, width), BF16)
    scratch = [pltpu.VMEM((size, 3 * tall, width), BF16)]
    return on_device(body, "cut_ff", [shape] * size, scratch, me, (gate_up_weight, down_weight))


def join_lanes(me, blocks):
    size = len(blocks)
    rows, width = blocks[0].shape

    def body(me_ref, *refs):
        ins, out, held = refs[:size], refs[size], refs[size + 1]
        for o in range(size):
            held[me_ref[0] ^ o] = ins[o][...]
        out[...] = jnp.concatenate([held[q].astype(F32) for q in range(size)], 1).astype(BF16)

    return on_device(
        body,
        "join_lanes",
        [jax.ShapeDtypeStruct((rows, size * width), BF16)],
        [pltpu.VMEM((size, rows, width), BF16)],
        me,
        blocks,
    )[0]


def join_both(me, pieces, rows):
    size, parts_each = len(pieces), len(pieces[0])
    _, tall, width = pieces[0][0].shape
    count = sum(part.shape[0] for part in pieces[0])
    inner = count // OUTER
    order = [k * inner + m for m in range(inner) for k in range(OUTER)]
    shapes = [jax.ShapeDtypeStruct((count, rows, size * width), BF16)]
    if tall > rows:
        shapes.append(jax.ShapeDtypeStruct((count, tall - rows, width), BF16))

    def body(me_ref, *refs):
        ins, out, held = refs[: size * parts_each], refs[size * parts_each], refs[-1]
        for o in range(size):
            at = 0
            for part in ins[o * parts_each : (o + 1) * parts_each]:
                for j in range(part.shape[0]):
                    place = me_ref[1] ^ order[at]
                    held[me_ref[0] ^ o, place] = part[j]
                    if tall > rows and o == 0:
                        refs[size * parts_each + 1][place] = part[j, rows:]
                    at += 1
        for f in range(count):
            parts = [held[q, f, :rows].astype(F32) for q in range(size)]
            out[f] = jnp.concatenate(parts, axis=1).astype(BF16)

    return on_device(
        body,
        "join_both",
        shapes,
        [pltpu.VMEM((size, count, tall, width), BF16)],
        me,
        [block for row in pieces for block in row],
    )


def cut_lanes(me, sums, size):
    rows = sum(s.shape[0] for s in sums)
    width = sums[0].shape[1] // size

    def body(me_ref, *refs):
        ins, outs, held = refs[: len(sums)], refs[len(sums) : -1], refs[-1]
        whole = jnp.concatenate([r[...] for r in ins], axis=0)
        for q in range(size):
            held[q] = whole[:, q * width : (q + 1) * width].astype(BF16)
        for o in range(size):
            outs[o][...] = held[me_ref[0] ^ o]

    shape = jax.ShapeDtypeStruct((rows, width), BF16)
    scratch = [pltpu.VMEM((size, rows, width), BF16)]
    return on_device(body, "cut_lanes", [shape] * size, scratch, me, sums)


def join_ff(me, blocks, strip):
    size = len(blocks)
    rows, width = blocks[0].shape
    tall = rows // 3

    def body(me_ref, *refs):
        ins, gu, down, held = refs[:size], refs[size], refs[size + 1], refs[size + 2]
        for o in range(size):
            held[me_ref[0] ^ o] = ins[o][...].astype(F32)
        cut = [
            [held[q, i * tall : i * tall + strip] for q in range(size)] for i in range(3)
        ]
        gu[...] = jnp.concatenate(cut[0] + cut[1], axis=0).T
        down[...] = jnp.concatenate(cut[2], axis=0)

    return on_device(
        body,
        "join_ff",
        [
            jax.ShapeDtypeStruct((width, 2 * size * strip), F32),
            jax.ShapeDtypeStruct((size * strip, width), F32),
        ],
        [pltpu.VMEM((size, rows, width), F32)],
        me,
        blocks,
    )


def feed_forward(me, weight_blocks, row_blocks, cot_blocks):
    count, size = len(weight_blocks), len(row_blocks)
    rows, width = row_blocks[0].shape
    tall = weight_blocks[0].shape[0] // 3
    units = count * tall
    step_units = 256

    def body(me_ref, *refs):
        blocks = refs[:count]
        xs, gs = refs[count : count + size], refs[count + size : count + 2 * size]
        outs = refs[count + 2 * size : count + 2 * size + 9]
        hid, gg, gu, gn_kept, gn_given, part_kept, part_given, x_out, g_out = outs
        gu_w, d_w, x_all, g_all, held, sems = refs[count + 2 * size + 9 :]
        step = pl.program_id(0)
        core = me_ref[0] % 2
        handed = [
            pltpu.make_async_copy(src, dst, sems.at[2 * count + 2 * size + i])
            for i, (src, dst) in enumerate(((x_all, x_out), (g_all, g_out)))
        ]

        @pl.when(step == 0)
        def _():
            copies = []
            for o in range(count):
                f = me_ref[1] ^ o
                copies.append((blocks[o].at[pl.ds(0, 2 * tall)], gu_w.at[f]))
                copies.append((blocks[o].at[pl.ds(2 * tall, tall)], d_w.at[f]))
            for o in range(size):
                copies.append((xs[o], x_all.at[me_ref[0] ^ o]))
                copies.append((gs[o], g_all.at[me_ref[0] ^ o]))
            started = [
                pltpu.make_async_copy(src, dst, sems.at[i]) for i, (src, dst) in enumerate(copies)
            ]
            for copy in started:
                copy.start()
            for copy in started:
                copy.wait()
            for copy in handed:
                copy.start()

        x = x_all[pl.ds(2 * step, 2)].reshape(2 * rows, width)
        g = g_all[pl.ds(2 * step, 2)].reshape(2 * rows, width)
        gate_w = gu_w[: count // 2].reshape(units, width)
        up_w = gu_w[count // 2 :].reshape(units, width)
        down_w = d_w[...].reshape(units, width)
        for begin in range(0, units, step_units):
            at = slice(begin, begin + step_units)
            gate = dot(x, gate_w[at], 1, 1)
            up = dot(x, up_w[at], 1, 1)
            grad_hidden = dot(g, down_w[at], 1, 1)
            sigmoid = 0.5 * jnp.tanh(0.5 * gate) + 0.5
            silu = gate * sigmoid
            hid[:, at] = (silu * up).astype(BF16)
            gg[:, at] = (grad_hidden * up * (sigmoid + silu * (1.0 - sigmoid))).astype(BF16)
            gu[:, at] = (grad_hidden * silu).astype(BF16)

        def hand_out(value, kept, given):
            held[...] = value.astype(BF16).reshape(2, rows, width)
            kept[0] = held[core]
            given[0] = held[1 - core]

        hand_out(dot(gg[...], gate_w, 1, 0) + dot(gu[...], up_w, 1, 0), gn_kept, gn_given)
        hand_out(dot(hid[...], down_w, 1, 0), part_kept, part_given)

        @pl.when(step == size // 2 - 1)
        def _():
            for copy in handed:
                copy.wait()

    hbm = pl.BlockSpec(memory_space=pl.ANY)
    by_rows = pl.BlockSpec((2 * rows, units), lambda i: (i, 0))
    by_pair = pl.BlockSpec((1, rows, width), lambda i: (i, 0, 0))
    like = jax.ShapeDtypeStruct
    return pl.pallas_call(
        body,
        grid=(size // 2,),
        in_specs=[pl.BlockSpec(memory_space=pltpu.SMEM)]
        + [hbm] * (count + 2 * size),
        out_specs=[by_rows] * 3 + [by_pair] * 4 + [hbm] * 2,
        out_shape=[like((size * rows, units), BF16)] * 3
        + [like((size // 2, rows, width), BF16)] * 4
        + [like((size, rows, width), BF16)] * 2,
        scratch_shapes=[
            pltpu.VMEM((count, 2 * tall, width), BF16),
            pltpu.VMEM((count, tall, width), BF16),
            pltpu.VMEM((size, rows, width), BF16),
            pltpu.VMEM((size, rows, width), BF16),
            pltpu.VMEM((2, rows, width), BF16),
            pltpu.SemaphoreType.DMA((2 * count + 2 * size + 2,)),
        ],
        compiler_params=pltpu.CompilerParams(vmem_limit_bytes=VMEM_LIMIT),
        cost_estimate=pl.CostEstimate(flops=1, bytes_accessed=1, transcendentals=0),
        name="feed_forward",
    )(me, *weight_blocks, *row_blocks, *cot_blocks)


def both_heads(pair):
    lane = lax.broadcasted_iota(jnp.int32, pair.shape, 1)
    zero = jnp.zeros_like(pair)
    return jnp.concatenate(
        [jnp.where(lane < HEAD, pair, zero), jnp.where(lane < HEAD, zero, pair)], axis=0
    )


def fill_bias(low_ref, high_ref, place_ref, bias_ref):
    place = place_ref[...]
    allowed = (place >= low_ref[...]) & (place <= high_ref[...])
    bias = jnp.where(allowed, 0.0, MASKED).astype(F32)
    rows = bias.shape[1]
    bias_ref[:, :rows] = bias
    bias_ref[:, rows:] = bias


def own_rows(wide, rows):
    return jnp.concatenate([wide[:HEAD, :rows], wide[HEAD:, rows:]], axis=0)


def pairing(kv_ref, pair, begin):
    both = kv_ref[:, begin : begin + PAIR].astype(F32)
    crossed = pltpu.roll(both, HEAD, 1)
    lane = lax.broadcasted_iota(jnp.int32, both.shape, 1)
    first = jnp.where(pair <= PAIRS // 2, both, crossed)
    second = jnp.where(pair < PAIRS // 2, crossed, both)
    return jnp.where(lane < HEAD, first, second)


def new_pairing(step, pair):
    return (step == 0) | (pair == PAIRS // 2) | (pair == PAIRS // 2 + 1)


def attend_kernel(
    begin_pair, low_ref, high_ref, place_ref, q_ref, kv_ref,
    o_ref, lse_ref, bias_ref, k_ref, vt_ref,
):
    step = pl.program_id(0)
    pair = step + begin_pair

    @pl.when(step == 0)
    def _():
        fill_bias(low_ref, high_ref, place_ref, bias_ref)

    @pl.when(new_pairing(step, pair))
    def _():
        k_ref[...] = pairing(kv_ref, pair, 0).astype(BF16)
        vt_ref[...] = pairing(kv_ref, pair, PAIR).T.astype(BF16)

    rows = q_ref.shape[0]
    queries = both_heads(q_ref[...])
    keys = k_ref[...]
    values_t = vt_ref[...]
    outs, totals = [], []
    for begin in range(0, 2 * rows, 256):
        scores = dot(keys, queries[begin : begin + 256], 1, 1) + bias_ref[:, begin : begin + 256]
        top = jnp.max(scores, axis=0, keepdims=True)
        probs = jnp.exp(scores - top)
        total = jnp.sum(probs, axis=0, keepdims=True)
        outs.append(dot(values_t, probs.astype(BF16), 1, 0) / total)
        totals.append(top + jnp.log(total))
    wide = jnp.concatenate(outs, axis=1)
    o_ref[...] = own_rows(wide, rows).T.astype(BF16)
    lse_ref[0] = jnp.concatenate(totals, axis=1)


def attend_back_kernel(
    begin_pair, low_ref, high_ref, place_ref, q_ref, g_ref, o_ref, lse_ref, kv_ref, *refs,
):
    dq_ref, dkv_ref, bias_ref, k_ref, kt_ref, v_ref, dk_ref, dv_ref = refs[-8:]
    step = pl.program_id(0)
    pair = step + begin_pair

    @pl.when(step == 0)
    def _():
        fill_bias(low_ref, high_ref, place_ref, bias_ref)
        dkv_ref[...] = refs[0][...] if begin_pair else jnp.zeros_like(dkv_ref)

    @pl.when(new_pairing(step, pair))
    def _():
        keys_now = pairing(kv_ref, pair, 0)
        k_ref[...] = keys_now.astype(BF16)
        kt_ref[...] = keys_now.T.astype(BF16)
        v_ref[...] = pairing(kv_ref, pair, PAIR).astype(BF16)
        dk_ref[...] = jnp.zeros_like(dk_ref)
        dv_ref[...] = jnp.zeros_like(dv_ref)

    rows = q_ref.shape[0]
    queries = both_heads(q_ref[...])
    grads = both_heads(g_ref[...])
    keys = k_ref[...]
    keys_t = kt_ref[...]
    values = v_ref[...]
    product = (g_ref[...].astype(F32) * o_ref[...].astype(F32)).T
    delta = jnp.concatenate(
        [
            jnp.sum(product[:HEAD], axis=0, keepdims=True),
            jnp.sum(product[HEAD:], axis=0, keepdims=True),
        ],
        axis=1,
    )
    lse = lse_ref[0]
    outs = []
    for begin in range(0, 2 * rows, 256):
        part = slice(begin, begin + 256)
        scores = dot(keys, queries[part], 1, 1) + bias_ref[:, part]
        probs = jnp.exp(scores - lse[:, part])
        grad_probs = dot(values, grads[part], 1, 1)
        grad_scores = (probs * (grad_probs - delta[:, part])).astype(BF16)
        outs.append(dot(keys_t, grad_scores, 1, 0))
        dk_ref[...] += dot(grad_scores, queries[part], 1, 0)
        dv_ref[...] += dot(probs.astype(BF16), grads[part], 1, 0)
    wide = jnp.concatenate(outs, axis=1)
    dq_ref[...] = own_rows(wide, rows).T * 0.125

    def fold(own_lanes):
        for at, sums in ((0, dk_ref), (PAIR, dv_ref)):
            sums_now = sums[...]
            lane = lax.broadcasted_iota(jnp.int32, sums_now.shape, 1)
            both = sums_now + pltpu.roll(sums_now, HEAD, 1)
            kept = jnp.where((lane < HEAD) == own_lanes, both, 0.0)
            dkv_ref[:, at : at + PAIR] += kept

    @pl.when(pair == PAIRS // 2 - 1)
    def _():
        fold(True)

    @pl.when(pair == PAIRS // 2)
    def _():
        dkv_ref[:, :PAIR] += dk_ref[...]
        dkv_ref[:, PAIR:] += dv_ref[...]

    @pl.when(pair == PAIRS - 1)
    def _():
        fold(False)


def whole(shape):
    return pl.BlockSpec(shape, lambda i: (0,) * len(shape))


def attend(low, high, place, queries, kv_all, begin, pairs):
    rows, count = queries.shape[0], place.shape[0]
    taken = pl.BlockSpec((rows, PAIR), lambda i: (0, i + begin))
    made = pl.BlockSpec((rows, PAIR), lambda i: (0, i))
    return pl.pallas_call(
        functools.partial(attend_kernel, begin),
        grid=(pairs,),
        in_specs=[whole((1, rows)), whole((1, rows)), whole((count, 1)), taken]
        + [whole((count, 2 * KVW))],
        out_specs=[made, pl.BlockSpec((1, 1, 2 * rows), lambda i: (i, 0, 0))],
        out_shape=[
            jax.ShapeDtypeStruct((rows, pairs * PAIR), BF16),
            jax.ShapeDtypeStruct((pairs, 1, 2 * rows), F32),
        ],
        scratch_shapes=[
            pltpu.VMEM((count, 2 * rows), F32),
            pltpu.VMEM((count, PAIR), BF16),
            pltpu.VMEM((PAIR, count), BF16),
        ],
        compiler_params=pltpu.CompilerParams(vmem_limit_bytes=VMEM_LIMIT),
        cost_estimate=pl.CostEstimate(flops=1, bytes_accessed=1, transcendentals=0),
        name="attend",
    )(low, high, place, queries, kv_all)


def attend_back(low, high, place, queries, grads, outs, lse, kv_all, begin, pairs, so_far):
    rows, count = queries.shape[0], place.shape[0]
    taken = pl.BlockSpec((rows, PAIR), lambda i: (0, i + begin))
    made = pl.BlockSpec((rows, PAIR), lambda i: (0, i))
    sums = whole((count, 2 * KVW))
    return pl.pallas_call(
        functools.partial(attend_back_kernel, begin),
        grid=(pairs,),
        in_specs=[whole((1, rows)), whole((1, rows)), whole((count, 1)), taken, taken, made]
        + [pl.BlockSpec((1, 1, 2 * rows), lambda i: (i, 0, 0)), sums]
        + [sums] * len(so_far),
        out_specs=[made, sums],
        out_shape=[
            jax.ShapeDtypeStruct((rows, pairs * PAIR), F32),
            jax.ShapeDtypeStruct((count, 2 * KVW), F32),
        ],
        scratch_shapes=[
            pltpu.VMEM((count, 2 * rows), F32),
            pltpu.VMEM((count, PAIR), BF16),
            pltpu.VMEM((PAIR, count), BF16),
            pltpu.VMEM((count, PAIR), BF16),
            pltpu.VMEM((count, PAIR), F32),
            pltpu.VMEM((count, PAIR), F32),
        ],
        compiler_params=pltpu.CompilerParams(vmem_limit_bytes=VMEM_LIMIT),
        cost_estimate=pl.CostEstimate(flops=1, bytes_accessed=1, transcendentals=0),
        name="attend_back",
    )(low, high, place, queries, grads, outs, lse, kv_all, *so_far)


def rms_scale(values_in):
    return lax.rsqrt(jnp.mean(values_in * values_in, axis=-1, keepdims=True) + EPSILON)


def angle_tables(places):
    exponent = jnp.arange(HEAD // 2, dtype=F32) * 2.0 / HEAD
    frequency = ROPE_BASE ** (-exponent)
    turn = places.astype(F32)[:, None] * frequency[None, :]
    cosine, sine = lax.optimization_barrier((jnp.cos(turn), jnp.sin(turn)))
    return jnp.concatenate([cosine] * 4, axis=1), jnp.concatenate([sine] * 4, axis=1)


def widen(table, width):
    return jnp.concatenate([table] * (width // PAIR), axis=1)


def first_halves(shape):
    return lax.broadcasted_iota(jnp.int32, shape, 1) % HEAD < HEAD // 2


def rotate(tensor, cosine, sine):
    half = HEAD // 2
    ahead, behind = jnp.roll(tensor, -half, axis=1), jnp.roll(tensor, half, axis=1)
    turned = jnp.where(first_halves(tensor.shape), -ahead, behind)
    width = tensor.shape[1]
    return tensor * widen(cosine, width) + turned * widen(sine, width)


def rotate_back(grad_in, cosine, sine):
    half = HEAD // 2
    width = grad_in.shape[1]
    scaled = grad_in * widen(sine, width)
    ahead, behind = jnp.roll(scaled, -half, axis=1), jnp.roll(scaled, half, axis=1)
    return grad_in * widen(cosine, width) + jnp.where(
        first_halves(grad_in.shape), ahead, -behind
    )


def norm_back(grad_in, row_data, scale_in, gain_in):
    gain_term = jnp.sum(grad_in * row_data * scale_in, axis=0)
    grad_normed = grad_in * gain_in
    inner_mean = jnp.mean(grad_normed * row_data, axis=-1, keepdims=True)
    return (
        scale_in * grad_normed - row_data * scale_in * scale_in * scale_in * inner_mean,
        gain_term,
    )


def pad_row(vector, width):
    return jnp.pad(vector, (0, width - vector.shape[0]))[None, :]


def stack_from_lanes(array, count):
    rows, width = array.shape
    return jnp.transpose(array.reshape(rows, count, width // count), (1, 0, 2))


def per_device(
    seq_size, fsdp_size, tokens, segment_ids, positions, norm_one, qkv_weight, qkv_bias,
    out_weight, norm_two, gate_up_weight, down_weight, cotangent,
):
    my_seq, my_fsdp = lax.axis_index("seq"), lax.axis_index("fsdp")
    me = jnp.stack([my_seq, my_fsdp]).astype(jnp.int32)
    offsets = range(seq_size)
    row_count = tokens.shape[0]
    width = qkv_weight.shape[0]
    qkv_rows = qkv_weight.shape[1]
    strip = down_weight.shape[0] // seq_size
    tall = padded(strip)

    ff_cut = cut_ff(me, gate_up_weight, down_weight, seq_size)
    ff_share = [ff_cut[0]] + [swap(ff_cut[o], "seq", seq_size, o) for o in offsets if o]
    qkv_tall = padded(qkv_rows)
    packed = jnp.concatenate(
        [
            jnp.pad(qkv_weight.T, ((0, qkv_tall - qkv_rows), (0, 0))),
            pad_row(norm_one, width),
            pad_row(qkv_bias, width),
            pad_row(norm_two, width),
            jnp.zeros((13, width), BF16),
            out_weight,
        ],
        axis=0,
    )
    packed = after(packed, ff_cut[0])
    ff_block = join_lanes(me, ff_share)
    columns = ff_spread(
        after(column_gather(packed, fsdp_size), ff_block), fsdp_size
    )
    wide = qkv_tall + 16
    out_stack = jnp.concatenate([columns[m][:, wide:] for m in sorted(columns)], axis=0)
    columns[0] = after(columns[0], ff_block)
    packed_pieces = [seq_gather(columns[m][:, :wide], seq_size) for m in sorted(columns)]
    ff_blocks = {0: ff_block}
    for bit in fsdp_bits(fsdp_size)[:2]:
        ff_blocks.update({o ^ bit: swap(b, "fsdp", fsdp_size, bit) for o, b in ff_blocks.items()})
    inner = fsdp_size // OUTER

    qkv_pieces = [[piece[o] for piece in packed_pieces] for o in offsets]
    qkv_t, vectors = join_both(me, qkv_pieces, qkv_tall)
    own_x = ff_spread(ff_block, fsdp_size)
    qkv_t = after(qkv_t, ff_blocks[2 * inner], ff_blocks[inner], *own_x.values())[:, :qkv_rows].reshape(fsdp_size * qkv_rows, -1)
    gain_one = vectors[:, 0, : norm_one.shape[0]].reshape(-1).astype(F32)
    bias_full = vectors[:, 1, : qkv_bias.shape[0]].reshape(-1).astype(F32)
    gain_two = vectors[:, 2, : norm_two.shape[0]].reshape(-1).astype(F32)

    out_blocks = seq_gather(after(out_stack, packed_pieces[-1][seq_size // 2]), seq_size)

    inputs = tokens.astype(F32)
    scale_one = rms_scale(inputs)
    normed_one = (inputs * scale_one * gain_one).astype(BF16)
    joined = dot(normed_one, qkv_t, 1, 1) + bias_full
    cosine, sine = angle_tables(positions)
    turned = rotate(joined[:, : QW + KVW], cosine, sine).astype(BF16)
    queries = turned[:, :QW] * jnp.asarray(0.125, BF16)
    kv_local = jnp.concatenate([turned[:, QW:], joined[:, QW + KVW :].astype(BF16)], axis=1)
    kv_all = lax.all_gather(kv_local, "seq", axis=0, tiled=True)
    kv_all = after(kv_all, ff_blocks[2 * inner])
    cot_blocks = seq_gather(after(cotangent, kv_all), seq_size)
    row_place = jnp.arange(row_count, dtype=jnp.int32)
    high = my_seq * row_count + row_place
    low = high - positions
    place = jnp.arange(seq_size * row_count, dtype=jnp.int32)[:, None]
    low, high = low[None, :], high[None, :]
    split = PAIRS // 2 + 1
    spread = lambda block: ff_spread(block, fsdp_size)
    near = ff_blocks[inner]
    far, last = ff_blocks[2 * inner], ff_blocks[3 * inner]
    near_x = spread(after(near, kv_all))
    attn_one, lse_one = attend(
        low, high, place, after(queries, far), kv_all, 0, split
    )
    far_x = spread(after(far, kv_all))
    queries_two = after(queries, attn_one, cot_blocks[seq_size // 2], *near_x.values())
    attn_two, lse_two = attend(low, high, place, queries_two, kv_all, split, PAIRS - split)
    last_x = spread(last)
    for base, row in ((0, own_x), (inner, near_x), (2 * inner, far_x), (3 * inner, last_x)):
        ff_blocks.update({base + m: block for m, block in row.items()})
    attn_flat = jnp.concatenate([attn_one, attn_two], axis=1)

    out_list = [[out_blocks[o]] for o in offsets]
    out_list[0][0] = after(out_list[0][0], attn_one)
    out_full = join_both(me, out_list, out_weight.shape[0])[0].reshape(QW, -1)

    residual = inputs + dot(attn_flat, out_full, 1, 0)
    scale_two = rms_scale(residual)
    normed_two = (residual * scale_two * gain_two).astype(BF16)
    normed_two = after(normed_two, *far_x.values())
    normed_blocks = {0: normed_two}
    bit = seq_size // 2
    while bit:
        if bit == 1:
            top = seq_size // 2
            normed_blocks[top] = after(normed_blocks[top], last)
        normed_blocks.update(
            {o ^ bit: swap(b, "seq", seq_size, bit) for o, b in normed_blocks.items()}
        )
        bit //= 2
    (
        hidden, grad_gate, grad_up, kept, given, kept_layer, given_layer, normed_all, cot_all,
    ) = feed_forward(
        me,
        [ff_blocks[o] for o in range(fsdp_size)],
        [normed_blocks[o] for o in offsets],
        [cot_blocks[o] for o in offsets],
    )
    normed_all = normed_all.reshape(seq_size * row_count, -1)
    cot_all = cot_all.reshape(seq_size * row_count, -1)
    by_seq = lambda rows: rows.reshape(seq_size, row_count, -1)

    normed_sum = add(kept, swap(given, "seq", seq_size, 1))
    bit = 2
    while bit < seq_size:
        kept, given = halve(normed_sum, 1, my_seq // bit)
        normed_sum = add(kept, swap(given, "seq", seq_size, bit))
        bit *= 2
    grad_normed_two = normed_sum[0]
    hidden = after(hidden, given)
    down_term = dot(hidden, cot_all, 0, 0).astype(BF16).reshape(fsdp_size, tall, -1)
    grad_gate, grad_up = after(grad_gate, down_term), after(grad_up, down_term)
    gate_term = dot(grad_gate, normed_all, 0, 0).astype(BF16).reshape(fsdp_size // 2, 2, tall, -1)
    up_term = dot(grad_up, normed_all, 0, 0).astype(BF16).reshape(fsdp_size // 2, 2, tall, -1)

    bits = list(reversed(fsdp_bits(fsdp_size)))

    def give(stack, at):
        kept, given = fsdp_halve(stack, fsdp_size, bits[at], my_fsdp, bits[:at])
        return kept, given

    def send(given, at):
        return swap(given, "fsdp", fsdp_size, bits[at])

    def finish(kept, got, at):
        stack = add(kept, got)
        for later in range(at + 1, len(bits)):
            kept, given = give(stack, later)
            stack = add(kept, send(given, later))
        return stack[0]

    kept_one, given = give(down_term, 0)
    got_one = send(given, 0)
    kept_two, given = give(jnp.concatenate([gate_term[:, 0], up_term[:, 0]], axis=0), 0)
    got_two = send(after(given, grad_normed_two), 0)
    kept_three, given_three = give(jnp.concatenate([gate_term[:, 1], up_term[:, 1]], axis=0), 0)

    grad_path, norm_two_term = norm_back(grad_normed_two, residual, scale_two, gain_two)
    grad_residual = cotangent.astype(F32) + grad_path
    grad_branch = grad_residual.astype(BF16)
    grad_attn = dot(grad_branch, out_full, 1, 1).astype(BF16)
    grad_attn = after(grad_attn, gate_term, up_term)
    dq_one, kv_terms = attend_back(
        low, high, place, queries, grad_attn, attn_one, lse_one, kv_all, 0, split, ()
    )
    got_one = after(got_one, dq_one)
    got_three = send(after(given_three, got_one), 0)
    kept_one, given_one = give(add(kept_one, got_one), 1)
    next_one = send(given_one, 1)
    queries_two = after(queries, kv_terms, given_one)
    dq_two, kv_terms = attend_back(
        low, high, place, queries_two, grad_attn, attn_two, lse_two, kv_all, split,
        PAIRS - split, (kv_terms,),
    )
    got_two = after(got_two, dq_two)
    kept_two, given = give(add(kept_two, got_two), 1)
    next_two = send(given, 1)
    kept, given = halve(by_seq(kv_terms), 1, my_seq)
    kv_sum = add(kept, swap(given, "seq", seq_size, 1))
    bit = 2
    while bit < seq_size:
        kept, given = halve(kv_sum, 1, my_seq // bit)
        kv_sum = add(kept, swap(after(given, got_two), "seq", seq_size, bit))
        bit *= 2
    kv_mine = kv_sum[0]
    next_one, next_two = after(next_one, kv_mine), after(next_two, kv_mine)
    down_sum = finish(kept_one, next_one, 1)

    attn_late = after(attn_flat, dq_two)
    out_term = stack_from_lanes(dot(attn_late, grad_branch, 0, 0).astype(BF16), seq_size)
    kept, given = halve(out_term, 1, my_seq)
    out_sum = add(kept, swap(given, "seq", seq_size, 1))
    layer_sum = add(kept_layer, swap(after(given_layer, dq_two), "seq", seq_size, 1))
    kept_layer, given_layer = halve(layer_sum, 1, my_seq // 2)
    bit = 2
    while bit < seq_size:
        kept, given = halve(out_sum, 1, my_seq // bit)
        out_sum = add(kept, swap(after(given, kv_mine), "seq", seq_size, bit))
        bit *= 2
    out_mine = out_sum[0].reshape(fsdp_size, -1, width)
    got_three = after(got_three, kv_mine)
    kept_three, given = give(add(kept_three, got_three), 1)
    next_three = send(given, 1)
    turned_back = rotate_back(
        jnp.concatenate([dq_one, dq_two, kv_mine[:, :KVW]], axis=1), cosine, sine
    )
    grad_joined = jnp.concatenate([turned_back, kv_mine[:, KVW:]], axis=1).astype(BF16)
    grad_normed_one = dot(grad_joined, qkv_t, 1, 0)
    grad_path_one, norm_one_term = norm_back(grad_normed_one, inputs, scale_one, gain_one)
    grad_tokens = grad_residual + grad_path_one
    bias_term = jnp.sum(grad_joined.astype(F32), axis=0)

    def vector_rows(vector):
        rows = vector.reshape(fsdp_size, 1, -1)
        return jnp.pad(rows, ((0, 0), (0, 0), (0, width - rows.shape[2])))

    vector_terms = [norm_one_term, bias_term[: QW + KVW], bias_term[QW + KVW :], norm_two_term]
    small = jnp.concatenate([vector_rows(v) for v in vector_terms], axis=1).astype(BF16)
    small = jnp.pad(small, ((0, 0), (0, 16 - len(vector_terms)), (0, 0)))
    qkv_term = stack_from_lanes(dot(grad_joined, normed_one, 0, 0).astype(BF16), seq_size)
    qkv_term = qkv_term.reshape(seq_size, fsdp_size, qkv_rows, width)
    tail = jnp.concatenate(
        [qkv_term, jnp.broadcast_to(small[None], (seq_size,) + small.shape)], axis=2
    )
    tail = after(tail, next_two)
    tail_mine = seq_scatter(tail, seq_size, my_seq)
    got_layer = swap(after(given_layer, kv_mine), "seq", seq_size, 2)
    layer_sum = add(kept_layer, got_layer)
    bit = 4
    while bit < seq_size:
        kept, given = halve(layer_sum, 1, my_seq // bit)
        layer_sum = add(kept, swap(given, "seq", seq_size, bit))
        bit *= 2
    layer_out = residual + layer_sum[0]
    one_sum = finish(kept_two, next_two, 1)
    two_sum = finish(kept_three, next_three, 1)

    ff_back = cut_lanes(me, (one_sum, two_sum, down_sum), seq_size)
    ff_got = [ff_back[0]] + [swap(ff_back[o], "seq", seq_size, o) for o in offsets if o]
    grad_gate_up, grad_down = join_ff(me, ff_got, strip)

    tail_sum = fsdp_scatter(
        jnp.concatenate([tail_mine, out_mine], axis=1), fsdp_size, my_fsdp, next_three
    )
    pieces = [
        tail_sum[qkv_rows + i, : v.shape[0] // fsdp_size] for i, v in enumerate(vector_terms)
    ]
    return (
        layer_out.astype(BF16),
        grad_tokens,
        pieces[0],
        tail_sum[:qkv_rows].T,
        pieces[1],
        pieces[2],
        tail_sum[qkv_rows + 16 :],
        pieces[3],
        grad_gate_up,
        grad_down,
    )


def solution(mesh):
    rows, both = P(("fsdp", "seq"), None), P(("fsdp", "seq"))
    return jax.shard_map(
        functools.partial(per_device, mesh.shape["seq"], mesh.shape["fsdp"]),
        mesh=mesh,
        in_specs=(
            rows, both, both, P("fsdp"), P("seq", "fsdp"), P("fsdp"), P("fsdp", "seq"),
            P("fsdp"), P("seq", "fsdp"), P("fsdp", "seq"), rows,
        ),
        out_specs=(
            rows, rows, P("fsdp"), P("seq", "fsdp"), P("fsdp"), P("fsdp"), P("fsdp", "seq"),
            P("fsdp"), P("seq", "fsdp"), P("fsdp", "seq"),
        ),
        check_vma=False,
    )
```

```python
import functools

import jax
import jax.numpy as jnp
from jax import lax
from jax.experimental import pallas as pl
from jax.experimental.pallas import tpu as pltpu
from jax.sharding import PartitionSpec as P

HEADS = 14
KV_HEADS = 2
HEAD = 64
FF = 4864
QW = 896
KVW = 128
PAIR = 2 * HEAD
PAIRS = HEADS // 2
OUTER = 4

EPSILON = 1e-06
ROPE_BASE = 1000000.0
MASKED = -1e30
VMEM_LIMIT = 50 * 1024 * 1024

F32 = jnp.float32
BF16 = jnp.bfloat16


def dot(left, right, left_dim, right_dim):
    return lax.dot_general(
        left, right, (((left_dim,), (right_dim,)), ((), ())), preferred_element_type=F32
    )


def swap(block, axis, size, bits):
    return lax.ppermute(block, axis, [(i, i ^ bits) for i in range(size)])


def after(array, *others):
    return lax.optimization_barrier((array,) + others)[0]


def seq_gather(block, size):
    blocks = {0: block}
    bit = size // 2
    while bit:
        blocks.update({o ^ bit: swap(b, "seq", size, bit) for o, b in blocks.items()})
        bit //= 2
    return blocks


def fsdp_bits(size):
    inner = size // OUTER
    outer_bits, inner_bits = [], []
    bit = 1
    while bit < size:
        (outer_bits if bit >= inner else inner_bits).append(bit)
        bit *= 2
    return outer_bits + inner_bits


def column_gather(block, size):
    inner = size // OUTER
    return jnp.stack([block] + [swap(block, "fsdp", size, k * inner) for k in range(1, OUTER)])


def ff_spread(block, size):
    blocks = {0: block}
    for bit in fsdp_bits(size)[2:]:
        blocks.update({o ^ bit: swap(b, "fsdp", size, bit) for o, b in blocks.items()})
    return blocks


def halve(stack, bit, me):
    above = stack.shape[0] // (2 * bit)
    cut = stack.reshape((above, 2, bit) + stack.shape[1:])
    digit = (me // bit) % 2
    kept = lax.dynamic_index_in_dim(cut, digit, 1, keepdims=False)
    given = lax.dynamic_index_in_dim(cut, 1 - digit, 1, keepdims=False)
    merge = lambda part: part.reshape((above * bit,) + stack.shape[1:])
    return merge(kept), merge(given).astype(BF16)


def add(kept, got):
    return kept.astype(F32) + got.astype(F32)


def seq_scatter(stack, size, me):
    bit = 1
    while bit < size:
        kept, given = halve(stack, 1, me // bit)
        stack = add(kept, swap(given, "seq", size, bit))
        bit *= 2
    return stack[0]


def fsdp_halve(stack, size, bit, me, resolved):
    place = bit
    digit = me // bit
    for taken in resolved:
        if taken < bit:
            place //= 2
    kept, given = halve(stack, place, digit * place)
    return kept, given


def fsdp_scatter(stack, size, me, earlier):
    inner = size // OUTER
    resolved = []
    for bit in reversed(fsdp_bits(size)[2:]):
        kept, given = fsdp_halve(stack, size, bit, me, resolved)
        stack = add(kept, swap(given, "fsdp", size, bit))
        resolved.append(bit)
    place = me // inner
    low = after(stack.astype(BF16), earlier)
    total = lax.dynamic_index_in_dim(stack, place, 0, keepdims=False)
    for k in range(1, OUTER):
        given = lax.dynamic_index_in_dim(low, place ^ k, 0, keepdims=False)
        total = add(total, swap(given, "fsdp", size, k * inner))
    return total


def on_device(body, name, out_shapes, scratch, me, arrays):
    vmem = pl.BlockSpec(memory_space=pltpu.VMEM)
    return pl.pallas_call(
        body,
        in_specs=[pl.BlockSpec(memory_space=pltpu.SMEM)] + [vmem] * len(arrays),
        out_specs=[vmem] * len(out_shapes),
        out_shape=out_shapes,
        scratch_shapes=scratch,
        compiler_params=pltpu.CompilerParams(vmem_limit_bytes=VMEM_LIMIT),
        name=name,
    )(me, *arrays)


def padded(rows):
    return -(-rows // 16) * 16


def cut_ff(me, gate_up_weight, down_weight, size):
    width = gate_up_weight.shape[0]
    half = down_weight.shape[0]
    strip = half // size
    tall = padded(strip)

    def body(me_ref, gu_ref, d_ref, *refs):
        outs, held = refs[:size], refs[size]
        turned = gu_ref[...].astype(F32).T
        down = d_ref[...].astype(F32)
        blank = jnp.zeros((tall - strip, width), F32)
        for q in range(size):
            one = turned[q * strip : (q + 1) * strip]
            two = turned[half + q * strip : half + (q + 1) * strip]
            three = down[q * strip : (q + 1) * strip]
            parts = [one, blank, two, blank, three, blank]
            held[q] = jnp.concatenate(parts, axis=0).astype(BF16)
        for o in range(size):
            outs[o][...] = held[me_ref[0] ^ o]

    shape = jax.ShapeDtypeStruct((3 * tall, width), BF16)
    scratch = [pltpu.VMEM((size, 3 * tall, width), BF16)]
    return on_device(body, "cut_ff", [shape] * size, scratch, me, (gate_up_weight, down_weight))


def join_lanes(me, blocks):
    size = len(blocks)
    rows, width = blocks[0].shape

    def body(me_ref, *refs):
        ins, out, held = refs[:size], refs[size], refs[size + 1]
        for o in range(size):
            held[me_ref[0] ^ o] = ins[o][...]
        out[...] = jnp.concatenate([held[q].astype(F32) for q in range(size)], 1).astype(BF16)

    return on_device(
        body,
        "join_lanes",
        [jax.ShapeDtypeStruct((rows, size * width), BF16)],
        [pltpu.VMEM((size, rows, width), BF16)],
        me,
        blocks,
    )[0]


def join_both(me, pieces, rows):
    size, parts_each = len(pieces), len(pieces[0])
    _, tall, width = pieces[0][0].shape
    count = sum(part.shape[0] for part in pieces[0])
    inner = count // OUTER
    order = [k * inner + m for m in range(inner) for k in range(OUTER)]
    shapes = [jax.ShapeDtypeStruct((count, rows, size * width), BF16)]
    if tall > rows:
        shapes.append(jax.ShapeDtypeStruct((count, tall - rows, width), BF16))

    def body(me_ref, *refs):
        ins, out, held = refs[: size * parts_each], refs[size * parts_each], refs[-1]
        for o in range(size):
            at = 0
            for part in ins[o * parts_each : (o + 1) * parts_each]:
                for j in range(part.shape[0]):
                    place = me_ref[1] ^ order[at]
                    held[me_ref[0] ^ o, place] = part[j]
                    if tall > rows and o == 0:
                        refs[size * parts_each + 1][place] = part[j, rows:]
                    at += 1
        for f in range(count):
            parts = [held[q, f, :rows].astype(F32) for q in range(size)]
            out[f] = jnp.concatenate(parts, axis=1).astype(BF16)

    return on_device(
        body,
        "join_both",
        shapes,
        [pltpu.VMEM((size, count, tall, width), BF16)],
        me,
        [block for row in pieces for block in row],
    )


def cut_lanes(me, sums, size):
    rows = sum(s.shape[0] for s in sums)
    width = sums[0].shape[1] // size

    def body(me_ref, *refs):
        ins, outs, held = refs[: len(sums)], refs[len(sums) : -1], refs[-1]
        whole = jnp.concatenate([r[...] for r in ins], axis=0)
        for q in range(size):
            held[q] = whole[:, q * width : (q + 1) * width].astype(BF16)
        for o in range(size):
            outs[o][...] = held[me_ref[0] ^ o]

    shape = jax.ShapeDtypeStruct((rows, width), BF16)
    scratch = [pltpu.VMEM((size, rows, width), BF16)]
    return on_device(body, "cut_lanes", [shape] * size, scratch, me, sums)


def join_ff(me, blocks, strip):
    size = len(blocks)
    rows, width = blocks[0].shape
    tall = rows // 3

    def body(me_ref, *refs):
        ins, gu, down, held = refs[:size], refs[size], refs[size + 1], refs[size + 2]
        for o in range(size):
            held[me_ref[0] ^ o] = ins[o][...].astype(F32)
        cut = [
            [held[q, i * tall : i * tall + strip] for q in range(size)] for i in range(3)
        ]
        gu[...] = jnp.concatenate(cut[0] + cut[1], axis=0).T
        down[...] = jnp.concatenate(cut[2], axis=0)

    return on_device(
        body,
        "join_ff",
        [
            jax.ShapeDtypeStruct((width, 2 * size * strip), F32),
            jax.ShapeDtypeStruct((size * strip, width), F32),
        ],
        [pltpu.VMEM((size, rows, width), F32)],
        me,
        blocks,
    )


def feed_forward(me, weight_blocks, row_blocks, cot_blocks):
    count, size = len(weight_blocks), len(row_blocks)
    rows, width = row_blocks[0].shape
    tall = weight_blocks[0].shape[0] // 3
    units = count * tall
    step_units = 256

    def body(me_ref, *refs):
        blocks = refs[:count]
        xs, gs = refs[count : count + size], refs[count + size : count + 2 * size]
        outs = refs[count + 2 * size : count + 2 * size + 9]
        hid, gg, gu, gn_kept, gn_given, part_kept, part_given, x_out, g_out = outs
        gu_w, d_w, x_all, g_all, sems = refs[count + 2 * size + 9 :]
        step = pl.program_id(0)
        core = me_ref[0] % 2
        handed = [
            pltpu.make_async_copy(src, dst, sems.at[2 * count + 2 * size + i])
            for i, (src, dst) in enumerate(((x_all, x_out), (g_all, g_out)))
        ]

        @pl.when(step == 0)
        def _():
            copies = []
            for o in range(count):
                f = me_ref[1] ^ o
                copies.append((blocks[o].at[pl.ds(0, 2 * tall)], gu_w.at[f]))
                copies.append((blocks[o].at[pl.ds(2 * tall, tall)], d_w.at[f]))
            for o in range(size):
                copies.append((xs[o], x_all.at[me_ref[0] ^ o]))
                copies.append((gs[o], g_all.at[me_ref[0] ^ o]))
            started = [
                pltpu.make_async_copy(src, dst, sems.at[i]) for i, (src, dst) in enumerate(copies)
            ]
            for copy in started:
                copy.start()
            for copy in started:
                copy.wait()
            for copy in handed:
                copy.start()

        x = x_all[step]
        g = g_all[step]
        gate_w = gu_w[: count // 2].reshape(units, width)
        up_w = gu_w[count // 2 :].reshape(units, width)
        down_w = d_w[...].reshape(units, width)
        for begin in range(0, units, step_units):
            at = slice(begin, begin + step_units)
            gate = dot(x, gate_w[at], 1, 1)
            up = dot(x, up_w[at], 1, 1)
            grad_hidden = dot(g, down_w[at], 1, 1)
            sigmoid = 0.5 * jnp.tanh(0.5 * gate) + 0.5
            silu = gate * sigmoid
            hid[:, at] = (silu * up).astype(BF16)
            gg[:, at] = (grad_hidden * up * (sigmoid + silu * (1.0 - sigmoid))).astype(BF16)
            gu[:, at] = (grad_hidden * silu).astype(BF16)

        mine = step % 2 == core

        def hand_out(value, kept, given):
            low = value.astype(BF16)

            @pl.when(mine)
            def _():
                kept[0] = low

            @pl.when(jnp.logical_not(mine))
            def _():
                given[0] = low

        hand_out(dot(gg[...], gate_w, 1, 0) + dot(gu[...], up_w, 1, 0), gn_kept, gn_given)
        hand_out(dot(hid[...], down_w, 1, 0), part_kept, part_given)

        @pl.when(step == size - 1)
        def _():
            for copy in handed:
                copy.wait()

    hbm = pl.BlockSpec(memory_space=pl.ANY)
    by_rows = pl.BlockSpec((rows, units), lambda i: (i, 0))
    by_pair = pl.BlockSpec((1, rows, width), lambda i: (i // 2, 0, 0))
    like = jax.ShapeDtypeStruct
    return pl.pallas_call(
        body,
        grid=(size,),
        in_specs=[pl.BlockSpec(memory_space=pltpu.SMEM)]
        + [hbm] * (count + 2 * size),
        out_specs=[by_rows] * 3 + [by_pair] * 4 + [hbm] * 2,
        out_shape=[like((size * rows, units), BF16)] * 3
        + [like((size // 2, rows, width), BF16)] * 4
        + [like((size, rows, width), BF16)] * 2,
        scratch_shapes=[
            pltpu.VMEM((count, 2 * tall, width), BF16),
            pltpu.VMEM((count, tall, width), BF16),
            pltpu.VMEM((size, rows, width), BF16),
            pltpu.VMEM((size, rows, width), BF16),
            pltpu.SemaphoreType.DMA((2 * count + 2 * size + 2,)),
        ],
        compiler_params=pltpu.CompilerParams(vmem_limit_bytes=VMEM_LIMIT),
        cost_estimate=pl.CostEstimate(flops=1, bytes_accessed=1, transcendentals=0),
        name="feed_forward",
    )(me, *weight_blocks, *row_blocks, *cot_blocks)


def both_heads(pair):
    lane = lax.broadcasted_iota(jnp.int32, pair.shape, 1)
    zero = jnp.zeros_like(pair)
    return jnp.concatenate(
        [jnp.where(lane < HEAD, pair, zero), jnp.where(lane < HEAD, zero, pair)], axis=0
    )


def fill_bias(low_ref, high_ref, place_ref, bias_ref):
    place = place_ref[...]
    allowed = (place >= low_ref[...]) & (place <= high_ref[...])
    bias = jnp.where(allowed, 0.0, MASKED).astype(F32)
    rows = bias.shape[1]
    bias_ref[:, :rows] = bias
    bias_ref[:, rows:] = bias


def own_rows(wide, rows):
    return jnp.concatenate([wide[:HEAD, :rows], wide[HEAD:, rows:]], axis=0)


def pairing(kv_ref, pair, begin):
    both = kv_ref[:, begin : begin + PAIR].astype(F32)
    crossed = pltpu.roll(both, HEAD, 1)
    lane = lax.broadcasted_iota(jnp.int32, both.shape, 1)
    first = jnp.where(pair <= PAIRS // 2, both, crossed)
    second = jnp.where(pair < PAIRS // 2, crossed, both)
    return jnp.where(lane < HEAD, first, second)


def new_pairing(step, pair):
    return (step == 0) | (pair == PAIRS // 2) | (pair == PAIRS // 2 + 1)


def attend_kernel(
    begin_pair, low_ref, high_ref, place_ref, q_ref, kv_ref,
    o_ref, lse_ref, bias_ref, k_ref, vt_ref,
):
    step = pl.program_id(0)
    pair = step + begin_pair

    @pl.when(step == 0)
    def _():
        fill_bias(low_ref, high_ref, place_ref, bias_ref)

    @pl.when(new_pairing(step, pair))
    def _():
        k_ref[...] = pairing(kv_ref, pair, 0).astype(BF16)
        vt_ref[...] = pairing(kv_ref, pair, PAIR).T.astype(BF16)

    rows = q_ref.shape[0]
    queries = both_heads(q_ref[...])
    keys = k_ref[...]
    values_t = vt_ref[...]
    outs, totals = [], []
    for begin in range(0, 2 * rows, 256):
        scores = dot(keys, queries[begin : begin + 256], 1, 1) + bias_ref[:, begin : begin + 256]
        top = jnp.max(scores, axis=0, keepdims=True)
        probs = jnp.exp(scores - top)
        total = jnp.sum(probs, axis=0, keepdims=True)
        outs.append(dot(values_t, probs.astype(BF16), 1, 0) / total)
        totals.append(top + jnp.log(total))
    wide = jnp.concatenate(outs, axis=1)
    o_ref[...] = own_rows(wide, rows).T.astype(BF16)
    lse_ref[0] = jnp.concatenate(totals, axis=1)


def attend_back_kernel(
    begin_pair, low_ref, high_ref, place_ref, q_ref, g_ref, o_ref, lse_ref, kv_ref, *refs,
):
    dq_ref, dkv_ref, bias_ref, k_ref, kt_ref, v_ref, dk_ref, dv_ref = refs[-8:]
    step = pl.program_id(0)
    pair = step + begin_pair

    @pl.when(step == 0)
    def _():
        fill_bias(low_ref, high_ref, place_ref, bias_ref)
        dkv_ref[...] = refs[0][...] if begin_pair else jnp.zeros_like(dkv_ref)

    @pl.when(new_pairing(step, pair))
    def _():
        keys_now = pairing(kv_ref, pair, 0)
        k_ref[...] = keys_now.astype(BF16)
        kt_ref[...] = keys_now.T.astype(BF16)
        v_ref[...] = pairing(kv_ref, pair, PAIR).astype(BF16)
        dk_ref[...] = jnp.zeros_like(dk_ref)
        dv_ref[...] = jnp.zeros_like(dv_ref)

    rows = q_ref.shape[0]
    queries = both_heads(q_ref[...])
    grads = both_heads(g_ref[...])
    keys = k_ref[...]
    keys_t = kt_ref[...]
    values = v_ref[...]
    product = (g_ref[...].astype(F32) * o_ref[...].astype(F32)).T
    delta = jnp.concatenate(
        [
            jnp.sum(product[:HEAD], axis=0, keepdims=True),
            jnp.sum(product[HEAD:], axis=0, keepdims=True),
        ],
        axis=1,
    )
    lse = lse_ref[0]
    outs = []
    for begin in range(0, 2 * rows, 256):
        part = slice(begin, begin + 256)
        scores = dot(keys, queries[part], 1, 1) + bias_ref[:, part]
        probs = jnp.exp(scores - lse[:, part])
        grad_probs = dot(values, grads[part], 1, 1)
        grad_scores = (probs * (grad_probs - delta[:, part])).astype(BF16)
        outs.append(dot(keys_t, grad_scores, 1, 0))
        dk_ref[...] += dot(grad_scores, queries[part], 1, 0)
        dv_ref[...] += dot(probs.astype(BF16), grads[part], 1, 0)
    wide = jnp.concatenate(outs, axis=1)
    dq_ref[...] = own_rows(wide, rows).T * 0.125

    def fold(own_lanes):
        for at, sums in ((0, dk_ref), (PAIR, dv_ref)):
            sums_now = sums[...]
            lane = lax.broadcasted_iota(jnp.int32, sums_now.shape, 1)
            both = sums_now + pltpu.roll(sums_now, HEAD, 1)
            kept = jnp.where((lane < HEAD) == own_lanes, both, 0.0)
            dkv_ref[:, at : at + PAIR] += kept

    @pl.when(pair == PAIRS // 2 - 1)
    def _():
        fold(True)

    @pl.when(pair == PAIRS // 2)
    def _():
        dkv_ref[:, :PAIR] += dk_ref[...]
        dkv_ref[:, PAIR:] += dv_ref[...]

    @pl.when(pair == PAIRS - 1)
    def _():
        fold(False)


def whole(shape):
    return pl.BlockSpec(shape, lambda i: (0,) * len(shape))


def attend(low, high, place, queries, kv_all, begin, pairs):
    rows, count = queries.shape[0], place.shape[0]
    taken = pl.BlockSpec((rows, PAIR), lambda i: (0, i + begin))
    made = pl.BlockSpec((rows, PAIR), lambda i: (0, i))
    return pl.pallas_call(
        functools.partial(attend_kernel, begin),
        grid=(pairs,),
        in_specs=[whole((1, rows)), whole((1, rows)), whole((count, 1)), taken]
        + [whole((count, 2 * KVW))],
        out_specs=[made, pl.BlockSpec((1, 1, 2 * rows), lambda i: (i, 0, 0))],
        out_shape=[
            jax.ShapeDtypeStruct((rows, pairs * PAIR), BF16),
            jax.ShapeDtypeStruct((pairs, 1, 2 * rows), F32),
        ],
        scratch_shapes=[
            pltpu.VMEM((count, 2 * rows), F32),
            pltpu.VMEM((count, PAIR), BF16),
            pltpu.VMEM((PAIR, count), BF16),
        ],
        compiler_params=pltpu.CompilerParams(vmem_limit_bytes=VMEM_LIMIT),
        cost_estimate=pl.CostEstimate(flops=1, bytes_accessed=1, transcendentals=0),
        name="attend",
    )(low, high, place, queries, kv_all)


def attend_back(low, high, place, queries, grads, outs, lse, kv_all, begin, pairs, so_far):
    rows, count = queries.shape[0], place.shape[0]
    taken = pl.BlockSpec((rows, PAIR), lambda i: (0, i + begin))
    made = pl.BlockSpec((rows, PAIR), lambda i: (0, i))
    sums = whole((count, 2 * KVW))
    return pl.pallas_call(
        functools.partial(attend_back_kernel, begin),
        grid=(pairs,),
        in_specs=[whole((1, rows)), whole((1, rows)), whole((count, 1)), taken, taken, made]
        + [pl.BlockSpec((1, 1, 2 * rows), lambda i: (i, 0, 0)), sums]
        + [sums] * len(so_far),
        out_specs=[made, sums],
        out_shape=[
            jax.ShapeDtypeStruct((rows, pairs * PAIR), F32),
            jax.ShapeDtypeStruct((count, 2 * KVW), F32),
        ],
        scratch_shapes=[
            pltpu.VMEM((count, 2 * rows), F32),
            pltpu.VMEM((count, PAIR), BF16),
            pltpu.VMEM((PAIR, count), BF16),
            pltpu.VMEM((count, PAIR), BF16),
            pltpu.VMEM((count, PAIR), F32),
            pltpu.VMEM((count, PAIR), F32),
        ],
        compiler_params=pltpu.CompilerParams(vmem_limit_bytes=VMEM_LIMIT),
        cost_estimate=pl.CostEstimate(flops=1, bytes_accessed=1, transcendentals=0),
        name="attend_back",
    )(low, high, place, queries, grads, outs, lse, kv_all, *so_far)


def rms_scale(values_in):
    return lax.rsqrt(jnp.mean(values_in * values_in, axis=-1, keepdims=True) + EPSILON)


def angle_tables(places):
    exponent = jnp.arange(HEAD // 2, dtype=F32) * 2.0 / HEAD
    frequency = ROPE_BASE ** (-exponent)
    turn = places.astype(F32)[:, None] * frequency[None, :]
    cosine, sine = lax.optimization_barrier((jnp.cos(turn), jnp.sin(turn)))
    return jnp.concatenate([cosine] * 4, axis=1), jnp.concatenate([sine] * 4, axis=1)


def widen(table, width):
    return jnp.concatenate([table] * (width // PAIR), axis=1)


def first_halves(shape):
    return lax.broadcasted_iota(jnp.int32, shape, 1) % HEAD < HEAD // 2


def rotate(tensor, cosine, sine):
    half = HEAD // 2
    ahead, behind = jnp.roll(tensor, -half, axis=1), jnp.roll(tensor, half, axis=1)
    turned = jnp.where(first_halves(tensor.shape), -ahead, behind)
    width = tensor.shape[1]
    return tensor * widen(cosine, width) + turned * widen(sine, width)


def norm_back_rows(grad_in, row_data, scale_in, gain_in):
    gain_term = jnp.sum(grad_in * row_data * scale_in, axis=0, keepdims=True)
    grad_normed = grad_in * gain_in
    inner_mean = jnp.mean(grad_normed * row_data, axis=-1, keepdims=True)
    return (
        scale_in * grad_normed - row_data * scale_in * scale_in * scale_in * inner_mean,
        gain_term,
    )


def residual_back(me, kept, got, residual, scale_two, gain_two, cotangent, out_full):
    rows, width = residual.shape

    def body(me_ref, kept_ref, got_ref, res_ref, scale_ref, gain_ref, cot_ref, out_ref,
             grad_ref, branch_ref, attn_ref, term_ref):
        grad = kept_ref[...] + got_ref[...].astype(F32)
        path, term_ref[...] = norm_back_rows(grad, res_ref[...], scale_ref[...], gain_ref[...])
        full = cot_ref[...].astype(F32) + path
        grad_ref[...] = full
        branch_ref[...] = full.astype(BF16)
        attn_ref[...] = dot(full.astype(BF16), out_ref[...], 1, 1).astype(BF16)

    shapes = [
        jax.ShapeDtypeStruct((rows, width), F32),
        jax.ShapeDtypeStruct((rows, width), BF16),
        jax.ShapeDtypeStruct((rows, QW), BF16),
        jax.ShapeDtypeStruct((1, width), F32),
    ]
    arrays = (kept, got, residual, scale_two, gain_two[None, :], cotangent, out_full)
    return on_device(body, "residual_back", shapes, [], me, arrays)


def joined_back(
    me, dq_one, dq_two, kept, got, cosine, sine, qkv_t, tokens, scale_one, gain_one,
    grad_residual, normed_one, norm_two_term, seq_size, fsdp_size,
):
    rows, width = tokens.shape
    total = qkv_t.shape[0]
    each, lanes = total // fsdp_size, width // seq_size
    tall = padded(each)

    def body(me_ref, dq1_ref, dq2_ref, kept_ref, got_ref, cos_ref, sin_ref, w_ref, x_ref,
             scale_ref, gain_ref, res_ref, n1_ref, term_ref,
             tokens_ref, mine_ref, other_ref, held):
        kv = kept_ref[...] + got_ref[...].astype(F32)
        turned = jnp.concatenate([dq1_ref[...], dq2_ref[...], kv[:, :KVW]], axis=1)
        across = turned.shape[1]
        scaled = turned * widen(sin_ref[...], across)
        ahead = pltpu.roll(scaled, across - HEAD // 2, 1)
        behind = pltpu.roll(scaled, HEAD // 2, 1)
        turned = turned * widen(cos_ref[...], across) + jnp.where(
            first_halves(turned.shape), ahead, -behind
        )
        joined = jnp.concatenate([turned, kv[:, KVW:]], axis=1).astype(BF16)
        wide = joined.astype(F32)
        grad_normed = dot(joined, w_ref[...], 1, 0)
        path, one_term = norm_back_rows(
            grad_normed, x_ref[...].astype(F32), scale_ref[...], gain_ref[...]
        )
        tokens_ref[...] = res_ref[...] + path
        bias = jnp.sum(wide, axis=0, keepdims=True)
        weight = dot(wide.T.astype(BF16), n1_ref[...], 1, 0)
        vectors = [one_term, bias[:, : QW + KVW], bias[:, QW + KVW :], term_ref[...]]
        for f in range(fsdp_size):
            lines = []
            for vector in vectors:
                n = vector.shape[1] // fsdp_size
                piece = vector[:, f * n : (f + 1) * n]
                lines.append(jnp.concatenate([piece, jnp.zeros((1, lanes - n), F32)], axis=1))
            blank = jnp.zeros((tall - each, lanes), F32)
            below = [blank] * (tall > each) + lines + [jnp.zeros((12, lanes), F32)]
            for s in range(seq_size):
                part = weight[f * each : (f + 1) * each, s * lanes : (s + 1) * lanes]
                held[s, f] = jnp.concatenate([part] + below, axis=0).astype(BF16)
        core = me_ref[0] % 2
        for y in range(seq_size // 2):
            mine_ref[y] = held[2 * y + core]
            other_ref[y] = held[2 * y + 1 - core]

    block = (fsdp_size, tall + 16, lanes)
    half = jax.ShapeDtypeStruct((seq_size // 2,) + block, BF16)
    shapes = [jax.ShapeDtypeStruct((rows, width), F32), half, half]
    arrays = (
        dq_one, dq_two, kept, got, cosine, sine, qkv_t, tokens, scale_one, gain_one[None, :],
        grad_residual, normed_one, norm_two_term,
    )
    scratch = [pltpu.VMEM((seq_size,) + block, BF16)]
    return on_device(body, "joined_back", shapes, scratch, me, arrays)


def pad_row(vector, width):
    return jnp.pad(vector, (0, width - vector.shape[0]))[None, :]


def stack_from_lanes(array, count):
    rows, width = array.shape
    return jnp.transpose(array.reshape(rows, count, width // count), (1, 0, 2))


def per_device(
    seq_size, fsdp_size, tokens, segment_ids, positions, norm_one, qkv_weight, qkv_bias,
    out_weight, norm_two, gate_up_weight, down_weight, cotangent,
):
    my_seq, my_fsdp = lax.axis_index("seq"), lax.axis_index("fsdp")
    me = jnp.stack([my_seq, my_fsdp]).astype(jnp.int32)
    offsets = range(seq_size)
    row_count = tokens.shape[0]
    width = qkv_weight.shape[0]
    qkv_rows = qkv_weight.shape[1]
    strip = down_weight.shape[0] // seq_size
    tall = padded(strip)

    ff_cut = cut_ff(me, gate_up_weight, down_weight, seq_size)
    ff_share = [ff_cut[0]] + [swap(ff_cut[o], "seq", seq_size, o) for o in offsets if o]
    qkv_tall = padded(qkv_rows)
    packed = jnp.concatenate(
        [
            jnp.pad(qkv_weight.T, ((0, qkv_tall - qkv_rows), (0, 0))),
            pad_row(norm_one, width),
            pad_row(qkv_bias, width),
            pad_row(norm_two, width),
            jnp.zeros((13, width), BF16),
            out_weight,
        ],
        axis=0,
    )
    packed = after(packed, ff_cut[0])
    ff_block = join_lanes(me, ff_share)
    columns = ff_spread(
        after(column_gather(packed, fsdp_size), ff_block), fsdp_size
    )
    wide = qkv_tall + 16
    columns[0] = after(columns[0], ff_block)
    packed_pieces = [seq_gather(columns[m][:, :wide], seq_size) for m in sorted(columns)]
    ff_blocks = {0: ff_block}
    inner = fsdp_size // OUTER
    near = swap(ff_block, "fsdp", fsdp_size, inner)
    far = swap(ff_block, "fsdp", fsdp_size, 2 * inner)

    qkv_pieces = [[piece[o] for piece in packed_pieces] for o in offsets]
    qkv_t, vectors = join_both(me, qkv_pieces, qkv_tall)
    out_stack = jnp.concatenate([columns[m][:, wide:] for m in sorted(columns)], axis=0)
    out_stack = after(out_stack, packed_pieces[-1][seq_size // 2])
    out_blocks = seq_gather(out_stack, seq_size)

    own_x = ff_spread(ff_block, fsdp_size)
    last = swap(after(near, qkv_t), "fsdp", fsdp_size, 2 * inner)
    qkv_t = after(qkv_t, far, near, *own_x.values())[:, :qkv_rows].reshape(fsdp_size * qkv_rows, -1)
    gain_one = vectors[:, 0, : norm_one.shape[0]].reshape(-1).astype(F32)
    bias_full = vectors[:, 1, : qkv_bias.shape[0]].reshape(-1).astype(F32)
    gain_two = vectors[:, 2, : norm_two.shape[0]].reshape(-1).astype(F32)

    inputs = tokens.astype(F32)
    scale_one = rms_scale(inputs)
    normed_one = (inputs * scale_one * gain_one).astype(BF16)
    joined = dot(normed_one, qkv_t, 1, 1) + bias_full
    cosine, sine = angle_tables(positions)
    turned = rotate(joined[:, : QW + KVW], cosine, sine).astype(BF16)
    queries = turned[:, :QW] * jnp.asarray(0.125, BF16)
    kv_local = jnp.concatenate([turned[:, QW:], joined[:, QW + KVW :].astype(BF16)], axis=1)
    kv_all = lax.all_gather(kv_local, "seq", axis=0, tiled=True)
    cot_blocks = seq_gather(after(cotangent, kv_all), seq_size)
    row_place = jnp.arange(row_count, dtype=jnp.int32)
    high = my_seq * row_count + row_place
    low = high - positions
    place = jnp.arange(seq_size * row_count, dtype=jnp.int32)[:, None]
    low, high = low[None, :], high[None, :]
    split = PAIRS // 2 + 1
    spread = lambda block: ff_spread(block, fsdp_size)
    near_x = spread(after(near, kv_all))
    attn_one, lse_one = attend(
        low, high, place, after(queries, far), kv_all, 0, split
    )
    far_x = spread(after(far, kv_all))
    queries_two = after(queries, attn_one, last, cot_blocks[seq_size // 2], *near_x.values())
    attn_two, lse_two = attend(low, high, place, queries_two, kv_all, split, PAIRS - split)
    last_x = spread(last)
    for base, row in ((0, own_x), (inner, near_x), (2 * inner, far_x), (3 * inner, last_x)):
        ff_blocks.update({base + m: block for m, block in row.items()})
    attn_flat = jnp.concatenate([attn_one, attn_two], axis=1)

    out_list = [[out_blocks[o]] for o in offsets]
    out_list[0][0] = after(out_list[0][0], attn_one)
    out_full = join_both(me, out_list, out_weight.shape[0])[0].reshape(QW, -1)

    residual = inputs + dot(attn_flat, out_full, 1, 0)
    scale_two = rms_scale(residual)
    normed_two = (residual * scale_two * gain_two).astype(BF16)
    normed_blocks = {0: normed_two}
    bit = seq_size // 2
    while bit:
        if bit == 1:
            top = seq_size // 2
            normed_blocks[top] = after(normed_blocks[top], *far_x.values())
        normed_blocks.update(
            {o ^ bit: swap(b, "seq", seq_size, bit) for o, b in normed_blocks.items()}
        )
        bit //= 2
    (
        hidden, grad_gate, grad_up, kept, given, kept_layer, given_layer, normed_all, cot_all,
    ) = feed_forward(
        me,
        [ff_blocks[o] for o in range(fsdp_size)],
        [normed_blocks[o] for o in offsets],
        [cot_blocks[o] for o in offsets],
    )
    normed_all = normed_all.reshape(seq_size * row_count, -1)
    cot_all = cot_all.reshape(seq_size * row_count, -1)
    by_seq = lambda rows: rows.reshape(seq_size, row_count, -1)

    normed_sum = add(kept, swap(given, "seq", seq_size, 1))
    bit = 2
    while bit < seq_size:
        kept, given = halve(normed_sum, 1, my_seq // bit)
        got = swap(given, "seq", seq_size, bit)
        normed_sum = add(kept, got)
        bit *= 2
    normed_kept, normed_got = kept[0], got[0]
    hidden = after(hidden, given)
    down_term = dot(hidden, cot_all, 0, 0).astype(BF16).reshape(fsdp_size, tall, -1)
    grad_gate, grad_up = after(grad_gate, down_term), after(grad_up, down_term)
    gate_term = dot(grad_gate, normed_all, 0, 0).astype(BF16).reshape(fsdp_size // 2, 2, tall, -1)
    up_term = dot(grad_up, normed_all, 0, 0).astype(BF16).reshape(fsdp_size // 2, 2, tall, -1)

    bits = list(reversed(fsdp_bits(fsdp_size)))

    def give(stack, at):
        kept, given = fsdp_halve(stack, fsdp_size, bits[at], my_fsdp, bits[:at])
        return kept, given

    def send(given, at):
        return swap(given, "fsdp", fsdp_size, bits[at])

    def finish(kept, got, at):
        stack = add(kept, got)
        for later in range(at + 1, len(bits)):
            kept, given = give(stack, later)
            stack = add(kept, send(given, later))
        return stack[0]

    kept_one, given = give(down_term, 0)
    got_one = send(given, 0)
    kept_two, given = give(jnp.concatenate([gate_term[:, 0], up_term[:, 0]], axis=0), 0)
    got_two = send(after(given, normed_got), 0)
    kept_three, given_three = give(jnp.concatenate([gate_term[:, 1], up_term[:, 1]], axis=0), 0)

    grad_residual, grad_branch, grad_attn, norm_two_term = residual_back(
        me, normed_kept, normed_got, residual, scale_two, gain_two, cotangent, out_full
    )
    grad_attn = after(grad_attn, gate_term, up_term)
    dq_one, kv_terms = attend_back(
        low, high, place, queries, grad_attn, attn_one, lse_one, kv_all, 0, split, ()
    )
    got_one = after(got_one, dq_one)
    got_three = send(after(given_three, got_one), 0)
    kept_one, given_one = give(add(kept_one, got_one), 1)
    next_one = send(given_one, 1)
    queries_two = after(queries, kv_terms, given_one)
    dq_two, kv_terms = attend_back(
        low, high, place, queries_two, grad_attn, attn_two, lse_two, kv_all, split,
        PAIRS - split, (kv_terms,),
    )
    got_two = after(got_two, dq_two)
    kept_two, given = give(add(kept_two, got_two), 1)
    next_two = send(given, 1)
    kept, given = halve(by_seq(kv_terms), 1, my_seq)
    kv_sum = add(kept, swap(given, "seq", seq_size, 1))
    bit = 2
    while bit < seq_size:
        kv_kept, given = halve(kv_sum, 1, my_seq // bit)
        kv_got = swap(after(given, got_two), "seq", seq_size, bit)
        kv_sum = add(kv_kept, kv_got)
        bit *= 2
    kv_mine = kv_got

    attn_late = after(attn_flat, dq_two)
    out_term = stack_from_lanes(dot(attn_late, grad_branch, 0, 0).astype(BF16), seq_size)
    kept, given = halve(out_term, 1, my_seq)
    out_sum = add(kept, swap(given, "seq", seq_size, 1))
    layer_sum = add(kept_layer, swap(after(given_layer, dq_two), "seq", seq_size, 1))
    kept_layer, given_layer = halve(layer_sum, 1, my_seq // 2)
    bit = 2
    while bit < seq_size:
        kept, given = halve(out_sum, 1, my_seq // bit)
        out_sum = add(kept, swap(after(given, kv_mine), "seq", seq_size, bit))
        bit *= 2
    out_mine = out_sum[0].reshape(fsdp_size, -1, width)
    got_three = after(got_three, kv_mine)
    kept_three, given = give(add(kept_three, got_three), 1)
    next_three = send(given, 1)
    grad_tokens, kept, given = joined_back(
        me, dq_one, dq_two, kv_kept[0], kv_got[0], cosine, sine, qkv_t, tokens, scale_one,
        gain_one, grad_residual, normed_one, norm_two_term, seq_size, fsdp_size,
    )

    next_one, next_two = after(next_one, grad_tokens), after(next_two, grad_tokens)
    down_sum = finish(kept_one, next_one, 1)

    tail_sum = add(kept, swap(given, "seq", seq_size, 1))
    bit = 2
    while bit < seq_size:
        kept, given = halve(tail_sum, 1, my_seq // bit)
        tail_sum = add(kept, swap(given, "seq", seq_size, bit))
        bit *= 2
    tail_mine = tail_sum[0]
    got_layer = swap(after(given_layer, kv_mine), "seq", seq_size, 2)
    layer_sum = add(kept_layer, got_layer)
    bit = 4
    while bit < seq_size:
        kept, given = halve(layer_sum, 1, my_seq // bit)
        layer_sum = add(kept, swap(given, "seq", seq_size, bit))
        bit *= 2
    layer_out = residual + layer_sum[0]
    one_sum = finish(kept_two, next_two, 1)
    two_sum = finish(kept_three, next_three, 1)

    ff_back = cut_lanes(me, (one_sum, two_sum, down_sum), seq_size)
    ff_got = [ff_back[0]] + [swap(ff_back[o], "seq", seq_size, o) for o in offsets if o]
    grad_gate_up, grad_down = join_ff(me, ff_got, strip)

    tail_sum = fsdp_scatter(
        after(jnp.concatenate([tail_mine, out_mine], axis=1), next_two),
        fsdp_size,
        my_fsdp,
        next_three,

    )
    lengths = [width * seq_size, QW + KVW, KVW, width * seq_size]
    pieces = [tail_sum[qkv_tall + i, : n // fsdp_size] for i, n in enumerate(lengths)]
    return (
        layer_out.astype(BF16),
        grad_tokens,
        pieces[0],
        tail_sum[:qkv_rows].T,
        pieces[1],
        pieces[2],
        tail_sum[qkv_tall + 16 :],
        pieces[3],
        grad_gate_up,
        grad_down,
    )


def solution(mesh):
    rows, both = P(("fsdp", "seq"), None), P(("fsdp", "seq"))
    return jax.shard_map(
        functools.partial(per_device, mesh.shape["seq"], mesh.shape["fsdp"]),
        mesh=mesh,
        in_specs=(
            rows, both, both, P("fsdp"), P("seq", "fsdp"), P("fsdp"), P("fsdp", "seq"),
            P("fsdp"), P("seq", "fsdp"), P("fsdp", "seq"), rows,
        ),
        out_specs=(
            rows, rows, P("fsdp"), P("seq", "fsdp"), P("fsdp"), P("fsdp"), P("fsdp", "seq"),
            P("fsdp"), P("seq", "fsdp"), P("fsdp", "seq"),
        ),
        check_vma=False,
    )
```

```python
import functools

import jax
import jax.numpy as jnp
from jax import lax
from jax.experimental import pallas as pl
from jax.experimental.pallas import tpu as pltpu
from jax.sharding import PartitionSpec as P

HEADS = 14
KV_HEADS = 2
HEAD = 64
FF = 4864
QW = 896
KVW = 128
PAIR = 2 * HEAD
PAIRS = HEADS // 2
OUTER = 4

EPSILON = 1e-06
ROPE_BASE = 1000000.0
MASKED = -1e30
VMEM_LIMIT = 50 * 1024 * 1024

F32 = jnp.float32
BF16 = jnp.bfloat16


def dot(left, right, left_dim, right_dim):
    return lax.dot_general(
        left, right, (((left_dim,), (right_dim,)), ((), ())), preferred_element_type=F32
    )


def swap(block, axis, size, bits):
    return lax.ppermute(block, axis, [(i, i ^ bits) for i in range(size)])


def after(array, *others):
    return lax.optimization_barrier((array,) + others)[0]


def seq_gather(block, size):
    blocks = {0: block}
    bit = size // 2
    while bit:
        blocks.update({o ^ bit: swap(b, "seq", size, bit) for o, b in blocks.items()})
        bit //= 2
    return blocks


def fsdp_bits(size):
    inner = size // OUTER
    outer_bits, inner_bits = [], []
    bit = 1
    while bit < size:
        (outer_bits if bit >= inner else inner_bits).append(bit)
        bit *= 2
    return outer_bits + inner_bits


def column_gather(block, size):
    inner = size // OUTER
    return jnp.stack([block] + [swap(block, "fsdp", size, k * inner) for k in range(1, OUTER)])


def ff_spread(block, size):
    blocks = {0: block}
    for bit in fsdp_bits(size)[2:]:
        blocks.update({o ^ bit: swap(b, "fsdp", size, bit) for o, b in blocks.items()})
    return blocks


def halve(stack, bit, me):
    above = stack.shape[0] // (2 * bit)
    cut = stack.reshape((above, 2, bit) + stack.shape[1:])
    digit = (me // bit) % 2
    kept = lax.dynamic_index_in_dim(cut, digit, 1, keepdims=False)
    given = lax.dynamic_index_in_dim(cut, 1 - digit, 1, keepdims=False)
    merge = lambda part: part.reshape((above * bit,) + stack.shape[1:])
    return merge(kept), merge(given).astype(BF16)


def add(kept, got):
    return kept.astype(F32) + got.astype(F32)


def seq_scatter(stack, size, me):
    bit = 1
    while bit < size:
        kept, given = halve(stack, 1, me // bit)
        stack = add(kept, swap(given, "seq", size, bit))
        bit *= 2
    return stack[0]


def fsdp_halve(stack, size, bit, me, resolved):
    place = bit
    digit = me // bit
    for taken in resolved:
        if taken < bit:
            place //= 2
    kept, given = halve(stack, place, digit * place)
    return kept, given


def fsdp_scatter(stack, size, me, earlier):
    inner = size // OUTER
    resolved = []
    for bit in reversed(fsdp_bits(size)[2:]):
        kept, given = fsdp_halve(stack, size, bit, me, resolved)
        stack = add(kept, swap(given, "fsdp", size, bit))
        resolved.append(bit)
    place = me // inner
    low = after(stack.astype(BF16), earlier)
    total = lax.dynamic_index_in_dim(stack, place, 0, keepdims=False)
    for k in range(1, OUTER):
        given = lax.dynamic_index_in_dim(low, place ^ k, 0, keepdims=False)
        total = add(total, swap(given, "fsdp", size, k * inner))
    return total


def on_device(body, name, out_shapes, scratch, me, arrays):
    vmem = pl.BlockSpec(memory_space=pltpu.VMEM)
    return pl.pallas_call(
        body,
        in_specs=[pl.BlockSpec(memory_space=pltpu.SMEM)] + [vmem] * len(arrays),
        out_specs=[vmem] * len(out_shapes),
        out_shape=out_shapes,
        scratch_shapes=scratch,
        compiler_params=pltpu.CompilerParams(vmem_limit_bytes=VMEM_LIMIT),
        name=name,
    )(me, *arrays)


def padded(rows):
    return -(-rows // 16) * 16


def cut_ff(me, gate_up_weight, down_weight, size):
    width = gate_up_weight.shape[0]
    half = down_weight.shape[0]
    strip = half // size
    tall = padded(strip)

    def body(me_ref, gu_ref, d_ref, *refs):
        outs, held = refs[:size], refs[size]
        turned = gu_ref[...].astype(F32).T
        down = d_ref[...].astype(F32)
        blank = jnp.zeros((tall - strip, width), F32)
        for q in range(size):
            one = turned[q * strip : (q + 1) * strip]
            two = turned[half + q * strip : half + (q + 1) * strip]
            three = down[q * strip : (q + 1) * strip]
            parts = [one, blank, two, blank, three, blank]
            held[q] = jnp.concatenate(parts, axis=0).astype(BF16)
        for o in range(size):
            outs[o][...] = held[me_ref[0] ^ o]

    shape = jax.ShapeDtypeStruct((3 * tall, width), BF16)
    scratch = [pltpu.VMEM((size, 3 * tall, width), BF16)]
    return on_device(body, "cut_ff", [shape] * size, scratch, me, (gate_up_weight, down_weight))


def join_lanes(me, blocks):
    size = len(blocks)
    rows, width = blocks[0].shape

    def body(me_ref, *refs):
        ins, out, held = refs[:size], refs[size], refs[size + 1]
        for o in range(size):
            held[me_ref[0] ^ o] = ins[o][...]
        out[...] = jnp.concatenate([held[q].astype(F32) for q in range(size)], 1).astype(BF16)

    return on_device(
        body,
        "join_lanes",
        [jax.ShapeDtypeStruct((rows, size * width), BF16)],
        [pltpu.VMEM((size, rows, width), BF16)],
        me,
        blocks,
    )[0]


def join_both(me, pieces, rows):
    size, parts_each = len(pieces), len(pieces[0])
    _, tall, width = pieces[0][0].shape
    count = sum(part.shape[0] for part in pieces[0])
    inner = count // OUTER
    order = [k * inner + m for m in range(inner) for k in range(OUTER)]
    shapes = [jax.ShapeDtypeStruct((count, rows, size * width), BF16)]
    if tall > rows:
        shapes.append(jax.ShapeDtypeStruct((count, tall - rows, width), BF16))

    def body(me_ref, *refs):
        ins, out, held = refs[: size * parts_each], refs[size * parts_each], refs[-1]
        for o in range(size):
            at = 0
            for part in ins[o * parts_each : (o + 1) * parts_each]:
                for j in range(part.shape[0]):
                    place = me_ref[1] ^ order[at]
                    held[me_ref[0] ^ o, place] = part[j]
                    if tall > rows and o == 0:
                        refs[size * parts_each + 1][place] = part[j, rows:]
                    at += 1
        for f in range(count):
            parts = [held[q, f, :rows].astype(F32) for q in range(size)]
            out[f] = jnp.concatenate(parts, axis=1).astype(BF16)

    return on_device(
        body,
        "join_both",
        shapes,
        [pltpu.VMEM((size, count, tall, width), BF16)],
        me,
        [block for row in pieces for block in row],
    )


def cut_lanes(me, sums, size):
    rows = sum(s.shape[0] for s in sums)
    width = sums[0].shape[1] // size

    def body(me_ref, *refs):
        ins, outs, held = refs[: len(sums)], refs[len(sums) : -1], refs[-1]
        whole = jnp.concatenate([r[...] for r in ins], axis=0)
        for q in range(size):
            held[q] = whole[:, q * width : (q + 1) * width].astype(BF16)
        for o in range(size):
            outs[o][...] = held[me_ref[0] ^ o]

    shape = jax.ShapeDtypeStruct((rows, width), BF16)
    scratch = [pltpu.VMEM((size, rows, width), BF16)]
    return on_device(body, "cut_lanes", [shape] * size, scratch, me, sums)


def join_ff(me, blocks, strip):
    size = len(blocks)
    rows, width = blocks[0].shape
    tall = rows // 3

    def body(me_ref, *refs):
        ins, gu, down, held = refs[:size], refs[size], refs[size + 1], refs[size + 2]
        for o in range(size):
            held[me_ref[0] ^ o] = ins[o][...].astype(F32)
        cut = [
            [held[q, i * tall : i * tall + strip] for q in range(size)] for i in range(3)
        ]
        gu[...] = jnp.concatenate(cut[0] + cut[1], axis=0).T
        down[...] = jnp.concatenate(cut[2], axis=0)

    return on_device(
        body,
        "join_ff",
        [
            jax.ShapeDtypeStruct((width, 2 * size * strip), F32),
            jax.ShapeDtypeStruct((size * strip, width), F32),
        ],
        [pltpu.VMEM((size, rows, width), F32)],
        me,
        blocks,
    )


def feed_forward(me, weight_blocks, row_blocks, cot_blocks):
    count, size = len(weight_blocks), len(row_blocks)
    whole_blocks = [not isinstance(b, tuple) for b in weight_blocks]
    flat = [part for b in weight_blocks for part in (b if isinstance(b, tuple) else (b,))]
    given = len(flat)
    rows, width = row_blocks[0].shape
    tall = flat[0].shape[0] // 3
    units = count * tall
    step_units = 256

    def body(me_ref, *refs):
        blocks = list(refs[:given])
        xs, gs = refs[given : given + size], refs[given + size : given + 2 * size]
        hid, gg, gu, gn, part, x_out, g_out = refs[given + 2 * size : given + 2 * size + 7]
        gu_w, d_w, x_all, g_all, sems = refs[given + 2 * size + 7 :]
        step = pl.program_id(0)
        core = me_ref[0] % 2
        handed = [
            pltpu.make_async_copy(src, dst, sems.at[2 * count + 2 * size + i])
            for i, (src, dst) in enumerate(((x_all, x_out), (g_all, g_out)))
        ]

        @pl.when(step == 0)
        def _():
            copies = []
            for o in range(count):
                f = me_ref[1] ^ o
                if whole_blocks[o]:
                    block = blocks.pop(0)
                    copies.append((block.at[pl.ds(0, 2 * tall)], gu_w.at[f]))
                    copies.append((block.at[pl.ds(2 * tall, tall)], d_w.at[f]))
                else:
                    copies.append((blocks.pop(0), gu_w.at[f]))
                    copies.append((blocks.pop(0), d_w.at[f]))
            for o in range(size):
                copies.append((xs[o], x_all.at[me_ref[0] ^ o]))
                copies.append((gs[o], g_all.at[me_ref[0] ^ o]))
            started = [
                pltpu.make_async_copy(src, dst, sems.at[i]) for i, (src, dst) in enumerate(copies)
            ]
            for copy in started:
                copy.start()
            for copy in started:
                copy.wait()
            for copy in handed:
                copy.start()

        x = x_all[step]
        g = g_all[step]
        gate_w = gu_w[: count // 2].reshape(units, width)
        up_w = gu_w[count // 2 :].reshape(units, width)
        down_w = d_w[...].reshape(units, width)
        for begin in range(0, units, step_units):
            at = slice(begin, begin + step_units)
            gate = dot(x, gate_w[at], 1, 1)
            up = dot(x, up_w[at], 1, 1)
            grad_hidden = dot(g, down_w[at], 1, 1)
            sigmoid = 0.5 * jnp.tanh(0.5 * gate) + 0.5
            silu = gate * sigmoid
            hid[:, at] = (silu * up).astype(BF16)
            gg[:, at] = (grad_hidden * up * (sigmoid + silu * (1.0 - sigmoid))).astype(BF16)
            gu[:, at] = (grad_hidden * silu).astype(BF16)

        place = jnp.where(step % 2 == core, 0, 1)
        gn[place, 0] = (dot(gg[...], gate_w, 1, 0) + dot(gu[...], up_w, 1, 0)).astype(BF16)
        part[place, 0] = dot(hid[...], down_w, 1, 0).astype(BF16)

        @pl.when(step == size - 1)
        def _():
            for copy in handed:
                copy.wait()

    hbm = pl.BlockSpec(memory_space=pl.ANY)
    by_rows = lambda n: pl.BlockSpec((rows, n), lambda i: (i, 0))
    by_pair = pl.BlockSpec((2, 1, rows, width), lambda i: (0, i // 2, 0, 0))
    like = jax.ShapeDtypeStruct
    return pl.pallas_call(
        body,
        grid=(size,),
        in_specs=[pl.BlockSpec(memory_space=pltpu.SMEM)]
        + [hbm] * (given + 2 * size),
        out_specs=[by_rows(units)] * 3 + [by_pair] * 2 + [hbm] * 2,
        out_shape=[like((size * rows, units), BF16)] * 3
        + [like((2, size // 2, rows, width), BF16)] * 2
        + [like((size, rows, width), BF16)] * 2,
        scratch_shapes=[
            pltpu.VMEM((count, 2 * tall, width), BF16),
            pltpu.VMEM((count, tall, width), BF16),
            pltpu.VMEM((size, rows, width), BF16),
            pltpu.VMEM((size, rows, width), BF16),
            pltpu.SemaphoreType.DMA((2 * count + 2 * size + 2,)),
        ],
        compiler_params=pltpu.CompilerParams(vmem_limit_bytes=VMEM_LIMIT),
        cost_estimate=pl.CostEstimate(flops=1, bytes_accessed=1, transcendentals=0),
        name="feed_forward",
    )(me, *flat, *row_blocks, *cot_blocks)


def both_heads(pair):
    lane = lax.broadcasted_iota(jnp.int32, pair.shape, 1)
    zero = jnp.zeros_like(pair)
    return jnp.concatenate(
        [jnp.where(lane < HEAD, pair, zero), jnp.where(lane < HEAD, zero, pair)], axis=0
    )


def fill_bias(low_ref, high_ref, place_ref, bias_ref):
    place = place_ref[...]
    allowed = (place >= low_ref[...]) & (place <= high_ref[...])
    bias = jnp.where(allowed, 0.0, MASKED).astype(F32)
    rows = bias.shape[1]
    bias_ref[:, :rows] = bias
    bias_ref[:, rows:] = bias


def own_rows(wide, rows):
    return jnp.concatenate([wide[:HEAD, :rows], wide[HEAD:, rows:]], axis=0)


def pairing(kv_ref, pair, begin):
    both = kv_ref[:, begin : begin + PAIR].astype(F32)
    crossed = pltpu.roll(both, HEAD, 1)
    lane = lax.broadcasted_iota(jnp.int32, both.shape, 1)
    first = jnp.where(pair <= PAIRS // 2, both, crossed)
    second = jnp.where(pair < PAIRS // 2, crossed, both)
    return jnp.where(lane < HEAD, first, second)


def new_pairing(step, pair):
    return (step == 0) | (pair == PAIRS // 2) | (pair == PAIRS // 2 + 1)


def attend_kernel(
    begin_pair, low_ref, high_ref, place_ref, q_ref, kv_ref,
    o_ref, lse_ref, bias_ref, k_ref, vt_ref,
):
    step = pl.program_id(0)
    pair = step + begin_pair

    @pl.when(step == 0)
    def _():
        fill_bias(low_ref, high_ref, place_ref, bias_ref)

    @pl.when(new_pairing(step, pair))
    def _():
        k_ref[...] = pairing(kv_ref, pair, 0).astype(BF16)
        vt_ref[...] = pairing(kv_ref, pair, PAIR).T.astype(BF16)

    rows = q_ref.shape[0]
    queries = both_heads(q_ref[...])
    keys = k_ref[...]
    values_t = vt_ref[...]
    outs, totals = [], []
    for begin in range(0, 2 * rows, 256):
        scores = dot(keys, queries[begin : begin + 256], 1, 1) + bias_ref[:, begin : begin + 256]
        top = jnp.max(scores, axis=0, keepdims=True)
        probs = jnp.exp(scores - top)
        total = jnp.sum(probs, axis=0, keepdims=True)
        outs.append(dot(values_t, probs.astype(BF16), 1, 0) / total)
        totals.append(top + jnp.log(total))
    wide = jnp.concatenate(outs, axis=1)
    o_ref[...] = own_rows(wide, rows).T.astype(BF16)
    lse_ref[0] = jnp.concatenate(totals, axis=1)


def attend_back_kernel(
    begin_pair, low_ref, high_ref, place_ref, q_ref, g_ref, o_ref, lse_ref, kv_ref, *refs,
):
    dq_ref, dkv_ref, bias_ref, k_ref, kt_ref, v_ref, dk_ref, dv_ref = refs[-8:]
    step = pl.program_id(0)
    pair = step + begin_pair

    @pl.when(step == 0)
    def _():
        fill_bias(low_ref, high_ref, place_ref, bias_ref)
        dkv_ref[...] = refs[0][...] if begin_pair else jnp.zeros_like(dkv_ref)

    @pl.when(new_pairing(step, pair))
    def _():
        keys_now = pairing(kv_ref, pair, 0)
        k_ref[...] = keys_now.astype(BF16)
        kt_ref[...] = keys_now.T.astype(BF16)
        v_ref[...] = pairing(kv_ref, pair, PAIR).astype(BF16)
        dk_ref[...] = jnp.zeros_like(dk_ref)
        dv_ref[...] = jnp.zeros_like(dv_ref)

    rows = q_ref.shape[0]
    queries = both_heads(q_ref[...])
    grads = both_heads(g_ref[...])
    keys = k_ref[...]
    keys_t = kt_ref[...]
    values = v_ref[...]
    product = (g_ref[...].astype(F32) * o_ref[...].astype(F32)).T
    delta = jnp.concatenate(
        [
            jnp.sum(product[:HEAD], axis=0, keepdims=True),
            jnp.sum(product[HEAD:], axis=0, keepdims=True),
        ],
        axis=1,
    )
    lse = lse_ref[0]
    outs = []
    for begin in range(0, 2 * rows, 256):
        part = slice(begin, begin + 256)
        scores = dot(keys, queries[part], 1, 1) + bias_ref[:, part]
        probs = jnp.exp(scores - lse[:, part])
        grad_probs = dot(values, grads[part], 1, 1)
        grad_scores = (probs * (grad_probs - delta[:, part])).astype(BF16)
        outs.append(dot(keys_t, grad_scores, 1, 0))
        dk_ref[...] += dot(grad_scores, queries[part], 1, 0)
        dv_ref[...] += dot(probs.astype(BF16), grads[part], 1, 0)
    wide = jnp.concatenate(outs, axis=1)
    dq_ref[...] = own_rows(wide, rows).T * 0.125

    def fold(own_lanes):
        for at, sums in ((0, dk_ref), (PAIR, dv_ref)):
            sums_now = sums[...]
            lane = lax.broadcasted_iota(jnp.int32, sums_now.shape, 1)
            both = sums_now + pltpu.roll(sums_now, HEAD, 1)
            kept = jnp.where((lane < HEAD) == own_lanes, both, 0.0)
            dkv_ref[:, at : at + PAIR] += kept

    @pl.when(pair == PAIRS // 2 - 1)
    def _():
        fold(True)

    @pl.when(pair == PAIRS // 2)
    def _():
        dkv_ref[:, :PAIR] += dk_ref[...]
        dkv_ref[:, PAIR:] += dv_ref[...]

    @pl.when(pair == PAIRS - 1)
    def _():
        fold(False)


def whole(shape):
    return pl.BlockSpec(shape, lambda i: (0,) * len(shape))


def attend(low, high, place, queries, kv_all, begin, pairs):
    rows, count = queries.shape[0], place.shape[0]
    taken = pl.BlockSpec((rows, PAIR), lambda i: (0, i + begin))
    made = pl.BlockSpec((rows, PAIR), lambda i: (0, i))
    return pl.pallas_call(
        functools.partial(attend_kernel, begin),
        grid=(pairs,),
        in_specs=[whole((1, rows)), whole((1, rows)), whole((count, 1)), taken]
        + [whole((count, 2 * KVW))],
        out_specs=[made, pl.BlockSpec((1, 1, 2 * rows), lambda i: (i, 0, 0))],
        out_shape=[
            jax.ShapeDtypeStruct((rows, pairs * PAIR), BF16),
            jax.ShapeDtypeStruct((pairs, 1, 2 * rows), F32),
        ],
        scratch_shapes=[
            pltpu.VMEM((count, 2 * rows), F32),
            pltpu.VMEM((count, PAIR), BF16),
            pltpu.VMEM((PAIR, count), BF16),
        ],
        compiler_params=pltpu.CompilerParams(vmem_limit_bytes=VMEM_LIMIT),
        cost_estimate=pl.CostEstimate(flops=1, bytes_accessed=1, transcendentals=0),
        name="attend",
    )(low, high, place, queries, kv_all)


def attend_back(low, high, place, queries, grads, outs, lse, kv_all, begin, pairs, so_far):
    rows, count = queries.shape[0], place.shape[0]
    taken = pl.BlockSpec((rows, PAIR), lambda i: (0, i + begin))
    made = pl.BlockSpec((rows, PAIR), lambda i: (0, i))
    sums = whole((count, 2 * KVW))
    return pl.pallas_call(
        functools.partial(attend_back_kernel, begin),
        grid=(pairs,),
        in_specs=[whole((1, rows)), whole((1, rows)), whole((count, 1)), taken, taken, made]
        + [pl.BlockSpec((1, 1, 2 * rows), lambda i: (i, 0, 0)), sums]
        + [sums] * len(so_far),
        out_specs=[made, sums],
        out_shape=[
            jax.ShapeDtypeStruct((rows, pairs * PAIR), F32),
            jax.ShapeDtypeStruct((count, 2 * KVW), F32),
        ],
        scratch_shapes=[
            pltpu.VMEM((count, 2 * rows), F32),
            pltpu.VMEM((count, PAIR), BF16),
            pltpu.VMEM((PAIR, count), BF16),
            pltpu.VMEM((count, PAIR), BF16),
            pltpu.VMEM((count, PAIR), F32),
            pltpu.VMEM((count, PAIR), F32),
        ],
        compiler_params=pltpu.CompilerParams(vmem_limit_bytes=VMEM_LIMIT),
        cost_estimate=pl.CostEstimate(flops=1, bytes_accessed=1, transcendentals=0),
        name="attend_back",
    )(low, high, place, queries, grads, outs, lse, kv_all, *so_far)


def rms_scale(values_in):
    return lax.rsqrt(jnp.mean(values_in * values_in, axis=-1, keepdims=True) + EPSILON)


def angle_tables(places):
    exponent = jnp.arange(HEAD // 2, dtype=F32) * 2.0 / HEAD
    frequency = ROPE_BASE ** (-exponent)
    turn = places.astype(F32)[:, None] * frequency[None, :]
    cosine, sine = lax.optimization_barrier((jnp.cos(turn), jnp.sin(turn)))
    return jnp.concatenate([cosine] * 4, axis=1), jnp.concatenate([sine] * 4, axis=1)


def widen(table, width):
    return jnp.concatenate([table] * (width // PAIR), axis=1)


def first_halves(shape):
    return lax.broadcasted_iota(jnp.int32, shape, 1) % HEAD < HEAD // 2


def rotate(tensor, cosine, sine):
    half = HEAD // 2
    ahead, behind = jnp.roll(tensor, -half, axis=1), jnp.roll(tensor, half, axis=1)
    turned = jnp.where(first_halves(tensor.shape), -ahead, behind)
    width = tensor.shape[1]
    return tensor * widen(cosine, width) + turned * widen(sine, width)


def norm_back_rows(grad_in, row_data, scale_in, gain_in):
    gain_term = jnp.sum(grad_in * row_data * scale_in, axis=0, keepdims=True)
    grad_normed = grad_in * gain_in
    inner_mean = jnp.mean(grad_normed * row_data, axis=-1, keepdims=True)
    return (
        scale_in * grad_normed - row_data * scale_in * scale_in * scale_in * inner_mean,
        gain_term,
    )


def residual_back(me, kept, got, residual, scale_two, gain_two, cotangent, out_full):
    rows, width = residual.shape

    def body(me_ref, kept_ref, got_ref, res_ref, scale_ref, gain_ref, cot_ref, out_ref,
             grad_ref, branch_ref, attn_ref, term_ref):
        grad = kept_ref[...] + got_ref[...].astype(F32)
        path, term_ref[...] = norm_back_rows(grad, res_ref[...], scale_ref[...], gain_ref[...])
        full = cot_ref[...].astype(F32) + path
        grad_ref[...] = full
        branch_ref[...] = full.astype(BF16)
        attn_ref[...] = dot(full.astype(BF16), out_ref[...], 1, 1).astype(BF16)

    shapes = [
        jax.ShapeDtypeStruct((rows, width), F32),
        jax.ShapeDtypeStruct((rows, width), BF16),
        jax.ShapeDtypeStruct((rows, QW), BF16),
        jax.ShapeDtypeStruct((1, width), F32),
    ]
    arrays = (kept, got, residual, scale_two, gain_two[None, :], cotangent, out_full)
    return on_device(body, "residual_back", shapes, [], me, arrays)


def joined_back(
    me, dq_one, dq_two, kept, got, cosine, sine, qkv_t, tokens, scale_one, gain_one,
    grad_residual, normed_one, norm_two_term, seq_size, fsdp_size,
):
    rows, width = tokens.shape
    total = qkv_t.shape[0]
    each, lanes = total // fsdp_size, width // seq_size
    tall = padded(each)

    def body(me_ref, dq1_ref, dq2_ref, kept_ref, got_ref, cos_ref, sin_ref, w_ref, x_ref,
             scale_ref, gain_ref, res_ref, n1_ref, term_ref,
             tokens_ref, mine_ref, other_ref, held):
        kv = kept_ref[...] + got_ref[...].astype(F32)
        turned = jnp.concatenate([dq1_ref[...], dq2_ref[...], kv[:, :KVW]], axis=1)
        across = turned.shape[1]
        scaled = turned * widen(sin_ref[...], across)
        ahead = pltpu.roll(scaled, across - HEAD // 2, 1)
        behind = pltpu.roll(scaled, HEAD // 2, 1)
        turned = turned * widen(cos_ref[...], across) + jnp.where(
            first_halves(turned.shape), ahead, -behind
        )
        joined = jnp.concatenate([turned, kv[:, KVW:]], axis=1).astype(BF16)
        wide = joined.astype(F32)
        grad_normed = dot(joined, w_ref[...], 1, 0)
        path, one_term = norm_back_rows(
            grad_normed, x_ref[...].astype(F32), scale_ref[...], gain_ref[...]
        )
        tokens_ref[...] = res_ref[...] + path
        bias = jnp.sum(wide, axis=0, keepdims=True)
        weight = dot(wide.T.astype(BF16), n1_ref[...], 1, 0)
        vectors = [one_term, bias[:, : QW + KVW], bias[:, QW + KVW :], term_ref[...]]
        for f in range(fsdp_size):
            lines = []
            for vector in vectors:
                n = vector.shape[1] // fsdp_size
                piece = vector[:, f * n : (f + 1) * n]
                lines.append(jnp.concatenate([piece, jnp.zeros((1, lanes - n), F32)], axis=1))
            blank = jnp.zeros((tall - each, lanes), F32)
            below = [blank] * (tall > each) + lines + [jnp.zeros((12, lanes), F32)]
            for s in range(seq_size):
                part = weight[f * each : (f + 1) * each, s * lanes : (s + 1) * lanes]
                held[s, f] = jnp.concatenate([part] + below, axis=0).astype(BF16)
        core = me_ref[0] % 2
        for y in range(seq_size // 2):
            mine_ref[y] = held[2 * y + core]
            other_ref[y] = held[2 * y + 1 - core]

    block = (fsdp_size, tall + 16, lanes)
    half = jax.ShapeDtypeStruct((seq_size // 2,) + block, BF16)
    shapes = [jax.ShapeDtypeStruct((rows, width), F32), half, half]
    arrays = (
        dq_one, dq_two, kept, got, cosine, sine, qkv_t, tokens, scale_one, gain_one[None, :],
        grad_residual, normed_one, norm_two_term,
    )
    scratch = [pltpu.VMEM((seq_size,) + block, BF16)]
    return on_device(body, "joined_back", shapes, scratch, me, arrays)


def pad_row(vector, width):
    return jnp.pad(vector, (0, width - vector.shape[0]))[None, :]


def stack_from_lanes(array, count):
    rows, width = array.shape
    return jnp.transpose(array.reshape(rows, count, width // count), (1, 0, 2))


def per_device(
    seq_size, fsdp_size, tokens, segment_ids, positions, norm_one, qkv_weight, qkv_bias,
    out_weight, norm_two, gate_up_weight, down_weight, cotangent,
):
    my_seq, my_fsdp = lax.axis_index("seq"), lax.axis_index("fsdp")
    me = jnp.stack([my_seq, my_fsdp]).astype(jnp.int32)
    offsets = range(seq_size)
    row_count = tokens.shape[0]
    width = qkv_weight.shape[0]
    qkv_rows = qkv_weight.shape[1]
    strip = down_weight.shape[0] // seq_size
    tall = padded(strip)

    ff_cut = cut_ff(me, gate_up_weight, down_weight, seq_size)
    ff_share = [ff_cut[0]] + [swap(ff_cut[o], "seq", seq_size, o) for o in offsets if o]
    qkv_tall = padded(qkv_rows)
    packed = jnp.concatenate(
        [
            jnp.pad(qkv_weight.T, ((0, qkv_tall - qkv_rows), (0, 0))),
            pad_row(norm_one, width),
            pad_row(qkv_bias, width),
            pad_row(norm_two, width),
            jnp.zeros((13, width), BF16),
            out_weight,
        ],
        axis=0,
    )
    packed = after(packed, ff_cut[0])
    ff_block = join_lanes(me, ff_share)
    columns = ff_spread(
        after(column_gather(packed, fsdp_size), ff_block), fsdp_size
    )
    wide = qkv_tall + 16
    columns[0] = after(columns[0], ff_block)
    packed_pieces = [seq_gather(columns[m][:, :wide], seq_size) for m in sorted(columns)]
    ff_blocks = {0: ff_block}
    inner = fsdp_size // OUTER
    near = swap(ff_block, "fsdp", fsdp_size, inner)
    far = swap(ff_block, "fsdp", fsdp_size, 2 * inner)

    qkv_pieces = [[piece[o] for piece in packed_pieces] for o in offsets]
    qkv_t, vectors = join_both(me, qkv_pieces, qkv_tall)
    out_stack = jnp.concatenate([columns[m][:, wide:] for m in sorted(columns)], axis=0)
    out_stack = after(out_stack, packed_pieces[-1][seq_size // 2])
    out_blocks = seq_gather(out_stack, seq_size)

    own_x = ff_spread(ff_block, fsdp_size)
    last = swap(after(near, qkv_t), "fsdp", fsdp_size, 2 * inner)
    qkv_t = after(qkv_t, far, near, *own_x.values())[:, :qkv_rows].reshape(fsdp_size * qkv_rows, -1)
    gain_one = vectors[:, 0, : norm_one.shape[0]].reshape(-1).astype(F32)
    bias_full = vectors[:, 1, : qkv_bias.shape[0]].reshape(-1).astype(F32)
    gain_two = vectors[:, 2, : norm_two.shape[0]].reshape(-1).astype(F32)

    inputs = tokens.astype(F32)
    scale_one = rms_scale(inputs)
    normed_one = (inputs * scale_one * gain_one).astype(BF16)
    joined = dot(normed_one, qkv_t, 1, 1) + bias_full
    cosine, sine = angle_tables(positions)
    turned = rotate(joined[:, : QW + KVW], cosine, sine).astype(BF16)
    queries = turned[:, :QW] * jnp.asarray(0.125, BF16)
    kv_local = jnp.concatenate([turned[:, QW:], joined[:, QW + KVW :].astype(BF16)], axis=1)
    kv_all = lax.all_gather(kv_local, "seq", axis=0, tiled=True)
    cot_blocks = seq_gather(after(cotangent, kv_all), seq_size)
    row_place = jnp.arange(row_count, dtype=jnp.int32)
    high = my_seq * row_count + row_place
    low = high - positions
    place = jnp.arange(seq_size * row_count, dtype=jnp.int32)[:, None]
    low, high = low[None, :], high[None, :]
    split = PAIRS // 2 + 1
    spread = lambda block: ff_spread(block, fsdp_size)
    near_x = spread(after(near, kv_all))
    attn_one, lse_one = attend(
        low, high, place, after(queries, far), kv_all, 0, split
    )
    far_x = spread(after(far, kv_all))
    queries_two = after(queries, attn_one, cot_blocks[seq_size // 2], *near_x.values())
    attn_two, lse_two = attend(low, high, place, queries_two, kv_all, split, PAIRS - split)
    last_x = spread(last)
    for base, row in ((0, own_x), (inner, near_x), (2 * inner, far_x), (3 * inner, last_x)):
        ff_blocks.update({base + m: block for m, block in row.items()})
    attn_flat = jnp.concatenate([attn_one, attn_two], axis=1)

    out_list = [[out_blocks[o]] for o in offsets]
    out_list[0][0] = after(out_list[0][0], attn_one)
    out_full = join_both(me, out_list, out_weight.shape[0])[0].reshape(QW, -1)

    residual = inputs + dot(attn_flat, out_full, 1, 0)
    scale_two = rms_scale(residual)
    normed_two = (residual * scale_two * gain_two).astype(BF16)
    normed_blocks = {0: normed_two}
    bit = seq_size // 2
    while bit:
        if bit == 1:
            top = seq_size // 2
            normed_blocks[top] = after(normed_blocks[top], last, *far_x.values())
        normed_blocks.update(
            {o ^ bit: swap(b, "seq", seq_size, bit) for o, b in normed_blocks.items()}
        )
        bit //= 2
    hidden, grad_gate, grad_up, grad_normed, layer_part, normed_all, cot_all = feed_forward(
        me,
        [ff_blocks[o] for o in range(fsdp_size)],
        [normed_blocks[o] for o in offsets],
        [cot_blocks[o] for o in offsets],
    )
    kept, given = grad_normed[0], grad_normed[1]
    kept_layer, given_layer = layer_part[0], layer_part[1]
    normed_all = normed_all.reshape(seq_size * row_count, -1)
    cot_all = cot_all.reshape(seq_size * row_count, -1)
    by_seq = lambda rows: rows.reshape(seq_size, row_count, -1)

    normed_sum = add(kept, swap(given, "seq", seq_size, 1))
    bit = 2
    while bit < seq_size:
        kept, given = halve(normed_sum, 1, my_seq // bit)
        got = swap(given, "seq", seq_size, bit)
        normed_sum = add(kept, got)
        bit *= 2
    normed_kept, normed_got = kept[0], got[0]
    hidden = after(hidden, given)
    down_term = dot(hidden, cot_all, 0, 0).astype(BF16).reshape(fsdp_size, tall, -1)
    grad_gate, grad_up = after(grad_gate, down_term), after(grad_up, down_term)
    gate_term = dot(grad_gate, normed_all, 0, 0).astype(BF16).reshape(fsdp_size // 2, 2, tall, -1)
    up_term = dot(grad_up, normed_all, 0, 0).astype(BF16).reshape(fsdp_size // 2, 2, tall, -1)

    bits = list(reversed(fsdp_bits(fsdp_size)))

    def give(stack, at):
        kept, given = fsdp_halve(stack, fsdp_size, bits[at], my_fsdp, bits[:at])
        return kept, given

    def send(given, at):
        return swap(given, "fsdp", fsdp_size, bits[at])

    def finish(kept, got, at):
        stack = add(kept, got)
        for later in range(at + 1, len(bits)):
            kept, given = give(stack, later)
            stack = add(kept, send(given, later))
        return stack[0]

    def finish_pair(stacks, at):
        for later in range(at, len(bits)):
            halves = [give(stack, later) for stack in stacks]
            got = send(jnp.concatenate([given for _, given in halves], axis=0), later)
            n = halves[0][1].shape[0]
            stacks = [add(halves[0][0], got[:n]), add(halves[1][0], got[n:])]
        return stacks[0][0], stacks[1][0]

    kept_one, given = give(down_term, 0)
    got_one = send(given, 0)
    kept_two, given = give(jnp.concatenate([gate_term[:, 0], up_term[:, 0]], axis=0), 0)
    got_two = send(after(given, normed_got), 0)
    kept_three, given_three = give(jnp.concatenate([gate_term[:, 1], up_term[:, 1]], axis=0), 0)

    grad_residual, grad_branch, grad_attn, norm_two_term = residual_back(
        me, normed_kept, normed_got, residual, scale_two, gain_two, cotangent, out_full
    )
    kept_one, given_one = give(add(kept_one, got_one), 1)
    next_one = send(given_one, 1)
    grad_attn = after(grad_attn, gate_term, up_term, given_one)
    dq_one, kv_terms = attend_back(
        low, high, place, queries, grad_attn, attn_one, lse_one, kv_all, 0, split, ()
    )
    got_three = send(after(given_three, dq_one), 0)
    queries_two = after(queries, kv_terms)
    dq_two, kv_terms = attend_back(
        low, high, place, queries_two, grad_attn, attn_two, lse_two, kv_all, split,
        PAIRS - split, (kv_terms,),
    )
    got_two = after(got_two, dq_two)
    kept_two, given = give(add(kept_two, got_two), 1)
    next_two = send(given, 1)
    kept, given = halve(after(by_seq(kv_terms), next_one), 1, my_seq)
    kv_sum = add(kept, swap(given, "seq", seq_size, 1))
    bit = 2
    while bit < seq_size:
        kv_kept, given_kv = halve(kv_sum, 1, my_seq // bit)
        kv_got = swap(given_kv, "seq", seq_size, bit)
        kv_sum = add(kv_kept, kv_got)
        bit *= 2
    kv_mine = kv_got

    attn_late = after(attn_flat, given_kv)
    out_term = stack_from_lanes(dot(attn_late, grad_branch, 0, 0).astype(BF16), seq_size)
    kept, given = halve(out_term, 1, my_seq)
    out_got = swap(given, "seq", seq_size, 1)
    out_sum = add(kept, out_got)
    layer_got = swap(after(given_layer, given_kv), "seq", seq_size, 1)
    layer_sum = add(kept_layer, layer_got)
    kept_layer, given_layer = halve(layer_sum, 1, my_seq // 2)
    grad_tokens, kept, given = joined_back(
        me, dq_one, dq_two, kv_kept[0], after(kv_got[0], layer_got), cosine, sine, qkv_t, tokens, scale_one,
        gain_one, grad_residual, normed_one, norm_two_term, seq_size, fsdp_size,
    )

    got_three = after(got_three, grad_tokens)
    kept_three, given_last = give(add(kept_three, got_three), 1)
    next_three = send(given_last, 1)
    next_one, next_two = after(next_one, grad_tokens), after(next_two, grad_tokens)
    both = [add(kept_one, next_one), add(kept_two, next_two)]
    down_sum, one_sum = finish_pair(both, 2)

    bit = 2
    while bit < seq_size:
        kept_out, given_out = halve(out_sum, 1, my_seq // bit)
        out_sum = add(kept_out, swap(after(given_out, grad_tokens), "seq", seq_size, bit))
        bit *= 2
    out_mine = out_sum[0].reshape(fsdp_size, -1, width)
    tail_sum = add(kept, swap(given, "seq", seq_size, 1))
    bit = 2
    while bit < seq_size:
        kept, given = halve(tail_sum, 1, my_seq // bit)
        tail_sum = add(kept, swap(given, "seq", seq_size, bit))
        bit *= 2
    tail_mine = tail_sum[0]
    got_layer = swap(after(given_layer, kv_mine), "seq", seq_size, 2)
    layer_sum = add(kept_layer, got_layer)
    bit = 4
    while bit < seq_size:
        kept, given = halve(layer_sum, 1, my_seq // bit)
        layer_sum = add(kept, swap(given, "seq", seq_size, bit))
        bit *= 2
    layer_out = residual + layer_sum[0]
    two_sum = finish(kept_three, next_three, 1)

    ff_back = cut_lanes(me, (one_sum, two_sum, down_sum), seq_size)
    ff_got = [ff_back[0]] + [swap(ff_back[o], "seq", seq_size, o) for o in offsets if o]
    grad_gate_up, grad_down = join_ff(me, ff_got, strip)

    tail_sum = fsdp_scatter(
        after(jnp.concatenate([tail_mine, out_mine], axis=1), next_two),
        fsdp_size,
        my_fsdp,
        next_three,

    )
    lengths = [width * seq_size, QW + KVW, KVW, width * seq_size]
    pieces = [tail_sum[qkv_tall + i, : n // fsdp_size] for i, n in enumerate(lengths)]
    return (
        layer_out.astype(BF16),
        grad_tokens,
        pieces[0],
        tail_sum[:qkv_rows].T,
        pieces[1],
        pieces[2],
        tail_sum[qkv_tall + 16 :],
        pieces[3],
        grad_gate_up,
        grad_down,
    )


def solution(mesh):
    rows, both = P(("fsdp", "seq"), None), P(("fsdp", "seq"))
    return jax.shard_map(
        functools.partial(per_device, mesh.shape["seq"], mesh.shape["fsdp"]),
        mesh=mesh,
        in_specs=(
            rows, both, both, P("fsdp"), P("seq", "fsdp"), P("fsdp"), P("fsdp", "seq"),
            P("fsdp"), P("seq", "fsdp"), P("fsdp", "seq"), rows,
        ),
        out_specs=(
            rows, rows, P("fsdp"), P("seq", "fsdp"), P("fsdp"), P("fsdp"), P("fsdp", "seq"),
            P("fsdp"), P("seq", "fsdp"), P("fsdp", "seq"),
        ),
        check_vma=False,
    )
```

```python
import functools

import jax
import jax.numpy as jnp
from jax import lax
from jax.experimental import pallas as pl
from jax.experimental.pallas import tpu as pltpu
from jax.sharding import PartitionSpec as P

HEADS = 14
KV_HEADS = 2
HEAD = 64
FF = 4864
QW = 896
KVW = 128
PAIR = 2 * HEAD
PAIRS = HEADS // 2
OUTER = 4

EPSILON = 1e-06
ROPE_BASE = 1000000.0
MASKED = -1e30
VMEM_LIMIT = 50 * 1024 * 1024

F32 = jnp.float32
BF16 = jnp.bfloat16


def dot(left, right, left_dim, right_dim):
    return lax.dot_general(
        left, right, (((left_dim,), (right_dim,)), ((), ())), preferred_element_type=F32
    )


def swap(block, axis, size, bits):
    return lax.ppermute(block, axis, [(i, i ^ bits) for i in range(size)])


def after(array, *others):
    return lax.optimization_barrier((array,) + others)[0]


def seq_gather(block, size):
    blocks = {0: block}
    bit = size // 2
    while bit:
        blocks.update({o ^ bit: swap(b, "seq", size, bit) for o, b in blocks.items()})
        bit //= 2
    return blocks


def fsdp_bits(size):
    inner = size // OUTER
    outer_bits, inner_bits = [], []
    bit = 1
    while bit < size:
        (outer_bits if bit >= inner else inner_bits).append(bit)
        bit *= 2
    return outer_bits[::-1] + inner_bits


def column_gather(block, size):
    inner = size // OUTER
    return jnp.stack([block] + [swap(block, "fsdp", size, k * inner) for k in range(1, OUTER)])


def ff_spread(block, size):
    blocks = {0: block}
    for bit in fsdp_bits(size)[2:]:
        blocks.update({o ^ bit: swap(b, "fsdp", size, bit) for o, b in blocks.items()})
    return blocks


def halve(stack, bit, me):
    above = stack.shape[0] // (2 * bit)
    cut = stack.reshape((above, 2, bit) + stack.shape[1:])
    digit = (me // bit) % 2
    kept = lax.dynamic_index_in_dim(cut, digit, 1, keepdims=False)
    given = lax.dynamic_index_in_dim(cut, 1 - digit, 1, keepdims=False)
    merge = lambda part: part.reshape((above * bit,) + stack.shape[1:])
    return merge(kept), merge(given).astype(BF16)


def add(kept, got):
    return kept.astype(F32) + got.astype(F32)


def seq_scatter(stack, size, me):
    bit = 1
    while bit < size:
        kept, given = halve(stack, 1, me // bit)
        stack = add(kept, swap(given, "seq", size, bit))
        bit *= 2
    return stack[0]


def fsdp_halve(stack, size, bit, me, resolved):
    place = bit
    digit = me // bit
    for taken in resolved:
        if taken < bit:
            place //= 2
    kept, given = halve(stack, place, digit * place)
    return kept, given


def fsdp_scatter(stack, size, me, earlier):
    inner = size // OUTER
    resolved = []
    for bit in reversed(fsdp_bits(size)[2:]):
        kept, given = fsdp_halve(stack, size, bit, me, resolved)
        stack = add(kept, swap(given, "fsdp", size, bit))
        resolved.append(bit)
    place = me // inner
    low = after(stack.astype(BF16), earlier)
    total = lax.dynamic_index_in_dim(stack, place, 0, keepdims=False)
    for k in range(1, OUTER):
        given = lax.dynamic_index_in_dim(low, place ^ k, 0, keepdims=False)
        total = add(total, swap(given, "fsdp", size, k * inner))
    return total


def on_device(body, name, out_shapes, scratch, me, arrays):
    vmem = pl.BlockSpec(memory_space=pltpu.VMEM)
    return pl.pallas_call(
        body,
        in_specs=[pl.BlockSpec(memory_space=pltpu.SMEM)] + [vmem] * len(arrays),
        out_specs=[vmem] * len(out_shapes),
        out_shape=out_shapes,
        scratch_shapes=scratch,
        compiler_params=pltpu.CompilerParams(vmem_limit_bytes=VMEM_LIMIT),
        name=name,
    )(me, *arrays)


def padded(rows):
    return -(-rows // 16) * 16


def cut_ff(me, gate_up_weight, down_weight, size):
    width = gate_up_weight.shape[0]
    half = down_weight.shape[0]
    strip = half // size
    tall = padded(strip)

    def body(me_ref, gu_ref, d_ref, *refs):
        outs, held = refs[:size], refs[size]
        turned = gu_ref[...].astype(F32).T
        down = d_ref[...].astype(F32)
        blank = jnp.zeros((tall - strip, width), F32)
        for q in range(size):
            one = turned[q * strip : (q + 1) * strip]
            two = turned[half + q * strip : half + (q + 1) * strip]
            three = down[q * strip : (q + 1) * strip]
            parts = [one, blank, two, blank, three, blank]
            held[q] = jnp.concatenate(parts, axis=0).astype(BF16)
        for o in range(size):
            outs[o][...] = held[me_ref[0] ^ o]

    shape = jax.ShapeDtypeStruct((3 * tall, width), BF16)
    scratch = [pltpu.VMEM((size, 3 * tall, width), BF16)]
    return on_device(body, "cut_ff", [shape] * size, scratch, me, (gate_up_weight, down_weight))


def join_lanes(me, blocks):
    size = len(blocks)
    rows, width = blocks[0].shape

    def body(me_ref, *refs):
        ins, out, held = refs[:size], refs[size], refs[size + 1]
        for o in range(size):
            held[me_ref[0] ^ o] = ins[o][...]
        out[...] = jnp.concatenate([held[q].astype(F32) for q in range(size)], 1).astype(BF16)

    return on_device(
        body,
        "join_lanes",
        [jax.ShapeDtypeStruct((rows, size * width), BF16)],
        [pltpu.VMEM((size, rows, width), BF16)],
        me,
        blocks,
    )[0]


def join_both(me, pieces, rows):
    size, parts_each = len(pieces), len(pieces[0])
    _, tall, width = pieces[0][0].shape
    count = sum(part.shape[0] for part in pieces[0])
    inner = count // OUTER
    order = [k * inner + m for m in range(inner) for k in range(OUTER)]
    shapes = [jax.ShapeDtypeStruct((count, rows, size * width), BF16)]
    if tall > rows:
        shapes.append(jax.ShapeDtypeStruct((count, tall - rows, width), BF16))

    def body(me_ref, *refs):
        ins, out, held = refs[: size * parts_each], refs[size * parts_each], refs[-1]
        for o in range(size):
            at = 0
            for part in ins[o * parts_each : (o + 1) * parts_each]:
                for j in range(part.shape[0]):
                    place = me_ref[1] ^ order[at]
                    held[me_ref[0] ^ o, place] = part[j]
                    if tall > rows and o == 0:
                        refs[size * parts_each + 1][place] = part[j, rows:]
                    at += 1
        for f in range(count):
            parts = [held[q, f, :rows].astype(F32) for q in range(size)]
            out[f] = jnp.concatenate(parts, axis=1).astype(BF16)

    return on_device(
        body,
        "join_both",
        shapes,
        [pltpu.VMEM((size, count, tall, width), BF16)],
        me,
        [block for row in pieces for block in row],
    )


def cut_lanes(me, sums, size):
    rows = sum(s.shape[0] for s in sums)
    width = sums[0].shape[1] // size

    def body(me_ref, *refs):
        ins, outs, held = refs[: len(sums)], refs[len(sums) : -1], refs[-1]
        whole = jnp.concatenate([r[...] for r in ins], axis=0)
        for q in range(size):
            held[q] = whole[:, q * width : (q + 1) * width].astype(BF16)
        for o in range(size):
            outs[o][...] = held[me_ref[0] ^ o]

    shape = jax.ShapeDtypeStruct((rows, width), BF16)
    scratch = [pltpu.VMEM((size, rows, width), BF16)]
    return on_device(body, "cut_lanes", [shape] * size, scratch, me, sums)


def join_ff(me, blocks, strip):
    size = len(blocks)
    rows, width = blocks[0].shape
    tall = rows // 3

    def body(me_ref, *refs):
        ins, gu, down, held = refs[:size], refs[size], refs[size + 1], refs[size + 2]
        for o in range(size):
            held[me_ref[0] ^ o] = ins[o][...].astype(F32)
        cut = [
            [held[q, i * tall : i * tall + strip] for q in range(size)] for i in range(3)
        ]
        gu[...] = jnp.concatenate(cut[0] + cut[1], axis=0).T
        down[...] = jnp.concatenate(cut[2], axis=0)

    return on_device(
        body,
        "join_ff",
        [
            jax.ShapeDtypeStruct((width, 2 * size * strip), F32),
            jax.ShapeDtypeStruct((size * strip, width), F32),
        ],
        [pltpu.VMEM((size, rows, width), F32)],
        me,
        blocks,
    )


def feed_forward(me, weight_blocks, row_blocks, cot_blocks):
    count, size = len(weight_blocks), len(row_blocks)
    rows, width = row_blocks[0].shape
    tall = weight_blocks[0].shape[0] // 3
    units = count * tall
    step_units = 256

    def body(me_ref, *refs):
        blocks = refs[:count]
        xs, gs = refs[count : count + size], refs[count + size : count + 2 * size]
        outs = refs[count + 2 * size : count + 2 * size + 9]
        hid, gg, gu, gn_kept, gn_given, part_kept, part_given, x_out, g_out = outs
        gu_w, d_w, x_all, g_all, held, sems = refs[count + 2 * size + 9 :]
        step = pl.program_id(0)
        core = me_ref[0] % 2
        handed = [
            pltpu.make_async_copy(src, dst, sems.at[2 * count + 2 * size + i])
            for i, (src, dst) in enumerate(((x_all, x_out), (g_all, g_out)))
        ]

        @pl.when(step == 0)
        def _():
            copies = []
            for o in range(count):
                f = me_ref[1] ^ o
                copies.append((blocks[o].at[pl.ds(0, 2 * tall)], gu_w.at[f]))
                copies.append((blocks[o].at[pl.ds(2 * tall, tall)], d_w.at[f]))
            for o in range(size):
                copies.append((xs[o], x_all.at[me_ref[0] ^ o]))
                copies.append((gs[o], g_all.at[me_ref[0] ^ o]))
            started = [
                pltpu.make_async_copy(src, dst, sems.at[i]) for i, (src, dst) in enumerate(copies)
            ]
            for copy in started:
                copy.start()
            for copy in started:
                copy.wait()
            for copy in handed:
                copy.start()

        x = x_all[pl.ds(2 * step, 2)].reshape(2 * rows, width)
        g = g_all[pl.ds(2 * step, 2)].reshape(2 * rows, width)
        gate_w = gu_w[: count // 2].reshape(units, width)
        up_w = gu_w[count // 2 :].reshape(units, width)
        down_w = d_w[...].reshape(units, width)
        for begin in range(0, units, step_units):
            at = slice(begin, begin + step_units)
            gate = dot(x, gate_w[at], 1, 1)
            up = dot(x, up_w[at], 1, 1)
            grad_hidden = dot(g, down_w[at], 1, 1)
            sigmoid = 0.5 * jnp.tanh(0.5 * gate) + 0.5
            silu = gate * sigmoid
            hid[:, at] = (silu * up).astype(BF16)
            gg[:, at] = (grad_hidden * up * (sigmoid + silu * (1.0 - sigmoid))).astype(BF16)
            gu[:, at] = (grad_hidden * silu).astype(BF16)

        def hand_out(value, kept, given):
            held[...] = value.astype(BF16).reshape(2, rows, width)
            kept[0] = held[core]
            given[0] = held[1 - core]

        hand_out(dot(gg[...], gate_w, 1, 0) + dot(gu[...], up_w, 1, 0), gn_kept, gn_given)
        hand_out(dot(hid[...], down_w, 1, 0), part_kept, part_given)

        @pl.when(step == size // 2 - 1)
        def _():
            for copy in handed:
                copy.wait()

    hbm = pl.BlockSpec(memory_space=pl.ANY)
    by_rows = pl.BlockSpec((2 * rows, units), lambda i: (i, 0))
    by_pair = pl.BlockSpec((1, rows, width), lambda i: (i, 0, 0))
    like = jax.ShapeDtypeStruct
    return pl.pallas_call(
        body,
        grid=(size // 2,),
        in_specs=[pl.BlockSpec(memory_space=pltpu.SMEM)]
        + [hbm] * (count + 2 * size),
        out_specs=[by_rows] * 3 + [by_pair] * 4 + [hbm] * 2,
        out_shape=[like((size * rows, units), BF16)] * 3
        + [like((size // 2, rows, width), BF16)] * 4
        + [like((size, rows, width), BF16)] * 2,
        scratch_shapes=[
            pltpu.VMEM((count, 2 * tall, width), BF16),
            pltpu.VMEM((count, tall, width), BF16),
            pltpu.VMEM((size, rows, width), BF16),
            pltpu.VMEM((size, rows, width), BF16),
            pltpu.VMEM((2, rows, width), BF16),
            pltpu.SemaphoreType.DMA((2 * count + 2 * size + 2,)),
        ],
        compiler_params=pltpu.CompilerParams(vmem_limit_bytes=VMEM_LIMIT),
        cost_estimate=pl.CostEstimate(flops=1, bytes_accessed=1, transcendentals=0),
        name="feed_forward",
    )(me, *weight_blocks, *row_blocks, *cot_blocks)


def both_heads(pair):
    lane = lax.broadcasted_iota(jnp.int32, pair.shape, 1)
    zero = jnp.zeros_like(pair)
    return jnp.concatenate(
        [jnp.where(lane < HEAD, pair, zero), jnp.where(lane < HEAD, zero, pair)], axis=0
    )


def fill_bias(low_ref, high_ref, place_ref, bias_ref):
    place = place_ref[...]
    allowed = (place >= low_ref[...]) & (place <= high_ref[...])
    bias = jnp.where(allowed, 0.0, MASKED).astype(F32)
    rows = bias.shape[1]
    bias_ref[:, :rows] = bias
    bias_ref[:, rows:] = bias


def own_rows(wide, rows):
    return jnp.concatenate([wide[:HEAD, :rows], wide[HEAD:, rows:]], axis=0)


def pairing(kv_ref, pair, begin):
    both = kv_ref[:, begin : begin + PAIR].astype(F32)
    crossed = pltpu.roll(both, HEAD, 1)
    lane = lax.broadcasted_iota(jnp.int32, both.shape, 1)
    first = jnp.where(pair <= PAIRS // 2, both, crossed)
    second = jnp.where(pair < PAIRS // 2, crossed, both)
    return jnp.where(lane < HEAD, first, second)


def new_pairing(step, pair):
    return (step == 0) | (pair == PAIRS // 2) | (pair == PAIRS // 2 + 1)


def attend_kernel(
    begin_pair, low_ref, high_ref, place_ref, q_ref, kv_ref,
    o_ref, lse_ref, bias_ref, k_ref, vt_ref,
):
    step = pl.program_id(0)
    pair = step + begin_pair

    @pl.when(step == 0)
    def _():
        fill_bias(low_ref, high_ref, place_ref, bias_ref)

    @pl.when(new_pairing(step, pair))
    def _():
        k_ref[...] = pairing(kv_ref, pair, 0).astype(BF16)
        vt_ref[...] = pairing(kv_ref, pair, PAIR).T.astype(BF16)

    rows = q_ref.shape[0]
    queries = both_heads(q_ref[...])
    keys = k_ref[...]
    values_t = vt_ref[...]
    outs, totals = [], []
    for begin in range(0, 2 * rows, 256):
        scores = dot(keys, queries[begin : begin + 256], 1, 1) + bias_ref[:, begin : begin + 256]
        top = jnp.max(scores, axis=0, keepdims=True)
        probs = jnp.exp(scores - top)
        total = jnp.sum(probs, axis=0, keepdims=True)
        outs.append(dot(values_t, probs.astype(BF16), 1, 0) / total)
        totals.append(top + jnp.log(total))
    wide = jnp.concatenate(outs, axis=1)
    o_ref[...] = own_rows(wide, rows).T.astype(BF16)
    lse_ref[0] = jnp.concatenate(totals, axis=1)


def attend_back_kernel(
    begin_pair, low_ref, high_ref, place_ref, q_ref, g_ref, o_ref, lse_ref, kv_ref, *refs,
):
    dq_ref, dkv_ref, bias_ref, k_ref, kt_ref, v_ref, dk_ref, dv_ref = refs[-8:]
    step = pl.program_id(0)
    pair = step + begin_pair

    @pl.when(step == 0)
    def _():
        fill_bias(low_ref, high_ref, place_ref, bias_ref)
        dkv_ref[...] = refs[0][...] if begin_pair else jnp.zeros_like(dkv_ref)

    @pl.when(new_pairing(step, pair))
    def _():
        keys_now = pairing(kv_ref, pair, 0)
        k_ref[...] = keys_now.astype(BF16)
        kt_ref[...] = keys_now.T.astype(BF16)
        v_ref[...] = pairing(kv_ref, pair, PAIR).astype(BF16)
        dk_ref[...] = jnp.zeros_like(dk_ref)
        dv_ref[...] = jnp.zeros_like(dv_ref)

    rows = q_ref.shape[0]
    queries = both_heads(q_ref[...])
    grads = both_heads(g_ref[...])
    keys = k_ref[...]
    keys_t = kt_ref[...]
    values = v_ref[...]
    product = (g_ref[...].astype(F32) * o_ref[...].astype(F32)).T
    delta = jnp.concatenate(
        [
            jnp.sum(product[:HEAD], axis=0, keepdims=True),
            jnp.sum(product[HEAD:], axis=0, keepdims=True),
        ],
        axis=1,
    )
    lse = lse_ref[0]
    outs = []
    for begin in range(0, 2 * rows, 256):
        part = slice(begin, begin + 256)
        scores = dot(keys, queries[part], 1, 1) + bias_ref[:, part]
        probs = jnp.exp(scores - lse[:, part])
        grad_probs = dot(values, grads[part], 1, 1)
        grad_scores = (probs * (grad_probs - delta[:, part])).astype(BF16)
        outs.append(dot(keys_t, grad_scores, 1, 0))
        dk_ref[...] += dot(grad_scores, queries[part], 1, 0)
        dv_ref[...] += dot(probs.astype(BF16), grads[part], 1, 0)
    wide = jnp.concatenate(outs, axis=1)
    dq_ref[...] = own_rows(wide, rows).T * 0.125

    def fold(own_lanes):
        for at, sums in ((0, dk_ref), (PAIR, dv_ref)):
            sums_now = sums[...]
            lane = lax.broadcasted_iota(jnp.int32, sums_now.shape, 1)
            both = sums_now + pltpu.roll(sums_now, HEAD, 1)
            kept = jnp.where((lane < HEAD) == own_lanes, both, 0.0)
            dkv_ref[:, at : at + PAIR] += kept

    @pl.when(pair == PAIRS // 2 - 1)
    def _():
        fold(True)

    @pl.when(pair == PAIRS // 2)
    def _():
        dkv_ref[:, :PAIR] += dk_ref[...]
        dkv_ref[:, PAIR:] += dv_ref[...]

    @pl.when(pair == PAIRS - 1)
    def _():
        fold(False)


def whole(shape):
    return pl.BlockSpec(shape, lambda i: (0,) * len(shape))


def attend(low, high, place, queries, kv_all, begin, pairs):
    rows, count = queries.shape[0], place.shape[0]
    taken = pl.BlockSpec((rows, PAIR), lambda i: (0, i + begin))
    made = pl.BlockSpec((rows, PAIR), lambda i: (0, i))
    return pl.pallas_call(
        functools.partial(attend_kernel, begin),
        grid=(pairs,),
        in_specs=[whole((1, rows)), whole((1, rows)), whole((count, 1)), taken]
        + [whole((count, 2 * KVW))],
        out_specs=[made, pl.BlockSpec((1, 1, 2 * rows), lambda i: (i, 0, 0))],
        out_shape=[
            jax.ShapeDtypeStruct((rows, pairs * PAIR), BF16),
            jax.ShapeDtypeStruct((pairs, 1, 2 * rows), F32),
        ],
        scratch_shapes=[
            pltpu.VMEM((count, 2 * rows), F32),
            pltpu.VMEM((count, PAIR), BF16),
            pltpu.VMEM((PAIR, count), BF16),
        ],
        compiler_params=pltpu.CompilerParams(vmem_limit_bytes=VMEM_LIMIT),
        cost_estimate=pl.CostEstimate(flops=1, bytes_accessed=1, transcendentals=0),
        name="attend",
    )(low, high, place, queries, kv_all)


def attend_back(low, high, place, queries, grads, outs, lse, kv_all, begin, pairs, so_far):
    rows, count = queries.shape[0], place.shape[0]
    taken = pl.BlockSpec((rows, PAIR), lambda i: (0, i + begin))
    made = pl.BlockSpec((rows, PAIR), lambda i: (0, i))
    sums = whole((count, 2 * KVW))
    return pl.pallas_call(
        functools.partial(attend_back_kernel, begin),
        grid=(pairs,),
        in_specs=[whole((1, rows)), whole((1, rows)), whole((count, 1)), taken, taken, made]
        + [pl.BlockSpec((1, 1, 2 * rows), lambda i: (i, 0, 0)), sums]
        + [sums] * len(so_far),
        out_specs=[made, sums],
        out_shape=[
            jax.ShapeDtypeStruct((rows, pairs * PAIR), F32),
            jax.ShapeDtypeStruct((count, 2 * KVW), F32),
        ],
        scratch_shapes=[
            pltpu.VMEM((count, 2 * rows), F32),
            pltpu.VMEM((count, PAIR), BF16),
            pltpu.VMEM((PAIR, count), BF16),
            pltpu.VMEM((count, PAIR), BF16),
            pltpu.VMEM((count, PAIR), F32),
            pltpu.VMEM((count, PAIR), F32),
        ],
        compiler_params=pltpu.CompilerParams(vmem_limit_bytes=VMEM_LIMIT),
        cost_estimate=pl.CostEstimate(flops=1, bytes_accessed=1, transcendentals=0),
        name="attend_back",
    )(low, high, place, queries, grads, outs, lse, kv_all, *so_far)


def rms_scale(values_in):
    return lax.rsqrt(jnp.mean(values_in * values_in, axis=-1, keepdims=True) + EPSILON)


def angle_tables(places):
    exponent = jnp.arange(HEAD // 2, dtype=F32) * 2.0 / HEAD
    frequency = ROPE_BASE ** (-exponent)
    turn = places.astype(F32)[:, None] * frequency[None, :]
    cosine, sine = lax.optimization_barrier((jnp.cos(turn), jnp.sin(turn)))
    return jnp.concatenate([cosine] * 4, axis=1), jnp.concatenate([sine] * 4, axis=1)


def widen(table, width):
    return jnp.concatenate([table] * (width // PAIR), axis=1)


def first_halves(shape):
    return lax.broadcasted_iota(jnp.int32, shape, 1) % HEAD < HEAD // 2


def rotate(tensor, cosine, sine):
    half = HEAD // 2
    ahead, behind = jnp.roll(tensor, -half, axis=1), jnp.roll(tensor, half, axis=1)
    turned = jnp.where(first_halves(tensor.shape), -ahead, behind)
    width = tensor.shape[1]
    return tensor * widen(cosine, width) + turned * widen(sine, width)


def norm_back_rows(grad_in, row_data, scale_in, gain_in):
    gain_term = jnp.sum(grad_in * row_data * scale_in, axis=0, keepdims=True)
    grad_normed = grad_in * gain_in
    inner_mean = jnp.mean(grad_normed * row_data, axis=-1, keepdims=True)
    return (
        scale_in * grad_normed - row_data * scale_in * scale_in * scale_in * inner_mean,
        gain_term,
    )


def residual_back(me, kept, got, residual, scale_two, gain_two, cotangent, out_full):
    rows, width = residual.shape

    def body(me_ref, kept_ref, got_ref, res_ref, scale_ref, gain_ref, cot_ref, out_ref,
             grad_ref, branch_ref, attn_ref, term_ref):
        grad = kept_ref[...] + got_ref[...].astype(F32)
        path, term_ref[...] = norm_back_rows(grad, res_ref[...], scale_ref[...], gain_ref[...])
        full = cot_ref[...].astype(F32) + path
        grad_ref[...] = full
        branch_ref[...] = full.astype(BF16)
        attn_ref[...] = dot(full.astype(BF16), out_ref[...], 1, 1).astype(BF16)

    shapes = [
        jax.ShapeDtypeStruct((rows, width), F32),
        jax.ShapeDtypeStruct((rows, width), BF16),
        jax.ShapeDtypeStruct((rows, QW), BF16),
        jax.ShapeDtypeStruct((1, width), F32),
    ]
    arrays = (kept, got, residual, scale_two, gain_two[None, :], cotangent, out_full)
    return on_device(body, "residual_back", shapes, [], me, arrays)


def joined_back(
    me, dq_one, dq_two, kept, got, cosine, sine, qkv_t, tokens, scale_one, gain_one,
    grad_residual, normed_one, norm_two_term, seq_size, fsdp_size,
):
    rows, width = tokens.shape
    total = qkv_t.shape[0]
    each, lanes = total // fsdp_size, width // seq_size
    tall = padded(each)

    def body(me_ref, dq1_ref, dq2_ref, kept_ref, got_ref, cos_ref, sin_ref, w_ref, x_ref,
             scale_ref, gain_ref, res_ref, n1_ref, term_ref,
             tokens_ref, mine_ref, other_ref, held):
        kv = kept_ref[...] + got_ref[...].astype(F32)
        turned = jnp.concatenate([dq1_ref[...], dq2_ref[...], kv[:, :KVW]], axis=1)
        across = turned.shape[1]
        scaled = turned * widen(sin_ref[...], across)
        ahead = pltpu.roll(scaled, across - HEAD // 2, 1)
        behind = pltpu.roll(scaled, HEAD // 2, 1)
        turned = turned * widen(cos_ref[...], across) + jnp.where(
            first_halves(turned.shape), ahead, -behind
        )
        joined = jnp.concatenate([turned, kv[:, KVW:]], axis=1).astype(BF16)
        wide = joined.astype(F32)
        grad_normed = dot(joined, w_ref[...], 1, 0)
        path, one_term = norm_back_rows(
            grad_normed, x_ref[...].astype(F32), scale_ref[...], gain_ref[...]
        )
        tokens_ref[...] = res_ref[...] + path
        bias = jnp.sum(wide, axis=0, keepdims=True)
        weight = dot(wide.T.astype(BF16), n1_ref[...], 1, 0)
        vectors = [one_term, bias[:, : QW + KVW], bias[:, QW + KVW :], term_ref[...]]
        for f in range(fsdp_size):
            lines = []
            for vector in vectors:
                n = vector.shape[1] // fsdp_size
                piece = vector[:, f * n : (f + 1) * n]
                lines.append(jnp.concatenate([piece, jnp.zeros((1, lanes - n), F32)], axis=1))
            blank = jnp.zeros((tall - each, lanes), F32)
            below = [blank] * (tall > each) + lines + [jnp.zeros((12, lanes), F32)]
            for s in range(seq_size):
                part = weight[f * each : (f + 1) * each, s * lanes : (s + 1) * lanes]
                held[s, f] = jnp.concatenate([part] + below, axis=0).astype(BF16)
        core = me_ref[0] % 2
        for y in range(seq_size // 2):
            mine_ref[y] = held[2 * y + core]
            other_ref[y] = held[2 * y + 1 - core]

    block = (fsdp_size, tall + 16, lanes)
    half = jax.ShapeDtypeStruct((seq_size // 2,) + block, BF16)
    shapes = [jax.ShapeDtypeStruct((rows, width), F32), half, half]
    arrays = (
        dq_one, dq_two, kept, got, cosine, sine, qkv_t, tokens, scale_one, gain_one[None, :],
        grad_residual, normed_one, norm_two_term,
    )
    scratch = [pltpu.VMEM((seq_size,) + block, BF16)]
    return on_device(body, "joined_back", shapes, scratch, me, arrays)


def pad_row(vector, width):
    return jnp.pad(vector, (0, width - vector.shape[0]))[None, :]


def stack_from_lanes(array, count):
    rows, width = array.shape
    return jnp.transpose(array.reshape(rows, count, width // count), (1, 0, 2))


def per_device(
    seq_size, fsdp_size, tokens, segment_ids, positions, norm_one, qkv_weight, qkv_bias,
    out_weight, norm_two, gate_up_weight, down_weight, cotangent,
):
    my_seq, my_fsdp = lax.axis_index("seq"), lax.axis_index("fsdp")
    me = jnp.stack([my_seq, my_fsdp]).astype(jnp.int32)
    offsets = range(seq_size)
    row_count = tokens.shape[0]
    width = qkv_weight.shape[0]
    qkv_rows = qkv_weight.shape[1]
    strip = down_weight.shape[0] // seq_size
    tall = padded(strip)

    ff_cut = cut_ff(me, gate_up_weight, down_weight, seq_size)
    ff_share = [ff_cut[0]] + [swap(ff_cut[o], "seq", seq_size, o) for o in offsets if o]
    qkv_tall = padded(qkv_rows)
    packed = jnp.concatenate(
        [
            jnp.pad(qkv_weight.T, ((0, qkv_tall - qkv_rows), (0, 0))),
            pad_row(norm_one, width),
            pad_row(qkv_bias, width),
            pad_row(norm_two, width),
            jnp.zeros((13, width), BF16),
            out_weight,
        ],
        axis=0,
    )
    packed = after(packed, ff_cut[0])
    ff_block = join_lanes(me, ff_share)
    columns = ff_spread(
        after(column_gather(packed, fsdp_size), ff_block), fsdp_size
    )
    wide = qkv_tall + 16
    columns[0] = after(columns[0], ff_block)
    packed_pieces = [seq_gather(columns[m][:, :wide], seq_size) for m in sorted(columns)]
    ff_blocks = {0: ff_block}
    inner = fsdp_size // OUTER
    near = swap(ff_block, "fsdp", fsdp_size, inner)
    far = swap(ff_block, "fsdp", fsdp_size, 2 * inner)

    qkv_pieces = [[piece[o] for piece in packed_pieces] for o in offsets]
    qkv_t, vectors = join_both(me, qkv_pieces, qkv_tall)
    out_stack = jnp.concatenate([columns[m][:, wide:] for m in sorted(columns)], axis=0)
    out_stack = after(out_stack, packed_pieces[-1][seq_size // 2])
    out_blocks = seq_gather(out_stack, seq_size)

    own_x = ff_spread(ff_block, fsdp_size)
    last = swap(after(far, qkv_t), "fsdp", fsdp_size, inner)
    qkv_t = after(qkv_t, far, near, *own_x.values())[:, :qkv_rows].reshape(fsdp_size * qkv_rows, -1)
    gain_one = vectors[:, 0, : norm_one.shape[0]].reshape(-1).astype(F32)
    bias_full = vectors[:, 1, : qkv_bias.shape[0]].reshape(-1).astype(F32)
    gain_two = vectors[:, 2, : norm_two.shape[0]].reshape(-1).astype(F32)

    inputs = tokens.astype(F32)
    scale_one = rms_scale(inputs)
    normed_one = (inputs * scale_one * gain_one).astype(BF16)
    joined = dot(normed_one, qkv_t, 1, 1) + bias_full
    cosine, sine = angle_tables(positions)
    turned = rotate(joined[:, : QW + KVW], cosine, sine).astype(BF16)
    queries = turned[:, :QW] * jnp.asarray(0.125, BF16)
    kv_local = jnp.concatenate([turned[:, QW:], joined[:, QW + KVW :].astype(BF16)], axis=1)
    kv_all = lax.all_gather(kv_local, "seq", axis=0, tiled=True)
    cot_blocks = seq_gather(after(cotangent, kv_all), seq_size)
    row_place = jnp.arange(row_count, dtype=jnp.int32)
    high = my_seq * row_count + row_place
    low = high - positions
    place = jnp.arange(seq_size * row_count, dtype=jnp.int32)[:, None]
    low, high = low[None, :], high[None, :]
    split = PAIRS // 2 + 1
    spread = lambda block: ff_spread(block, fsdp_size)
    near_x = spread(after(near, kv_all))
    attn_one, lse_one = attend(
        low, high, place, after(queries, far), kv_all, 0, split
    )
    far_x = spread(after(far, kv_all))
    queries_two = after(queries, attn_one, cot_blocks[seq_size // 2], *near_x.values())
    attn_two, lse_two = attend(low, high, place, queries_two, kv_all, split, PAIRS - split)
    last_x = spread(last)
    for base, row in ((0, own_x), (inner, near_x), (2 * inner, far_x), (3 * inner, last_x)):
        ff_blocks.update({base + m: block for m, block in row.items()})
    attn_flat = jnp.concatenate([attn_one, attn_two], axis=1)

    out_list = [[out_blocks[o]] for o in offsets]
    out_list[0][0] = after(out_list[0][0], attn_one)
    out_full = join_both(me, out_list, out_weight.shape[0])[0].reshape(QW, -1)

    residual = inputs + dot(attn_flat, out_full, 1, 0)
    scale_two = rms_scale(residual)
    normed_two = (residual * scale_two * gain_two).astype(BF16)
    normed_blocks = {0: normed_two}
    bit = seq_size // 2
    while bit:
        if bit == 1:
            top = seq_size // 2
            normed_blocks[top] = after(normed_blocks[top], last, *far_x.values())
        normed_blocks.update(
            {o ^ bit: swap(b, "seq", seq_size, bit) for o, b in normed_blocks.items()}
        )
        bit //= 2
    (
        hidden, grad_gate, grad_up, kept, given, kept_layer, given_layer, normed_all, cot_all,
    ) = feed_forward(
        me,
        [ff_blocks[o] for o in range(fsdp_size)],
        [normed_blocks[o] for o in offsets],
        [cot_blocks[o] for o in offsets],
    )
    normed_all = normed_all.reshape(seq_size * row_count, -1)
    cot_all = cot_all.reshape(seq_size * row_count, -1)
    by_seq = lambda rows: rows.reshape(seq_size, row_count, -1)

    normed_sum = add(kept, swap(given, "seq", seq_size, 1))
    bit = 2
    while bit < seq_size:
        kept, given = halve(normed_sum, 1, my_seq // bit)
        got = swap(given, "seq", seq_size, bit)
        normed_sum = add(kept, got)
        bit *= 2
    normed_kept, normed_got = kept[0], got[0]
    hidden = after(hidden, given)
    down_term = dot(hidden, cot_all, 0, 0).astype(BF16).reshape(fsdp_size, tall, -1)
    grad_gate, grad_up = after(grad_gate, down_term), after(grad_up, down_term)
    gate_term = dot(grad_gate, normed_all, 0, 0).astype(BF16).reshape(fsdp_size // 2, 2, tall, -1)
    up_term = dot(grad_up, normed_all, 0, 0).astype(BF16).reshape(fsdp_size // 2, 2, tall, -1)

    bits = list(reversed(fsdp_bits(fsdp_size)))

    def give(stack, at):
        kept, given = fsdp_halve(stack, fsdp_size, bits[at], my_fsdp, bits[:at])
        return kept, given

    def send(given, at):
        return swap(given, "fsdp", fsdp_size, bits[at])

    def finish(kept, got, at):
        stack = add(kept, got)
        for later in range(at + 1, len(bits)):
            kept, given = give(stack, later)
            stack = add(kept, send(given, later))
        return stack[0]

    kept_one, given = give(down_term, 0)
    got_one = send(given, 0)
    kept_two, given = give(jnp.concatenate([gate_term[:, 0], up_term[:, 0]], axis=0), 0)
    got_two = send(after(given, normed_got), 0)
    kept_three, given_three = give(jnp.concatenate([gate_term[:, 1], up_term[:, 1]], axis=0), 0)

    grad_residual, grad_branch, grad_attn, norm_two_term = residual_back(
        me, normed_kept, normed_got, residual, scale_two, gain_two, cotangent, out_full
    )
    grad_attn = after(grad_attn, gate_term, up_term)
    dq_one, kv_terms = attend_back(
        low, high, place, queries, grad_attn, attn_one, lse_one, kv_all, 0, split, ()
    )
    got_one = after(got_one, dq_one)
    got_three = send(after(given_three, got_one), 0)
    kept_one, given_one = give(add(kept_one, got_one), 1)
    next_one = send(given_one, 1)
    queries_two = after(queries, kv_terms, given_one)
    dq_two, kv_terms = attend_back(
        low, high, place, queries_two, grad_attn, attn_two, lse_two, kv_all, split,
        PAIRS - split, (kv_terms,),
    )
    got_two = after(got_two, dq_two)
    kept_two, given = give(add(kept_two, got_two), 1)
    next_two = send(given, 1)
    kept, given = halve(by_seq(kv_terms), 1, my_seq)
    kv_sum = add(kept, swap(given, "seq", seq_size, 1))
    bit = 2
    while bit < seq_size:
        kv_kept, given = halve(kv_sum, 1, my_seq // bit)
        kv_got = swap(after(given, got_two), "seq", seq_size, bit)
        kv_sum = add(kv_kept, kv_got)
        bit *= 2
    kv_mine = kv_got

    attn_late = after(attn_flat, dq_two)
    out_term = stack_from_lanes(dot(attn_late, grad_branch, 0, 0).astype(BF16), seq_size)
    kept, given = halve(out_term, 1, my_seq)
    out_sum = add(kept, swap(given, "seq", seq_size, 1))
    layer_got = swap(after(given_layer, dq_two), "seq", seq_size, 1)
    layer_sum = add(kept_layer, layer_got)
    kept_layer, given_layer = halve(layer_sum, 1, my_seq // 2)
    grad_tokens, kept, given = joined_back(
        me, dq_one, dq_two, kv_kept[0], after(kv_got[0], layer_got), cosine, sine, qkv_t, tokens, scale_one,
        gain_one, grad_residual, normed_one, norm_two_term, seq_size, fsdp_size,
    )

    got_three = after(got_three, grad_tokens)
    kept_three, given_last = give(add(kept_three, got_three), 1)
    next_three = send(given_last, 1)
    next_one, next_two = after(next_one, grad_tokens), after(next_two, grad_tokens)
    down_sum = finish(kept_one, next_one, 1)

    bit = 2
    while bit < seq_size:
        kept_out, given_out = halve(out_sum, 1, my_seq // bit)
        out_sum = add(kept_out, swap(after(given_out, grad_tokens), "seq", seq_size, bit))
        bit *= 2
    out_mine = out_sum[0].reshape(fsdp_size, -1, width)
    tail_sum = add(kept, swap(given, "seq", seq_size, 1))
    bit = 2
    while bit < seq_size:
        kept, given = halve(tail_sum, 1, my_seq // bit)
        tail_sum = add(kept, swap(given, "seq", seq_size, bit))
        bit *= 2
    tail_mine = tail_sum[0]
    got_layer = swap(after(given_layer, kv_mine), "seq", seq_size, 2)
    layer_sum = add(kept_layer, got_layer)
    bit = 4
    while bit < seq_size:
        kept, given = halve(layer_sum, 1, my_seq // bit)
        layer_sum = add(kept, swap(given, "seq", seq_size, bit))
        bit *= 2
    layer_out = residual + layer_sum[0]
    one_sum = finish(kept_two, next_two, 1)
    two_sum = finish(kept_three, next_three, 1)

    ff_back = cut_lanes(me, (one_sum, two_sum, down_sum), seq_size)
    ff_got = [ff_back[0]] + [swap(ff_back[o], "seq", seq_size, o) for o in offsets if o]
    grad_gate_up, grad_down = join_ff(me, ff_got, strip)

    tail_sum = fsdp_scatter(
        after(jnp.concatenate([tail_mine, out_mine], axis=1), next_two),
        fsdp_size,
        my_fsdp,
        next_three,

    )
    lengths = [width * seq_size, QW + KVW, KVW, width * seq_size]
    pieces = [tail_sum[qkv_tall + i, : n // fsdp_size] for i, n in enumerate(lengths)]
    return (
        layer_out.astype(BF16),
        grad_tokens,
        pieces[0],
        tail_sum[:qkv_rows].T,
        pieces[1],
        pieces[2],
        tail_sum[qkv_tall + 16 :],
        pieces[3],
        grad_gate_up,
        grad_down,
    )


def solution(mesh):
    rows, both = P(("fsdp", "seq"), None), P(("fsdp", "seq"))
    return jax.shard_map(
        functools.partial(per_device, mesh.shape["seq"], mesh.shape["fsdp"]),
        mesh=mesh,
        in_specs=(
            rows, both, both, P("fsdp"), P("seq", "fsdp"), P("fsdp"), P("fsdp", "seq"),
            P("fsdp"), P("seq", "fsdp"), P("fsdp", "seq"), rows,
        ),
        out_specs=(
            rows, rows, P("fsdp"), P("seq", "fsdp"), P("fsdp"), P("fsdp"), P("fsdp", "seq"),
            P("fsdp"), P("seq", "fsdp"), P("fsdp", "seq"),
        ),
        check_vma=False,
    )
```

```python
import functools

import jax
import jax.numpy as jnp
from jax import lax
from jax.experimental import pallas as pl
from jax.experimental.pallas import tpu as pltpu
from jax.sharding import PartitionSpec as P

HEADS = 14
KV_HEADS = 2
HEAD = 64
FF = 4864
QW = 896
KVW = 128
PAIR = 2 * HEAD
PAIRS = HEADS // 2
OUTER = 4

EPSILON = 1e-06
ROPE_BASE = 1000000.0
MASKED = -1e30
VMEM_LIMIT = 50 * 1024 * 1024

F32 = jnp.float32
BF16 = jnp.bfloat16


def dot(left, right, left_dim, right_dim):
    return lax.dot_general(
        left, right, (((left_dim,), (right_dim,)), ((), ())), preferred_element_type=F32
    )


def swap(block, axis, size, bits):
    return lax.ppermute(block, axis, [(i, i ^ bits) for i in range(size)])


def after(array, *others):
    return lax.optimization_barrier((array,) + others)[0]


def seq_gather(block, size):
    blocks = {0: block}
    bit = size // 2
    while bit:
        blocks.update({o ^ bit: swap(b, "seq", size, bit) for o, b in blocks.items()})
        bit //= 2
    return blocks


def fsdp_bits(size):
    inner = size // OUTER
    outer_bits, inner_bits = [], []
    bit = 1
    while bit < size:
        (outer_bits if bit >= inner else inner_bits).append(bit)
        bit *= 2
    return outer_bits[::-1] + inner_bits


def column_gather(block, size):
    inner = size // OUTER
    return jnp.stack([block] + [swap(block, "fsdp", size, k * inner) for k in range(1, OUTER)])


def ff_spread(block, size):
    blocks = {0: block}
    for bit in fsdp_bits(size)[2:]:
        blocks.update({o ^ bit: swap(b, "fsdp", size, bit) for o, b in blocks.items()})
    return blocks


def halve(stack, bit, me):
    above = stack.shape[0] // (2 * bit)
    cut = stack.reshape((above, 2, bit) + stack.shape[1:])
    digit = (me // bit) % 2
    kept = lax.dynamic_index_in_dim(cut, digit, 1, keepdims=False)
    given = lax.dynamic_index_in_dim(cut, 1 - digit, 1, keepdims=False)
    merge = lambda part: part.reshape((above * bit,) + stack.shape[1:])
    return merge(kept), merge(given).astype(BF16)


def add(kept, got):
    return kept.astype(F32) + got.astype(F32)


def seq_scatter(stack, size, me):
    bit = 1
    while bit < size:
        kept, given = halve(stack, 1, me // bit)
        stack = add(kept, swap(given, "seq", size, bit))
        bit *= 2
    return stack[0]


def fsdp_halve(stack, size, bit, me, resolved):
    place = bit
    digit = me // bit
    for taken in resolved:
        if taken < bit:
            place //= 2
    kept, given = halve(stack, place, digit * place)
    return kept, given


def fsdp_scatter(stack, size, me, earlier):
    inner = size // OUTER
    resolved = []
    for bit in reversed(fsdp_bits(size)[2:]):
        kept, given = fsdp_halve(stack, size, bit, me, resolved)
        stack = add(kept, swap(given, "fsdp", size, bit))
        resolved.append(bit)
    place = me // inner
    low = after(stack.astype(BF16), earlier)
    total = lax.dynamic_index_in_dim(stack, place, 0, keepdims=False)
    for k in range(1, OUTER):
        given = lax.dynamic_index_in_dim(low, place ^ k, 0, keepdims=False)
        total = add(total, swap(given, "fsdp", size, k * inner))
    return total


def on_device(body, name, out_shapes, scratch, me, arrays):
    vmem = pl.BlockSpec(memory_space=pltpu.VMEM)
    return pl.pallas_call(
        body,
        in_specs=[pl.BlockSpec(memory_space=pltpu.SMEM)] + [vmem] * len(arrays),
        out_specs=[vmem] * len(out_shapes),
        out_shape=out_shapes,
        scratch_shapes=scratch,
        compiler_params=pltpu.CompilerParams(vmem_limit_bytes=VMEM_LIMIT),
        name=name,
    )(me, *arrays)


def padded(rows):
    return -(-rows // 16) * 16


def cut_ff(me, gate_up_weight, down_weight, size):
    width = gate_up_weight.shape[0]
    half = down_weight.shape[0]
    strip = half // size
    tall = padded(strip)

    def body(me_ref, gu_ref, d_ref, *refs):
        outs, held = refs[:size], refs[size]
        turned = gu_ref[...].astype(F32).T
        down = d_ref[...].astype(F32)
        blank = jnp.zeros((tall - strip, width), F32)
        for q in range(size):
            one = turned[q * strip : (q + 1) * strip]
            two = turned[half + q * strip : half + (q + 1) * strip]
            three = down[q * strip : (q + 1) * strip]
            parts = [one, blank, two, blank, three, blank]
            held[q] = jnp.concatenate(parts, axis=0).astype(BF16)
        for o in range(size):
            outs[o][...] = held[me_ref[0] ^ o]

    shape = jax.ShapeDtypeStruct((3 * tall, width), BF16)
    scratch = [pltpu.VMEM((size, 3 * tall, width), BF16)]
    return on_device(body, "cut_ff", [shape] * size, scratch, me, (gate_up_weight, down_weight))


def join_lanes(me, blocks):
    size = len(blocks)
    rows, width = blocks[0].shape

    def body(me_ref, *refs):
        ins, out, held = refs[:size], refs[size], refs[size + 1]
        for o in range(size):
            held[me_ref[0] ^ o] = ins[o][...]
        out[...] = jnp.concatenate([held[q].astype(F32) for q in range(size)], 1).astype(BF16)

    return on_device(
        body,
        "join_lanes",
        [jax.ShapeDtypeStruct((rows, size * width), BF16)],
        [pltpu.VMEM((size, rows, width), BF16)],
        me,
        blocks,
    )[0]


def join_both(me, pieces, rows):
    size, parts_each = len(pieces), len(pieces[0])
    _, tall, width = pieces[0][0].shape
    count = sum(part.shape[0] for part in pieces[0])
    inner = count // OUTER
    order = [k * inner + m for m in range(inner) for k in range(OUTER)]
    shapes = [jax.ShapeDtypeStruct((count, rows, size * width), BF16)]
    if tall > rows:
        shapes.append(jax.ShapeDtypeStruct((count, tall - rows, width), BF16))

    def body(me_ref, *refs):
        ins, out, held = refs[: size * parts_each], refs[size * parts_each], refs[-1]
        for o in range(size):
            at = 0
            for part in ins[o * parts_each : (o + 1) * parts_each]:
                for j in range(part.shape[0]):
                    place = me_ref[1] ^ order[at]
                    held[me_ref[0] ^ o, place] = part[j]
                    if tall > rows and o == 0:
                        refs[size * parts_each + 1][place] = part[j, rows:]
                    at += 1
        for f in range(count):
            parts = [held[q, f, :rows].astype(F32) for q in range(size)]
            out[f] = jnp.concatenate(parts, axis=1).astype(BF16)

    return on_device(
        body,
        "join_both",
        shapes,
        [pltpu.VMEM((size, count, tall, width), BF16)],
        me,
        [block for row in pieces for block in row],
    )


def cut_lanes(me, sums, size):
    rows = sum(s.shape[0] for s in sums)
    width = sums[0].shape[1] // size

    def body(me_ref, *refs):
        ins, outs, held = refs[: len(sums)], refs[len(sums) : -1], refs[-1]
        whole = jnp.concatenate([r[...] for r in ins], axis=0)
        for q in range(size):
            held[q] = whole[:, q * width : (q + 1) * width].astype(BF16)
        for o in range(size):
            outs[o][...] = held[me_ref[0] ^ o]

    shape = jax.ShapeDtypeStruct((rows, width), BF16)
    scratch = [pltpu.VMEM((size, rows, width), BF16)]
    return on_device(body, "cut_lanes", [shape] * size, scratch, me, sums)


def join_ff(me, blocks, strip):
    size = len(blocks)
    rows, width = blocks[0].shape
    tall = rows // 3

    def body(me_ref, *refs):
        ins, gu, down, held = refs[:size], refs[size], refs[size + 1], refs[size + 2]
        for o in range(size):
            held[me_ref[0] ^ o] = ins[o][...].astype(F32)
        cut = [
            [held[q, i * tall : i * tall + strip] for q in range(size)] for i in range(3)
        ]
        gu[...] = jnp.concatenate(cut[0] + cut[1], axis=0).T
        down[...] = jnp.concatenate(cut[2], axis=0)

    return on_device(
        body,
        "join_ff",
        [
            jax.ShapeDtypeStruct((width, 2 * size * strip), F32),
            jax.ShapeDtypeStruct((size * strip, width), F32),
        ],
        [pltpu.VMEM((size, rows, width), F32)],
        me,
        blocks,
    )


def feed_forward(me, weight_blocks, row_blocks, cot_blocks):
    count, size = len(weight_blocks), len(row_blocks)
    rows, width = row_blocks[0].shape
    tall = weight_blocks[0].shape[0] // 3
    units = count * tall
    step_units = 256

    def body(me_ref, *refs):
        blocks = refs[:count]
        xs, gs = refs[count : count + size], refs[count + size : count + 2 * size]
        outs = refs[count + 2 * size : count + 2 * size + 9]
        hid, gg, gu, gn_kept, gn_given, part_kept, part_given, x_out, g_out = outs
        gu_w, d_w, x_all, g_all, held, sems = refs[count + 2 * size + 9 :]
        step = pl.program_id(0)
        core = me_ref[0] % 2
        handed = [
            pltpu.make_async_copy(src, dst, sems.at[2 * count + 2 * size + i])
            for i, (src, dst) in enumerate(((x_all, x_out), (g_all, g_out)))
        ]

        @pl.when(step == 0)
        def _():
            copies = []
            for o in range(count):
                f = me_ref[1] ^ o
                copies.append((blocks[o].at[pl.ds(0, 2 * tall)], gu_w.at[f]))
                copies.append((blocks[o].at[pl.ds(2 * tall, tall)], d_w.at[f]))
            for o in range(size):
                copies.append((xs[o], x_all.at[me_ref[0] ^ o]))
                copies.append((gs[o], g_all.at[me_ref[0] ^ o]))
            started = [
                pltpu.make_async_copy(src, dst, sems.at[i]) for i, (src, dst) in enumerate(copies)
            ]
            for copy in started:
                copy.start()
            for copy in started:
                copy.wait()
            for copy in handed:
                copy.start()

        x = x_all[pl.ds(2 * step, 2)].reshape(2 * rows, width)
        g = g_all[pl.ds(2 * step, 2)].reshape(2 * rows, width)
        gate_w = gu_w[: count // 2].reshape(units, width)
        up_w = gu_w[count // 2 :].reshape(units, width)
        down_w = d_w[...].reshape(units, width)
        for begin in range(0, units, step_units):
            at = slice(begin, begin + step_units)
            gate = dot(x, gate_w[at], 1, 1)
            up = dot(x, up_w[at], 1, 1)
            grad_hidden = dot(g, down_w[at], 1, 1)
            sigmoid = 0.5 * jnp.tanh(0.5 * gate) + 0.5
            silu = gate * sigmoid
            hid[:, at] = (silu * up).astype(BF16)
            gg[:, at] = (grad_hidden * up * (sigmoid + silu * (1.0 - sigmoid))).astype(BF16)
            gu[:, at] = (grad_hidden * silu).astype(BF16)

        def hand_out(value, kept, given):
            held[...] = value.astype(BF16).reshape(2, rows, width)
            kept[0] = held[core]
            given[0] = held[1 - core]

        hand_out(dot(gg[...], gate_w, 1, 0) + dot(gu[...], up_w, 1, 0), gn_kept, gn_given)
        hand_out(dot(hid[...], down_w, 1, 0), part_kept, part_given)

        @pl.when(step == size // 2 - 1)
        def _():
            for copy in handed:
                copy.wait()

    hbm = pl.BlockSpec(memory_space=pl.ANY)
    by_rows = pl.BlockSpec((2 * rows, units), lambda i: (i, 0))
    by_pair = pl.BlockSpec((1, rows, width), lambda i: (i, 0, 0))
    like = jax.ShapeDtypeStruct
    return pl.pallas_call(
        body,
        grid=(size // 2,),
        in_specs=[pl.BlockSpec(memory_space=pltpu.SMEM)]
        + [hbm] * (count + 2 * size),
        out_specs=[by_rows] * 3 + [by_pair] * 4 + [hbm] * 2,
        out_shape=[like((size * rows, units), BF16)] * 3
        + [like((size // 2, rows, width), BF16)] * 4
        + [like((size, rows, width), BF16)] * 2,
        scratch_shapes=[
            pltpu.VMEM((count, 2 * tall, width), BF16),
            pltpu.VMEM((count, tall, width), BF16),
            pltpu.VMEM((size, rows, width), BF16),
            pltpu.VMEM((size, rows, width), BF16),
            pltpu.VMEM((2, rows, width), BF16),
            pltpu.SemaphoreType.DMA((2 * count + 2 * size + 2,)),
        ],
        compiler_params=pltpu.CompilerParams(vmem_limit_bytes=VMEM_LIMIT),
        cost_estimate=pl.CostEstimate(flops=1, bytes_accessed=1, transcendentals=0),
        name="feed_forward",
    )(me, *weight_blocks, *row_blocks, *cot_blocks)


def both_heads(pair):
    lane = lax.broadcasted_iota(jnp.int32, pair.shape, 1)
    zero = jnp.zeros_like(pair)
    return jnp.concatenate(
        [jnp.where(lane < HEAD, pair, zero), jnp.where(lane < HEAD, zero, pair)], axis=0
    )


def fill_bias(low_ref, high_ref, place_ref, bias_ref):
    place = place_ref[...]
    allowed = (place >= low_ref[...]) & (place <= high_ref[...])
    bias = jnp.where(allowed, 0.0, MASKED).astype(F32)
    rows = bias.shape[1]
    bias_ref[:, :rows] = bias
    bias_ref[:, rows:] = bias


def own_rows(wide, rows):
    return jnp.concatenate([wide[:HEAD, :rows], wide[HEAD:, rows:]], axis=0)


def pairing(kv_ref, pair, begin):
    both = kv_ref[:, begin : begin + PAIR].astype(F32)
    crossed = pltpu.roll(both, HEAD, 1)
    lane = lax.broadcasted_iota(jnp.int32, both.shape, 1)
    first = jnp.where(pair <= PAIRS // 2, both, crossed)
    second = jnp.where(pair < PAIRS // 2, crossed, both)
    return jnp.where(lane < HEAD, first, second)


def new_pairing(step, pair):
    return (step == 0) | (pair == PAIRS // 2) | (pair == PAIRS // 2 + 1)


def attend_kernel(
    begin_pair, low_ref, high_ref, place_ref, q_ref, kv_ref,
    o_ref, lse_ref, bias_ref, k_ref, vt_ref,
):
    step = pl.program_id(0)
    pair = step + begin_pair

    @pl.when(step == 0)
    def _():
        fill_bias(low_ref, high_ref, place_ref, bias_ref)

    @pl.when(new_pairing(step, pair))
    def _():
        k_ref[...] = pairing(kv_ref, pair, 0).astype(BF16)
        vt_ref[...] = pairing(kv_ref, pair, PAIR).T.astype(BF16)

    rows = q_ref.shape[0]
    queries = both_heads(q_ref[...])
    keys = k_ref[...]
    values_t = vt_ref[...]
    outs, totals = [], []
    for begin in range(0, 2 * rows, 256):
        scores = dot(keys, queries[begin : begin + 256], 1, 1) + bias_ref[:, begin : begin + 256]
        top = jnp.max(scores, axis=0, keepdims=True)
        probs = jnp.exp(scores - top)
        total = jnp.sum(probs, axis=0, keepdims=True)
        outs.append(dot(values_t, probs.astype(BF16), 1, 0) / total)
        totals.append(top + jnp.log(total))
    wide = jnp.concatenate(outs, axis=1)
    o_ref[...] = own_rows(wide, rows).T.astype(BF16)
    lse_ref[0] = jnp.concatenate(totals, axis=1)


def attend_back_kernel(
    begin_pair, low_ref, high_ref, place_ref, q_ref, g_ref, o_ref, lse_ref, kv_ref, *refs,
):
    dq_ref, dkv_ref, bias_ref, k_ref, kt_ref, v_ref, dk_ref, dv_ref = refs[-8:]
    step = pl.program_id(0)
    pair = step + begin_pair

    @pl.when(step == 0)
    def _():
        fill_bias(low_ref, high_ref, place_ref, bias_ref)
        dkv_ref[...] = refs[0][...] if begin_pair else jnp.zeros_like(dkv_ref)

    @pl.when(new_pairing(step, pair))
    def _():
        keys_now = pairing(kv_ref, pair, 0)
        k_ref[...] = keys_now.astype(BF16)
        kt_ref[...] = keys_now.T.astype(BF16)
        v_ref[...] = pairing(kv_ref, pair, PAIR).astype(BF16)
        dk_ref[...] = jnp.zeros_like(dk_ref)
        dv_ref[...] = jnp.zeros_like(dv_ref)

    rows = q_ref.shape[0]
    queries = both_heads(q_ref[...])
    grads = both_heads(g_ref[...])
    keys = k_ref[...]
    keys_t = kt_ref[...]
    values = v_ref[...]
    product = (g_ref[...].astype(F32) * o_ref[...].astype(F32)).T
    delta = jnp.concatenate(
        [
            jnp.sum(product[:HEAD], axis=0, keepdims=True),
            jnp.sum(product[HEAD:], axis=0, keepdims=True),
        ],
        axis=1,
    )
    lse = lse_ref[0]
    outs = []
    for begin in range(0, 2 * rows, 256):
        part = slice(begin, begin + 256)
        scores = dot(keys, queries[part], 1, 1) + bias_ref[:, part]
        probs = jnp.exp(scores - lse[:, part])
        grad_probs = dot(values, grads[part], 1, 1)
        grad_scores = (probs * (grad_probs - delta[:, part])).astype(BF16)
        outs.append(dot(keys_t, grad_scores, 1, 0))
        dk_ref[...] += dot(grad_scores, queries[part], 1, 0)
        dv_ref[...] += dot(probs.astype(BF16), grads[part], 1, 0)
    wide = jnp.concatenate(outs, axis=1)
    dq_ref[...] = own_rows(wide, rows).T * 0.125

    def fold(own_lanes):
        for at, sums in ((0, dk_ref), (PAIR, dv_ref)):
            sums_now = sums[...]
            lane = lax.broadcasted_iota(jnp.int32, sums_now.shape, 1)
            both = sums_now + pltpu.roll(sums_now, HEAD, 1)
            kept = jnp.where((lane < HEAD) == own_lanes, both, 0.0)
            dkv_ref[:, at : at + PAIR] += kept

    @pl.when(pair == PAIRS // 2 - 1)
    def _():
        fold(True)

    @pl.when(pair == PAIRS // 2)
    def _():
        dkv_ref[:, :PAIR] += dk_ref[...]
        dkv_ref[:, PAIR:] += dv_ref[...]

    @pl.when(pair == PAIRS - 1)
    def _():
        fold(False)


def whole(shape):
    return pl.BlockSpec(shape, lambda i: (0,) * len(shape))


def attend(low, high, place, queries, kv_all, begin, pairs):
    rows, count = queries.shape[0], place.shape[0]
    taken = pl.BlockSpec((rows, PAIR), lambda i: (0, i + begin))
    made = pl.BlockSpec((rows, PAIR), lambda i: (0, i))
    return pl.pallas_call(
        functools.partial(attend_kernel, begin),
        grid=(pairs,),
        in_specs=[whole((1, rows)), whole((1, rows)), whole((count, 1)), taken]
        + [whole((count, 2 * KVW))],
        out_specs=[made, pl.BlockSpec((1, 1, 2 * rows), lambda i: (i, 0, 0))],
        out_shape=[
            jax.ShapeDtypeStruct((rows, pairs * PAIR), BF16),
            jax.ShapeDtypeStruct((pairs, 1, 2 * rows), F32),
        ],
        scratch_shapes=[
            pltpu.VMEM((count, 2 * rows), F32),
            pltpu.VMEM((count, PAIR), BF16),
            pltpu.VMEM((PAIR, count), BF16),
        ],
        compiler_params=pltpu.CompilerParams(vmem_limit_bytes=VMEM_LIMIT),
        cost_estimate=pl.CostEstimate(flops=1, bytes_accessed=1, transcendentals=0),
        name="attend",
    )(low, high, place, queries, kv_all)


def attend_back(low, high, place, queries, grads, outs, lse, kv_all, begin, pairs, so_far):
    rows, count = queries.shape[0], place.shape[0]
    taken = pl.BlockSpec((rows, PAIR), lambda i: (0, i + begin))
    made = pl.BlockSpec((rows, PAIR), lambda i: (0, i))
    sums = whole((count, 2 * KVW))
    return pl.pallas_call(
        functools.partial(attend_back_kernel, begin),
        grid=(pairs,),
        in_specs=[whole((1, rows)), whole((1, rows)), whole((count, 1)), taken, taken, made]
        + [pl.BlockSpec((1, 1, 2 * rows), lambda i: (i, 0, 0)), sums]
        + [sums] * len(so_far),
        out_specs=[made, sums],
        out_shape=[
            jax.ShapeDtypeStruct((rows, pairs * PAIR), F32),
            jax.ShapeDtypeStruct((count, 2 * KVW), F32),
        ],
        scratch_shapes=[
            pltpu.VMEM((count, 2 * rows), F32),
            pltpu.VMEM((count, PAIR), BF16),
            pltpu.VMEM((PAIR, count), BF16),
            pltpu.VMEM((count, PAIR), BF16),
            pltpu.VMEM((count, PAIR), F32),
            pltpu.VMEM((count, PAIR), F32),
        ],
        compiler_params=pltpu.CompilerParams(vmem_limit_bytes=VMEM_LIMIT),
        cost_estimate=pl.CostEstimate(flops=1, bytes_accessed=1, transcendentals=0),
        name="attend_back",
    )(low, high, place, queries, grads, outs, lse, kv_all, *so_far)


def rms_scale(values_in):
    return lax.rsqrt(jnp.mean(values_in * values_in, axis=-1, keepdims=True) + EPSILON)


def angle_tables(places):
    exponent = jnp.arange(HEAD // 2, dtype=F32) * 2.0 / HEAD
    frequency = ROPE_BASE ** (-exponent)
    turn = places.astype(F32)[:, None] * frequency[None, :]
    cosine, sine = lax.optimization_barrier((jnp.cos(turn), jnp.sin(turn)))
    return jnp.concatenate([cosine] * 4, axis=1), jnp.concatenate([sine] * 4, axis=1)


def widen(table, width):
    return jnp.concatenate([table] * (width // PAIR), axis=1)


def first_halves(shape):
    return lax.broadcasted_iota(jnp.int32, shape, 1) % HEAD < HEAD // 2


def rotate(tensor, cosine, sine):
    half = HEAD // 2
    ahead, behind = jnp.roll(tensor, -half, axis=1), jnp.roll(tensor, half, axis=1)
    turned = jnp.where(first_halves(tensor.shape), -ahead, behind)
    width = tensor.shape[1]
    return tensor * widen(cosine, width) + turned * widen(sine, width)


def norm_back_rows(grad_in, row_data, scale_in, gain_in):
    gain_term = jnp.sum(grad_in * row_data * scale_in, axis=0, keepdims=True)
    grad_normed = grad_in * gain_in
    inner_mean = jnp.mean(grad_normed * row_data, axis=-1, keepdims=True)
    return (
        scale_in * grad_normed - row_data * scale_in * scale_in * scale_in * inner_mean,
        gain_term,
    )


def residual_back(me, kept, got, residual, scale_two, gain_two, cotangent, out_full):
    rows, width = residual.shape

    def body(me_ref, kept_ref, got_ref, res_ref, scale_ref, gain_ref, cot_ref, out_ref,
             grad_ref, branch_ref, attn_ref, term_ref):
        grad = kept_ref[...] + got_ref[...].astype(F32)
        path, term_ref[...] = norm_back_rows(grad, res_ref[...], scale_ref[...], gain_ref[...])
        full = cot_ref[...].astype(F32) + path
        grad_ref[...] = full
        branch_ref[...] = full.astype(BF16)
        attn_ref[...] = dot(full.astype(BF16), out_ref[...], 1, 1).astype(BF16)

    shapes = [
        jax.ShapeDtypeStruct((rows, width), F32),
        jax.ShapeDtypeStruct((rows, width), BF16),
        jax.ShapeDtypeStruct((rows, QW), BF16),
        jax.ShapeDtypeStruct((1, width), F32),
    ]
    arrays = (kept, got, residual, scale_two, gain_two[None, :], cotangent, out_full)
    return on_device(body, "residual_back", shapes, [], me, arrays)


def joined_back(
    me, dq_one, dq_two, kept, got, cosine, sine, qkv_t, tokens, scale_one, gain_one,
    grad_residual, normed_one, norm_two_term, seq_size, fsdp_size,
):
    rows, width = tokens.shape
    total = qkv_t.shape[0]
    each, lanes = total // fsdp_size, width // seq_size
    tall = padded(each)

    def body(me_ref, dq1_ref, dq2_ref, kept_ref, got_ref, cos_ref, sin_ref, w_ref, x_ref,
             scale_ref, gain_ref, res_ref, n1_ref, term_ref,
             tokens_ref, mine_ref, other_ref, held):
        kv = kept_ref[...] + got_ref[...].astype(F32)
        turned = jnp.concatenate([dq1_ref[...], dq2_ref[...], kv[:, :KVW]], axis=1)
        across = turned.shape[1]
        scaled = turned * widen(sin_ref[...], across)
        ahead = pltpu.roll(scaled, across - HEAD // 2, 1)
        behind = pltpu.roll(scaled, HEAD // 2, 1)
        turned = turned * widen(cos_ref[...], across) + jnp.where(
            first_halves(turned.shape), ahead, -behind
        )
        joined = jnp.concatenate([turned, kv[:, KVW:]], axis=1).astype(BF16)
        wide = joined.astype(F32)
        grad_normed = dot(joined, w_ref[...], 1, 0)
        path, one_term = norm_back_rows(
            grad_normed, x_ref[...].astype(F32), scale_ref[...], gain_ref[...]
        )
        tokens_ref[...] = res_ref[...] + path
        bias = jnp.sum(wide, axis=0, keepdims=True)
        weight = dot(wide.T.astype(BF16), n1_ref[...], 1, 0)
        vectors = [one_term, bias[:, : QW + KVW], bias[:, QW + KVW :], term_ref[...]]
        for f in range(fsdp_size):
            lines = []
            for vector in vectors:
                n = vector.shape[1] // fsdp_size
                piece = vector[:, f * n : (f + 1) * n]
                lines.append(jnp.concatenate([piece, jnp.zeros((1, lanes - n), F32)], axis=1))
            blank = jnp.zeros((tall - each, lanes), F32)
            below = [blank] * (tall > each) + lines + [jnp.zeros((12, lanes), F32)]
            for s in range(seq_size):
                part = weight[f * each : (f + 1) * each, s * lanes : (s + 1) * lanes]
                held[s, f] = jnp.concatenate([part] + below, axis=0).astype(BF16)
        core = me_ref[0] % 2
        for y in range(seq_size // 2):
            mine_ref[y] = held[2 * y + core]
            other_ref[y] = held[2 * y + 1 - core]

    block = (fsdp_size, tall + 16, lanes)
    half = jax.ShapeDtypeStruct((seq_size // 2,) + block, BF16)
    shapes = [jax.ShapeDtypeStruct((rows, width), F32), half, half]
    arrays = (
        dq_one, dq_two, kept, got, cosine, sine, qkv_t, tokens, scale_one, gain_one[None, :],
        grad_residual, normed_one, norm_two_term,
    )
    scratch = [pltpu.VMEM((seq_size,) + block, BF16)]
    return on_device(body, "joined_back", shapes, scratch, me, arrays)


def pad_row(vector, width):
    return jnp.pad(vector, (0, width - vector.shape[0]))[None, :]


def stack_from_lanes(array, count):
    rows, width = array.shape
    return jnp.transpose(array.reshape(rows, count, width // count), (1, 0, 2))


def per_device(
    seq_size, fsdp_size, tokens, segment_ids, positions, norm_one, qkv_weight, qkv_bias,
    out_weight, norm_two, gate_up_weight, down_weight, cotangent,
):
    my_seq, my_fsdp = lax.axis_index("seq"), lax.axis_index("fsdp")
    me = jnp.stack([my_seq, my_fsdp]).astype(jnp.int32)
    offsets = range(seq_size)
    row_count = tokens.shape[0]
    width = qkv_weight.shape[0]
    qkv_rows = qkv_weight.shape[1]
    strip = down_weight.shape[0] // seq_size
    tall = padded(strip)

    ff_cut = cut_ff(me, gate_up_weight, down_weight, seq_size)
    ff_share = [ff_cut[0]] + [swap(ff_cut[o], "seq", seq_size, o) for o in offsets if o]
    qkv_tall = padded(qkv_rows)
    packed = jnp.concatenate(
        [
            jnp.pad(qkv_weight.T, ((0, qkv_tall - qkv_rows), (0, 0))),
            pad_row(norm_one, width),
            pad_row(qkv_bias, width),
            pad_row(norm_two, width),
            jnp.zeros((13, width), BF16),
            out_weight,
        ],
        axis=0,
    )
    packed = after(packed, ff_cut[0])
    ff_block = join_lanes(me, ff_share)
    columns = ff_spread(
        after(column_gather(packed, fsdp_size), ff_block), fsdp_size
    )
    wide = qkv_tall + 16
    columns[0] = after(columns[0], ff_block)
    packed_pieces = [seq_gather(columns[m][:, :wide], seq_size) for m in sorted(columns)]
    ff_blocks = {0: ff_block}
    inner = fsdp_size // OUTER
    near = swap(ff_block, "fsdp", fsdp_size, inner)
    far = swap(ff_block, "fsdp", fsdp_size, 2 * inner)

    qkv_pieces = [[piece[o] for piece in packed_pieces] for o in offsets]
    qkv_t, vectors = join_both(me, qkv_pieces, qkv_tall)
    out_stack = jnp.concatenate([columns[m][:, wide:] for m in sorted(columns)], axis=0)
    out_stack = after(out_stack, packed_pieces[-1][seq_size // 2])
    out_blocks = seq_gather(out_stack, seq_size)

    own_x = ff_spread(ff_block, fsdp_size)
    last = swap(after(far, qkv_t), "fsdp", fsdp_size, inner)
    qkv_t = after(qkv_t, far, near, *own_x.values())[:, :qkv_rows].reshape(fsdp_size * qkv_rows, -1)
    gain_one = vectors[:, 0, : norm_one.shape[0]].reshape(-1).astype(F32)
    bias_full = vectors[:, 1, : qkv_bias.shape[0]].reshape(-1).astype(F32)
    gain_two = vectors[:, 2, : norm_two.shape[0]].reshape(-1).astype(F32)

    inputs = tokens.astype(F32)
    scale_one = rms_scale(inputs)
    normed_one = (inputs * scale_one * gain_one).astype(BF16)
    joined = dot(normed_one, qkv_t, 1, 1) + bias_full
    cosine, sine = angle_tables(positions)
    turned = rotate(joined[:, : QW + KVW], cosine, sine).astype(BF16)
    queries = turned[:, :QW] * jnp.asarray(0.125, BF16)
    kv_local = jnp.concatenate([turned[:, QW:], joined[:, QW + KVW :].astype(BF16)], axis=1)
    kv_all = lax.all_gather(kv_local, "seq", axis=0, tiled=True)
    cot_blocks = seq_gather(after(cotangent, kv_all), seq_size)
    row_place = jnp.arange(row_count, dtype=jnp.int32)
    high = my_seq * row_count + row_place
    low = high - positions
    place = jnp.arange(seq_size * row_count, dtype=jnp.int32)[:, None]
    low, high = low[None, :], high[None, :]
    split = PAIRS // 2 + 1
    spread = lambda block: ff_spread(block, fsdp_size)
    near_x = spread(after(near, kv_all))
    attn_one, lse_one = attend(
        low, high, place, after(queries, far), kv_all, 0, split
    )
    far_x = spread(after(far, kv_all))
    queries_two = after(queries, attn_one, cot_blocks[seq_size // 2], *near_x.values())
    attn_two, lse_two = attend(low, high, place, queries_two, kv_all, split, PAIRS - split)
    last_x = spread(last)
    for base, row in ((0, own_x), (inner, near_x), (2 * inner, far_x), (3 * inner, last_x)):
        ff_blocks.update({base + m: block for m, block in row.items()})
    attn_flat = jnp.concatenate([attn_one, attn_two], axis=1)

    out_list = [[out_blocks[o]] for o in offsets]
    out_list[0][0] = after(out_list[0][0], attn_one)
    out_full = join_both(me, out_list, out_weight.shape[0])[0].reshape(QW, -1)

    residual = inputs + dot(attn_flat, out_full, 1, 0)
    scale_two = rms_scale(residual)
    normed_two = (residual * scale_two * gain_two).astype(BF16)
    normed_blocks = {0: normed_two}
    bit = seq_size // 2
    while bit:
        if bit == 1:
            top = seq_size // 2
            normed_blocks[top] = after(normed_blocks[top], last, *far_x.values())
        normed_blocks.update(
            {o ^ bit: swap(b, "seq", seq_size, bit) for o, b in normed_blocks.items()}
        )
        bit //= 2
    (
        hidden, grad_gate, grad_up, kept, given, kept_layer, given_layer, normed_all, cot_all,
    ) = feed_forward(
        me,
        [ff_blocks[o] for o in range(fsdp_size)],
        [normed_blocks[o] for o in offsets],
        [cot_blocks[o] for o in offsets],
    )
    normed_all = normed_all.reshape(seq_size * row_count, -1)
    cot_all = cot_all.reshape(seq_size * row_count, -1)
    by_seq = lambda rows: rows.reshape(seq_size, row_count, -1)

    normed_sum = add(kept, swap(given, "seq", seq_size, 1))
    bit = 2
    while bit < seq_size:
        kept, given = halve(normed_sum, 1, my_seq // bit)
        got = swap(given, "seq", seq_size, bit)
        normed_sum = add(kept, got)
        bit *= 2
    normed_kept, normed_got = kept[0], got[0]
    layer_sum = add(kept_layer, swap(after(given_layer, given), "seq", seq_size, 1))
    kept_layer, given_layer = halve(layer_sum, 1, my_seq // 2)
    got_layer = swap(after(given_layer, normed_got), "seq", seq_size, 2)
    hidden = after(hidden, given)
    down_term = dot(hidden, cot_all, 0, 0).astype(BF16).reshape(fsdp_size, tall, -1)
    grad_gate, grad_up = after(grad_gate, down_term), after(grad_up, down_term)
    gate_term = dot(grad_gate, normed_all, 0, 0).astype(BF16).reshape(fsdp_size // 2, 2, tall, -1)
    up_term = dot(grad_up, normed_all, 0, 0).astype(BF16).reshape(fsdp_size // 2, 2, tall, -1)

    bits = list(reversed(fsdp_bits(fsdp_size)))

    def give(stack, at):
        kept, given = fsdp_halve(stack, fsdp_size, bits[at], my_fsdp, bits[:at])
        return kept, given

    def send(given, at):
        return swap(given, "fsdp", fsdp_size, bits[at])

    def finish(kept, got, at):
        stack = add(kept, got)
        for later in range(at + 1, len(bits)):
            kept, given = give(stack, later)
            stack = add(kept, send(given, later))
        return stack[0]

    kept_one, given = give(down_term, 0)
    got_one = send(given, 0)
    kept_two, given = give(jnp.concatenate([gate_term[:, 0], up_term[:, 0]], axis=0), 0)
    got_two = send(after(given, normed_got), 0)
    kept_three, given_three = give(jnp.concatenate([gate_term[:, 1], up_term[:, 1]], axis=0), 0)

    grad_residual, grad_branch, grad_attn, norm_two_term = residual_back(
        me, normed_kept, normed_got, residual, scale_two, gain_two, cotangent, out_full
    )
    grad_attn = after(grad_attn, gate_term, up_term, given_layer)
    dq_one, kv_terms = attend_back(
        low, high, place, queries, grad_attn, attn_one, lse_one, kv_all, 0, split, ()
    )
    got_one = after(got_one, dq_one)
    got_three = send(after(given_three, got_one), 0)
    kept_one, given_one = give(add(kept_one, got_one), 1)
    next_one = send(given_one, 1)
    queries_two = after(queries, kv_terms, given_one)
    dq_two, kv_terms = attend_back(
        low, high, place, queries_two, grad_attn, attn_two, lse_two, kv_all, split,
        PAIRS - split, (kv_terms,),
    )
    got_two = after(got_two, dq_two)
    kept_two, given = give(add(kept_two, got_two), 1)
    next_two = send(given, 1)
    kept, given = halve(after(by_seq(kv_terms), got_layer), 1, my_seq)
    kv_sum = add(kept, swap(given, "seq", seq_size, 1))
    bit = 2
    while bit < seq_size:
        kv_kept, given = halve(kv_sum, 1, my_seq // bit)
        given_kv = given
        kv_got = swap(given_kv, "seq", seq_size, bit)
        kv_sum = add(kv_kept, kv_got)
        bit *= 2
    kv_mine = kv_got

    attn_late = after(attn_flat, given_kv)
    out_term = stack_from_lanes(dot(attn_late, grad_branch, 0, 0).astype(BF16), seq_size)
    kept, given = halve(out_term, 1, my_seq)
    out_sum = add(kept, swap(given, "seq", seq_size, 1))
    grad_tokens, kept, given = joined_back(
        me, dq_one, dq_two, kv_kept[0], kv_got[0], cosine, sine, qkv_t, tokens, scale_one,
        gain_one, grad_residual, normed_one, norm_two_term, seq_size, fsdp_size,
    )

    got_three = after(got_three, grad_tokens)
    kept_three, given_last = give(add(kept_three, got_three), 1)
    next_three = send(given_last, 1)
    next_one, next_two = after(next_one, grad_tokens), after(next_two, grad_tokens)
    down_sum = finish(kept_one, next_one, 1)

    bit = 2
    while bit < seq_size:
        kept_out, given_out = halve(out_sum, 1, my_seq // bit)
        out_sum = add(kept_out, swap(after(given_out, kv_got), "seq", seq_size, bit))
        bit *= 2
    out_mine = out_sum[0].reshape(fsdp_size, -1, width)
    tail_sum = add(kept, swap(given, "seq", seq_size, 1))
    bit = 2
    while bit < seq_size:
        kept, given = halve(tail_sum, 1, my_seq // bit)
        tail_sum = add(kept, swap(given, "seq", seq_size, bit))
        bit *= 2
    tail_mine = tail_sum[0]
    layer_sum = add(kept_layer, got_layer)
    bit = 4
    while bit < seq_size:
        kept, given = halve(layer_sum, 1, my_seq // bit)
        layer_sum = add(kept, swap(given, "seq", seq_size, bit))
        bit *= 2
    layer_out = residual + layer_sum[0]
    one_sum = finish(kept_two, next_two, 1)
    two_sum = finish(kept_three, next_three, 1)

    ff_back = cut_lanes(me, (one_sum, two_sum, down_sum), seq_size)
    ff_got = [ff_back[0]] + [swap(ff_back[o], "seq", seq_size, o) for o in offsets if o]
    grad_gate_up, grad_down = join_ff(me, ff_got, strip)

    tail_sum = fsdp_scatter(
        after(jnp.concatenate([tail_mine, out_mine], axis=1), next_two),
        fsdp_size,
        my_fsdp,
        next_three,

    )
    lengths = [width * seq_size, QW + KVW, KVW, width * seq_size]
    pieces = [tail_sum[qkv_tall + i, : n // fsdp_size] for i, n in enumerate(lengths)]
    return (
        layer_out.astype(BF16),
        grad_tokens,
        pieces[0],
        tail_sum[:qkv_rows].T,
        pieces[1],
        pieces[2],
        tail_sum[qkv_tall + 16 :],
        pieces[3],
        grad_gate_up,
        grad_down,
    )


def solution(mesh):
    rows, both = P(("fsdp", "seq"), None), P(("fsdp", "seq"))
    return jax.shard_map(
        functools.partial(per_device, mesh.shape["seq"], mesh.shape["fsdp"]),
        mesh=mesh,
        in_specs=(
            rows, both, both, P("fsdp"), P("seq", "fsdp"), P("fsdp"), P("fsdp", "seq"),
            P("fsdp"), P("seq", "fsdp"), P("fsdp", "seq"), rows,
        ),
        out_specs=(
            rows, rows, P("fsdp"), P("seq", "fsdp"), P("fsdp"), P("fsdp"), P("fsdp", "seq"),
            P("fsdp"), P("seq", "fsdp"), P("fsdp", "seq"),
        ),
        check_vma=False,
    )
```

```python
import functools

import jax
import jax.numpy as jnp
from jax import lax
from jax.experimental import pallas as pl
from jax.experimental.pallas import tpu as pltpu
from jax.sharding import PartitionSpec as P

HEADS = 14
KV_HEADS = 2
HEAD = 64
FF = 4864
QW = 896
KVW = 128
PAIR = 2 * HEAD
PAIRS = HEADS // 2
OUTER = 4

EPSILON = 1e-06
ROPE_BASE = 1000000.0
MASKED = -1e30
VMEM_LIMIT = 50 * 1024 * 1024

F32 = jnp.float32
BF16 = jnp.bfloat16


def dot(left, right, left_dim, right_dim):
    return lax.dot_general(
        left, right, (((left_dim,), (right_dim,)), ((), ())), preferred_element_type=F32
    )


def swap(block, axis, size, bits):
    return lax.ppermute(block, axis, [(i, i ^ bits) for i in range(size)])


def after(array, *others):
    return lax.optimization_barrier((array,) + others)[0]


def seq_gather(block, size):
    blocks = {0: block}
    bit = size // 2
    while bit:
        blocks.update({o ^ bit: swap(b, "seq", size, bit) for o, b in blocks.items()})
        bit //= 2
    return blocks


def fsdp_bits(size):
    inner = size // OUTER
    outer_bits, inner_bits = [], []
    bit = 1
    while bit < size:
        (outer_bits if bit >= inner else inner_bits).append(bit)
        bit *= 2
    return outer_bits[::-1] + inner_bits


def column_gather(block, size):
    inner = size // OUTER
    return jnp.stack([block] + [swap(block, "fsdp", size, k * inner) for k in range(1, OUTER)])


def ff_spread(block, size):
    blocks = {0: block}
    for bit in fsdp_bits(size)[2:]:
        blocks.update({o ^ bit: swap(b, "fsdp", size, bit) for o, b in blocks.items()})
    return blocks


def halve(stack, bit, me):
    above = stack.shape[0] // (2 * bit)
    cut = stack.reshape((above, 2, bit) + stack.shape[1:])
    digit = (me // bit) % 2
    kept = lax.dynamic_index_in_dim(cut, digit, 1, keepdims=False)
    given = lax.dynamic_index_in_dim(cut, 1 - digit, 1, keepdims=False)
    merge = lambda part: part.reshape((above * bit,) + stack.shape[1:])
    return merge(kept), merge(given).astype(BF16)


def add(kept, got):
    return kept.astype(F32) + got.astype(F32)


def seq_scatter(stack, size, me):
    bit = 1
    while bit < size:
        kept, given = halve(stack, 1, me // bit)
        stack = add(kept, swap(given, "seq", size, bit))
        bit *= 2
    return stack[0]


def fsdp_halve(stack, size, bit, me, resolved):
    place = bit
    digit = me // bit
    for taken in resolved:
        if taken < bit:
            place //= 2
    kept, given = halve(stack, place, digit * place)
    return kept, given


def fsdp_scatter(stack, size, me, earlier):
    inner = size // OUTER
    resolved = []
    for bit in reversed(fsdp_bits(size)[2:]):
        kept, given = fsdp_halve(stack, size, bit, me, resolved)
        stack = add(kept, swap(given, "fsdp", size, bit))
        resolved.append(bit)
    place = me // inner
    low = after(stack.astype(BF16), earlier)
    total = lax.dynamic_index_in_dim(stack, place, 0, keepdims=False)
    for k in range(1, OUTER):
        given = lax.dynamic_index_in_dim(low, place ^ k, 0, keepdims=False)
        total = add(total, swap(given, "fsdp", size, k * inner))
    return total


def on_device(body, name, out_shapes, scratch, me, arrays):
    vmem = pl.BlockSpec(memory_space=pltpu.VMEM)
    return pl.pallas_call(
        body,
        in_specs=[pl.BlockSpec(memory_space=pltpu.SMEM)] + [vmem] * len(arrays),
        out_specs=[vmem] * len(out_shapes),
        out_shape=out_shapes,
        scratch_shapes=scratch,
        compiler_params=pltpu.CompilerParams(vmem_limit_bytes=VMEM_LIMIT),
        name=name,
    )(me, *arrays)


def padded(rows):
    return -(-rows // 16) * 16


def cut_ff(me, gate_up_weight, down_weight, size):
    width = gate_up_weight.shape[0]
    half = down_weight.shape[0]
    strip = half // size
    tall = padded(strip)

    def body(me_ref, gu_ref, d_ref, *refs):
        outs, held = refs[:size], refs[size]
        turned = gu_ref[...].astype(F32).T
        down = d_ref[...].astype(F32)
        blank = jnp.zeros((tall - strip, width), F32)
        for q in range(size):
            one = turned[q * strip : (q + 1) * strip]
            two = turned[half + q * strip : half + (q + 1) * strip]
            three = down[q * strip : (q + 1) * strip]
            parts = [one, blank, two, blank, three, blank]
            held[q] = jnp.concatenate(parts, axis=0).astype(BF16)
        for o in range(size):
            outs[o][...] = held[me_ref[0] ^ o]

    shape = jax.ShapeDtypeStruct((3 * tall, width), BF16)
    scratch = [pltpu.VMEM((size, 3 * tall, width), BF16)]
    return on_device(body, "cut_ff", [shape] * size, scratch, me, (gate_up_weight, down_weight))


def join_lanes(me, blocks):
    size = len(blocks)
    rows, width = blocks[0].shape

    def body(me_ref, *refs):
        ins, out, held = refs[:size], refs[size], refs[size + 1]
        for o in range(size):
            held[me_ref[0] ^ o] = ins[o][...]
        out[...] = jnp.concatenate([held[q].astype(F32) for q in range(size)], 1).astype(BF16)

    return on_device(
        body,
        "join_lanes",
        [jax.ShapeDtypeStruct((rows, size * width), BF16)],
        [pltpu.VMEM((size, rows, width), BF16)],
        me,
        blocks,
    )[0]


def join_both(me, pieces, rows):
    size, parts_each = len(pieces), len(pieces[0])
    _, tall, width = pieces[0][0].shape
    count = sum(part.shape[0] for part in pieces[0])
    inner = count // OUTER
    order = [k * inner + m for m in range(inner) for k in range(OUTER)]
    shapes = [jax.ShapeDtypeStruct((count, rows, size * width), BF16)]
    if tall > rows:
        shapes.append(jax.ShapeDtypeStruct((count, tall - rows, width), BF16))

    def body(me_ref, *refs):
        ins, out, held = refs[: size * parts_each], refs[size * parts_each], refs[-1]
        for o in range(size):
            at = 0
            for part in ins[o * parts_each : (o + 1) * parts_each]:
                for j in range(part.shape[0]):
                    place = me_ref[1] ^ order[at]
                    held[me_ref[0] ^ o, place] = part[j]
                    if tall > rows and o == 0:
                        refs[size * parts_each + 1][place] = part[j, rows:]
                    at += 1
        for f in range(count):
            parts = [held[q, f, :rows].astype(F32) for q in range(size)]
            out[f] = jnp.concatenate(parts, axis=1).astype(BF16)

    return on_device(
        body,
        "join_both",
        shapes,
        [pltpu.VMEM((size, count, tall, width), BF16)],
        me,
        [block for row in pieces for block in row],
    )


def cut_lanes(me, sums, size):
    rows = sum(s.shape[0] for s in sums)
    width = sums[0].shape[1] // size

    def body(me_ref, *refs):
        ins, outs, held = refs[: len(sums)], refs[len(sums) : -1], refs[-1]
        whole = jnp.concatenate([r[...] for r in ins], axis=0)
        for q in range(size):
            held[q] = whole[:, q * width : (q + 1) * width].astype(BF16)
        for o in range(size):
            outs[o][...] = held[me_ref[0] ^ o]

    shape = jax.ShapeDtypeStruct((rows, width), BF16)
    scratch = [pltpu.VMEM((size, rows, width), BF16)]
    return on_device(body, "cut_lanes", [shape] * size, scratch, me, sums)


def join_ff(me, blocks, strip):
    size = len(blocks)
    rows, width = blocks[0].shape
    tall = rows // 3

    def body(me_ref, *refs):
        ins, gu, down, held = refs[:size], refs[size], refs[size + 1], refs[size + 2]
        for o in range(size):
            held[me_ref[0] ^ o] = ins[o][...].astype(F32)
        cut = [
            [held[q, i * tall : i * tall + strip] for q in range(size)] for i in range(3)
        ]
        gu[...] = jnp.concatenate(cut[0] + cut[1], axis=0).T
        down[...] = jnp.concatenate(cut[2], axis=0)

    return on_device(
        body,
        "join_ff",
        [
            jax.ShapeDtypeStruct((width, 2 * size * strip), F32),
            jax.ShapeDtypeStruct((size * strip, width), F32),
        ],
        [pltpu.VMEM((size, rows, width), F32)],
        me,
        blocks,
    )


def feed_forward(me, weight_blocks, row_blocks, cot_blocks):
    count, size = len(weight_blocks), len(row_blocks)
    rows, width = row_blocks[0].shape
    tall = weight_blocks[0].shape[0] // 3
    units = count * tall
    step_units = 256

    def body(me_ref, *refs):
        blocks = refs[:count]
        xs, gs = refs[count : count + size], refs[count + size : count + 2 * size]
        outs = refs[count + 2 * size : count + 2 * size + 9]
        hid, gg, gu, gn_kept, gn_given, part_kept, part_given, x_out, g_out = outs
        gu_w, d_w, x_all, g_all, held, sems = refs[count + 2 * size + 9 :]
        step = pl.program_id(0)
        core = me_ref[0] % 2
        handed = [
            pltpu.make_async_copy(src, dst, sems.at[2 * count + 2 * size + i])
            for i, (src, dst) in enumerate(((x_all, x_out), (g_all, g_out)))
        ]

        @pl.when(step == 0)
        def _():
            copies = []
            for o in range(count):
                f = me_ref[1] ^ o
                copies.append((blocks[o].at[pl.ds(0, 2 * tall)], gu_w.at[f]))
                copies.append((blocks[o].at[pl.ds(2 * tall, tall)], d_w.at[f]))
            for o in range(size):
                copies.append((xs[o], x_all.at[me_ref[0] ^ o]))
                copies.append((gs[o], g_all.at[me_ref[0] ^ o]))
            started = [
                pltpu.make_async_copy(src, dst, sems.at[i]) for i, (src, dst) in enumerate(copies)
            ]
            for copy in started:
                copy.start()
            for copy in started:
                copy.wait()
            for copy in handed:
                copy.start()

        x = x_all[pl.ds(2 * step, 2)].reshape(2 * rows, width)
        g = g_all[pl.ds(2 * step, 2)].reshape(2 * rows, width)
        gate_w = gu_w[: count // 2].reshape(units, width)
        up_w = gu_w[count // 2 :].reshape(units, width)
        down_w = d_w[...].reshape(units, width)
        for begin in range(0, units, step_units):
            at = slice(begin, begin + step_units)
            gate = dot(x, gate_w[at], 1, 1)
            up = dot(x, up_w[at], 1, 1)
            grad_hidden = dot(g, down_w[at], 1, 1)
            sigmoid = 0.5 * jnp.tanh(0.5 * gate) + 0.5
            silu = gate * sigmoid
            hid[:, at] = (silu * up).astype(BF16)
            gg[:, at] = (grad_hidden * up * (sigmoid + silu * (1.0 - sigmoid))).astype(BF16)
            gu[:, at] = (grad_hidden * silu).astype(BF16)

        def hand_out(value, kept, given):
            held[...] = value.astype(BF16).reshape(2, rows, width)
            kept[0] = held[core]
            given[0] = held[1 - core]

        hand_out(dot(gg[...], gate_w, 1, 0) + dot(gu[...], up_w, 1, 0), gn_kept, gn_given)
        hand_out(dot(hid[...], down_w, 1, 0), part_kept, part_given)

        @pl.when(step == size // 2 - 1)
        def _():
            for copy in handed:
                copy.wait()

    hbm = pl.BlockSpec(memory_space=pl.ANY)
    by_rows = pl.BlockSpec((2 * rows, units), lambda i: (i, 0))
    by_pair = pl.BlockSpec((1, rows, width), lambda i: (i, 0, 0))
    like = jax.ShapeDtypeStruct
    return pl.pallas_call(
        body,
        grid=(size // 2,),
        in_specs=[pl.BlockSpec(memory_space=pltpu.SMEM)]
        + [hbm] * (count + 2 * size),
        out_specs=[by_rows] * 3 + [by_pair] * 4 + [hbm] * 2,
        out_shape=[like((size * rows, units), BF16)] * 3
        + [like((size // 2, rows, width), BF16)] * 4
        + [like((size, rows, width), BF16)] * 2,
        scratch_shapes=[
            pltpu.VMEM((count, 2 * tall, width), BF16),
            pltpu.VMEM((count, tall, width), BF16),
            pltpu.VMEM((size, rows, width), BF16),
            pltpu.VMEM((size, rows, width), BF16),
            pltpu.VMEM((2, rows, width), BF16),
            pltpu.SemaphoreType.DMA((2 * count + 2 * size + 2,)),
        ],
        compiler_params=pltpu.CompilerParams(vmem_limit_bytes=VMEM_LIMIT),
        cost_estimate=pl.CostEstimate(flops=1, bytes_accessed=1, transcendentals=0),
        name="feed_forward",
    )(me, *weight_blocks, *row_blocks, *cot_blocks)


def both_heads(pair):
    lane = lax.broadcasted_iota(jnp.int32, pair.shape, 1)
    zero = jnp.zeros_like(pair)
    return jnp.concatenate(
        [jnp.where(lane < HEAD, pair, zero), jnp.where(lane < HEAD, zero, pair)], axis=0
    )


def fill_bias(low_ref, high_ref, place_ref, bias_ref):
    place = place_ref[...]
    allowed = (place >= low_ref[...]) & (place <= high_ref[...])
    bias = jnp.where(allowed, 0.0, MASKED).astype(F32)
    rows = bias.shape[1]
    bias_ref[:, :rows] = bias
    bias_ref[:, rows:] = bias


def own_rows(wide, rows):
    return jnp.concatenate([wide[:HEAD, :rows], wide[HEAD:, rows:]], axis=0)


def pairing(kv_ref, pair, begin):
    both = kv_ref[:, begin : begin + PAIR].astype(F32)
    crossed = pltpu.roll(both, HEAD, 1)
    lane = lax.broadcasted_iota(jnp.int32, both.shape, 1)
    first = jnp.where(pair <= PAIRS // 2, both, crossed)
    second = jnp.where(pair < PAIRS // 2, crossed, both)
    return jnp.where(lane < HEAD, first, second)


def new_pairing(step, pair):
    return (step == 0) | (pair == PAIRS // 2) | (pair == PAIRS // 2 + 1)


def attend_kernel(
    begin_pair, low_ref, high_ref, place_ref, q_ref, kv_ref,
    o_ref, lse_ref, bias_ref, k_ref, vt_ref,
):
    step = pl.program_id(0)
    pair = step + begin_pair

    @pl.when(step == 0)
    def _():
        fill_bias(low_ref, high_ref, place_ref, bias_ref)

    @pl.when(new_pairing(step, pair))
    def _():
        k_ref[...] = pairing(kv_ref, pair, 0).astype(BF16)
        vt_ref[...] = pairing(kv_ref, pair, PAIR).T.astype(BF16)

    rows = q_ref.shape[0]
    queries = both_heads(q_ref[...])
    keys = k_ref[...]
    values_t = vt_ref[...]
    outs, totals = [], []
    for begin in range(0, 2 * rows, 256):
        scores = dot(keys, queries[begin : begin + 256], 1, 1) + bias_ref[:, begin : begin + 256]
        top = jnp.max(scores, axis=0, keepdims=True)
        probs = jnp.exp(scores - top)
        total = jnp.sum(probs, axis=0, keepdims=True)
        outs.append(dot(values_t, probs.astype(BF16), 1, 0) / total)
        totals.append(top + jnp.log(total))
    wide = jnp.concatenate(outs, axis=1)
    o_ref[...] = own_rows(wide, rows).T.astype(BF16)
    lse_ref[0] = jnp.concatenate(totals, axis=1)


def attend_back_kernel(
    begin_pair, low_ref, high_ref, place_ref, q_ref, g_ref, o_ref, lse_ref, kv_ref, *refs,
):
    dq_ref, dkv_ref, bias_ref, k_ref, kt_ref, v_ref, dk_ref, dv_ref = refs[-8:]
    step = pl.program_id(0)
    pair = step + begin_pair

    @pl.when(step == 0)
    def _():
        fill_bias(low_ref, high_ref, place_ref, bias_ref)
        dkv_ref[...] = refs[0][...] if begin_pair else jnp.zeros_like(dkv_ref)

    @pl.when(new_pairing(step, pair))
    def _():
        keys_now = pairing(kv_ref, pair, 0)
        k_ref[...] = keys_now.astype(BF16)
        kt_ref[...] = keys_now.T.astype(BF16)
        v_ref[...] = pairing(kv_ref, pair, PAIR).astype(BF16)
        dk_ref[...] = jnp.zeros_like(dk_ref)
        dv_ref[...] = jnp.zeros_like(dv_ref)

    rows = q_ref.shape[0]
    queries = both_heads(q_ref[...])
    grads = both_heads(g_ref[...])
    keys = k_ref[...]
    keys_t = kt_ref[...]
    values = v_ref[...]
    product = (g_ref[...].astype(F32) * o_ref[...].astype(F32)).T
    delta = jnp.concatenate(
        [
            jnp.sum(product[:HEAD], axis=0, keepdims=True),
            jnp.sum(product[HEAD:], axis=0, keepdims=True),
        ],
        axis=1,
    )
    lse = lse_ref[0]
    outs = []
    for begin in range(0, 2 * rows, 256):
        part = slice(begin, begin + 256)
        scores = dot(keys, queries[part], 1, 1) + bias_ref[:, part]
        probs = jnp.exp(scores - lse[:, part])
        grad_probs = dot(values, grads[part], 1, 1)
        grad_scores = (probs * (grad_probs - delta[:, part])).astype(BF16)
        outs.append(dot(keys_t, grad_scores, 1, 0))
        dk_ref[...] += dot(grad_scores, queries[part], 1, 0)
        dv_ref[...] += dot(probs.astype(BF16), grads[part], 1, 0)
    wide = jnp.concatenate(outs, axis=1)
    dq_ref[...] = own_rows(wide, rows).T * 0.125

    def fold(own_lanes):
        for at, sums in ((0, dk_ref), (PAIR, dv_ref)):
            sums_now = sums[...]
            lane = lax.broadcasted_iota(jnp.int32, sums_now.shape, 1)
            both = sums_now + pltpu.roll(sums_now, HEAD, 1)
            kept = jnp.where((lane < HEAD) == own_lanes, both, 0.0)
            dkv_ref[:, at : at + PAIR] += kept

    @pl.when(pair == PAIRS // 2 - 1)
    def _():
        fold(True)

    @pl.when(pair == PAIRS // 2)
    def _():
        dkv_ref[:, :PAIR] += dk_ref[...]
        dkv_ref[:, PAIR:] += dv_ref[...]

    @pl.when(pair == PAIRS - 1)
    def _():
        fold(False)


def whole(shape):
    return pl.BlockSpec(shape, lambda i: (0,) * len(shape))


def attend(low, high, place, queries, kv_all, begin, pairs):
    rows, count = queries.shape[0], place.shape[0]
    taken = pl.BlockSpec((rows, PAIR), lambda i: (0, i + begin))
    made = pl.BlockSpec((rows, PAIR), lambda i: (0, i))
    return pl.pallas_call(
        functools.partial(attend_kernel, begin),
        grid=(pairs,),
        in_specs=[whole((1, rows)), whole((1, rows)), whole((count, 1)), taken]
        + [whole((count, 2 * KVW))],
        out_specs=[made, pl.BlockSpec((1, 1, 2 * rows), lambda i: (i, 0, 0))],
        out_shape=[
            jax.ShapeDtypeStruct((rows, pairs * PAIR), BF16),
            jax.ShapeDtypeStruct((pairs, 1, 2 * rows), F32),
        ],
        scratch_shapes=[
            pltpu.VMEM((count, 2 * rows), F32),
            pltpu.VMEM((count, PAIR), BF16),
            pltpu.VMEM((PAIR, count), BF16),
        ],
        compiler_params=pltpu.CompilerParams(vmem_limit_bytes=VMEM_LIMIT),
        cost_estimate=pl.CostEstimate(flops=1, bytes_accessed=1, transcendentals=0),
        name="attend",
    )(low, high, place, queries, kv_all)


def attend_back(low, high, place, queries, grads, outs, lse, kv_all, begin, pairs, so_far):
    rows, count = queries.shape[0], place.shape[0]
    taken = pl.BlockSpec((rows, PAIR), lambda i: (0, i + begin))
    made = pl.BlockSpec((rows, PAIR), lambda i: (0, i))
    sums = whole((count, 2 * KVW))
    return pl.pallas_call(
        functools.partial(attend_back_kernel, begin),
        grid=(pairs,),
        in_specs=[whole((1, rows)), whole((1, rows)), whole((count, 1)), taken, taken, made]
        + [pl.BlockSpec((1, 1, 2 * rows), lambda i: (i, 0, 0)), sums]
        + [sums] * len(so_far),
        out_specs=[made, sums],
        out_shape=[
            jax.ShapeDtypeStruct((rows, pairs * PAIR), F32),
            jax.ShapeDtypeStruct((count, 2 * KVW), F32),
        ],
        scratch_shapes=[
            pltpu.VMEM((count, 2 * rows), F32),
            pltpu.VMEM((count, PAIR), BF16),
            pltpu.VMEM((PAIR, count), BF16),
            pltpu.VMEM((count, PAIR), BF16),
            pltpu.VMEM((count, PAIR), F32),
            pltpu.VMEM((count, PAIR), F32),
        ],
        compiler_params=pltpu.CompilerParams(vmem_limit_bytes=VMEM_LIMIT),
        cost_estimate=pl.CostEstimate(flops=1, bytes_accessed=1, transcendentals=0),
        name="attend_back",
    )(low, high, place, queries, grads, outs, lse, kv_all, *so_far)


def rms_scale(values_in):
    return lax.rsqrt(jnp.mean(values_in * values_in, axis=-1, keepdims=True) + EPSILON)


def angle_tables(places):
    exponent = jnp.arange(HEAD // 2, dtype=F32) * 2.0 / HEAD
    frequency = ROPE_BASE ** (-exponent)
    turn = places.astype(F32)[:, None] * frequency[None, :]
    cosine, sine = lax.optimization_barrier((jnp.cos(turn), jnp.sin(turn)))
    return jnp.concatenate([cosine] * 4, axis=1), jnp.concatenate([sine] * 4, axis=1)


def widen(table, width):
    return jnp.concatenate([table] * (width // PAIR), axis=1)


def first_halves(shape):
    return lax.broadcasted_iota(jnp.int32, shape, 1) % HEAD < HEAD // 2


def rotate(tensor, cosine, sine):
    half = HEAD // 2
    ahead, behind = jnp.roll(tensor, -half, axis=1), jnp.roll(tensor, half, axis=1)
    turned = jnp.where(first_halves(tensor.shape), -ahead, behind)
    width = tensor.shape[1]
    return tensor * widen(cosine, width) + turned * widen(sine, width)


def norm_back_rows(grad_in, row_data, scale_in, gain_in):
    gain_term = jnp.sum(grad_in * row_data * scale_in, axis=0, keepdims=True)
    grad_normed = grad_in * gain_in
    inner_mean = jnp.mean(grad_normed * row_data, axis=-1, keepdims=True)
    return (
        scale_in * grad_normed - row_data * scale_in * scale_in * scale_in * inner_mean,
        gain_term,
    )


def residual_back(me, kept, got, residual, scale_two, gain_two, cotangent, out_full):
    rows, width = residual.shape

    def body(me_ref, kept_ref, got_ref, res_ref, scale_ref, gain_ref, cot_ref, out_ref,
             grad_ref, branch_ref, attn_ref, term_ref):
        grad = kept_ref[...] + got_ref[...].astype(F32)
        path, term_ref[...] = norm_back_rows(grad, res_ref[...], scale_ref[...], gain_ref[...])
        full = cot_ref[...].astype(F32) + path
        grad_ref[...] = full
        branch_ref[...] = full.astype(BF16)
        attn_ref[...] = dot(full.astype(BF16), out_ref[...], 1, 1).astype(BF16)

    shapes = [
        jax.ShapeDtypeStruct((rows, width), F32),
        jax.ShapeDtypeStruct((rows, width), BF16),
        jax.ShapeDtypeStruct((rows, QW), BF16),
        jax.ShapeDtypeStruct((1, width), F32),
    ]
    arrays = (kept, got, residual, scale_two, gain_two[None, :], cotangent, out_full)
    return on_device(body, "residual_back", shapes, [], me, arrays)


def joined_back(
    me, dq_one, dq_two, kept, got, cosine, sine, qkv_t, tokens, scale_one, gain_one,
    grad_residual, normed_one, norm_two_term, seq_size, fsdp_size,
):
    rows, width = tokens.shape
    total = qkv_t.shape[0]
    each, lanes = total // fsdp_size, width // seq_size
    tall = padded(each)

    def body(me_ref, dq1_ref, dq2_ref, kept_ref, got_ref, cos_ref, sin_ref, w_ref, x_ref,
             scale_ref, gain_ref, res_ref, n1_ref, term_ref,
             tokens_ref, mine_ref, other_ref, held):
        kv = kept_ref[...] + got_ref[...].astype(F32)
        turned = jnp.concatenate([dq1_ref[...], dq2_ref[...], kv[:, :KVW]], axis=1)
        across = turned.shape[1]
        scaled = turned * widen(sin_ref[...], across)
        ahead = pltpu.roll(scaled, across - HEAD // 2, 1)
        behind = pltpu.roll(scaled, HEAD // 2, 1)
        turned = turned * widen(cos_ref[...], across) + jnp.where(
            first_halves(turned.shape), ahead, -behind
        )
        joined = jnp.concatenate([turned, kv[:, KVW:]], axis=1).astype(BF16)
        wide = joined.astype(F32)
        grad_normed = dot(joined, w_ref[...], 1, 0)
        path, one_term = norm_back_rows(
            grad_normed, x_ref[...].astype(F32), scale_ref[...], gain_ref[...]
        )
        tokens_ref[...] = res_ref[...] + path
        bias = jnp.sum(wide, axis=0, keepdims=True)
        weight = dot(wide.T.astype(BF16), n1_ref[...], 1, 0)
        vectors = [one_term, bias[:, : QW + KVW], bias[:, QW + KVW :], term_ref[...]]
        for f in range(fsdp_size):
            lines = []
            for vector in vectors:
                n = vector.shape[1] // fsdp_size
                piece = vector[:, f * n : (f + 1) * n]
                lines.append(jnp.concatenate([piece, jnp.zeros((1, lanes - n), F32)], axis=1))
            blank = jnp.zeros((tall - each, lanes), F32)
            below = [blank] * (tall > each) + lines + [jnp.zeros((12, lanes), F32)]
            for s in range(seq_size):
                part = weight[f * each : (f + 1) * each, s * lanes : (s + 1) * lanes]
                held[s, f] = jnp.concatenate([part] + below, axis=0).astype(BF16)
        core = me_ref[0] % 2
        for y in range(seq_size // 2):
            mine_ref[y] = held[2 * y + core]
            other_ref[y] = held[2 * y + 1 - core]

    block = (fsdp_size, tall + 16, lanes)
    half = jax.ShapeDtypeStruct((seq_size // 2,) + block, BF16)
    shapes = [jax.ShapeDtypeStruct((rows, width), F32), half, half]
    arrays = (
        dq_one, dq_two, kept, got, cosine, sine, qkv_t, tokens, scale_one, gain_one[None, :],
        grad_residual, normed_one, norm_two_term,
    )
    scratch = [pltpu.VMEM((seq_size,) + block, BF16)]
    return on_device(body, "joined_back", shapes, scratch, me, arrays)


def pad_row(vector, width):
    return jnp.pad(vector, (0, width - vector.shape[0]))[None, :]


def stack_from_lanes(array, count):
    rows, width = array.shape
    return jnp.transpose(array.reshape(rows, count, width // count), (1, 0, 2))


def per_device(
    seq_size, fsdp_size, tokens, segment_ids, positions, norm_one, qkv_weight, qkv_bias,
    out_weight, norm_two, gate_up_weight, down_weight, cotangent,
):
    my_seq, my_fsdp = lax.axis_index("seq"), lax.axis_index("fsdp")
    me = jnp.stack([my_seq, my_fsdp]).astype(jnp.int32)
    offsets = range(seq_size)
    row_count = tokens.shape[0]
    width = qkv_weight.shape[0]
    qkv_rows = qkv_weight.shape[1]
    strip = down_weight.shape[0] // seq_size
    tall = padded(strip)

    ff_cut = cut_ff(me, gate_up_weight, down_weight, seq_size)
    ff_share = [ff_cut[0]] + [swap(ff_cut[o], "seq", seq_size, o) for o in offsets if o]
    qkv_tall = padded(qkv_rows)
    packed = jnp.concatenate(
        [
            jnp.pad(qkv_weight.T, ((0, qkv_tall - qkv_rows), (0, 0))),
            pad_row(norm_one, width),
            pad_row(qkv_bias, width),
            pad_row(norm_two, width),
            jnp.zeros((13, width), BF16),
            out_weight,
        ],
        axis=0,
    )
    packed = after(packed, ff_cut[0])
    ff_block = join_lanes(me, ff_share)
    columns = ff_spread(
        after(column_gather(packed, fsdp_size), ff_block), fsdp_size
    )
    wide = qkv_tall + 16
    columns[0] = after(columns[0], ff_block)
    packed_pieces = [seq_gather(columns[m][:, :wide], seq_size) for m in sorted(columns)]
    ff_blocks = {0: ff_block}
    inner = fsdp_size // OUTER
    near = swap(ff_block, "fsdp", fsdp_size, inner)
    far = swap(ff_block, "fsdp", fsdp_size, 2 * inner)

    qkv_pieces = [[piece[o] for piece in packed_pieces] for o in offsets]
    qkv_t, vectors = join_both(me, qkv_pieces, qkv_tall)
    out_stack = jnp.concatenate([columns[m][:, wide:] for m in sorted(columns)], axis=0)
    out_stack = after(out_stack, packed_pieces[-1][seq_size // 2])
    out_blocks = seq_gather(out_stack, seq_size)

    own_x = ff_spread(ff_block, fsdp_size)
    last = swap(after(far, qkv_t), "fsdp", fsdp_size, inner)
    qkv_t = after(qkv_t, far, near, *own_x.values())[:, :qkv_rows].reshape(fsdp_size * qkv_rows, -1)
    gain_one = vectors[:, 0, : norm_one.shape[0]].reshape(-1).astype(F32)
    bias_full = vectors[:, 1, : qkv_bias.shape[0]].reshape(-1).astype(F32)
    gain_two = vectors[:, 2, : norm_two.shape[0]].reshape(-1).astype(F32)

    inputs = tokens.astype(F32)
    scale_one = rms_scale(inputs)
    normed_one = (inputs * scale_one * gain_one).astype(BF16)
    joined = dot(normed_one, qkv_t, 1, 1) + bias_full
    cosine, sine = angle_tables(positions)
    turned = rotate(joined[:, : QW + KVW], cosine, sine).astype(BF16)
    queries = turned[:, :QW] * jnp.asarray(0.125, BF16)
    kv_local = jnp.concatenate([turned[:, QW:], joined[:, QW + KVW :].astype(BF16)], axis=1)
    kv_all = lax.all_gather(kv_local, "seq", axis=0, tiled=True)
    cot_blocks = seq_gather(after(cotangent, kv_all), seq_size)
    row_place = jnp.arange(row_count, dtype=jnp.int32)
    high = my_seq * row_count + row_place
    low = high - positions
    place = jnp.arange(seq_size * row_count, dtype=jnp.int32)[:, None]
    low, high = low[None, :], high[None, :]
    split = PAIRS // 2 + 1
    spread = lambda block: ff_spread(block, fsdp_size)
    near_x = spread(after(near, kv_all))
    attn_one, lse_one = attend(
        low, high, place, after(queries, far), kv_all, 0, split
    )
    far_x = spread(after(far, kv_all))
    queries_two = after(queries, attn_one, cot_blocks[seq_size // 2], *near_x.values())
    attn_two, lse_two = attend(low, high, place, queries_two, kv_all, split, PAIRS - split)
    last_x = spread(last)
    for base, row in ((0, own_x), (inner, near_x), (2 * inner, far_x), (3 * inner, last_x)):
        ff_blocks.update({base + m: block for m, block in row.items()})
    attn_flat = jnp.concatenate([attn_one, attn_two], axis=1)

    out_list = [[out_blocks[o]] for o in offsets]
    out_list[0][0] = after(out_list[0][0], attn_one)
    out_full = join_both(me, out_list, out_weight.shape[0])[0].reshape(QW, -1)

    residual = inputs + dot(attn_flat, out_full, 1, 0)
    scale_two = rms_scale(residual)
    normed_two = (residual * scale_two * gain_two).astype(BF16)
    normed_blocks = {0: normed_two}
    bit = seq_size // 2
    while bit:
        if bit == 1:
            top = seq_size // 2
            normed_blocks[top] = after(normed_blocks[top], last, *far_x.values())
        normed_blocks.update(
            {o ^ bit: swap(b, "seq", seq_size, bit) for o, b in normed_blocks.items()}
        )
        bit //= 2
    (
        hidden, grad_gate, grad_up, kept, given, kept_layer, given_layer, normed_all, cot_all,
    ) = feed_forward(
        me,
        [ff_blocks[o] for o in range(fsdp_size)],
        [normed_blocks[o] for o in offsets],
        [cot_blocks[o] for o in offsets],
    )
    normed_all = normed_all.reshape(seq_size * row_count, -1)
    cot_all = cot_all.reshape(seq_size * row_count, -1)
    by_seq = lambda rows: rows.reshape(seq_size, row_count, -1)

    normed_sum = add(kept, swap(given, "seq", seq_size, 1))
    bit = 2
    while bit < seq_size:
        kept, given = halve(normed_sum, 1, my_seq // bit)
        got = swap(given, "seq", seq_size, bit)
        normed_sum = add(kept, got)
        bit *= 2
    normed_kept, normed_got = kept[0], got[0]
    layer_sum = add(kept_layer, swap(after(given_layer, given), "seq", seq_size, 1))
    kept_layer, given_layer = halve(layer_sum, 1, my_seq // 2)
    got_layer = swap(after(given_layer, normed_got), "seq", seq_size, 2)
    hidden = after(hidden, given)
    down_term = dot(hidden, cot_all, 0, 0).astype(BF16).reshape(fsdp_size, tall, -1)
    grad_gate, grad_up = after(grad_gate, down_term), after(grad_up, down_term)
    gate_term = dot(grad_gate, normed_all, 0, 0).astype(BF16).reshape(fsdp_size // 2, 2, tall, -1)
    up_term = dot(grad_up, normed_all, 0, 0).astype(BF16).reshape(fsdp_size // 2, 2, tall, -1)

    bits = list(reversed(fsdp_bits(fsdp_size)))

    def give(stack, at):
        kept, given = fsdp_halve(stack, fsdp_size, bits[at], my_fsdp, bits[:at])
        return kept, given

    def send(given, at):
        return swap(given, "fsdp", fsdp_size, bits[at])

    def finish(kept, got, at):
        stack = add(kept, got)
        for later in range(at + 1, len(bits)):
            kept, given = give(stack, later)
            stack = add(kept, send(given, later))
        return stack[0]

    kept_one, given = give(down_term, 0)
    got_one = send(given, 0)
    kept_two, given = give(jnp.concatenate([gate_term[:, 0], up_term[:, 0]], axis=0), 0)
    got_two = send(after(given, normed_got), 0)
    kept_three, given_three = give(jnp.concatenate([gate_term[:, 1], up_term[:, 1]], axis=0), 0)

    grad_residual, grad_branch, grad_attn, norm_two_term = residual_back(
        me, normed_kept, normed_got, residual, scale_two, gain_two, cotangent, out_full
    )
    grad_attn = after(grad_attn, gate_term, up_term, given_layer)
    dq_one, kv_terms = attend_back(
        low, high, place, queries, grad_attn, attn_one, lse_one, kv_all, 0, split, ()
    )
    got_one = after(got_one, dq_one)
    got_three = send(after(given_three, got_one), 0)
    kept_one, given_one = give(add(kept_one, got_one), 1)
    next_one = send(given_one, 1)
    queries_two = after(queries, kv_terms, given_one)
    dq_two, kv_terms = attend_back(
        low, high, place, queries_two, grad_attn, attn_two, lse_two, kv_all, split,
        PAIRS - split, (kv_terms,),
    )
    got_two = after(got_two, dq_two)
    kept_two, given = give(add(kept_two, got_two), 1)
    next_two = send(given, 1)
    kept, given = halve(after(by_seq(kv_terms), got_layer), 1, my_seq)
    kv_sum = add(kept, swap(given, "seq", seq_size, 1))
    bit = 2
    while bit < seq_size:
        kv_kept, given = halve(kv_sum, 1, my_seq // bit)
        given_kv = given
        kv_got = swap(given_kv, "seq", seq_size, bit)
        kv_sum = add(kv_kept, kv_got)
        bit *= 2
    kv_mine = kv_got

    attn_late = after(attn_flat, given_kv)
    out_term = stack_from_lanes(dot(attn_late, grad_branch, 0, 0).astype(BF16), seq_size)
    kept, given = halve(out_term, 1, my_seq)
    out_sum = add(kept, swap(given, "seq", seq_size, 1))
    grad_tokens, kept, given = joined_back(
        me, dq_one, dq_two, kv_kept[0], kv_got[0], cosine, sine, qkv_t, tokens, scale_one,
        gain_one, grad_residual, normed_one, norm_two_term, seq_size, fsdp_size,
    )

    got_three = after(got_three, grad_tokens)
    kept_three, given_last = give(add(kept_three, got_three), 1)
    next_three = send(given_last, 1)
    next_one, next_two = after(next_one, grad_tokens), after(next_two, grad_tokens)

    bit = 2
    while bit < seq_size:
        kept_out, given_out = halve(out_sum, 1, my_seq // bit)
        out_sum = add(kept_out, swap(after(given_out, kv_got), "seq", seq_size, bit))
        bit *= 2
    out_mine = out_sum[0].reshape(fsdp_size, -1, width)
    tail_sum = add(kept, swap(given, "seq", seq_size, 1))
    bit = 2
    while bit < seq_size:
        kept, given = halve(tail_sum, 1, my_seq // bit)
        tail_sum = add(kept, swap(given, "seq", seq_size, bit))
        bit *= 2
    tail_mine = tail_sum[0]
    down_sum = finish(kept_one, after(next_one, given), 1)
    layer_sum = add(kept_layer, got_layer)
    bit = 4
    while bit < seq_size:
        kept, given = halve(layer_sum, 1, my_seq // bit)
        layer_sum = add(kept, swap(given, "seq", seq_size, bit))
        bit *= 2
    layer_out = residual + layer_sum[0]
    one_sum = finish(kept_two, next_two, 1)
    two_sum = finish(kept_three, after(next_three, given), 1)

    ff_back = cut_lanes(me, (one_sum, two_sum, down_sum), seq_size)
    ff_got = [ff_back[0]] + [swap(ff_back[o], "seq", seq_size, o) for o in offsets if o]
    grad_gate_up, grad_down = join_ff(me, ff_got, strip)

    tail_sum = fsdp_scatter(
        after(jnp.concatenate([tail_mine, out_mine], axis=1), next_two),
        fsdp_size,
        my_fsdp,
        next_three,

    )
    lengths = [width * seq_size, QW + KVW, KVW, width * seq_size]
    pieces = [tail_sum[qkv_tall + i, : n // fsdp_size] for i, n in enumerate(lengths)]
    return (
        layer_out.astype(BF16),
        grad_tokens,
        pieces[0],
        tail_sum[:qkv_rows].T,
        pieces[1],
        pieces[2],
        tail_sum[qkv_tall + 16 :],
        pieces[3],
        grad_gate_up,
        grad_down,
    )


def solution(mesh):
    rows, both = P(("fsdp", "seq"), None), P(("fsdp", "seq"))
    return jax.shard_map(
        functools.partial(per_device, mesh.shape["seq"], mesh.shape["fsdp"]),
        mesh=mesh,
        in_specs=(
            rows, both, both, P("fsdp"), P("seq", "fsdp"), P("fsdp"), P("fsdp", "seq"),
            P("fsdp"), P("seq", "fsdp"), P("fsdp", "seq"), rows,
        ),
        out_specs=(
            rows, rows, P("fsdp"), P("seq", "fsdp"), P("fsdp"), P("fsdp"), P("fsdp", "seq"),
            P("fsdp"), P("seq", "fsdp"), P("fsdp", "seq"),
        ),
        check_vma=False,
    )
```
